32 devices in a mesh: parts: 2 (over x), ep: 8 (over z, y), mod: 2 (over core).
Axes of the slice: x: 2, y: 2, z: 4, core: 2. Of those that a mesh axis runs over, the one named last changes fastest.
Arguments:
- tokens: bfloat16 [2048, 4096], P(('parts', 'ep')), parts along dimension 0, may hold values from -6 to 6
- cotangent: bfloat16 [2048, 4096], P(('parts', 'ep')), parts along dimension 0, may hold values from -6 to 6
- modality: int32 [2048], P(('parts', 'ep')), parts along dimension 0, may hold values from 0 to 1, as said below
- picks: int32 [2048, 2], P(('parts', 'ep')), parts along dimension 0, may hold values from 0 to 3, as said below
- gate_weights: float32 [2048, 2], P(('parts', 'ep')), parts along dimension 0, may hold values from 0.2 to 1
- gate_proj: bfloat16 [2, 4096, 8192], P('mod', None, 'ep'), may hold values from -0.09375 to 0.09375
- up_proj: bfloat16 [2, 4096, 8192], P('mod', None, 'ep'), may hold values from -0.09375 to 0.09375
- down_proj: bfloat16 [2, 8192, 4096], P('mod', 'ep'), may hold values from -0.125 to 0.125
Outputs:
- token_grad: bfloat16 [2048, 4096], P(('parts', 'ep'), 'mod'), parts along dimension 0
- gate_grad: float32 [2048, 2], P(('parts', 'ep'), 'mod'), parts along dimension 0
The draws below stay inside these ranges and needn't reach their ends.
There are 2 independent parts, one for each index of `parts`. The reference program is written for one: setup_inputs(seed, part) draws one part's arguments, and reference() takes and returns one part's arrays. A program takes and returns all parts, laid end to end along the dimension named above; an argument that names none is the same for every part. Nothing has to cross between parts.
Inputs may be any that keep to these rules, and one draw needn't show every extreme that they name: `modality`: 0 marks a text token, 1 a vision token. The 2 picks of a token are different experts of its modality.
All inputs are finite; a program needn't handle non-finite values.
Results may differ from the reference program's by a relative error of at most 0.0057.
Values may be sent and summed in bfloat16 or wider, within the bound.
No kernel may reach another device: no remote copies, remote signals or barrier semaphores. Data moves between devices by JAX's collectives and lax.ppermute only.
A program may use at most 128 MiB of HBM per device.

```python
import jax
import jax.numpy as jnp
from jax import lax

D = 4096
FW = 2048
E_MOD = 4
TOPK = 2
TOK_DEV = 128
CAP = 16
TOKENS = 1024
N_EP = 8


def routing_tables(key):
    blocks = TOKENS // TOK_DEV
    subkeys = jax.random.split(key, 7)
    text_count = jax.random.randint(subkeys[0], (blocks, 1), CAP, TOK_DEV - CAP + 1)
    order_first = jax.vmap(lambda subkey: jax.random.permutation(subkey, TOK_DEV))(jax.random.split(subkeys[1], blocks))
    modal_ids = (order_first >= text_count).astype(jnp.int32)
    order_second = jax.vmap(lambda subkey: jax.random.permutation(subkey, TOK_DEV))(jax.random.split(subkeys[2], blocks))
    same_modal = modal_ids[:, :, None] == modal_ids[:, None, :]
    before = order_second[:, None, :] < order_second[:, :, None]
    rank_within = jnp.sum((same_modal & before).astype(jnp.int32), axis=2)
    modal_counts = jnp.concatenate([text_count, TOK_DEV - text_count], axis=1)
    hot_counts = jax.random.randint(subkeys[3], (blocks, 2), CAP, modal_counts + 1)
    hot_here = jnp.take_along_axis(hot_counts, modal_ids, axis=1)
    hot_expert = jax.random.randint(subkeys[4], (2,), 0, E_MOD)
    hot_of = hot_expert[modal_ids]
    offset = jax.random.randint(subkeys[5], (blocks, TOK_DEV), 1, E_MOD)
    first_pick = jnp.where(rank_within < hot_here, hot_of, (hot_of + offset) % E_MOD)
    token_keys = jax.random.split(subkeys[6], blocks * TOK_DEV)
    shuffled = jax.vmap(lambda subkey: jax.random.permutation(subkey, E_MOD - 1))(token_keys)
    shuffled = shuffled[:, :TOPK - 1].reshape(blocks, TOK_DEV, TOPK - 1)
    rest_picks = (first_pick[:, :, None] + 1 + shuffled) % E_MOD
    all_picks = jnp.concatenate([first_pick[:, :, None], rest_picks], axis=2)
    return (modal_ids.reshape(TOKENS).astype(jnp.int32), all_picks.reshape(TOKENS, TOPK).astype(jnp.int32))


def draw_modality(key, part):
    shared = routing_tables(key)
    return shared[0]


def draw_picks(key, part):
    shared = routing_tables(key)
    return shared[1]


def shard_levels(key, extent, cuts, least, top_value):
    level = 1.0
    for position, blocks in cuts:
        steps = jax.random.uniform(jax.random.fold_in(jax.random.fold_in(key, 6), position), (blocks,), jnp.float32, least / len(cuts), top_value / len(cuts))
        level = level * jnp.repeat(jnp.exp(steps), extent[position] // blocks).reshape((-1,) + (1,) * (len(extent) - 1 - position))
    return level


def scatter_about(stream_key, shape, scale, limit, pieces=(), kind=jnp.bfloat16):
    result = jax.random.normal(stream_key, shape, jnp.float32) * scale
    if len(pieces) > 0:
        result = shard_levels(stream_key, shape, pieces, -0.22, 0.18) * result
    return jnp.clip(result, min=-limit, max=limit).astype(kind)


def setup_inputs(seed: int = 0, part: int = 0) -> dict:
    arg_keys = jax.random.split(jax.random.key(seed), 9)
    own_keys = jax.random.split(jax.random.fold_in(arg_keys[8], part), 9)
    tokens = scatter_about(own_keys[0], (TOKENS, D), 1.0, 6.0, ((0, 8),))
    cotangent = scatter_about(own_keys[1], (TOKENS, D), 1.0, 6.0, ((0, 8),))
    modality = draw_modality(jax.random.fold_in(jax.random.fold_in(arg_keys[8], part), 71), part)
    picks = draw_picks(jax.random.fold_in(jax.random.fold_in(arg_keys[8], part), 71), part)
    gate_weights = jnp.clip(0.2 + 0.8 * jax.random.uniform(own_keys[4], (TOKENS, TOPK), jnp.float32) ** shard_levels(own_keys[4], (TOKENS, TOPK), ((0, 8),), -0.2, 0.2), 0.2, 1.0)
    gate_proj = scatter_about(arg_keys[5], (2, D, E_MOD * FW), D ** -0.5, 0.09375, ((0, 2), (2, 8)))
    up_proj = scatter_about(arg_keys[6], (2, D, E_MOD * FW), D ** -0.5, 0.09375, ((0, 2), (2, 8)))
    down_proj = scatter_about(arg_keys[7], (2, E_MOD * FW, D), FW ** -0.5, 0.125, ((0, 2), (1, 8)))
    return dict(tokens=tokens, cotangent=cotangent, modality=modality, picks=picks, gate_weights=gate_weights, gate_proj=gate_proj, up_proj=up_proj, down_proj=down_proj)


def piece_terms(token_rows, grad_rows, gate_piece, up_piece, down_piece):
    gate_pre = jnp.dot(token_rows, gate_piece, preferred_element_type=jnp.float32)
    up_pre = jnp.dot(token_rows, up_piece, preferred_element_type=jnp.float32)
    hidden_grad = jnp.dot(grad_rows, down_piece.T, preferred_element_type=jnp.float32)
    sigmoid_gate = jax.nn.sigmoid(gate_pre)
    activated = gate_pre * sigmoid_gate
    slope_term = sigmoid_gate * (1.0 + gate_pre * (1.0 - sigmoid_gate))
    part_gate = jnp.sum(activated * up_pre * hidden_grad, axis=1).astype(jnp.bfloat16)
    grad_gate_pre = (hidden_grad * up_pre * slope_term).astype(jnp.bfloat16)
    grad_up_pre = (hidden_grad * activated).astype(jnp.bfloat16)
    part_dx = jnp.dot(grad_gate_pre, gate_piece.T, preferred_element_type=jnp.float32)
    part_dx = part_dx + jnp.dot(grad_up_pre, up_piece.T, preferred_element_type=jnp.float32)
    return part_dx.astype(jnp.bfloat16), part_gate


def reference(tokens, cotangent, modality, picks, gate_weights, gate_proj, up_proj, down_proj):
    group_size = N_EP // E_MOD
    piece_width = FW // group_size
    pair_count = TOK_DEV * TOPK
    label = jnp.repeat(modality.reshape(N_EP, TOK_DEV), TOPK, axis=1) * E_MOD + picks.reshape(N_EP, pair_count)
    label = label.astype(jnp.int32)
    positions = jnp.arange(pair_count).astype(jnp.int32)
    earlier = positions[None, :] < positions[:, None]
    same_label = (label[:, :, None] == label[:, None, :]) & earlier[None, :, :]
    slot_index = jnp.sum(same_label.astype(jnp.int32), axis=2).astype(jnp.int32)
    kept_pairs = slot_index < CAP
    block_ids = jnp.arange(N_EP).astype(jnp.int32)
    token_of = (block_ids[:, None] * TOK_DEV + positions[None, :] // TOPK).astype(jnp.int32)
    slot_match = slot_index[:, :, None] == jnp.arange(CAP).astype(jnp.int32)[None, None, :]
    tables_dx = []
    tables_gate = []
    for modal in range(2):
        for expert in range(E_MOD):
            chosen = kept_pairs & (label == modal * E_MOD + expert)
            hits = (slot_match & chosen[:, :, None]).astype(jnp.int32)
            row_index = jnp.sum(hits * token_of[:, :, None], axis=1).reshape(-1).astype(jnp.int32)
            valid = (jnp.sum(hits, axis=1).reshape(-1) > 0)[:, None]
            token_rows = jnp.where(valid, tokens[row_index], 0)
            grad_rows = jnp.where(valid, cotangent[row_index], 0)
            gate_full = gate_proj[modal]
            up_full = up_proj[modal]
            down_full = down_proj[modal]

            def add_piece(member, totals):
                start = expert * FW + member * piece_width
                gate_piece = lax.dynamic_slice_in_dim(gate_full, start, piece_width, 1)
                up_piece = lax.dynamic_slice_in_dim(up_full, start, piece_width, 1)
                down_piece = lax.dynamic_slice_in_dim(down_full, start, piece_width, 0)
                part_dx, part_gate = piece_terms(token_rows, grad_rows, gate_piece, up_piece, down_piece)
                return (totals[0] + part_dx.astype(jnp.float32), totals[1] + part_gate.astype(jnp.float32))

            zeros_dx = jnp.zeros((N_EP * CAP, D), jnp.float32)
            zeros_gate = jnp.zeros((N_EP * CAP,), jnp.float32)
            sum_dx, sum_gate = lax.fori_loop(0, group_size, add_piece, (zeros_dx, zeros_gate))
            tables_dx.append(sum_dx)
            tables_gate.append(sum_gate)
    table_dx = jnp.stack(tables_dx).reshape(-1, D)
    table_gate = jnp.stack(tables_gate).reshape(-1)
    flat_index = label * (N_EP * CAP) + block_ids[:, None] * CAP + jnp.minimum(slot_index, CAP - 1)
    flat_index = flat_index.reshape(-1).astype(jnp.int32)
    kept_flat = kept_pairs.reshape(-1)
    weight = jnp.where(kept_flat, gate_weights.reshape(-1), 0.0)
    pair_dx = table_dx[flat_index] * weight[:, None]
    token_grad = jnp.sum(pair_dx.reshape(TOKENS, TOPK, D), axis=1).astype(jnp.bfloat16)
    gate_grad = jnp.where(kept_flat, table_gate[flat_index], 0.0).reshape(TOKENS, TOPK)
    return token_grad, gate_grad
```

```python
import functools

import jax
import jax.numpy as jnp
from jax import lax
from jax.experimental import pallas as pl
from jax.experimental.pallas import tpu as pltpu
from jax.sharding import PartitionSpec as P

E_MOD = 4
CAP = 16
EXT = 128
BF16 = jnp.bfloat16
F32 = jnp.float32
MIB = 1024 * 1024


def cost(flops, nbytes):
    return pl.CostEstimate(flops=flops, bytes_accessed=nbytes, transcendentals=0)


def whole(shape):
    return pl.BlockSpec(shape, lambda *_: (0,) * len(shape))


def nt_dot(lhs, rhs):
    return lax.dot_general(lhs, rhs, (((1,), (1,)), ((), ())), preferred_element_type=F32)


def slot_of_labels(ids_ref, modality_ref, picks_ref):
    tok_rows = modality_ref.shape[1]
    label = lax.broadcasted_iota(jnp.int32, (2 * E_MOD, tok_rows), 0)
    expert = jnp.bitwise_xor(label % E_MOD, ids_ref[0])
    modal = jnp.bitwise_xor(label // E_MOD, ids_ref[1])
    mine = modality_ref[...] == modal
    first = mine & (picks_ref[0:1, :] == expert)
    second = mine & (picks_ref[1:2, :] == expert)
    member = first | second
    row = lax.broadcasted_iota(jnp.int32, (tok_rows, tok_rows), 0)
    col = lax.broadcasted_iota(jnp.int32, (tok_rows, tok_rows), 1)
    earlier = (row < col).astype(F32)
    count = jnp.dot(member.astype(F32), earlier, preferred_element_type=F32).astype(jnp.int32)
    return count, first, second, member


def gather_kernel(ids_ref, modality_ref, picks_ref, rows_ref, *out_refs):
    count, _, _, member = slot_of_labels(ids_ref, modality_ref, picks_ref)
    slot = jnp.where(member, count, -1)
    tok_rows = slot.shape[1]
    want = lax.broadcasted_iota(jnp.int32, (CAP, tok_rows), 0)
    chosen = jnp.concatenate(
        [(slot[s : s + 1, :] == want).astype(F32) for s in range(E_MOD)], axis=0
    ).astype(BF16)
    picked = jnp.dot(chosen, rows_ref[...], preferred_element_type=F32).astype(BF16)
    for s in range(E_MOD):
        out_refs[s][...] = picked[s * CAP : (s + 1) * CAP, :]


def gather_slots(ids, modality, picks, rows):
    tok_rows, width = rows.shape
    chunk = width // 4
    return pl.pallas_call(
        gather_kernel,
        grid=(width // chunk,),
        in_specs=[
            pl.BlockSpec(memory_space=pltpu.SMEM),
            whole(modality.shape),
            whole(picks.shape),
            pl.BlockSpec((tok_rows, chunk), lambda i: (0, i)),
        ],
        out_specs=[pl.BlockSpec((CAP, chunk), lambda i: (0, i))] * E_MOD,
        out_shape=[jax.ShapeDtypeStruct((CAP, width), BF16)] * E_MOD,
        cost_estimate=cost(2 * E_MOD * CAP * tok_rows * width, 3 * tok_rows * width),
        name="gather_slots",
    )(ids, modality, picks, rows)


def pre_kernel(count, *refs):
    blocks, (gate_ref, up_ref, gate_out, up_out, rows) = refs[:count], refs[count:]

    @pl.when(pl.program_id(0) == 0)
    def _():
        for i in range(count):
            rows[i * CAP : (i + 1) * CAP, :] = blocks[i][...]

    gate_out[...] = jnp.dot(rows[...], gate_ref[0], preferred_element_type=F32)
    up_out[...] = jnp.dot(rows[...], up_ref[0], preferred_element_type=F32)


def pre_activations(blocks, gate_proj, up_proj):
    count = len(blocks)
    _, width, hidden = gate_proj.shape
    total = count * CAP
    chunk = min(256, hidden)
    weight = pl.BlockSpec((1, width, chunk), lambda i: (0, 0, i))
    out = pl.BlockSpec((total, chunk), lambda i: (0, i))
    return pl.pallas_call(
        functools.partial(pre_kernel, count),
        grid=(hidden // chunk,),
        in_specs=[whole((CAP, width))] * count + [weight] * 2,
        out_specs=[out] * 2,
        out_shape=[jax.ShapeDtypeStruct((total, hidden), F32)] * 2,
        scratch_shapes=[pltpu.VMEM((total, width), BF16)],
        compiler_params=pltpu.CompilerParams(vmem_limit_bytes=24 * MIB),
        cost_estimate=cost(4 * total * width * hidden, 4 * width * hidden),
        name="pre_activations",
    )(*blocks, gate_proj, up_proj)


def hidden_kernel(count, *refs):
    blocks = refs[:count]
    down_ref, gate_ref, up_ref, dgate_out, dup_out, part_out, rows, part = refs[count:]
    step = pl.program_id(0)

    @pl.when(step == 0)
    def _():
        for i in range(count):
            rows[i * CAP : (i + 1) * CAP, :] = blocks[i][...]
        part[...] = jnp.zeros_like(part)

    grad = nt_dot(rows[...], down_ref[...])
    gate_pre = gate_ref[...]
    up_pre = up_ref[...]
    sig = jax.nn.sigmoid(gate_pre)
    act = gate_pre * sig
    grad_act = grad * act
    part[...] += jnp.sum(grad_act * up_pre, axis=1, keepdims=True)
    dgate_out[...] = (grad * up_pre * (sig * (1.0 + gate_pre * (1.0 - sig)))).astype(BF16)
    dup_out[...] = grad_act.astype(BF16)

    @pl.when(step == pl.num_programs(0) - 1)
    def _():
        part_out[...] = two_terms(part[...])


def two_terms(value):
    high = value.astype(BF16).astype(F32)
    low = value - high
    lane = lax.broadcasted_iota(jnp.int32, (value.shape[0], EXT), 1)
    return jnp.where(lane == 0, high, jnp.where(lane == 1, low, 0.0)).astype(BF16)


def hidden_grads(blocks, down_piece, gate_pre, up_pre):
    count = len(blocks)
    hidden, width = down_piece.shape
    total = count * CAP
    chunk = min(256, hidden)
    tile = pl.BlockSpec((total, chunk), lambda i: (0, i))
    return pl.pallas_call(
        functools.partial(hidden_kernel, count),
        grid=(hidden // chunk,),
        in_specs=[whole((CAP, width))] * count
        + [pl.BlockSpec((chunk, width), lambda i: (i, 0)), tile, tile],
        out_specs=[tile, tile, whole((total, EXT))],
        out_shape=[jax.ShapeDtypeStruct((total, hidden), BF16)] * 2
        + [jax.ShapeDtypeStruct((total, EXT), BF16)],
        scratch_shapes=[pltpu.VMEM((total, width), BF16), pltpu.VMEM((total, 1), F32)],
        compiler_params=pltpu.CompilerParams(vmem_limit_bytes=24 * MIB),
        cost_estimate=cost(2 * total * width * hidden, 2 * width * hidden),
        name="hidden_grads",
    )(*blocks, down_piece, gate_pre, up_pre)


def back_kernel(groups, half_ref, dgate_ref, dup_ref, part_ref, gate_ref, up_ref, *outs):
    step = pl.program_id(0)
    chunk = gate_ref.shape[1]
    wide = outs[0].shape[1] - EXT
    own_rows = outs[0].shape[0]
    grad = nt_dot(dgate_ref[...], gate_ref[0]) + nt_dot(dup_ref[...], up_ref[0])
    grad = grad.astype(BF16)
    start = pl.multiple_of(step * chunk, chunk)
    for t in range(groups):
        outs[t][:, pl.ds(start, chunk)] = grad[t * own_rows : (t + 1) * own_rows, :]

    @pl.when(step == 0)
    def _():
        for t in range(groups):
            outs[t][:, wide:] = part_ref[t * own_rows : (t + 1) * own_rows, :]


def back_half(groups, half, dgate, dup, part, gate_proj, up_proj):
    _, width, hidden = gate_proj.shape
    total = dgate.shape[0]
    own_rows = total // groups
    wide = width // 2
    chunk = 512
    steps = wide // chunk
    weight = pl.BlockSpec((1, chunk, hidden), lambda i, half_ref: (0, half_ref[0] * steps + i, 0))
    shape = (own_rows, wide + EXT)
    return pl.pallas_call(
        functools.partial(back_kernel, groups),
        grid_spec=pltpu.PrefetchScalarGridSpec(
            num_scalar_prefetch=1,
            grid=(steps,),
            in_specs=[whole(dgate.shape), whole(dup.shape), whole(part.shape), weight, weight],
            out_specs=[whole(shape)] * groups,
        ),
        out_shape=[jax.ShapeDtypeStruct(shape, BF16)] * groups,
        compiler_params=pltpu.CompilerParams(vmem_limit_bytes=24 * MIB),
        cost_estimate=cost(4 * total * wide * hidden, 4 * wide * hidden),
        name="back_half",
    )(half, dgate, dup, part, gate_proj, up_proj)


def sum_kernel(groups, *refs):
    ins, outs = refs[:groups], refs[groups:]
    wide = ins[0].shape[1] - EXT
    for s in range(E_MOD):
        rows = slice(s * CAP, (s + 1) * CAP)
        total = ins[0][rows, :].astype(F32)
        for t in range(1, groups):
            total = total + ins[t][rows, :].astype(F32)
        outs[s][:, :wide] = total[:, :wide].astype(BF16)
        outs[s][:, wide:] = two_terms(jnp.sum(total[:, wide:], axis=1, keepdims=True))


def sum_pieces(partials):
    groups = len(partials)
    own_rows, wide = partials[0].shape
    return pl.pallas_call(
        functools.partial(sum_kernel, groups),
        out_shape=[jax.ShapeDtypeStruct((CAP, wide), BF16)] * E_MOD,
        cost_estimate=cost(own_rows * wide, 4 * groups * own_rows * wide),
        name="sum_pieces",
    )(*partials)


def combine_kernel(ids_ref, modality_ref, picks_ref, weights_ref, *refs):
    blocks, (grad_out, gate_out, table) = refs[: 2 * E_MOD], refs[2 * E_MOD :]
    wide = grad_out.shape[1]
    for i in range(2 * E_MOD):
        table[i * CAP : (i + 1) * CAP, :] = blocks[i][...]
    count, first, second, member = slot_of_labels(ids_ref, modality_ref, picks_ref)
    slot = jnp.where(member, count, -1)
    scale = jnp.where(first, weights_ref[0:1, :], jnp.where(second, weights_ref[1:2, :], 0.0))
    own = jnp.where(ids_ref[1] == 0, first.astype(F32), second.astype(F32))
    tok_rows = slot.shape[1]
    want = lax.broadcasted_iota(jnp.int32, (CAP, tok_rows), 0)
    mix = []
    gate = jnp.zeros((1, tok_rows), F32)
    for i in range(2 * E_MOD):
        hit = slot[i : i + 1, :] == want
        mix.append(jnp.where(hit, scale[i : i + 1, :], 0.0))
        part = jnp.sum(table[i * CAP : (i + 1) * CAP, wide:].astype(F32), axis=1, keepdims=True)
        gate = gate + jnp.sum(
            jnp.where(hit, own[i : i + 1, :] * part, 0.0), axis=0, keepdims=True
        )
    gate_out[...] = gate
    mix = jnp.concatenate(mix, axis=0).T
    high = mix.astype(BF16)
    low = (mix - high.astype(F32)).astype(BF16)
    values = table[:, :wide]
    total = jnp.dot(high, values, preferred_element_type=F32)
    total = total + jnp.dot(low, values, preferred_element_type=F32)
    grad_out[...] = total.astype(BF16)


def combine(ids, modality, picks, weights, blocks):
    tok_rows = modality.shape[1]
    wide = blocks[0].shape[1] - EXT
    count = len(blocks)
    vmem = pl.BlockSpec(memory_space=pltpu.VMEM)
    return pl.pallas_call(
        combine_kernel,
        in_specs=[pl.BlockSpec(memory_space=pltpu.SMEM)] + [vmem] * (3 + count),
        out_specs=[vmem] * 2,
        out_shape=[
            jax.ShapeDtypeStruct((tok_rows, wide), BF16),
            jax.ShapeDtypeStruct((1, tok_rows), F32),
        ],
        scratch_shapes=[pltpu.VMEM((count * CAP, wide + EXT), BF16)],
        cost_estimate=cost(4 * count * CAP * tok_rows * wide, 4 * tok_rows * wide),
        name="combine",
    )(ids, modality, picks, weights, *blocks)


def local(tokens, cotangent, modality, picks, gate_weights, gate_proj, up_proj, down_proj):
    device_count = lax.axis_size("ep")
    groups = device_count // E_MOD
    core = lax.axis_index("mod")
    expert = lax.axis_index("ep") // groups
    ids = jnp.stack([expert, core]).astype(jnp.int32)
    modality = modality.reshape(1, -1)
    picks = picks.T
    weights = gate_weights.T

    def to_expert(x, s):
        return lax.ppermute(
            x,
            "ep",
            [(e * groups + j, (e ^ s) * groups + j) for e in range(E_MOD) for j in range(groups)],
        )

    def to_piece(x, t):
        return lax.ppermute(
            x,
            "ep",
            [
                (e * groups + j, e * groups + (j + t) % groups)
                for e in range(E_MOD)
                for j in range(groups)
            ],
        )

    def to_source(x, s, flip):
        return lax.ppermute(
            x,
            ("ep", "mod"),
            [
                ((e * groups + j) * 2 + m, ((e ^ s) * groups + j) * 2 + (m ^ flip))
                for e in range(E_MOD)
                for j in range(groups)
                for m in range(2)
            ],
        )

    def spread(rows):
        sent = gather_slots(ids, modality, picks, rows)
        here = [sent[0]] + [to_expert(sent[s], s) for s in range(1, E_MOD)]
        return here + [to_piece(x, t) for t in range(1, groups) for x in here]

    token_blocks = spread(tokens)
    grad_blocks = spread(cotangent)
    gate_pre, up_pre = pre_activations(token_blocks, gate_proj, up_proj)
    dgate, dup, part = hidden_grads(grad_blocks, down_proj[0], gate_pre, up_pre)
    arrived = []
    for flip in (1, 0):
        half = (core ^ flip).astype(jnp.int32).reshape(1)
        partials = back_half(groups, half, dgate, dup, part, gate_proj, up_proj)
        partials = [partials[0]] + [to_piece(partials[t], groups - t) for t in range(1, groups)]
        sums = sum_pieces(partials)
        arrived.append(
            [sums[s] if s + flip == 0 else to_source(sums[s], s, flip) for s in range(E_MOD)]
        )
    token_grad, gate_grad = combine(ids, modality, picks, weights, arrived[1] + arrived[0])
    return token_grad, gate_grad.reshape(-1, 1)


def solution(mesh):
    in_specs = (
        P(("parts", "ep"), None),
        P(("parts", "ep"), None),
        P(("parts", "ep")),
        P(("parts", "ep"), None),
        P(("parts", "ep"), None),
        P("mod", None, "ep"),
        P("mod", None, "ep"),
        P("mod", "ep", None),
    )
    out_specs = (P(("parts", "ep"), "mod"), P(("parts", "ep"), "mod"))
    return jax.shard_map(local, mesh=mesh, in_specs=in_specs, out_specs=out_specs, check_vma=False)
```

```python
import functools

import jax
import jax.numpy as jnp
from jax import lax
from jax.experimental import pallas as pl
from jax.experimental.pallas import tpu as pltpu
from jax.sharding import PartitionSpec as P

E_MOD = 4
CAP = 16
EXT = 128
BF16 = jnp.bfloat16
F32 = jnp.float32
MIB = 1024 * 1024


def cost(flops, nbytes):
    return pl.CostEstimate(flops=flops, bytes_accessed=nbytes, transcendentals=0)


def whole(shape):
    return pl.BlockSpec(shape, lambda *_: (0,) * len(shape))


def nt_dot(lhs, rhs):
    return lax.dot_general(lhs, rhs, (((1,), (1,)), ((), ())), preferred_element_type=F32)


def slot_of_labels(ids_ref, modality_ref, picks_ref):
    tok_rows = modality_ref.shape[1]
    label = lax.broadcasted_iota(jnp.int32, (2 * E_MOD, tok_rows), 0)
    expert = jnp.bitwise_xor(label % E_MOD, ids_ref[0])
    modal = jnp.bitwise_xor(label // E_MOD, ids_ref[1])
    mine = modality_ref[...] == modal
    first = mine & (picks_ref[0:1, :] == expert)
    second = mine & (picks_ref[1:2, :] == expert)
    member = first | second
    row = lax.broadcasted_iota(jnp.int32, (tok_rows, tok_rows), 0)
    col = lax.broadcasted_iota(jnp.int32, (tok_rows, tok_rows), 1)
    earlier = (row < col).astype(F32)
    count = jnp.dot(member.astype(F32), earlier, preferred_element_type=F32).astype(jnp.int32)
    return count, first, second, member


def gather_kernel(ids_ref, modality_ref, picks_ref, rows_ref, grads_ref, *refs):
    outs, chosen = refs[:-1], refs[-1]

    @pl.when(pl.program_id(0) == 0)
    def _():
        count, _, _, member = slot_of_labels(ids_ref, modality_ref, picks_ref)
        slot = jnp.where(member, count, -1)
        want = lax.broadcasted_iota(jnp.int32, (CAP, slot.shape[1]), 0)
        for s in range(E_MOD):
            hit = (slot[s : s + 1, :] == want).astype(F32)
            chosen[s * CAP : (s + 1) * CAP, :] = hit.astype(BF16)

    both = [
        jnp.dot(chosen[...], ref[...], preferred_element_type=F32).astype(BF16)
        for ref in (rows_ref, grads_ref)
    ]
    for s in range(2):
        for a in range(2):
            outs[s][a * CAP : (a + 1) * CAP, :] = both[a][s * CAP : (s + 1) * CAP, :]
    for s in range(2, E_MOD):
        for a in range(2):
            outs[2 * s - 2 + a][...] = both[a][s * CAP : (s + 1) * CAP, :]


def gather_slots(ids, modality, picks, rows, grads):
    tok_rows, width = rows.shape
    chunk = width // 4
    heights = [2 * CAP] * 2 + [CAP] * (2 * E_MOD - 4)
    source = pl.BlockSpec((tok_rows, chunk), lambda i: (0, i))
    return pl.pallas_call(
        gather_kernel,
        grid=(width // chunk,),
        in_specs=[
            pl.BlockSpec(memory_space=pltpu.SMEM),
            whole(modality.shape),
            whole(picks.shape),
            source,
            source,
        ],
        out_specs=[pl.BlockSpec((h, chunk), lambda i: (0, i)) for h in heights],
        out_shape=[jax.ShapeDtypeStruct((h, width), BF16) for h in heights],
        scratch_shapes=[pltpu.VMEM((E_MOD * CAP, tok_rows), BF16)],
        compiler_params=pltpu.CompilerParams(vmem_limit_bytes=8 * MIB),
        cost_estimate=cost(4 * E_MOD * CAP * tok_rows * width, 6 * tok_rows * width),
        name="gather_slots",
    )(ids, modality, picks, rows, grads)


def load_kernel(parts, src, dst, sems):
    rows = src.shape[1] // parts
    copies = [
        pltpu.make_async_copy(
            src.at[:, pl.ds(i * rows, rows), :], dst.at[:, pl.ds(i * rows, rows), :], sems.at[i]
        )
        for i in range(parts)
    ]
    for copy in copies:
        copy.start()
    for copy in copies:
        copy.wait()


def load(weight):
    parts = 8
    return pl.pallas_call(
        functools.partial(load_kernel, parts),
        in_specs=[pl.BlockSpec(memory_space=pl.ANY)],
        out_specs=pl.BlockSpec(memory_space=pltpu.VMEM),
        out_shape=pltpu.VMEM(weight.shape, weight.dtype),
        scratch_shapes=[pltpu.SemaphoreType.DMA((parts,))],
        compiler_params=pltpu.CompilerParams(vmem_limit_bytes=MIB),
        cost_estimate=cost(0, 2 * weight.size * weight.dtype.itemsize),
        name="load",
    )(pltpu.with_memory_space_constraint(weight, pltpu.HBM))


def in_vmem(x):
    return pltpu.with_memory_space_constraint(x, pltpu.VMEM)


def fill(rows, refs, places):
    for i, (index, start) in enumerate(places):
        rows[i * CAP : (i + 1) * CAP, :] = refs[index][start : start + CAP, :]


def pre_kernel(count, places, *refs):
    blocks, (gate_ref, up_ref, act_out, slope_out, both_out, rows) = refs[:count], refs[count:]
    fill(rows, blocks, places)
    hidden = gate_ref.shape[2]
    chunk = min(256, hidden)
    for start in range(0, hidden, chunk):
        cols = slice(start, start + chunk)
        gate_pre = jnp.dot(rows[...], gate_ref[0, :, cols], preferred_element_type=F32)
        up_pre = jnp.dot(rows[...], up_ref[0, :, cols], preferred_element_type=F32)
        sig = jax.nn.sigmoid(gate_pre)
        act = gate_pre * sig
        act_out[:, cols] = act
        slope_out[:, cols] = up_pre * (sig * (1.0 + gate_pre * (1.0 - sig)))
        both_out[:, cols] = act * up_pre


def pre_activations(blocks, places, gate_piece, up_piece):
    count = len(blocks)
    _, width, hidden = gate_piece.shape
    total = len(places) * CAP
    vmem = pl.BlockSpec(memory_space=pltpu.VMEM)
    return pl.pallas_call(
        functools.partial(pre_kernel, count, places),
        in_specs=[vmem] * (count + 2),
        out_specs=[vmem] * 3,
        out_shape=[jax.ShapeDtypeStruct((total, hidden), F32)] * 3,
        scratch_shapes=[pltpu.VMEM((total, width), BF16)],
        compiler_params=pltpu.CompilerParams(vmem_limit_bytes=16 * MIB),
        cost_estimate=cost(4 * total * width * hidden, 4 * total * hidden),
        name="pre_activations",
    )(*blocks, in_vmem(gate_piece), in_vmem(up_piece))


def back_columns(groups, half, dgate_ref, dup_ref, part, gate_ref, up_ref, outs):
    wide = outs[0].shape[1] - EXT
    own_rows = outs[0].shape[0]
    chunk = 512
    for step in range(wide // chunk):
        rows = pl.ds(pl.multiple_of(half * wide + step * chunk, chunk), chunk)
        grad = nt_dot(dgate_ref[...], gate_ref[0, rows, :]) + nt_dot(dup_ref[...], up_ref[0, rows, :])
        grad = grad.astype(BF16)
        for t in range(groups):
            outs[t][:, step * chunk : (step + 1) * chunk] = grad[t * own_rows : (t + 1) * own_rows, :]
    for t in range(groups):
        outs[t][:, wide:] = part[t * own_rows : (t + 1) * own_rows, :]


def hidden_kernel(count, places, groups, half_ref, *refs):
    blocks = refs[:count]
    act_ref, slope_ref, both_ref, down_ref, gate_ref, up_ref = refs[count : count + 6]
    outs = refs[count + 6 : count + 6 + groups]
    dgate, dup, part_out, rows = refs[count + 6 + groups :]
    fill(rows, blocks, places)
    hidden = gate_ref.shape[2]
    chunk = min(256, hidden)
    part = jnp.zeros((rows.shape[0], 1), F32)
    for start in range(0, hidden, chunk):
        cols = slice(start, start + chunk)
        grad = nt_dot(rows[...], down_ref[0, cols, :])
        part = part + jnp.sum(grad * both_ref[:, cols], axis=1, keepdims=True)
        dgate[:, cols] = (grad * slope_ref[:, cols]).astype(BF16)
        dup[:, cols] = (grad * act_ref[:, cols]).astype(BF16)
    part_out[...] = two_terms(part)
    back_columns(groups, half_ref[0], dgate, dup, part_out[...], gate_ref, up_ref, outs)


def hidden_grads(blocks, places, groups, half, factors, down_piece, gate_piece, up_piece):
    count = len(blocks)
    _, width, hidden = gate_piece.shape
    total = len(places) * CAP
    shape = (total // groups, width // 2 + EXT)
    vmem = pl.BlockSpec(memory_space=pltpu.VMEM)
    smem = pl.BlockSpec(memory_space=pltpu.SMEM)
    out = pl.pallas_call(
        functools.partial(hidden_kernel, count, places, groups),
        in_specs=[smem] + [vmem] * (count + 6),
        out_specs=[vmem] * (groups + 3),
        out_shape=[jax.ShapeDtypeStruct(shape, BF16)] * groups
        + [jax.ShapeDtypeStruct((total, hidden), BF16)] * 2
        + [jax.ShapeDtypeStruct((total, EXT), BF16)],
        scratch_shapes=[pltpu.VMEM((total, width), BF16)],
        compiler_params=pltpu.CompilerParams(vmem_limit_bytes=16 * MIB),
        cost_estimate=cost(4 * total * width * hidden, 4 * total * hidden),
        name="hidden_grads",
    )(half, *blocks, *factors, in_vmem(down_piece), in_vmem(gate_piece), in_vmem(up_piece))
    return out[:groups], out[groups:]


def back_kernel(groups, half_ref, dgate_ref, dup_ref, part_ref, gate_ref, up_ref, *outs):
    back_columns(groups, half_ref[0], dgate_ref, dup_ref, part_ref[...], gate_ref, up_ref, outs)


def back_half(groups, half, dgate, dup, part, gate_piece, up_piece):
    _, width, hidden = gate_piece.shape
    total = dgate.shape[0]
    shape = (total // groups, width // 2 + EXT)
    vmem = pl.BlockSpec(memory_space=pltpu.VMEM)
    smem = pl.BlockSpec(memory_space=pltpu.SMEM)
    return pl.pallas_call(
        functools.partial(back_kernel, groups),
        in_specs=[smem] + [vmem] * 5,
        out_specs=[vmem] * groups,
        out_shape=[jax.ShapeDtypeStruct(shape, BF16)] * groups,
        compiler_params=pltpu.CompilerParams(vmem_limit_bytes=16 * MIB),
        cost_estimate=cost(2 * total * width * hidden, 4 * total * hidden),
        name="back_half",
    )(half, dgate, dup, part, in_vmem(gate_piece), in_vmem(up_piece))


def two_terms(value):
    high = value.astype(BF16).astype(F32)
    low = value - high
    lane = lax.broadcasted_iota(jnp.int32, (value.shape[0], EXT), 1)
    return jnp.where(lane == 0, high, jnp.where(lane == 1, low, 0.0)).astype(BF16)


def sum_kernel(groups, *refs):
    ins, outs = refs[:groups], refs[groups:]
    wide = ins[0].shape[1] - EXT
    for s in range(E_MOD):
        rows = slice(s * CAP, (s + 1) * CAP)
        total = ins[0][rows, :].astype(F32)
        for t in range(1, groups):
            total = total + ins[t][rows, :].astype(F32)
        outs[s][:, :wide] = total[:, :wide].astype(BF16)
        outs[s][:, wide:] = two_terms(jnp.sum(total[:, wide:], axis=1, keepdims=True))


def sum_pieces(partials):
    groups = len(partials)
    own_rows, wide = partials[0].shape
    return pl.pallas_call(
        functools.partial(sum_kernel, groups),
        out_shape=[jax.ShapeDtypeStruct((CAP, wide), BF16)] * E_MOD,
        cost_estimate=cost(own_rows * wide, 4 * groups * own_rows * wide),
        compiler_params=pltpu.CompilerParams(vmem_limit_bytes=8 * MIB),
        name="sum_pieces",
    )(*partials)


def combine_kernel(ids_ref, modality_ref, picks_ref, weights_ref, *refs):
    blocks, (grad_out, gate_out, table) = refs[: 2 * E_MOD], refs[2 * E_MOD :]
    wide = grad_out.shape[1]
    for i in range(2 * E_MOD):
        table[i * CAP : (i + 1) * CAP, :] = blocks[i][...]
    count, first, second, member = slot_of_labels(ids_ref, modality_ref, picks_ref)
    slot = jnp.where(member, count, -1)
    scale = jnp.where(first, weights_ref[0:1, :], jnp.where(second, weights_ref[1:2, :], 0.0))
    own = jnp.where(ids_ref[1] == 0, first.astype(F32), second.astype(F32))
    tok_rows = slot.shape[1]
    want = lax.broadcasted_iota(jnp.int32, (CAP, tok_rows), 0)
    mix = []
    gate = jnp.zeros((1, tok_rows), F32)
    for i in range(2 * E_MOD):
        hit = slot[i : i + 1, :] == want
        mix.append(jnp.where(hit, scale[i : i + 1, :], 0.0))
        part = jnp.sum(table[i * CAP : (i + 1) * CAP, wide:].astype(F32), axis=1, keepdims=True)
        gate = gate + jnp.sum(
            jnp.where(hit, own[i : i + 1, :] * part, 0.0), axis=0, keepdims=True
        )
    gate_out[...] = gate
    mix = jnp.concatenate(mix, axis=0).T
    high = mix.astype(BF16)
    low = (mix - high.astype(F32)).astype(BF16)
    values = table[:, :wide]
    total = jnp.dot(high, values, preferred_element_type=F32)
    total = total + jnp.dot(low, values, preferred_element_type=F32)
    grad_out[...] = total.astype(BF16)


def combine(ids, modality, picks, weights, blocks):
    tok_rows = modality.shape[1]
    wide = blocks[0].shape[1] - EXT
    count = len(blocks)
    vmem = pl.BlockSpec(memory_space=pltpu.VMEM)
    return pl.pallas_call(
        combine_kernel,
        in_specs=[pl.BlockSpec(memory_space=pltpu.SMEM)] + [vmem] * (3 + count),
        out_specs=[vmem] * 2,
        out_shape=[
            jax.ShapeDtypeStruct((tok_rows, wide), BF16),
            jax.ShapeDtypeStruct((1, tok_rows), F32),
        ],
        scratch_shapes=[pltpu.VMEM((count * CAP, wide + EXT), BF16)],
        cost_estimate=cost(4 * count * CAP * tok_rows * wide, 4 * tok_rows * wide),
        compiler_params=pltpu.CompilerParams(vmem_limit_bytes=16 * MIB),
        name="combine",
    )(ids, modality, picks, weights, *blocks)


def local(tokens, cotangent, modality, picks, gate_weights, gate_proj, up_proj, down_proj):
    device_count = lax.axis_size("ep")
    groups = device_count // E_MOD
    core = lax.axis_index("mod")
    expert = lax.axis_index("ep") // groups
    ids = jnp.stack([expert, core]).astype(jnp.int32)
    modality = modality.reshape(1, -1)
    picks = picks.T
    weights = gate_weights.T

    def to_expert(x, s):
        return lax.ppermute(
            x,
            "ep",
            [(e * groups + j, (e ^ s) * groups + j) for e in range(E_MOD) for j in range(groups)],
        )

    def to_piece(x, t):
        return lax.ppermute(
            x,
            "ep",
            [
                (e * groups + j, e * groups + (j + t) % groups)
                for e in range(E_MOD)
                for j in range(groups)
            ],
        )

    def to_source(x, s, flip):
        return lax.ppermute(
            x,
            ("ep", "mod"),
            [
                ((e * groups + j) * 2 + m, ((e ^ s) * groups + j) * 2 + (m ^ flip))
                for e in range(E_MOD)
                for j in range(groups)
                for m in range(2)
            ],
        )

    sent = gather_slots(ids, modality, picks, tokens, cotangent)
    gate_piece, up_piece, down_piece = load(gate_proj), load(up_proj), load(down_proj)
    near = [sent[0], to_expert(sent[1], 1)]
    far = [[to_expert(sent[2 * s - 2 + a], s) for s in range(2, E_MOD)] for a in range(2)]
    near_pieces = [[to_piece(x, t) for x in near] for t in range(1, groups)]
    blocks, places = [], []
    for a in range(2):
        far_pieces = [[to_piece(x, t) for x in far[a]] for t in range(1, groups)]
        use, where = [], []
        for two, others in zip([near] + near_pieces, [far[a]] + far_pieces):
            where += [(len(use), a * CAP), (len(use) + 1, a * CAP)]
            where += [(len(use) + 2 + i, 0) for i in range(len(others))]
            use += two + others
        blocks.append(use)
        places.append(tuple(where))
    factors = pre_activations(blocks[0], places[0], gate_piece, up_piece)
    halves = [(core ^ flip).astype(jnp.int32).reshape(1) for flip in range(2)]
    first, (dgate, dup, part) = hidden_grads(
        blocks[1], places[1], groups, halves[1], factors, down_piece, gate_piece, up_piece
    )
    arrived = []
    for flip in (1, 0):
        if flip:
            partials = first
        else:
            partials = back_half(groups, halves[0], dgate, dup, part, gate_piece, up_piece)
        partials = [partials[0]] + [to_piece(partials[t], groups - t) for t in range(1, groups)]
        sums = sum_pieces(partials)
        arrived.append(
            [sums[s] if s + flip == 0 else to_source(sums[s], s, flip) for s in range(E_MOD)]
        )
    token_grad, gate_grad = combine(ids, modality, picks, weights, arrived[1] + arrived[0])
    return token_grad, gate_grad.reshape(-1, 1)


def solution(mesh):
    in_specs = (
        P(("parts", "ep"), None),
        P(("parts", "ep"), None),
        P(("parts", "ep")),
        P(("parts", "ep"), None),
        P(("parts", "ep"), None),
        P("mod", None, "ep"),
        P("mod", None, "ep"),
        P("mod", "ep", None),
    )
    out_specs = (P(("parts", "ep"), "mod"), P(("parts", "ep"), "mod"))
    return jax.shard_map(local, mesh=mesh, in_specs=in_specs, out_specs=out_specs, check_vma=False)
```

```python
import functools

import jax
import jax.numpy as jnp
from jax import lax
from jax.experimental import pallas as pl
from jax.experimental.pallas import tpu as pltpu
from jax.sharding import PartitionSpec as P

E_MOD = 4
CAP = 16
EXT = 128
BF16 = jnp.bfloat16
F32 = jnp.float32
MIB = 1024 * 1024


def cost(flops, nbytes):
    return pl.CostEstimate(flops=flops, bytes_accessed=nbytes, transcendentals=0)


def whole(shape):
    return pl.BlockSpec(shape, lambda *_: (0,) * len(shape))


def nt_dot(lhs, rhs):
    return lax.dot_general(lhs, rhs, (((1,), (1,)), ((), ())), preferred_element_type=F32)


def slot_of_labels(ids_ref, modality_ref, picks_ref):
    tok_rows = modality_ref.shape[1]
    label = lax.broadcasted_iota(jnp.int32, (2 * E_MOD, tok_rows), 0)
    expert = jnp.bitwise_xor(label % E_MOD, ids_ref[0])
    modal = jnp.bitwise_xor(label // E_MOD, ids_ref[1])
    mine = modality_ref[...] == modal
    first = mine & (picks_ref[0:1, :] == expert)
    second = mine & (picks_ref[1:2, :] == expert)
    member = first | second
    row = lax.broadcasted_iota(jnp.int32, (tok_rows, tok_rows), 0)
    col = lax.broadcasted_iota(jnp.int32, (tok_rows, tok_rows), 1)
    earlier = (row < col).astype(F32)
    count = jnp.dot(member.astype(F32), earlier, preferred_element_type=F32).astype(jnp.int32)
    return count, first, second, member


def gather_kernel(ids_ref, modality_ref, picks_ref, rows_ref, grads_ref, *refs):
    outs, chosen = refs[:-1], refs[-1]

    @pl.when(pl.program_id(0) == 0)
    def _():
        count, _, _, member = slot_of_labels(ids_ref, modality_ref, picks_ref)
        slot = jnp.where(member, count, -1)
        want = lax.broadcasted_iota(jnp.int32, (CAP, slot.shape[1]), 0)
        for s in range(E_MOD):
            hit = (slot[s : s + 1, :] == want).astype(F32)
            chosen[s * CAP : (s + 1) * CAP, :] = hit.astype(BF16)

    both = [
        jnp.dot(chosen[...], ref[...], preferred_element_type=F32).astype(BF16)
        for ref in (rows_ref, grads_ref)
    ]
    for s in range(2):
        for a in range(2):
            outs[s][a * CAP : (a + 1) * CAP, :] = both[a][s * CAP : (s + 1) * CAP, :]
    for s in range(2, E_MOD):
        for a in range(2):
            outs[2 * s - 2 + a][...] = both[a][s * CAP : (s + 1) * CAP, :]


def gather_slots(ids, modality, picks, rows, grads):
    tok_rows, width = rows.shape
    chunk = width // 4
    heights = [2 * CAP] * 2 + [CAP] * (2 * E_MOD - 4)
    source = pl.BlockSpec((tok_rows, chunk), lambda i: (0, i))
    return pl.pallas_call(
        gather_kernel,
        grid=(width // chunk,),
        in_specs=[
            pl.BlockSpec(memory_space=pltpu.SMEM),
            whole(modality.shape),
            whole(picks.shape),
            source,
            source,
        ],
        out_specs=[pl.BlockSpec((h, chunk), lambda i: (0, i)) for h in heights],
        out_shape=[jax.ShapeDtypeStruct((h, width), BF16) for h in heights],
        scratch_shapes=[pltpu.VMEM((E_MOD * CAP, tok_rows), BF16)],
        compiler_params=pltpu.CompilerParams(vmem_limit_bytes=8 * MIB),
        cost_estimate=cost(4 * E_MOD * CAP * tok_rows * width, 6 * tok_rows * width),
        name="gather_slots",
    )(ids, in_hbm(modality), in_hbm(picks), in_hbm(rows), in_hbm(grads))


def load_kernel(parts, ties, src, *refs):
    dst, sems = refs[ties], refs[-1]
    rows = src.shape[1] // parts
    copies = [
        pltpu.make_async_copy(
            src.at[:, pl.ds(i * rows, rows), :], dst.at[:, pl.ds(i * rows, rows), :], sems.at[i]
        )
        for i in range(parts)
    ]
    for copy in copies:
        copy.start()
    for copy in copies:
        copy.wait()


def load(weight, after, through=()):
    parts = 8
    place = pl.BlockSpec(memory_space=pl.ANY)
    ties = len(after) + len(through)
    return pl.pallas_call(
        functools.partial(load_kernel, parts, ties),
        in_specs=[place] * (1 + ties),
        out_specs=[pl.BlockSpec(memory_space=pltpu.VMEM)] + [place] * len(through),
        out_shape=[pltpu.VMEM(weight.shape, weight.dtype)]
        + [jax.ShapeDtypeStruct(tie.shape, tie.dtype) for tie in through],
        input_output_aliases={1 + len(after) + i: 1 + i for i in range(len(through))},
        scratch_shapes=[pltpu.SemaphoreType.DMA((parts,))],
        compiler_params=pltpu.CompilerParams(vmem_limit_bytes=MIB),
        cost_estimate=cost(0, 1024),
        name="load",
    )(in_hbm(weight), *after, *through)


def join_kernel(count, *refs):
    blocks, out = refs[:count], refs[-1]
    start = 0
    for block in blocks:
        out[start : start + block.shape[0], :] = block[...]
        start += block.shape[0]


def join_and_pass_kernel(count, through, *refs):
    join_kernel(count, *refs[:count], refs[count + through])


def join(blocks, through=()):
    count = len(blocks)
    total = sum(block.shape[0] for block in blocks)
    vmem = pl.BlockSpec(memory_space=pltpu.VMEM)
    ties = [pl.BlockSpec(memory_space=pl.ANY)] * len(through)
    return pl.pallas_call(
        functools.partial(join_and_pass_kernel, count, len(through)),
        in_specs=[vmem] * count + ties,
        out_specs=[vmem] + ties,
        out_shape=[jax.ShapeDtypeStruct((total, blocks[0].shape[1]), BF16)]
        + [jax.ShapeDtypeStruct(tie.shape, tie.dtype) for tie in through],
        input_output_aliases={count + i: 1 + i for i in range(len(through))},
        compiler_params=pltpu.CompilerParams(vmem_limit_bytes=8 * MIB),
        cost_estimate=cost(0, 1024),
        name="join",
    )(*blocks, *through)


def in_hbm(x):
    return pltpu.with_memory_space_constraint(x, pltpu.HBM)


def in_vmem(x):
    return pltpu.with_memory_space_constraint(x, pltpu.VMEM)


def fill(rows, refs, places):
    for i, (index, start) in enumerate(places):
        rows[i * CAP : (i + 1) * CAP, :] = refs[index][start : start + CAP, :]


def pre_kernel(count, places, *refs):
    blocks, (gate_ref, up_ref, act_out, slope_out, both_out, rows) = refs[:count], refs[count:]
    fill(rows, blocks, places)
    hidden = gate_ref.shape[2]
    chunk = min(256, hidden)
    for start in range(0, hidden, chunk):
        cols = slice(start, start + chunk)
        gate_pre = jnp.dot(rows[...], gate_ref[0, :, cols], preferred_element_type=F32)
        up_pre = jnp.dot(rows[...], up_ref[0, :, cols], preferred_element_type=F32)
        sig = jax.nn.sigmoid(gate_pre)
        act = gate_pre * sig
        act_out[:, cols] = act
        slope_out[:, cols] = up_pre * (sig * (1.0 + gate_pre * (1.0 - sig)))
        both_out[:, cols] = act * up_pre


def pre_activations(blocks, places, gate_piece, up_piece):
    count = len(blocks)
    _, width, hidden = gate_piece.shape
    total = len(places) * CAP
    vmem = pl.BlockSpec(memory_space=pltpu.VMEM)
    return pl.pallas_call(
        functools.partial(pre_kernel, count, places),
        in_specs=[vmem] * (count + 2),
        out_specs=[vmem] * 3,
        out_shape=[jax.ShapeDtypeStruct((total, hidden), F32)] * 3,
        scratch_shapes=[pltpu.VMEM((total, width), BF16)],
        compiler_params=pltpu.CompilerParams(vmem_limit_bytes=16 * MIB),
        cost_estimate=cost(1024, 1024),
        name="pre_activations",
    )(*blocks, in_vmem(gate_piece), in_vmem(up_piece))


def back_columns(groups, half, dgate_ref, dup_ref, part, gate_ref, up_ref, outs):
    wide = outs[0].shape[1] - EXT
    own_rows = outs[0].shape[0]
    chunk = 512
    for step in range(wide // chunk):
        rows = pl.ds(pl.multiple_of(half * wide + step * chunk, chunk), chunk)
        grad = nt_dot(dgate_ref[...], gate_ref[0, rows, :]) + nt_dot(dup_ref[...], up_ref[0, rows, :])
        grad = grad.astype(BF16)
        for t in range(groups):
            outs[t][:, step * chunk : (step + 1) * chunk] = grad[t * own_rows : (t + 1) * own_rows, :]
    for t in range(groups):
        outs[t][:, wide:] = part[t * own_rows : (t + 1) * own_rows, :]


def hidden_kernel(count, places, groups, half_ref, *refs):
    blocks = refs[:count]
    act_ref, slope_ref, both_ref, down_ref, gate_ref, up_ref = refs[count : count + 6]
    outs = refs[count + 6 : count + 6 + groups]
    dgate, dup, part_out, rows = refs[count + 6 + groups :]
    fill(rows, blocks, places)
    hidden = gate_ref.shape[2]
    chunk = min(256, hidden)
    part = jnp.zeros((rows.shape[0], 1), F32)
    for start in range(0, hidden, chunk):
        cols = slice(start, start + chunk)
        grad = nt_dot(rows[...], down_ref[0, cols, :])
        part = part + jnp.sum(grad * both_ref[:, cols], axis=1, keepdims=True)
        dgate[:, cols] = (grad * slope_ref[:, cols]).astype(BF16)
        dup[:, cols] = (grad * act_ref[:, cols]).astype(BF16)
    part_out[...] = two_terms(part)
    back_columns(groups, half_ref[0], dgate, dup, part_out[...], gate_ref, up_ref, outs)


def hidden_grads(blocks, places, groups, half, factors, down_piece, gate_piece, up_piece):
    count = len(blocks)
    _, width, hidden = gate_piece.shape
    total = len(places) * CAP
    shape = (total // groups, width // 2 + EXT)
    vmem = pl.BlockSpec(memory_space=pltpu.VMEM)
    smem = pl.BlockSpec(memory_space=pltpu.SMEM)
    out = pl.pallas_call(
        functools.partial(hidden_kernel, count, places, groups),
        in_specs=[smem] + [vmem] * (count + 6),
        out_specs=[vmem] * (groups + 3),
        out_shape=[jax.ShapeDtypeStruct(shape, BF16)] * groups
        + [jax.ShapeDtypeStruct((total, hidden), BF16)] * 2
        + [jax.ShapeDtypeStruct((total, EXT), BF16)],
        scratch_shapes=[pltpu.VMEM((total, width), BF16)],
        compiler_params=pltpu.CompilerParams(vmem_limit_bytes=16 * MIB),
        cost_estimate=cost(4 * total * width * hidden, 4 * width * hidden),
        name="hidden_grads",
    )(half, *blocks, *factors, in_vmem(down_piece), in_vmem(gate_piece), in_vmem(up_piece))
    return out[:groups], out[groups:]


def back_kernel(groups, half_ref, dgate_ref, dup_ref, part_ref, gate_ref, up_ref, *outs):
    back_columns(groups, half_ref[0], dgate_ref, dup_ref, part_ref[...], gate_ref, up_ref, outs)


def back_half(groups, half, dgate, dup, part, gate_piece, up_piece):
    _, width, hidden = gate_piece.shape
    total = dgate.shape[0]
    shape = (total // groups, width // 2 + EXT)
    vmem = pl.BlockSpec(memory_space=pltpu.VMEM)
    smem = pl.BlockSpec(memory_space=pltpu.SMEM)
    return pl.pallas_call(
        functools.partial(back_kernel, groups),
        in_specs=[smem] + [vmem] * 5,
        out_specs=[vmem] * groups,
        out_shape=[jax.ShapeDtypeStruct(shape, BF16)] * groups,
        compiler_params=pltpu.CompilerParams(vmem_limit_bytes=16 * MIB),
        cost_estimate=cost(2 * total * width * hidden, 2 * width * hidden),
        name="back_half",
    )(half, dgate, dup, part, in_vmem(gate_piece), in_vmem(up_piece))


def two_terms(value):
    high = value.astype(BF16).astype(F32)
    low = value - high
    lane = lax.broadcasted_iota(jnp.int32, (value.shape[0], EXT), 1)
    return jnp.where(lane == 0, high, jnp.where(lane == 1, low, 0.0)).astype(BF16)


def sum_kernel(groups, *refs):
    ins, outs = refs[:groups], refs[groups:]
    wide = ins[0].shape[1] - EXT
    for s in range(E_MOD):
        rows = slice(s * CAP, (s + 1) * CAP)
        total = ins[0][rows, :].astype(F32)
        for t in range(1, groups):
            total = total + ins[t][rows, :].astype(F32)
        outs[s][:, :wide] = total[:, :wide].astype(BF16)
        outs[s][:, wide:] = two_terms(jnp.sum(total[:, wide:], axis=1, keepdims=True))


def sum_pieces(partials):
    groups = len(partials)
    own_rows, wide = partials[0].shape
    return pl.pallas_call(
        functools.partial(sum_kernel, groups),
        out_shape=[jax.ShapeDtypeStruct((CAP, wide), BF16)] * E_MOD,
        cost_estimate=cost(own_rows * wide, 4 * groups * own_rows * wide),
        compiler_params=pltpu.CompilerParams(vmem_limit_bytes=8 * MIB),
        name="sum_pieces",
    )(*partials)


def combine_kernel(ids_ref, modality_ref, picks_ref, weights_ref, *refs):
    blocks, (grad_out, gate_out, table) = refs[: 2 * E_MOD], refs[2 * E_MOD :]
    wide = grad_out.shape[1]
    for i in range(2 * E_MOD):
        table[i * CAP : (i + 1) * CAP, :] = blocks[i][...]
    count, first, second, member = slot_of_labels(ids_ref, modality_ref, picks_ref)
    slot = jnp.where(member, count, -1)
    scale = jnp.where(first, weights_ref[0:1, :], jnp.where(second, weights_ref[1:2, :], 0.0))
    own = jnp.where(ids_ref[1] == 0, first.astype(F32), second.astype(F32))
    tok_rows = slot.shape[1]
    want = lax.broadcasted_iota(jnp.int32, (CAP, tok_rows), 0)
    mix = []
    gate = jnp.zeros((1, tok_rows), F32)
    for i in range(2 * E_MOD):
        hit = slot[i : i + 1, :] == want
        mix.append(jnp.where(hit, scale[i : i + 1, :], 0.0))
        part = jnp.sum(table[i * CAP : (i + 1) * CAP, wide:].astype(F32), axis=1, keepdims=True)
        gate = gate + jnp.sum(
            jnp.where(hit, own[i : i + 1, :] * part, 0.0), axis=0, keepdims=True
        )
    gate_out[...] = gate
    mix = jnp.concatenate(mix, axis=0).T
    high = mix.astype(BF16)
    low = (mix - high.astype(F32)).astype(BF16)
    values = table[:, :wide]
    total = jnp.dot(high, values, preferred_element_type=F32)
    total = total + jnp.dot(low, values, preferred_element_type=F32)
    grad_out[...] = total.astype(BF16)


def combine(ids, modality, picks, weights, blocks):
    tok_rows = modality.shape[1]
    wide = blocks[0].shape[1] - EXT
    count = len(blocks)
    vmem = pl.BlockSpec(memory_space=pltpu.VMEM)
    return pl.pallas_call(
        combine_kernel,
        in_specs=[pl.BlockSpec(memory_space=pltpu.SMEM)] + [vmem] * (3 + count),
        out_specs=[vmem] * 2,
        out_shape=[
            jax.ShapeDtypeStruct((tok_rows, wide), BF16),
            jax.ShapeDtypeStruct((1, tok_rows), F32),
        ],
        scratch_shapes=[pltpu.VMEM((count * CAP, wide + EXT), BF16)],
        cost_estimate=cost(4 * count * CAP * tok_rows * wide, 4 * tok_rows * wide),
        compiler_params=pltpu.CompilerParams(vmem_limit_bytes=16 * MIB),
        name="combine",
    )(ids, modality, picks, weights, *blocks)


def local(tokens, cotangent, modality, picks, gate_weights, gate_proj, up_proj, down_proj):
    device_count = lax.axis_size("ep")
    groups = device_count // E_MOD
    core = lax.axis_index("mod")
    expert = lax.axis_index("ep") // groups
    ids = jnp.stack([expert, core]).astype(jnp.int32)
    modality = modality.reshape(1, -1)
    picks = picks.T
    weights = gate_weights.T

    def to_expert(x, s, t=0):
        return lax.ppermute(
            x,
            "ep",
            [
                (e * groups + j, (e ^ s) * groups + (j + t) % groups)
                for e in range(E_MOD)
                for j in range(groups)
            ],
        )

    def to_piece(x, t):
        return to_expert(x, 0, t)

    def to_source(x, s, flip):
        return lax.ppermute(
            x,
            ("ep", "mod"),
            [
                ((e * groups + j) * 2 + m, ((e ^ s) * groups + j) * 2 + (m ^ flip))
                for e in range(E_MOD)
                for j in range(groups)
                for m in range(2)
            ],
        )

    sent = gather_slots(ids, modality, picks, tokens, cotangent)
    far = [[to_expert(sent[2 * s - 2], s) for s in range(2, E_MOD)]]
    near = to_expert(sent[1], 1)
    gate_piece, own = load(gate_proj, [], sent[:1])
    (near,) = join([own, near])
    near = [near] + [to_piece(near, t) for t in range(1, groups)]
    far[0], *later = join(far[0], [sent[2 * s - 1] for s in range(2, E_MOD)])
    far.append([to_expert(x, s) for x, s in zip(later, range(2, E_MOD))])
    up_piece, far[0] = load(up_proj, [], [far[0]])
    far[0] = [far[0]] + [to_piece(far[0], t) for t in range(1, groups)]
    (far[1],) = join(far[1])
    (down_piece,) = load(down_proj, [far[1]])
    far[1] = [far[1]] + [to_piece(far[1], t) for t in range(1, groups)]
    blocks = [near + far[a] for a in range(2)]
    places = [
        tuple(
            place
            for t in range(groups)
            for place in [(t, a * CAP), (t, (2 + a) * CAP)]
            + [(groups + t, i * CAP) for i in range(E_MOD - 2)]
        )
        for a in range(2)
    ]
    factors = pre_activations(blocks[0], places[0], gate_piece, up_piece)
    halves = [(core ^ flip).astype(jnp.int32).reshape(1) for flip in range(2)]
    first, (dgate, dup, part) = hidden_grads(
        blocks[1], places[1], groups, halves[1], factors, down_piece, gate_piece, up_piece
    )
    arrived = []
    for flip in (1, 0):
        if flip:
            partials = first
        else:
            partials = back_half(groups, halves[0], dgate, dup, part, gate_piece, up_piece)
        partials = [partials[0]] + [to_piece(partials[t], groups - t) for t in range(1, groups)]
        sums = sum_pieces(partials)
        arrived.append(
            [sums[s] if s + flip == 0 else to_source(sums[s], s, flip) for s in range(E_MOD)]
        )
    token_grad, gate_grad = combine(ids, modality, picks, weights, arrived[1] + arrived[0])
    return token_grad, gate_grad.reshape(-1, 1)


def solution(mesh):
    in_specs = (
        P(("parts", "ep"), None),
        P(("parts", "ep"), None),
        P(("parts", "ep")),
        P(("parts", "ep"), None),
        P(("parts", "ep"), None),
        P("mod", None, "ep"),
        P("mod", None, "ep"),
        P("mod", "ep", None),
    )
    out_specs = (P(("parts", "ep"), "mod"), P(("parts", "ep"), "mod"))
    return jax.shard_map(local, mesh=mesh, in_specs=in_specs, out_specs=out_specs, check_vma=False)
```

```python
import functools

import jax
import jax.numpy as jnp
from jax import lax
from jax.experimental import pallas as pl
from jax.experimental.pallas import tpu as pltpu
from jax.sharding import PartitionSpec as P

E_MOD = 4
CAP = 16
EXT = 128
BF16 = jnp.bfloat16
F32 = jnp.float32
MIB = 1024 * 1024
SCOPED = 16 * MIB


def cost(flops, nbytes):
    return pl.CostEstimate(flops=flops, bytes_accessed=nbytes, transcendentals=0)


def whole(shape):
    return pl.BlockSpec(shape, lambda *_: (0,) * len(shape))


def nt_dot(lhs, rhs):
    return lax.dot_general(lhs, rhs, (((1,), (1,)), ((), ())), preferred_element_type=F32)


def slot_of_labels(ids_ref, modality_ref, picks_ref):
    tok_rows = modality_ref.shape[1]
    label = lax.broadcasted_iota(jnp.int32, (2 * E_MOD, tok_rows), 0)
    expert = jnp.bitwise_xor(label % E_MOD, ids_ref[0])
    modal = jnp.bitwise_xor(label // E_MOD, ids_ref[1])
    mine = modality_ref[...] == modal
    first = mine & (picks_ref[0:1, :] == expert)
    second = mine & (picks_ref[1:2, :] == expert)
    member = first | second
    row = lax.broadcasted_iota(jnp.int32, (tok_rows, tok_rows), 0)
    col = lax.broadcasted_iota(jnp.int32, (tok_rows, tok_rows), 1)
    earlier = (row < col).astype(F32)
    count = jnp.dot(member.astype(F32), earlier, preferred_element_type=F32).astype(jnp.int32)
    return count, first, second, member


def gather_kernel(ids_ref, modality_ref, picks_ref, rows_ref, grads_ref, *refs):
    outs, chosen = refs[:-1], refs[-1]

    @pl.when(pl.program_id(0) == 0)
    def _():
        count, _, _, member = slot_of_labels(ids_ref, modality_ref, picks_ref)
        slot = jnp.where(member, count, -1)
        want = lax.broadcasted_iota(jnp.int32, (CAP, slot.shape[1]), 0)
        for s in range(E_MOD):
            hit = (slot[s : s + 1, :] == want).astype(F32)
            chosen[s * CAP : (s + 1) * CAP, :] = hit.astype(BF16)

    both = [
        jnp.dot(chosen[...], ref[...], preferred_element_type=F32).astype(BF16)
        for ref in (rows_ref, grads_ref)
    ]
    for s in range(2):
        for a in range(2):
            outs[s][a * CAP : (a + 1) * CAP, :] = both[a][s * CAP : (s + 1) * CAP, :]
    for s in range(2, E_MOD):
        for a in range(2):
            outs[2 * s - 2 + a][...] = both[a][s * CAP : (s + 1) * CAP, :]


def gather_slots(ids, modality, picks, rows, grads):
    tok_rows, width = rows.shape
    chunk = width // 4
    heights = [2 * CAP] * 2 + [CAP] * (2 * E_MOD - 4)
    source = pl.BlockSpec((tok_rows, chunk), lambda i: (0, i))
    return pl.pallas_call(
        gather_kernel,
        grid=(width // chunk,),
        in_specs=[
            pl.BlockSpec(memory_space=pltpu.SMEM),
            whole(modality.shape),
            whole(picks.shape),
            source,
            source,
        ],
        out_specs=[pl.BlockSpec((h, chunk), lambda i: (0, i)) for h in heights],
        out_shape=[jax.ShapeDtypeStruct((h, width), BF16) for h in heights],
        scratch_shapes=[pltpu.VMEM((E_MOD * CAP, tok_rows), BF16)],
        compiler_params=pltpu.CompilerParams(vmem_limit_bytes=SCOPED),
        cost_estimate=cost(4 * E_MOD * CAP * tok_rows * width, 6 * tok_rows * width),
        name="gather_slots",
    )(ids, in_hbm(modality), in_hbm(picks), in_hbm(rows), in_hbm(grads))


def load_kernel(parts, ties, src, *refs):
    dst, sems = refs[ties], refs[-1]
    rows = src.shape[1] // parts
    copies = [
        pltpu.make_async_copy(
            src.at[:, pl.ds(i * rows, rows), :], dst.at[:, pl.ds(i * rows, rows), :], sems.at[i]
        )
        for i in range(parts)
    ]
    for copy in copies:
        copy.start()
    for copy in copies:
        copy.wait()


def load(weight, after, through=()):
    parts = 8
    place = pl.BlockSpec(memory_space=pl.ANY)
    ties = len(after) + len(through)
    return pl.pallas_call(
        functools.partial(load_kernel, parts, ties),
        in_specs=[place] * (1 + ties),
        out_specs=[pl.BlockSpec(memory_space=pltpu.VMEM)] + [place] * len(through),
        out_shape=[pltpu.VMEM(weight.shape, weight.dtype)]
        + [jax.ShapeDtypeStruct(tie.shape, tie.dtype) for tie in through],
        input_output_aliases={1 + len(after) + i: 1 + i for i in range(len(through))},
        scratch_shapes=[pltpu.SemaphoreType.DMA((parts,))],
        compiler_params=pltpu.CompilerParams(vmem_limit_bytes=SCOPED),
        cost_estimate=cost(0, 1024),
        name="load",
    )(in_hbm(weight), *after, *through)


def join_kernel(count, *refs):
    blocks, out = refs[:count], refs[-1]
    start = 0
    for block in blocks:
        out[start : start + block.shape[0], :] = block[...]
        start += block.shape[0]


def join_and_pass_kernel(count, through, *refs):
    join_kernel(count, *refs[:count], refs[count + through])


def join(blocks, through=()):
    count = len(blocks)
    total = sum(block.shape[0] for block in blocks)
    vmem = pl.BlockSpec(memory_space=pltpu.VMEM)
    ties = [pl.BlockSpec(memory_space=pl.ANY)] * len(through)
    return pl.pallas_call(
        functools.partial(join_and_pass_kernel, count, len(through)),
        in_specs=[vmem] * count + ties,
        out_specs=[vmem] + ties,
        out_shape=[jax.ShapeDtypeStruct((total, blocks[0].shape[1]), BF16)]
        + [jax.ShapeDtypeStruct(tie.shape, tie.dtype) for tie in through],
        input_output_aliases={count + i: 1 + i for i in range(len(through))},
        compiler_params=pltpu.CompilerParams(vmem_limit_bytes=SCOPED),
        cost_estimate=cost(0, 1024),
        name="join",
    )(*blocks, *through)


def in_hbm(x):
    return pltpu.with_memory_space_constraint(x, pltpu.HBM)


def in_vmem(x):
    return pltpu.with_memory_space_constraint(x, pltpu.VMEM)


def fill(rows, refs, places):
    for i, (index, start) in enumerate(places):
        rows[i * CAP : (i + 1) * CAP, :] = refs[index][start : start + CAP, :]


def pre_kernel(count, places, *refs):
    blocks, (gate_ref, up_ref, act_out, slope_out, both_out, rows) = refs[:count], refs[count:]
    fill(rows, blocks, places)
    hidden = gate_ref.shape[2]
    chunk = min(256, hidden)
    for start in range(0, hidden, chunk):
        cols = slice(start, start + chunk)
        gate_pre = jnp.dot(rows[...], gate_ref[0, :, cols], preferred_element_type=F32)
        up_pre = jnp.dot(rows[...], up_ref[0, :, cols], preferred_element_type=F32)
        sig = jax.nn.sigmoid(gate_pre)
        act = gate_pre * sig
        act_out[:, cols] = act
        slope_out[:, cols] = up_pre * (sig * (1.0 + gate_pre * (1.0 - sig)))
        both_out[:, cols] = act * up_pre


def pre_activations(blocks, places, gate_piece, up_piece):
    count = len(blocks)
    _, width, hidden = gate_piece.shape
    total = len(places) * CAP
    vmem = pl.BlockSpec(memory_space=pltpu.VMEM)
    return pl.pallas_call(
        functools.partial(pre_kernel, count, places),
        in_specs=[vmem] * (count + 2),
        out_specs=[vmem] * 3,
        out_shape=[jax.ShapeDtypeStruct((total, hidden), F32)] * 3,
        scratch_shapes=[pltpu.VMEM((total, width), BF16)],
        compiler_params=pltpu.CompilerParams(vmem_limit_bytes=SCOPED),
        cost_estimate=cost(1024, 1024),
        name="pre_activations",
    )(*blocks, in_vmem(gate_piece), in_vmem(up_piece))


def back_columns(groups, half, dgate_ref, dup_ref, part, gate_ref, up_ref, outs):
    wide = outs[0].shape[1] - EXT
    own_rows = outs[0].shape[0]
    chunk = 512
    for step in range(wide // chunk):
        rows = pl.ds(pl.multiple_of(half * wide + step * chunk, chunk), chunk)
        grad = nt_dot(dgate_ref[...], gate_ref[0, rows, :]) + nt_dot(dup_ref[...], up_ref[0, rows, :])
        grad = grad.astype(BF16)
        for t in range(groups):
            outs[t][:, step * chunk : (step + 1) * chunk] = grad[t * own_rows : (t + 1) * own_rows, :]
    for t in range(groups):
        outs[t][:, wide:] = part[t * own_rows : (t + 1) * own_rows, :]


def hidden_kernel(count, places, groups, half_ref, *refs):
    blocks = refs[:count]
    act_ref, slope_ref, both_ref, down_ref, gate_ref, up_ref = refs[count : count + 6]
    outs = refs[count + 6 : count + 6 + groups]
    dgate, dup, part_out, rows = refs[count + 6 + groups :]
    fill(rows, blocks, places)
    hidden = gate_ref.shape[2]
    chunk = min(256, hidden)
    part = jnp.zeros((rows.shape[0], 1), F32)
    for start in range(0, hidden, chunk):
        cols = slice(start, start + chunk)
        grad = nt_dot(rows[...], down_ref[0, cols, :])
        part = part + jnp.sum(grad * both_ref[:, cols], axis=1, keepdims=True)
        dgate[:, cols] = (grad * slope_ref[:, cols]).astype(BF16)
        dup[:, cols] = (grad * act_ref[:, cols]).astype(BF16)
    part_out[...] = two_terms(part)
    back_columns(groups, half_ref[0], dgate, dup, part_out[...], gate_ref, up_ref, outs)


def hidden_grads(blocks, places, groups, half, factors, down_piece, gate_piece, up_piece):
    count = len(blocks)
    _, width, hidden = gate_piece.shape
    total = len(places) * CAP
    shape = (total // groups, width // 2 + EXT)
    vmem = pl.BlockSpec(memory_space=pltpu.VMEM)
    smem = pl.BlockSpec(memory_space=pltpu.SMEM)
    out = pl.pallas_call(
        functools.partial(hidden_kernel, count, places, groups),
        in_specs=[smem] + [vmem] * (count + 6),
        out_specs=[vmem] * (groups + 3),
        out_shape=[jax.ShapeDtypeStruct(shape, BF16)] * groups
        + [jax.ShapeDtypeStruct((total, hidden), BF16)] * 2
        + [jax.ShapeDtypeStruct((total, EXT), BF16)],
        scratch_shapes=[pltpu.VMEM((total, width), BF16)],
        compiler_params=pltpu.CompilerParams(vmem_limit_bytes=SCOPED),
        cost_estimate=cost(4 * total * width * hidden, 4 * width * hidden),
        name="hidden_grads",
    )(half, *blocks, *factors, in_vmem(down_piece), in_vmem(gate_piece), in_vmem(up_piece))
    return out[:groups], out[groups:]


def back_kernel(groups, half_ref, dgate_ref, dup_ref, part_ref, gate_ref, up_ref, *outs):
    back_columns(groups, half_ref[0], dgate_ref, dup_ref, part_ref[...], gate_ref, up_ref, outs)


def back_half(groups, half, dgate, dup, part, gate_piece, up_piece):
    _, width, hidden = gate_piece.shape
    total = dgate.shape[0]
    shape = (total // groups, width // 2 + EXT)
    vmem = pl.BlockSpec(memory_space=pltpu.VMEM)
    smem = pl.BlockSpec(memory_space=pltpu.SMEM)
    return pl.pallas_call(
        functools.partial(back_kernel, groups),
        in_specs=[smem] + [vmem] * 5,
        out_specs=[vmem] * groups,
        out_shape=[jax.ShapeDtypeStruct(shape, BF16)] * groups,
        compiler_params=pltpu.CompilerParams(vmem_limit_bytes=SCOPED),
        cost_estimate=cost(2 * total * width * hidden, 2 * width * hidden),
        name="back_half",
    )(half, dgate, dup, part, in_vmem(gate_piece), in_vmem(up_piece))


def two_terms(value):
    high = value.astype(BF16).astype(F32)
    low = value - high
    lane = lax.broadcasted_iota(jnp.int32, (value.shape[0], EXT), 1)
    return jnp.where(lane == 0, high, jnp.where(lane == 1, low, 0.0)).astype(BF16)


def sum_kernel(groups, *refs):
    ins, outs = refs[:groups], refs[groups:]
    wide = ins[0].shape[1] - EXT
    for s in range(E_MOD):
        rows = slice(s * CAP, (s + 1) * CAP)
        total = ins[0][rows, :].astype(F32)
        for t in range(1, groups):
            total = total + ins[t][rows, :].astype(F32)
        outs[s][:, :wide] = total[:, :wide].astype(BF16)
        outs[s][:, wide:] = two_terms(jnp.sum(total[:, wide:], axis=1, keepdims=True))


def sum_pieces(partials):
    groups = len(partials)
    own_rows, wide = partials[0].shape
    return pl.pallas_call(
        functools.partial(sum_kernel, groups),
        out_shape=[jax.ShapeDtypeStruct((CAP, wide), BF16)] * E_MOD,
        cost_estimate=cost(own_rows * wide, 4 * groups * own_rows * wide),
        compiler_params=pltpu.CompilerParams(vmem_limit_bytes=SCOPED),
        name="sum_pieces",
    )(*partials)


def combine_kernel(ids_ref, modality_ref, picks_ref, weights_ref, *refs):
    blocks, (grad_out, gate_out, table) = refs[: 2 * E_MOD], refs[2 * E_MOD :]
    wide = grad_out.shape[1]
    for i in range(2 * E_MOD):
        table[i * CAP : (i + 1) * CAP, :] = blocks[i][...]
    count, first, second, member = slot_of_labels(ids_ref, modality_ref, picks_ref)
    slot = jnp.where(member, count, -1)
    scale = jnp.where(first, weights_ref[0:1, :], jnp.where(second, weights_ref[1:2, :], 0.0))
    own = jnp.where(ids_ref[1] == 0, first.astype(F32), second.astype(F32))
    tok_rows = slot.shape[1]
    want = lax.broadcasted_iota(jnp.int32, (CAP, tok_rows), 0)
    mix = []
    gate = jnp.zeros((1, tok_rows), F32)
    for i in range(2 * E_MOD):
        hit = slot[i : i + 1, :] == want
        mix.append(jnp.where(hit, scale[i : i + 1, :], 0.0))
        part = jnp.sum(table[i * CAP : (i + 1) * CAP, wide:].astype(F32), axis=1, keepdims=True)
        gate = gate + jnp.sum(
            jnp.where(hit, own[i : i + 1, :] * part, 0.0), axis=0, keepdims=True
        )
    gate_out[...] = gate
    mix = jnp.concatenate(mix, axis=0).T
    high = mix.astype(BF16)
    low = (mix - high.astype(F32)).astype(BF16)
    values = table[:, :wide]
    total = jnp.dot(high, values, preferred_element_type=F32)
    total = total + jnp.dot(low, values, preferred_element_type=F32)
    grad_out[...] = total.astype(BF16)


def combine(ids, modality, picks, weights, blocks):
    tok_rows = modality.shape[1]
    wide = blocks[0].shape[1] - EXT
    count = len(blocks)
    vmem = pl.BlockSpec(memory_space=pltpu.VMEM)
    return pl.pallas_call(
        combine_kernel,
        in_specs=[pl.BlockSpec(memory_space=pltpu.SMEM)] + [vmem] * (3 + count),
        out_specs=[vmem] * 2,
        out_shape=[
            jax.ShapeDtypeStruct((tok_rows, wide), BF16),
            jax.ShapeDtypeStruct((1, tok_rows), F32),
        ],
        scratch_shapes=[pltpu.VMEM((count * CAP, wide + EXT), BF16)],
        cost_estimate=cost(4 * count * CAP * tok_rows * wide, 4 * tok_rows * wide),
        compiler_params=pltpu.CompilerParams(vmem_limit_bytes=SCOPED),
        name="combine",
    )(ids, modality, picks, weights, *blocks)


def local(tokens, cotangent, modality, picks, gate_weights, gate_proj, up_proj, down_proj):
    device_count = lax.axis_size("ep")
    groups = device_count // E_MOD
    core = lax.axis_index("mod")
    expert = lax.axis_index("ep") // groups
    ids = jnp.stack([expert, core]).astype(jnp.int32)
    modality = modality.reshape(1, -1)
    picks = picks.T
    weights = gate_weights.T

    def to_expert(x, s, t=0):
        return lax.ppermute(
            x,
            "ep",
            [
                (e * groups + j, (e ^ s) * groups + (j + t) % groups)
                for e in range(E_MOD)
                for j in range(groups)
            ],
        )

    def to_piece(x, t):
        return to_expert(x, 0, t)

    def to_source(x, s, flip):
        return lax.ppermute(
            x,
            ("ep", "mod"),
            [
                ((e * groups + j) * 2 + m, ((e ^ s) * groups + j) * 2 + (m ^ flip))
                for e in range(E_MOD)
                for j in range(groups)
                for m in range(2)
            ],
        )

    sent = gather_slots(ids, modality, picks, tokens, cotangent)
    far = [[to_expert(sent[2 * s - 2], s) for s in range(2, E_MOD)]]
    near = to_expert(sent[1], 1)
    gate_piece, own = load(gate_proj, [], sent[:1])
    (near,) = join([own, near])
    near = [near] + [to_piece(near, t) for t in range(1, groups)]
    far[0], *later = join(far[0], [sent[2 * s - 1] for s in range(2, E_MOD)])
    far.append([to_expert(x, s) for x, s in zip(later, range(2, E_MOD))])
    up_piece, far[0] = load(up_proj, [], [far[0]])
    far[0] = [far[0]] + [to_piece(far[0], t) for t in range(1, groups)]
    (far[1],) = join(far[1])
    (down_piece,) = load(down_proj, [far[1]])
    far[1] = [far[1]] + [to_piece(far[1], t) for t in range(1, groups)]
    blocks = [near + far[a] for a in range(2)]
    places = [
        tuple(
            place
            for t in range(groups)
            for place in [(t, a * CAP), (t, (2 + a) * CAP)]
            + [(groups + t, i * CAP) for i in range(E_MOD - 2)]
        )
        for a in range(2)
    ]
    factors = pre_activations(blocks[0], places[0], gate_piece, up_piece)
    halves = [(core ^ flip).astype(jnp.int32).reshape(1) for flip in range(2)]
    first, (dgate, dup, part) = hidden_grads(
        blocks[1], places[1], groups, halves[1], factors, down_piece, gate_piece, up_piece
    )
    arrived = []
    for flip in (1, 0):
        if flip:
            partials = first
        else:
            partials = back_half(groups, halves[0], dgate, dup, part, gate_piece, up_piece)
        partials = [partials[0]] + [to_piece(partials[t], groups - t) for t in range(1, groups)]
        sums = sum_pieces(partials)
        arrived.append(
            [sums[s] if s + flip == 0 else to_source(sums[s], s, flip) for s in range(E_MOD)]
        )
    token_grad, gate_grad = combine(ids, modality, picks, weights, arrived[1] + arrived[0])
    return token_grad, gate_grad.reshape(-1, 1)


def solution(mesh):
    in_specs = (
        P(("parts", "ep"), None),
        P(("parts", "ep"), None),
        P(("parts", "ep")),
        P(("parts", "ep"), None),
        P(("parts", "ep"), None),
        P("mod", None, "ep"),
        P("mod", None, "ep"),
        P("mod", "ep", None),
    )
    out_specs = (P(("parts", "ep"), "mod"), P(("parts", "ep"), "mod"))
    return jax.shard_map(local, mesh=mesh, in_specs=in_specs, out_specs=out_specs, check_vma=False)
```

```python
import functools

import jax
import jax.numpy as jnp
from jax import lax
from jax.experimental import pallas as pl
from jax.experimental.pallas import tpu as pltpu
from jax.sharding import PartitionSpec as P

E_MOD = 4
CAP = 16
EXT = 128
BF16 = jnp.bfloat16
F32 = jnp.float32
MIB = 1024 * 1024
SCOPED = 16 * MIB


def cost(flops, nbytes):
    return pl.CostEstimate(flops=flops, bytes_accessed=nbytes, transcendentals=0)


def whole(shape):
    return pl.BlockSpec(shape, lambda *_: (0,) * len(shape))


def nt_dot(lhs, rhs):
    return lax.dot_general(lhs, rhs, (((1,), (1,)), ((), ())), preferred_element_type=F32)


def slot_of_labels(ids_ref, modality_ref, picks_ref):
    tok_rows = modality_ref.shape[1]
    label = lax.broadcasted_iota(jnp.int32, (2 * E_MOD, tok_rows), 0)
    expert = jnp.bitwise_xor(label % E_MOD, ids_ref[0])
    modal = jnp.bitwise_xor(label // E_MOD, ids_ref[1])
    mine = modality_ref[...] == modal
    first = mine & (picks_ref[0:1, :] == expert)
    second = mine & (picks_ref[1:2, :] == expert)
    member = first | second
    row = lax.broadcasted_iota(jnp.int32, (tok_rows, tok_rows), 0)
    col = lax.broadcasted_iota(jnp.int32, (tok_rows, tok_rows), 1)
    earlier = (row < col).astype(F32)
    count = jnp.dot(member.astype(F32), earlier, preferred_element_type=F32).astype(jnp.int32)
    return count, first, second, member


def gather_kernel(ids_ref, modality_ref, picks_ref, rows_ref, grads_ref, *refs):
    outs, chosen = refs[:-1], refs[-1]

    @pl.when(pl.program_id(0) == 0)
    def _():
        count, _, _, member = slot_of_labels(ids_ref, modality_ref, picks_ref)
        slot = jnp.where(member, count, -1)
        want = lax.broadcasted_iota(jnp.int32, (CAP, slot.shape[1]), 0)
        for s in range(E_MOD):
            hit = (slot[s : s + 1, :] == want).astype(F32)
            chosen[s * CAP : (s + 1) * CAP, :] = hit.astype(BF16)

    both = [
        jnp.dot(chosen[...], ref[...], preferred_element_type=F32).astype(BF16)
        for ref in (rows_ref, grads_ref)
    ]
    for s in range(2):
        for a in range(2):
            outs[s][a * CAP : (a + 1) * CAP, :] = both[a][s * CAP : (s + 1) * CAP, :]
    for s in range(2, E_MOD):
        for a in range(2):
            outs[2 * s - 2 + a][...] = both[a][s * CAP : (s + 1) * CAP, :]


def gather_slots(ids, modality, picks, rows, grads):
    tok_rows, width = rows.shape
    chunk = width // 4
    heights = [2 * CAP] * 2 + [CAP] * (2 * E_MOD - 4)
    source = pl.BlockSpec((tok_rows, chunk), lambda i: (0, i))
    return pl.pallas_call(
        gather_kernel,
        grid=(width // chunk,),
        in_specs=[
            pl.BlockSpec(memory_space=pltpu.SMEM),
            whole(modality.shape),
            whole(picks.shape),
            source,
            source,
        ],
        out_specs=[pl.BlockSpec((h, chunk), lambda i: (0, i)) for h in heights],
        out_shape=[jax.ShapeDtypeStruct((h, width), BF16) for h in heights],
        scratch_shapes=[pltpu.VMEM((E_MOD * CAP, tok_rows), BF16)],
        compiler_params=pltpu.CompilerParams(vmem_limit_bytes=SCOPED),
        cost_estimate=cost(4 * E_MOD * CAP * tok_rows * width, 6 * tok_rows * width),
        name="gather_slots",
    )(ids, in_hbm(modality), in_hbm(picks), in_hbm(rows), in_hbm(grads))


def load_kernel(parts, src, *refs):
    dst, sems = refs[-2:]
    rows = src.shape[1] // parts
    copies = [
        pltpu.make_async_copy(
            src.at[:, pl.ds(i * rows, rows), :], dst.at[:, pl.ds(i * rows, rows), :], sems.at[i]
        )
        for i in range(parts)
    ]
    for copy in copies:
        copy.start()
    for copy in copies:
        copy.wait()


def load(weight, after):
    parts = 8
    return pl.pallas_call(
        functools.partial(load_kernel, parts),
        in_specs=[pl.BlockSpec(memory_space=pl.ANY)] * (1 + len(after)),
        out_specs=pl.BlockSpec(memory_space=pltpu.VMEM),
        out_shape=pltpu.VMEM(weight.shape, weight.dtype),
        scratch_shapes=[pltpu.SemaphoreType.DMA((parts,))],
        compiler_params=pltpu.CompilerParams(vmem_limit_bytes=SCOPED),
        cost_estimate=cost(0, 1024),
        name="load",
    )(in_hbm(weight), *after)


def load_turned_kernel(parts, src, *refs):
    dst, stage, sems = refs[-3:]
    rows, width = stage.shape[1:]
    copies = [
        pltpu.make_async_copy(src.at[0, pl.ds(i * rows, rows), :], stage.at[i], sems.at[i])
        for i in range(parts)
    ]
    for copy in copies:
        copy.start()
    chunk = 512
    for i in range(parts):
        copies[i].wait()
        for start in range(0, width, chunk):
            block = stage[i, :, start : start + chunk]
            dst[start : start + chunk, i * rows : (i + 1) * rows] = block.T


def load_turned(weight, after):
    _, height, width = weight.shape
    rows = 128
    parts = height // rows
    return pl.pallas_call(
        functools.partial(load_turned_kernel, parts),
        in_specs=[pl.BlockSpec(memory_space=pl.ANY)] * (1 + len(after)),
        out_specs=pl.BlockSpec(memory_space=pltpu.VMEM),
        out_shape=pltpu.VMEM((width, height), weight.dtype),
        scratch_shapes=[
            pltpu.VMEM((parts, rows, width), weight.dtype),
            pltpu.SemaphoreType.DMA((parts,)),
        ],
        compiler_params=pltpu.CompilerParams(vmem_limit_bytes=SCOPED),
        cost_estimate=cost(0, 1024),
        name="load_turned",
    )(in_hbm(weight), *after)


def pass_kernel(*refs):
    pass


def pass_after(block, need):
    place = pl.BlockSpec(memory_space=pl.ANY)
    return pl.pallas_call(
        pass_kernel,
        in_specs=[place] * 2,
        out_specs=place,
        out_shape=jax.ShapeDtypeStruct(block.shape, block.dtype),
        input_output_aliases={0: 0},
        compiler_params=pltpu.CompilerParams(vmem_limit_bytes=SCOPED),
        cost_estimate=cost(0, 1024),
        name="pass_after",
    )(block, in_vmem(need))


def join_kernel(count, *refs):
    blocks, out = refs[:count], refs[-1]
    start = 0
    for block in blocks:
        out[start : start + block.shape[0], :] = block[...]
        start += block.shape[0]


def join_and_pass_kernel(count, through, *refs):
    join_kernel(count, *refs[:count], refs[count + through])


def join(blocks, through=()):
    count = len(blocks)
    total = sum(block.shape[0] for block in blocks)
    vmem = pl.BlockSpec(memory_space=pltpu.VMEM)
    ties = [pl.BlockSpec(memory_space=pl.ANY)] * len(through)
    return pl.pallas_call(
        functools.partial(join_and_pass_kernel, count, len(through)),
        in_specs=[vmem] * count + ties,
        out_specs=[vmem] + ties,
        out_shape=[jax.ShapeDtypeStruct((total, blocks[0].shape[1]), BF16)]
        + [jax.ShapeDtypeStruct(tie.shape, tie.dtype) for tie in through],
        input_output_aliases={count + i: 1 + i for i in range(len(through))},
        compiler_params=pltpu.CompilerParams(vmem_limit_bytes=SCOPED),
        cost_estimate=cost(0, 1024),
        name="join",
    )(*blocks, *through)


def in_hbm(x):
    return pltpu.with_memory_space_constraint(x, pltpu.HBM)


def in_vmem(x):
    return pltpu.with_memory_space_constraint(x, pltpu.VMEM)


def fill(rows, refs, places):
    for i, (index, start) in enumerate(places):
        rows[i * CAP : (i + 1) * CAP, :] = refs[index][start : start + CAP, :]


def pre_kernel(count, places, *refs):
    blocks, (gate_ref, up_ref, act_out, slope_out, both_out, rows) = refs[:count], refs[count:]
    fill(rows, blocks, places)
    hidden = gate_ref.shape[2]
    chunk = min(256, hidden)
    for start in range(0, hidden, chunk):
        cols = slice(start, start + chunk)
        gate_pre = jnp.dot(rows[...], gate_ref[0, :, cols], preferred_element_type=F32)
        up_pre = jnp.dot(rows[...], up_ref[0, :, cols], preferred_element_type=F32)
        sig = jax.nn.sigmoid(gate_pre)
        act = gate_pre * sig
        act_out[:, cols] = act
        slope_out[:, cols] = up_pre * (sig * (1.0 + gate_pre * (1.0 - sig)))
        both_out[:, cols] = act * up_pre


def pre_activations(blocks, places, gate_piece, up_piece):
    count = len(blocks)
    _, width, hidden = gate_piece.shape
    total = len(places) * CAP
    vmem = pl.BlockSpec(memory_space=pltpu.VMEM)
    return pl.pallas_call(
        functools.partial(pre_kernel, count, places),
        in_specs=[vmem] * (count + 2),
        out_specs=[vmem] * 3,
        out_shape=[jax.ShapeDtypeStruct((total, hidden), F32)] * 3,
        scratch_shapes=[pltpu.VMEM((total, width), BF16)],
        compiler_params=pltpu.CompilerParams(vmem_limit_bytes=SCOPED),
        cost_estimate=cost(1024, 1024),
        name="pre_activations",
    )(*blocks, in_vmem(gate_piece), in_vmem(up_piece))


def back_columns(groups, half, dgate_ref, dup_ref, part, gate_ref, up_ref, outs):
    wide = outs[0].shape[1] - EXT
    own_rows = outs[0].shape[0]
    chunk = 512
    for step in range(wide // chunk):
        rows = pl.ds(pl.multiple_of(half * wide + step * chunk, chunk), chunk)
        grad = nt_dot(dgate_ref[...], gate_ref[0, rows, :]) + nt_dot(dup_ref[...], up_ref[0, rows, :])
        grad = grad.astype(BF16)
        for t in range(groups):
            outs[t][:, step * chunk : (step + 1) * chunk] = grad[t * own_rows : (t + 1) * own_rows, :]
    for t in range(groups):
        outs[t][:, wide:] = part[t * own_rows : (t + 1) * own_rows, :]


def hidden_kernel(count, places, groups, half_ref, *refs):
    blocks = refs[:count]
    act_ref, slope_ref, both_ref, down_ref, gate_ref, up_ref = refs[count : count + 6]
    outs = refs[count + 6 : count + 6 + groups]
    dgate, dup, part_out, rows = refs[count + 6 + groups :]
    fill(rows, blocks, places)
    hidden = gate_ref.shape[2]
    chunk = min(256, hidden)
    part = jnp.zeros((rows.shape[0], 1), F32)
    for start in range(0, hidden, chunk):
        cols = slice(start, start + chunk)
        grad = jnp.dot(rows[...], down_ref[:, cols], preferred_element_type=F32)
        part = part + jnp.sum(grad * both_ref[:, cols], axis=1, keepdims=True)
        dgate[:, cols] = (grad * slope_ref[:, cols]).astype(BF16)
        dup[:, cols] = (grad * act_ref[:, cols]).astype(BF16)
    part_out[...] = two_terms(part)
    back_columns(groups, half_ref[0], dgate, dup, part_out[...], gate_ref, up_ref, outs)


def hidden_grads(blocks, places, groups, half, factors, down_piece, gate_piece, up_piece):
    count = len(blocks)
    _, width, hidden = gate_piece.shape
    total = len(places) * CAP
    shape = (total // groups, width // 2 + EXT)
    vmem = pl.BlockSpec(memory_space=pltpu.VMEM)
    smem = pl.BlockSpec(memory_space=pltpu.SMEM)
    out = pl.pallas_call(
        functools.partial(hidden_kernel, count, places, groups),
        in_specs=[smem] + [vmem] * (count + 6),
        out_specs=[vmem] * (groups + 3),
        out_shape=[jax.ShapeDtypeStruct(shape, BF16)] * groups
        + [jax.ShapeDtypeStruct((total, hidden), BF16)] * 2
        + [jax.ShapeDtypeStruct((total, EXT), BF16)],
        scratch_shapes=[pltpu.VMEM((total, width), BF16)],
        compiler_params=pltpu.CompilerParams(vmem_limit_bytes=SCOPED),
        cost_estimate=cost(4 * total * width * hidden, 4 * width * hidden),
        name="hidden_grads",
    )(half, *blocks, *factors, in_vmem(down_piece), in_vmem(gate_piece), in_vmem(up_piece))
    return out[:groups], out[groups:]


def back_kernel(groups, half_ref, dgate_ref, dup_ref, part_ref, gate_ref, up_ref, *outs):
    back_columns(groups, half_ref[0], dgate_ref, dup_ref, part_ref[...], gate_ref, up_ref, outs)


def back_half(groups, half, dgate, dup, part, gate_piece, up_piece):
    _, width, hidden = gate_piece.shape
    total = dgate.shape[0]
    shape = (total // groups, width // 2 + EXT)
    vmem = pl.BlockSpec(memory_space=pltpu.VMEM)
    smem = pl.BlockSpec(memory_space=pltpu.SMEM)
    return pl.pallas_call(
        functools.partial(back_kernel, groups),
        in_specs=[smem] + [vmem] * 5,
        out_specs=[vmem] * groups,
        out_shape=[jax.ShapeDtypeStruct(shape, BF16)] * groups,
        compiler_params=pltpu.CompilerParams(vmem_limit_bytes=SCOPED),
        cost_estimate=cost(2 * total * width * hidden, 2 * width * hidden),
        name="back_half",
    )(half, dgate, dup, part, in_vmem(gate_piece), in_vmem(up_piece))


def two_terms(value):
    high = value.astype(BF16).astype(F32)
    low = value - high
    lane = lax.broadcasted_iota(jnp.int32, (value.shape[0], EXT), 1)
    return jnp.where(lane == 0, high, jnp.where(lane == 1, low, 0.0)).astype(BF16)


def sum_kernel(groups, *refs):
    ins, outs = refs[:groups], refs[groups:]
    wide = ins[0].shape[1] - EXT
    for s in range(E_MOD):
        rows = slice(s * CAP, (s + 1) * CAP)
        total = ins[0][rows, :].astype(F32)
        for t in range(1, groups):
            total = total + ins[t][rows, :].astype(F32)
        outs[s][:, :wide] = total[:, :wide].astype(BF16)
        outs[s][:, wide:] = two_terms(jnp.sum(total[:, wide:], axis=1, keepdims=True))


def sum_pieces(partials):
    groups = len(partials)
    own_rows, wide = partials[0].shape
    return pl.pallas_call(
        functools.partial(sum_kernel, groups),
        out_shape=[jax.ShapeDtypeStruct((CAP, wide), BF16)] * E_MOD,
        cost_estimate=cost(own_rows * wide, 4 * groups * own_rows * wide),
        compiler_params=pltpu.CompilerParams(vmem_limit_bytes=SCOPED),
        name="sum_pieces",
    )(*partials)


def combine_kernel(ids_ref, modality_ref, picks_ref, weights_ref, *refs):
    blocks, (grad_out, gate_out, table) = refs[: 2 * E_MOD], refs[2 * E_MOD :]
    wide = grad_out.shape[1]
    for i in range(2 * E_MOD):
        table[i * CAP : (i + 1) * CAP, :] = blocks[i][...]
    count, first, second, member = slot_of_labels(ids_ref, modality_ref, picks_ref)
    slot = jnp.where(member, count, -1)
    scale = jnp.where(first, weights_ref[0:1, :], jnp.where(second, weights_ref[1:2, :], 0.0))
    own = jnp.where(ids_ref[1] == 0, first.astype(F32), second.astype(F32))
    tok_rows = slot.shape[1]
    want = lax.broadcasted_iota(jnp.int32, (CAP, tok_rows), 0)
    mix = []
    gate = jnp.zeros((1, tok_rows), F32)
    for i in range(2 * E_MOD):
        hit = slot[i : i + 1, :] == want
        mix.append(jnp.where(hit, scale[i : i + 1, :], 0.0))
        part = jnp.sum(table[i * CAP : (i + 1) * CAP, wide:].astype(F32), axis=1, keepdims=True)
        gate = gate + jnp.sum(
            jnp.where(hit, own[i : i + 1, :] * part, 0.0), axis=0, keepdims=True
        )
    gate_out[...] = gate
    mix = jnp.concatenate(mix, axis=0).T
    high = mix.astype(BF16)
    low = (mix - high.astype(F32)).astype(BF16)
    values = table[:, :wide]
    total = jnp.dot(high, values, preferred_element_type=F32)
    total = total + jnp.dot(low, values, preferred_element_type=F32)
    grad_out[...] = total.astype(BF16)


def combine(ids, modality, picks, weights, blocks):
    tok_rows = modality.shape[1]
    wide = blocks[0].shape[1] - EXT
    count = len(blocks)
    vmem = pl.BlockSpec(memory_space=pltpu.VMEM)
    return pl.pallas_call(
        combine_kernel,
        in_specs=[pl.BlockSpec(memory_space=pltpu.SMEM)] + [vmem] * (3 + count),
        out_specs=[vmem] * 2,
        out_shape=[
            jax.ShapeDtypeStruct((tok_rows, wide), BF16),
            jax.ShapeDtypeStruct((1, tok_rows), F32),
        ],
        scratch_shapes=[pltpu.VMEM((count * CAP, wide + EXT), BF16)],
        cost_estimate=cost(4 * count * CAP * tok_rows * wide, 4 * tok_rows * wide),
        compiler_params=pltpu.CompilerParams(vmem_limit_bytes=SCOPED),
        name="combine",
    )(ids, modality, picks, weights, *blocks)


def local(tokens, cotangent, modality, picks, gate_weights, gate_proj, up_proj, down_proj):
    device_count = lax.axis_size("ep")
    groups = device_count // E_MOD
    core = lax.axis_index("mod")
    expert = lax.axis_index("ep") // groups
    ids = jnp.stack([expert, core]).astype(jnp.int32)
    modality = modality.reshape(1, -1)
    picks = picks.T
    weights = gate_weights.T

    def to_expert(x, s, t=0):
        return lax.ppermute(
            x,
            "ep",
            [
                (e * groups + j, (e ^ s) * groups + (j + t) % groups)
                for e in range(E_MOD)
                for j in range(groups)
            ],
        )

    def to_piece(x, t):
        return to_expert(x, 0, t)

    def to_source(x, s, flip):
        return lax.ppermute(
            x,
            ("ep", "mod"),
            [
                ((e * groups + j) * 2 + m, ((e ^ s) * groups + j) * 2 + (m ^ flip))
                for e in range(E_MOD)
                for j in range(groups)
                for m in range(2)
            ],
        )

    sent = gather_slots(ids, modality, picks, tokens, cotangent)
    far = [[to_expert(sent[2 * s - 2], s) for s in range(2, E_MOD)]]
    near = to_expert(sent[1], 1)
    gate_piece = load(gate_proj, sent[:1])
    (near,) = join([pass_after(sent[0], gate_piece), near])
    near = [near] + [to_piece(near, t) for t in range(1, groups)]
    far[0], *later = join(far[0], [sent[2 * s - 1] for s in range(2, E_MOD)])
    far.append([to_expert(x, s) for x, s in zip(later, range(2, E_MOD))])
    up_piece = load(up_proj, [far[0]])
    far[0] = pass_after(far[0], up_piece)
    far[0] = [far[0]] + [to_piece(far[0], t) for t in range(1, groups)]
    (far[1],) = join(far[1])
    down_piece = load_turned(down_proj, [far[1]])
    far[1] = [far[1]] + [to_piece(far[1], t) for t in range(1, groups)]
    blocks = [near + far[a] for a in range(2)]
    places = [
        tuple(
            place
            for t in range(groups)
            for place in [(t, a * CAP), (t, (2 + a) * CAP)]
            + [(groups + t, i * CAP) for i in range(E_MOD - 2)]
        )
        for a in range(2)
    ]
    factors = pre_activations(blocks[0], places[0], gate_piece, up_piece)
    halves = [(core ^ flip).astype(jnp.int32).reshape(1) for flip in range(2)]
    first, (dgate, dup, part) = hidden_grads(
        blocks[1], places[1], groups, halves[1], factors, down_piece, gate_piece, up_piece
    )
    arrived = []
    for flip in (1, 0):
        if flip:
            partials = first
        else:
            partials = back_half(groups, halves[0], dgate, dup, part, gate_piece, up_piece)
        partials = [partials[0]] + [to_piece(partials[t], groups - t) for t in range(1, groups)]
        sums = sum_pieces(partials)
        arrived.append(
            [sums[s] if s + flip == 0 else to_source(sums[s], s, flip) for s in range(E_MOD)]
        )
    token_grad, gate_grad = combine(ids, modality, picks, weights, arrived[1] + arrived[0])
    return token_grad, gate_grad.reshape(-1, 1)


def solution(mesh):
    in_specs = (
        P(("parts", "ep"), None),
        P(("parts", "ep"), None),
        P(("parts", "ep")),
        P(("parts", "ep"), None),
        P(("parts", "ep"), None),
        P("mod", None, "ep"),
        P("mod", None, "ep"),
        P("mod", "ep", None),
    )
    out_specs = (P(("parts", "ep"), "mod"), P(("parts", "ep"), "mod"))
    return jax.shard_map(local, mesh=mesh, in_specs=in_specs, out_specs=out_specs, check_vma=False)
```

```python
import functools

import jax
import jax.numpy as jnp
from jax import lax
from jax.experimental import pallas as pl
from jax.experimental.pallas import tpu as pltpu
from jax.sharding import PartitionSpec as P

E_MOD = 4
CAP = 16
EXT = 128
BF16 = jnp.bfloat16
F32 = jnp.float32
MIB = 1024 * 1024
SCOPED = 16 * MIB


def cost(flops, nbytes):
    return pl.CostEstimate(flops=flops, bytes_accessed=nbytes, transcendentals=0)


def whole(shape):
    return pl.BlockSpec(shape, lambda *_: (0,) * len(shape))


def nt_dot(lhs, rhs):
    return lax.dot_general(lhs, rhs, (((1,), (1,)), ((), ())), preferred_element_type=F32)


def position(groups):
    return lax.axis_index("ep") // groups, lax.axis_index("mod")


def slot_of_labels(groups, modality_ref, picks_ref):
    tok_rows = modality_ref.shape[1]
    label = lax.broadcasted_iota(jnp.int32, (2 * E_MOD, tok_rows), 0)
    own_expert, core = position(groups)
    expert = jnp.bitwise_xor(label % E_MOD, own_expert)
    modal = jnp.bitwise_xor(label // E_MOD, core)
    mine = modality_ref[...] == modal
    first = mine & (picks_ref[0:1, :] == expert)
    second = mine & (picks_ref[1:2, :] == expert)
    member = first | second
    row = lax.broadcasted_iota(jnp.int32, (tok_rows, tok_rows), 0)
    col = lax.broadcasted_iota(jnp.int32, (tok_rows, tok_rows), 1)
    earlier = (row < col).astype(F32)
    count = jnp.dot(member.astype(F32), earlier, preferred_element_type=F32).astype(jnp.int32)
    return count, first, second, member


def gather_kernel(groups, parts, modality_hbm, picks_hbm, rows_hbm, grads_hbm, *refs):
    outs, (modality, picks, rows, chosen, sems) = refs[:-5], refs[-5:]
    chunk = rows.shape[2] // parts
    small = [
        pltpu.make_async_copy(src, dst, sems.at[i])
        for i, (src, dst) in enumerate([(modality_hbm, modality), (picks_hbm, picks)])
    ]
    large = [
        [
            pltpu.make_async_copy(
                src.at[:, pl.ds(i * chunk, chunk)],
                rows.at[a, :, pl.ds(i * chunk, chunk)],
                sems.at[2 + 2 * i + a],
            )
            for a, src in enumerate([rows_hbm, grads_hbm])
        ]
        for i in range(parts)
    ]
    for copy in small + sum(large, []):
        copy.start()
    for copy in small:
        copy.wait()
    count, _, _, member = slot_of_labels(groups, modality, picks)
    slot = jnp.where(member, count, -1)
    want = lax.broadcasted_iota(jnp.int32, (CAP, slot.shape[1]), 0)
    for s in range(E_MOD):
        hit = (slot[s : s + 1, :] == want).astype(F32)
        chosen[s * CAP : (s + 1) * CAP, :] = hit.astype(BF16)
    for i in range(parts):
        cols = slice(i * chunk, (i + 1) * chunk)
        for a in range(2):
            large[i][a].wait()
            picked = jnp.dot(chosen[...], rows[a, :, cols], preferred_element_type=F32).astype(BF16)
            for s in range(E_MOD):
                block = picked[s * CAP : (s + 1) * CAP, :]
                if s < 2:
                    outs[s][a * CAP : (a + 1) * CAP, cols] = block
                else:
                    outs[2 * s - 2 + a][:, cols] = block


def gather_slots(groups, modality, picks, rows, grads):
    tok_rows, width = rows.shape
    parts = 4
    heights = [2 * CAP] * 2 + [CAP] * (2 * E_MOD - 4)
    return pl.pallas_call(
        functools.partial(gather_kernel, groups, parts),
        in_specs=[pl.BlockSpec(memory_space=pl.ANY)] * 4,
        out_specs=[pl.BlockSpec(memory_space=pltpu.VMEM)] * len(heights),
        out_shape=[jax.ShapeDtypeStruct((h, width), BF16) for h in heights],
        scratch_shapes=[
            pltpu.VMEM(modality.shape, jnp.int32),
            pltpu.VMEM(picks.shape, jnp.int32),
            pltpu.VMEM((2, tok_rows, width), BF16),
            pltpu.VMEM((E_MOD * CAP, tok_rows), BF16),
            pltpu.SemaphoreType.DMA((2 + 2 * parts,)),
        ],
        compiler_params=pltpu.CompilerParams(vmem_limit_bytes=SCOPED),
        cost_estimate=cost(4 * E_MOD * CAP * tok_rows * width, 6 * tok_rows * width),
        name="gather_slots",
    )(in_hbm(modality), in_hbm(picks), in_hbm(rows), in_hbm(grads))


def load_kernel(parts, src, *refs):
    dst, sems = refs[-2:]
    rows = src.shape[1] // parts
    copies = [
        pltpu.make_async_copy(
            src.at[:, pl.ds(i * rows, rows), :], dst.at[:, pl.ds(i * rows, rows), :], sems.at[i]
        )
        for i in range(parts)
    ]
    for copy in copies:
        copy.start()
    for copy in copies:
        copy.wait()


def load(weight, after):
    parts = 8
    return pl.pallas_call(
        functools.partial(load_kernel, parts),
        in_specs=[pl.BlockSpec(memory_space=pl.ANY)] * (1 + len(after)),
        out_specs=pl.BlockSpec(memory_space=pltpu.VMEM),
        out_shape=pltpu.VMEM(weight.shape, weight.dtype),
        scratch_shapes=[pltpu.SemaphoreType.DMA((parts,))],
        compiler_params=pltpu.CompilerParams(vmem_limit_bytes=SCOPED),
        cost_estimate=cost(0, 1024),
        name="load",
    )(in_hbm(weight), *after)


def load_turned_kernel(parts, src, *refs):
    dst, stage, sems = refs[-3:]
    rows, width = stage.shape[1:]
    copies = [
        pltpu.make_async_copy(src.at[0, pl.ds(i * rows, rows), :], stage.at[i], sems.at[i])
        for i in range(parts)
    ]
    for copy in copies:
        copy.start()
    chunk = 512
    for i in range(parts):
        copies[i].wait()
        for start in range(0, width, chunk):
            block = stage[i, :, start : start + chunk]
            dst[start : start + chunk, i * rows : (i + 1) * rows] = block.T


def load_turned(weight, after):
    _, height, width = weight.shape
    rows = 128
    parts = height // rows
    return pl.pallas_call(
        functools.partial(load_turned_kernel, parts),
        in_specs=[pl.BlockSpec(memory_space=pl.ANY)] * (1 + len(after)),
        out_specs=pl.BlockSpec(memory_space=pltpu.VMEM),
        out_shape=pltpu.VMEM((width, height), weight.dtype),
        scratch_shapes=[
            pltpu.VMEM((parts, rows, width), weight.dtype),
            pltpu.SemaphoreType.DMA((parts,)),
        ],
        compiler_params=pltpu.CompilerParams(vmem_limit_bytes=SCOPED),
        cost_estimate=cost(0, 1024),
        name="load_turned",
    )(in_hbm(weight), *after)


def pass_kernel(*refs):
    pass


def pass_after(block, *need):
    place = pl.BlockSpec(memory_space=pl.ANY)
    return pl.pallas_call(
        pass_kernel,
        in_specs=[place] * (1 + len(need)),
        out_specs=place,
        out_shape=jax.ShapeDtypeStruct(block.shape, block.dtype),
        input_output_aliases={0: 0},
        compiler_params=pltpu.CompilerParams(vmem_limit_bytes=SCOPED),
        cost_estimate=cost(0, 1024),
        name="pass_after",
    )(block, *[in_vmem(x) for x in need])


def join_kernel(count, *refs):
    blocks, out = refs[:count], refs[-1]
    start = 0
    for block in blocks:
        out[start : start + block.shape[0], :] = block[...]
        start += block.shape[0]


def join(blocks, *need):
    count = len(blocks)
    total = sum(block.shape[0] for block in blocks)
    vmem = pl.BlockSpec(memory_space=pltpu.VMEM)
    return pl.pallas_call(
        functools.partial(join_kernel, count),
        in_specs=[vmem] * count + [pl.BlockSpec(memory_space=pl.ANY)] * len(need),
        out_specs=vmem,
        out_shape=jax.ShapeDtypeStruct((total, blocks[0].shape[1]), BF16),
        compiler_params=pltpu.CompilerParams(vmem_limit_bytes=SCOPED),
        cost_estimate=cost(2 * 10**9, 1024),
        name="join",
    )(*blocks, *[in_vmem(x) for x in need])


def in_hbm(x):
    return pltpu.with_memory_space_constraint(x, pltpu.HBM)


def in_vmem(x):
    return pltpu.with_memory_space_constraint(x, pltpu.VMEM)


def fill(rows, refs, places):
    for i, (index, start) in enumerate(places):
        rows[i * CAP : (i + 1) * CAP, :] = refs[index][start : start + CAP, :]


def pre_kernel(count, places, *refs):
    blocks, (gate_ref, up_ref, act_out, slope_out, both_out, rows) = refs[:count], refs[count:]
    fill(rows, blocks, places)
    hidden = gate_ref.shape[2]
    chunk = min(256, hidden)
    for start in range(0, hidden, chunk):
        cols = slice(start, start + chunk)
        gate_pre = jnp.dot(rows[...], gate_ref[0, :, cols], preferred_element_type=F32)
        up_pre = jnp.dot(rows[...], up_ref[0, :, cols], preferred_element_type=F32)
        sig = jax.nn.sigmoid(gate_pre)
        act = gate_pre * sig
        act_out[:, cols] = act
        slope_out[:, cols] = up_pre * (sig * (1.0 + gate_pre * (1.0 - sig)))
        both_out[:, cols] = act * up_pre


def pre_activations(blocks, places, gate_piece, up_piece):
    count = len(blocks)
    _, width, hidden = gate_piece.shape
    total = len(places) * CAP
    vmem = pl.BlockSpec(memory_space=pltpu.VMEM)
    return pl.pallas_call(
        functools.partial(pre_kernel, count, places),
        in_specs=[vmem] * (count + 2),
        out_specs=[vmem] * 3,
        out_shape=[jax.ShapeDtypeStruct((total, hidden), F32)] * 3,
        scratch_shapes=[pltpu.VMEM((total, width), BF16)],
        compiler_params=pltpu.CompilerParams(vmem_limit_bytes=SCOPED),
        cost_estimate=cost(5 * 10**9, 1024),
        name="pre_activations",
    )(*blocks, in_vmem(gate_piece), in_vmem(up_piece))


def back_columns(groups, flip, dgate_ref, dup_ref, part, gate_ref, up_ref, outs):
    half = jnp.bitwise_xor(position(groups)[1], flip)
    wide = outs[0].shape[1] - EXT
    own_rows = outs[0].shape[0]
    chunk = 512
    for step in range(wide // chunk):
        rows = pl.ds(pl.multiple_of(half * wide + step * chunk, chunk), chunk)
        grad = nt_dot(dgate_ref[...], gate_ref[0, rows, :]) + nt_dot(dup_ref[...], up_ref[0, rows, :])
        grad = grad.astype(BF16)
        for t in range(groups):
            outs[t][:, step * chunk : (step + 1) * chunk] = grad[t * own_rows : (t + 1) * own_rows, :]
    for t in range(groups):
        outs[t][:, wide:] = part[t * own_rows : (t + 1) * own_rows, :]


def hidden_kernel(count, places, groups, *refs):
    blocks = refs[:count]
    act_ref, slope_ref, both_ref, down_ref, gate_ref, up_ref = refs[count : count + 6]
    outs = refs[count + 6 : count + 6 + groups]
    dgate, dup, part_out, rows = refs[count + 6 + groups :]
    fill(rows, blocks, places)
    hidden = gate_ref.shape[2]
    chunk = min(256, hidden)
    part = jnp.zeros((rows.shape[0], 1), F32)
    for start in range(0, hidden, chunk):
        cols = slice(start, start + chunk)
        grad = jnp.dot(rows[...], down_ref[:, cols], preferred_element_type=F32)
        part = part + jnp.sum(grad * both_ref[:, cols], axis=1, keepdims=True)
        dgate[:, cols] = (grad * slope_ref[:, cols]).astype(BF16)
        dup[:, cols] = (grad * act_ref[:, cols]).astype(BF16)
    part_out[...] = two_terms(part)
    back_columns(groups, 1, dgate, dup, part_out[...], gate_ref, up_ref, outs)


def hidden_grads(blocks, places, groups, factors, down_piece, gate_piece, up_piece):
    count = len(blocks)
    _, width, hidden = gate_piece.shape
    total = len(places) * CAP
    shape = (total // groups, width // 2 + EXT)
    vmem = pl.BlockSpec(memory_space=pltpu.VMEM)
    out = pl.pallas_call(
        functools.partial(hidden_kernel, count, places, groups),
        in_specs=[vmem] * (count + 6),
        out_specs=[vmem] * (groups + 3),
        out_shape=[jax.ShapeDtypeStruct(shape, BF16)] * groups
        + [jax.ShapeDtypeStruct((total, hidden), BF16)] * 2
        + [jax.ShapeDtypeStruct((total, EXT), BF16)],
        scratch_shapes=[pltpu.VMEM((total, width), BF16)],
        compiler_params=pltpu.CompilerParams(vmem_limit_bytes=SCOPED),
        cost_estimate=cost(4 * total * width * hidden, 4 * width * hidden),
        name="hidden_grads",
    )(*blocks, *factors, in_vmem(down_piece), in_vmem(gate_piece), in_vmem(up_piece))
    return out[:groups], out[groups:]


def back_kernel(groups, dgate_ref, dup_ref, part_ref, gate_ref, up_ref, *outs):
    back_columns(groups, 0, dgate_ref, dup_ref, part_ref[...], gate_ref, up_ref, outs)


def back_half(groups, dgate, dup, part, gate_piece, up_piece):
    _, width, hidden = gate_piece.shape
    total = dgate.shape[0]
    shape = (total // groups, width // 2 + EXT)
    vmem = pl.BlockSpec(memory_space=pltpu.VMEM)
    return pl.pallas_call(
        functools.partial(back_kernel, groups),
        in_specs=[vmem] * 5,
        out_specs=[vmem] * groups,
        out_shape=[jax.ShapeDtypeStruct(shape, BF16)] * groups,
        compiler_params=pltpu.CompilerParams(vmem_limit_bytes=SCOPED),
        cost_estimate=cost(2 * total * width * hidden, 2 * width * hidden),
        name="back_half",
    )(dgate, dup, part, in_vmem(gate_piece), in_vmem(up_piece))


def two_terms(value):
    high = value.astype(BF16).astype(F32)
    low = value - high
    lane = lax.broadcasted_iota(jnp.int32, (value.shape[0], EXT), 1)
    return jnp.where(lane == 0, high, jnp.where(lane == 1, low, 0.0)).astype(BF16)


def sum_kernel(groups, *refs):
    ins, outs = refs[:groups], refs[groups:]
    wide = ins[0].shape[1] - EXT
    for s in range(E_MOD):
        rows = slice(s * CAP, (s + 1) * CAP)
        total = ins[0][rows, :].astype(F32)
        for t in range(1, groups):
            total = total + ins[t][rows, :].astype(F32)
        outs[s][:, :wide] = total[:, :wide].astype(BF16)
        outs[s][:, wide:] = two_terms(jnp.sum(total[:, wide:], axis=1, keepdims=True))


def sum_pieces(partials):
    groups = len(partials)
    own_rows, wide = partials[0].shape
    return pl.pallas_call(
        functools.partial(sum_kernel, groups),
        out_shape=[jax.ShapeDtypeStruct((CAP, wide), BF16)] * E_MOD,
        cost_estimate=cost(own_rows * wide, 4 * groups * own_rows * wide),
        compiler_params=pltpu.CompilerParams(vmem_limit_bytes=SCOPED),
        name="sum_pieces",
    )(*partials)


def combine_kernel(groups, modality_ref, picks_ref, weights_ref, *refs):
    blocks, (grad_out, gate_out, table) = refs[: 2 * E_MOD], refs[2 * E_MOD :]
    wide = grad_out.shape[1]
    for i in range(2 * E_MOD):
        table[i * CAP : (i + 1) * CAP, :] = blocks[i][...]
    count, first, second, member = slot_of_labels(groups, modality_ref, picks_ref)
    slot = jnp.where(member, count, -1)
    scale = jnp.where(first, weights_ref[0:1, :], jnp.where(second, weights_ref[1:2, :], 0.0))
    own = jnp.where(position(groups)[1] == 0, first.astype(F32), second.astype(F32))
    tok_rows = slot.shape[1]
    want = lax.broadcasted_iota(jnp.int32, (CAP, tok_rows), 0)
    mix = []
    gate = jnp.zeros((1, tok_rows), F32)
    for i in range(2 * E_MOD):
        hit = slot[i : i + 1, :] == want
        mix.append(jnp.where(hit, scale[i : i + 1, :], 0.0))
        part = jnp.sum(table[i * CAP : (i + 1) * CAP, wide:].astype(F32), axis=1, keepdims=True)
        gate = gate + jnp.sum(
            jnp.where(hit, own[i : i + 1, :] * part, 0.0), axis=0, keepdims=True
        )
    gate_out[...] = gate
    mix = jnp.concatenate(mix, axis=0).T
    high = mix.astype(BF16)
    low = (mix - high.astype(F32)).astype(BF16)
    values = table[:, :wide]
    total = jnp.dot(high, values, preferred_element_type=F32)
    total = total + jnp.dot(low, values, preferred_element_type=F32)
    grad_out[...] = total.astype(BF16)


def combine(groups, modality, picks, weights, blocks):
    tok_rows = modality.shape[1]
    wide = blocks[0].shape[1] - EXT
    count = len(blocks)
    vmem = pl.BlockSpec(memory_space=pltpu.VMEM)
    return pl.pallas_call(
        functools.partial(combine_kernel, groups),
        in_specs=[vmem] * (3 + count),
        out_specs=[vmem] * 2,
        out_shape=[
            jax.ShapeDtypeStruct((tok_rows, wide), BF16),
            jax.ShapeDtypeStruct((1, tok_rows), F32),
        ],
        scratch_shapes=[pltpu.VMEM((count * CAP, wide + EXT), BF16)],
        cost_estimate=cost(4 * count * CAP * tok_rows * wide, 4 * tok_rows * wide),
        compiler_params=pltpu.CompilerParams(vmem_limit_bytes=SCOPED),
        name="combine",
    )(modality, picks, weights, *blocks)


def local(tokens, cotangent, modality, picks, gate_weights, gate_proj, up_proj, down_proj):
    device_count = lax.axis_size("ep")
    groups = device_count // E_MOD
    modality = modality.reshape(1, -1)
    picks = picks.T
    weights = gate_weights.T

    def to_expert(x, s, t=0):
        return lax.ppermute(
            x,
            "ep",
            [
                (e * groups + j, (e ^ s) * groups + (j + t) % groups)
                for e in range(E_MOD)
                for j in range(groups)
            ],
        )

    def to_piece(x, t):
        return to_expert(x, 0, t)

    def to_source(x, s, flip):
        return lax.ppermute(
            x,
            ("ep", "mod"),
            [
                ((e * groups + j) * 2 + m, ((e ^ s) * groups + j) * 2 + (m ^ flip))
                for e in range(E_MOD)
                for j in range(groups)
                for m in range(2)
            ],
        )

    sent = gather_slots(groups, modality, picks, tokens, cotangent)
    far = [[to_expert(sent[2 * s - 2 + a], s) for s in range(2, E_MOD)] for a in range(2)]
    near = to_expert(sent[1], 1)
    gate_piece = load(gate_proj, sent[:1])
    near = join([pass_after(sent[0], gate_piece), near])
    near = [near] + [to_piece(near, t) for t in range(1, groups)]
    far[0] = join(far[0], gate_piece)
    up_piece = load(up_proj, [far[0]])
    far[0] = pass_after(far[0], gate_piece, up_piece)
    far[0] = [far[0]] + [to_piece(far[0], t) for t in range(1, groups)]
    down_piece = load_turned(down_proj, [far[0][0], in_vmem(gate_piece), in_vmem(up_piece)])
    far[1] = join(far[1], gate_piece, up_piece, down_piece)
    far[1] = [far[1]] + [to_piece(far[1], t) for t in range(1, groups)]
    blocks = [near + far[a] for a in range(2)]
    places = [
        tuple(
            place
            for t in range(groups)
            for place in [(t, a * CAP), (t, (2 + a) * CAP)]
            + [(groups + t, i * CAP) for i in range(E_MOD - 2)]
        )
        for a in range(2)
    ]
    factors = pre_activations(blocks[0], places[0], gate_piece, up_piece)
    first, (dgate, dup, part) = hidden_grads(
        blocks[1], places[1], groups, factors, down_piece, gate_piece, up_piece
    )
    arrived = []
    for flip in (1, 0):
        if flip:
            partials = first
        else:
            partials = back_half(groups, dgate, dup, part, gate_piece, up_piece)
        partials = [partials[0]] + [to_piece(partials[t], groups - t) for t in range(1, groups)]
        sums = sum_pieces(partials)
        arrived.append(
            [sums[s] if s + flip == 0 else to_source(sums[s], s, flip) for s in range(E_MOD)]
        )
    token_grad, gate_grad = combine(groups, modality, picks, weights, arrived[1] + arrived[0])
    return token_grad, gate_grad.reshape(-1, 1)


def solution(mesh):
    in_specs = (
        P(("parts", "ep"), None),
        P(("parts", "ep"), None),
        P(("parts", "ep")),
        P(("parts", "ep"), None),
        P(("parts", "ep"), None),
        P("mod", None, "ep"),
        P("mod", None, "ep"),
        P("mod", "ep", None),
    )
    out_specs = (P(("parts", "ep"), "mod"), P(("parts", "ep"), "mod"))
    return jax.shard_map(local, mesh=mesh, in_specs=in_specs, out_specs=out_specs, check_vma=False)
```

```python
import functools

import jax
import jax.numpy as jnp
from jax import lax
from jax.experimental import pallas as pl
from jax.experimental.pallas import tpu as pltpu
from jax.sharding import PartitionSpec as P

E_MOD = 4
CAP = 16
EXT = 128
BF16 = jnp.bfloat16
F32 = jnp.float32
MIB = 1024 * 1024
SCOPED = 12 * MIB


def cost(flops, nbytes):
    return pl.CostEstimate(flops=flops, bytes_accessed=nbytes, transcendentals=0)


def whole(shape):
    return pl.BlockSpec(shape, lambda *_: (0,) * len(shape))


def nt_dot(lhs, rhs):
    return lax.dot_general(lhs, rhs, (((1,), (1,)), ((), ())), preferred_element_type=F32)


def position(groups):
    return lax.axis_index("ep") // groups, lax.axis_index("mod")


def slot_of_labels(groups, modality_ref, picks_ref):
    tok_rows = modality_ref.shape[1]
    label = lax.broadcasted_iota(jnp.int32, (2 * E_MOD, tok_rows), 0)
    own_expert, core = position(groups)
    expert = jnp.bitwise_xor(label % E_MOD, own_expert)
    modal = jnp.bitwise_xor(label // E_MOD, core)
    mine = modality_ref[...] == modal
    first = mine & (picks_ref[0:1, :] == expert)
    second = mine & (picks_ref[1:2, :] == expert)
    member = first | second
    row = lax.broadcasted_iota(jnp.int32, (tok_rows, tok_rows), 0)
    col = lax.broadcasted_iota(jnp.int32, (tok_rows, tok_rows), 1)
    earlier = (row < col).astype(F32)
    count = jnp.dot(member.astype(F32), earlier, preferred_element_type=F32).astype(jnp.int32)
    return count, first, second, member


def gather_kernel(groups, parts, modality_hbm, picks_hbm, rows_hbm, grads_hbm, *refs):
    outs, (modality, picks, rows, chosen, sems) = refs[:-5], refs[-5:]
    chunk = rows.shape[2] // parts
    small = [
        pltpu.make_async_copy(src, dst, sems.at[i])
        for i, (src, dst) in enumerate([(modality_hbm, modality), (picks_hbm, picks)])
    ]
    large = [
        [
            pltpu.make_async_copy(
                src.at[:, pl.ds(i * chunk, chunk)],
                rows.at[a, :, pl.ds(i * chunk, chunk)],
                sems.at[2 + 2 * i + a],
            )
            for a, src in enumerate([rows_hbm, grads_hbm])
        ]
        for i in range(parts)
    ]
    for copy in small + sum(large, []):
        copy.start()
    for copy in small:
        copy.wait()
    count, _, _, member = slot_of_labels(groups, modality, picks)
    slot = jnp.where(member, count, -1)
    want = lax.broadcasted_iota(jnp.int32, (CAP, slot.shape[1]), 0)
    for s in range(E_MOD):
        hit = (slot[s : s + 1, :] == want).astype(F32)
        chosen[s * CAP : (s + 1) * CAP, :] = hit.astype(BF16)
    for i in range(parts):
        cols = slice(i * chunk, (i + 1) * chunk)
        for a in range(2):
            large[i][a].wait()
            picked = jnp.dot(chosen[...], rows[a, :, cols], preferred_element_type=F32).astype(BF16)
            for s in range(E_MOD):
                block = picked[s * CAP : (s + 1) * CAP, :]
                if s < 2:
                    outs[s][a * CAP : (a + 1) * CAP, cols] = block
                else:
                    outs[2 * s - 2 + a][:, cols] = block


def gather_slots(groups, modality, picks, rows, grads):
    tok_rows, width = rows.shape
    parts = 4
    heights = [2 * CAP] * 2 + [CAP] * (2 * E_MOD - 4)
    return pl.pallas_call(
        functools.partial(gather_kernel, groups, parts),
        in_specs=[pl.BlockSpec(memory_space=pl.ANY)] * 4,
        out_specs=[pl.BlockSpec(memory_space=pltpu.VMEM)] * len(heights),
        out_shape=[jax.ShapeDtypeStruct((h, width), BF16) for h in heights],
        scratch_shapes=[
            pltpu.VMEM(modality.shape, jnp.int32),
            pltpu.VMEM(picks.shape, jnp.int32),
            pltpu.VMEM((2, tok_rows, width), BF16),
            pltpu.VMEM((E_MOD * CAP, tok_rows), BF16),
            pltpu.SemaphoreType.DMA((2 + 2 * parts,)),
        ],
        compiler_params=pltpu.CompilerParams(vmem_limit_bytes=SCOPED),
        cost_estimate=cost(4 * E_MOD * CAP * tok_rows * width, 6 * tok_rows * width),
        name="gather_slots",
    )(in_hbm(modality), in_hbm(picks), in_hbm(rows), in_hbm(grads))


def load_kernel(parts, src, *refs):
    dst, sems = refs[-2:]
    rows = src.shape[1] // parts
    copies = [
        pltpu.make_async_copy(
            src.at[:, pl.ds(i * rows, rows), :], dst.at[:, pl.ds(i * rows, rows), :], sems.at[i]
        )
        for i in range(parts)
    ]
    for copy in copies:
        copy.start()
    for copy in copies:
        copy.wait()


def load(weight, after):
    parts = 8
    return pl.pallas_call(
        functools.partial(load_kernel, parts),
        in_specs=[pl.BlockSpec(memory_space=pl.ANY)] * (1 + len(after)),
        out_specs=pl.BlockSpec(memory_space=pltpu.VMEM),
        out_shape=pltpu.VMEM(weight.shape, weight.dtype),
        scratch_shapes=[pltpu.SemaphoreType.DMA((parts,))],
        compiler_params=pltpu.CompilerParams(vmem_limit_bytes=SCOPED),
        cost_estimate=cost(0, 1024),
        name="load",
    )(in_hbm(weight), *after)


def load_turned_kernel(parts, src, *refs):
    dst, stage, sems = refs[-3:]
    rows, width = stage.shape[1:]
    copies = [
        pltpu.make_async_copy(src.at[0, pl.ds(i * rows, rows), :], stage.at[i], sems.at[i])
        for i in range(parts)
    ]
    for copy in copies:
        copy.start()
    chunk = 512
    for i in range(parts):
        copies[i].wait()
        for start in range(0, width, chunk):
            block = stage[i, :, start : start + chunk]
            dst[start : start + chunk, i * rows : (i + 1) * rows] = block.T


def load_turned(weight, after):
    _, height, width = weight.shape
    rows = 128
    parts = height // rows
    return pl.pallas_call(
        functools.partial(load_turned_kernel, parts),
        in_specs=[pl.BlockSpec(memory_space=pl.ANY)] * (1 + len(after)),
        out_specs=pl.BlockSpec(memory_space=pltpu.VMEM),
        out_shape=pltpu.VMEM((width, height), weight.dtype),
        scratch_shapes=[
            pltpu.VMEM((parts, rows, width), weight.dtype),
            pltpu.SemaphoreType.DMA((parts,)),
        ],
        compiler_params=pltpu.CompilerParams(vmem_limit_bytes=SCOPED),
        cost_estimate=cost(0, 1024),
        name="load_turned",
    )(in_hbm(weight), *after)


def pass_kernel(*refs):
    pass


def pass_after(blocks, *need):
    place = pl.BlockSpec(memory_space=pl.ANY)
    return pl.pallas_call(
        pass_kernel,
        in_specs=[place] * (len(blocks) + len(need)),
        out_specs=[place] * len(blocks),
        out_shape=[jax.ShapeDtypeStruct(block.shape, block.dtype) for block in blocks],
        input_output_aliases={i: i for i in range(len(blocks))},
        compiler_params=pltpu.CompilerParams(vmem_limit_bytes=SCOPED),
        cost_estimate=cost(0, 1024),
        name="pass_after",
    )(*blocks, *need)


def join_kernel(count, *refs):
    blocks, out = refs[:count], refs[-1]
    start = 0
    for block in blocks:
        out[start : start + block.shape[0], :] = block[...]
        start += block.shape[0]


def join(blocks, *need):
    count = len(blocks)
    total = sum(block.shape[0] for block in blocks)
    vmem = pl.BlockSpec(memory_space=pltpu.VMEM)
    return pl.pallas_call(
        functools.partial(join_kernel, count),
        in_specs=[vmem] * count + [pl.BlockSpec(memory_space=pl.ANY)] * len(need),
        out_specs=vmem,
        out_shape=jax.ShapeDtypeStruct((total, blocks[0].shape[1]), BF16),
        compiler_params=pltpu.CompilerParams(vmem_limit_bytes=SCOPED),
        cost_estimate=cost(2 * 10**9, 1024),
        name="join",
    )(*blocks, *need)


def in_hbm(x):
    return pltpu.with_memory_space_constraint(x, pltpu.HBM)


def in_vmem(x):
    return pltpu.with_memory_space_constraint(x, pltpu.VMEM)


def fill(rows, refs, places):
    for i, (index, start) in enumerate(places):
        rows[i * CAP : (i + 1) * CAP, :] = refs[index][start : start + CAP, :]


def pre_kernel(count, places, *refs):
    blocks, (gate_ref, up_ref, _, act_out, slope_out, both_out, rows) = refs[:count], refs[count:]
    fill(rows, blocks, places)
    hidden = gate_ref.shape[2]
    chunk = min(256, hidden)
    for start in range(0, hidden, chunk):
        cols = slice(start, start + chunk)
        gate_pre = jnp.dot(rows[...], gate_ref[0, :, cols], preferred_element_type=F32)
        up_pre = jnp.dot(rows[...], up_ref[0, :, cols], preferred_element_type=F32)
        sig = jax.nn.sigmoid(gate_pre)
        act = gate_pre * sig
        act_out[:, cols] = act
        slope_out[:, cols] = up_pre * (sig * (1.0 + gate_pre * (1.0 - sig)))
        both_out[:, cols] = act * up_pre


def pre_activations(blocks, places, gate_piece, up_piece, need):
    count = len(blocks)
    _, width, hidden = gate_piece.shape
    total = len(places) * CAP
    vmem = pl.BlockSpec(memory_space=pltpu.VMEM)
    return pl.pallas_call(
        functools.partial(pre_kernel, count, places),
        in_specs=[vmem] * (count + 2) + [pl.BlockSpec(memory_space=pl.ANY)],
        out_specs=[vmem] * 3,
        out_shape=[jax.ShapeDtypeStruct((total, hidden), F32)] * 3,
        scratch_shapes=[pltpu.VMEM((total, width), BF16)],
        compiler_params=pltpu.CompilerParams(vmem_limit_bytes=SCOPED),
        cost_estimate=cost(5 * 10**9, 1024),
        name="pre_activations",
    )(*blocks, in_vmem(gate_piece), in_vmem(up_piece), in_vmem(need))


def back_columns(groups, flip, dgate_ref, dup_ref, part, gate_ref, up_ref, outs):
    half = jnp.bitwise_xor(position(groups)[1], flip)
    wide = outs[0].shape[1] - EXT
    own_rows = outs[0].shape[0]
    chunk = 512
    for step in range(wide // chunk):
        rows = pl.ds(pl.multiple_of(half * wide + step * chunk, chunk), chunk)
        grad = nt_dot(dgate_ref[...], gate_ref[0, rows, :]) + nt_dot(dup_ref[...], up_ref[0, rows, :])
        grad = grad.astype(BF16)
        for t in range(groups):
            outs[t][:, step * chunk : (step + 1) * chunk] = grad[t * own_rows : (t + 1) * own_rows, :]
    for t in range(groups):
        outs[t][:, wide:] = part[t * own_rows : (t + 1) * own_rows, :]


def hidden_kernel(count, places, groups, *refs):
    blocks = refs[:count]
    act_ref, slope_ref, both_ref, down_ref, gate_ref, up_ref = refs[count : count + 6]
    outs = refs[count + 6 : count + 6 + groups]
    dgate, dup, part_out, rows = refs[count + 6 + groups :]
    fill(rows, blocks, places)
    hidden = gate_ref.shape[2]
    chunk = min(256, hidden)
    part = jnp.zeros((rows.shape[0], 1), F32)
    for start in range(0, hidden, chunk):
        cols = slice(start, start + chunk)
        grad = jnp.dot(rows[...], down_ref[:, cols], preferred_element_type=F32)
        part = part + jnp.sum(grad * both_ref[:, cols], axis=1, keepdims=True)
        dgate[:, cols] = (grad * slope_ref[:, cols]).astype(BF16)
        dup[:, cols] = (grad * act_ref[:, cols]).astype(BF16)
    part_out[...] = two_terms(part)
    back_columns(groups, 1, dgate, dup, part_out[...], gate_ref, up_ref, outs)


def hidden_grads(blocks, places, groups, factors, down_piece, gate_piece, up_piece):
    count = len(blocks)
    _, width, hidden = gate_piece.shape
    total = len(places) * CAP
    shape = (total // groups, width // 2 + EXT)
    vmem = pl.BlockSpec(memory_space=pltpu.VMEM)
    out = pl.pallas_call(
        functools.partial(hidden_kernel, count, places, groups),
        in_specs=[vmem] * (count + 6),
        out_specs=[vmem] * (groups + 3),
        out_shape=[jax.ShapeDtypeStruct(shape, BF16)] * groups
        + [jax.ShapeDtypeStruct((total, hidden), BF16)] * 2
        + [jax.ShapeDtypeStruct((total, EXT), BF16)],
        scratch_shapes=[pltpu.VMEM((total, width), BF16)],
        compiler_params=pltpu.CompilerParams(vmem_limit_bytes=SCOPED),
        cost_estimate=cost(4 * total * width * hidden, 4 * width * hidden),
        name="hidden_grads",
    )(*blocks, *factors, in_vmem(down_piece), in_vmem(gate_piece), in_vmem(up_piece))
    return out[:groups], out[groups:]


def back_kernel(groups, dgate_ref, dup_ref, part_ref, gate_ref, up_ref, *outs):
    back_columns(groups, 0, dgate_ref, dup_ref, part_ref[...], gate_ref, up_ref, outs)


def back_half(groups, dgate, dup, part, gate_piece, up_piece):
    _, width, hidden = gate_piece.shape
    total = dgate.shape[0]
    shape = (total // groups, width // 2 + EXT)
    vmem = pl.BlockSpec(memory_space=pltpu.VMEM)
    return pl.pallas_call(
        functools.partial(back_kernel, groups),
        in_specs=[vmem] * 5,
        out_specs=[vmem] * groups,
        out_shape=[jax.ShapeDtypeStruct(shape, BF16)] * groups,
        compiler_params=pltpu.CompilerParams(vmem_limit_bytes=SCOPED),
        cost_estimate=cost(2 * total * width * hidden, 2 * width * hidden),
        name="back_half",
    )(dgate, dup, part, in_vmem(gate_piece), in_vmem(up_piece))


def two_terms(value):
    high = value.astype(BF16).astype(F32)
    low = value - high
    lane = lax.broadcasted_iota(jnp.int32, (value.shape[0], EXT), 1)
    return jnp.where(lane == 0, high, jnp.where(lane == 1, low, 0.0)).astype(BF16)


def sum_kernel(groups, *refs):
    ins, outs = refs[:groups], refs[groups:]
    wide = ins[0].shape[1] - EXT
    for s in range(E_MOD):
        rows = slice(s * CAP, (s + 1) * CAP)
        total = ins[0][rows, :].astype(F32)
        for t in range(1, groups):
            total = total + ins[t][rows, :].astype(F32)
        outs[s][:, :wide] = total[:, :wide].astype(BF16)
        outs[s][:, wide:] = two_terms(jnp.sum(total[:, wide:], axis=1, keepdims=True))


def sum_pieces(partials):
    groups = len(partials)
    own_rows, wide = partials[0].shape
    return pl.pallas_call(
        functools.partial(sum_kernel, groups),
        out_shape=[jax.ShapeDtypeStruct((CAP, wide), BF16)] * E_MOD,
        cost_estimate=cost(own_rows * wide, 4 * groups * own_rows * wide),
        compiler_params=pltpu.CompilerParams(vmem_limit_bytes=SCOPED),
        name="sum_pieces",
    )(*partials)


def combine_kernel(groups, modality_ref, picks_ref, weights_ref, *refs):
    blocks, (grad_out, gate_out, table) = refs[: 2 * E_MOD], refs[2 * E_MOD :]
    wide = grad_out.shape[1]
    for i in range(2 * E_MOD):
        table[i * CAP : (i + 1) * CAP, :] = blocks[i][...]
    count, first, second, member = slot_of_labels(groups, modality_ref, picks_ref)
    slot = jnp.where(member, count, -1)
    scale = jnp.where(first, weights_ref[0:1, :], jnp.where(second, weights_ref[1:2, :], 0.0))
    own = jnp.where(position(groups)[1] == 0, first.astype(F32), second.astype(F32))
    tok_rows = slot.shape[1]
    want = lax.broadcasted_iota(jnp.int32, (CAP, tok_rows), 0)
    mix = []
    gate = jnp.zeros((1, tok_rows), F32)
    for i in range(2 * E_MOD):
        hit = slot[i : i + 1, :] == want
        mix.append(jnp.where(hit, scale[i : i + 1, :], 0.0))
        part = jnp.sum(table[i * CAP : (i + 1) * CAP, wide:].astype(F32), axis=1, keepdims=True)
        gate = gate + jnp.sum(
            jnp.where(hit, own[i : i + 1, :] * part, 0.0), axis=0, keepdims=True
        )
    gate_out[...] = gate
    mix = jnp.concatenate(mix, axis=0).T
    high = mix.astype(BF16)
    low = (mix - high.astype(F32)).astype(BF16)
    values = table[:, :wide]
    total = jnp.dot(high, values, preferred_element_type=F32)
    total = total + jnp.dot(low, values, preferred_element_type=F32)
    grad_out[...] = total.astype(BF16)


def combine(groups, modality, picks, weights, blocks):
    tok_rows = modality.shape[1]
    wide = blocks[0].shape[1] - EXT
    count = len(blocks)
    vmem = pl.BlockSpec(memory_space=pltpu.VMEM)
    return pl.pallas_call(
        functools.partial(combine_kernel, groups),
        in_specs=[vmem] * (3 + count),
        out_specs=[vmem] * 2,
        out_shape=[
            jax.ShapeDtypeStruct((tok_rows, wide), BF16),
            jax.ShapeDtypeStruct((1, tok_rows), F32),
        ],
        scratch_shapes=[pltpu.VMEM((count * CAP, wide + EXT), BF16)],
        cost_estimate=cost(4 * count * CAP * tok_rows * wide, 4 * tok_rows * wide),
        compiler_params=pltpu.CompilerParams(vmem_limit_bytes=SCOPED),
        name="combine",
    )(modality, picks, weights, *blocks)


def local(tokens, cotangent, modality, picks, gate_weights, gate_proj, up_proj, down_proj):
    device_count = lax.axis_size("ep")
    groups = device_count // E_MOD
    modality = modality.reshape(1, -1)
    picks = picks.T
    weights = gate_weights.T

    def to_expert(x, s, t=0):
        return lax.ppermute(
            x,
            "ep",
            [
                (e * groups + j, (e ^ s) * groups + (j + t) % groups)
                for e in range(E_MOD)
                for j in range(groups)
            ],
        )

    def to_piece(x, t):
        return to_expert(x, 0, t)

    def to_source(x, s, flip):
        return lax.ppermute(
            x,
            ("ep", "mod"),
            [
                ((e * groups + j) * 2 + m, ((e ^ s) * groups + j) * 2 + (m ^ flip))
                for e in range(E_MOD)
                for j in range(groups)
                for m in range(2)
            ],
        )

    sent = gather_slots(groups, modality, picks, tokens, cotangent)
    far = [[to_expert(sent[2 * s - 2], s) for s in range(2, E_MOD)]]
    near = [sent[0], to_expert(sent[1], 1)]
    near_pieces = [[to_piece(sent[0], t), to_expert(sent[1], 1, t)] for t in range(1, groups)]
    gate_piece = load(gate_proj, sent[:1])
    later = [sent[2 * s - 1] for s in range(2, E_MOD)]
    later = pass_after(later, in_vmem(gate_piece), near[1], *sum(near_pieces, []))
    far.append([to_expert(x, s) for x, s in zip(later, range(2, E_MOD))])
    far[0] = join(far[0], in_vmem(gate_piece))
    up_piece = load(up_proj, [far[0]])
    far[0] = [far[0]] + [to_piece(far[0], t) for t in range(1, groups)]
    down_piece = load_turned(down_proj, [far[0][0], in_vmem(gate_piece), in_vmem(up_piece)])
    far[1] = join(far[1], in_vmem(gate_piece), in_vmem(up_piece), in_vmem(down_piece))
    far[1] = [far[1]] + [to_piece(far[1], t) for t in range(1, groups)]
    near = near + sum(near_pieces, [])
    blocks = [near + far[a] for a in range(2)]
    places = [
        tuple(
            place
            for t in range(groups)
            for place in [(2 * t, a * CAP), (2 * t + 1, a * CAP)]
            + [(2 * groups + t, i * CAP) for i in range(E_MOD - 2)]
        )
        for a in range(2)
    ]
    factors = pre_activations(blocks[0], places[0], gate_piece, up_piece, down_piece)
    first, (dgate, dup, part) = hidden_grads(
        blocks[1], places[1], groups, factors, down_piece, gate_piece, up_piece
    )
    arrived = []
    for flip in (1, 0):
        if flip:
            partials = first
        else:
            partials = back_half(groups, dgate, dup, part, gate_piece, up_piece)
        partials = [partials[0]] + [to_piece(partials[t], groups - t) for t in range(1, groups)]
        sums = sum_pieces(partials)
        arrived.append(
            [sums[s] if s + flip == 0 else to_source(sums[s], s, flip) for s in range(E_MOD)]
        )
    token_grad, gate_grad = combine(groups, modality, picks, weights, arrived[1] + arrived[0])
    return token_grad, gate_grad.reshape(-1, 1)


def solution(mesh):
    in_specs = (
        P(("parts", "ep"), None),
        P(("parts", "ep"), None),
        P(("parts", "ep")),
        P(("parts", "ep"), None),
        P(("parts", "ep"), None),
        P("mod", None, "ep"),
        P("mod", None, "ep"),
        P("mod", "ep", None),
    )
    out_specs = (P(("parts", "ep"), "mod"), P(("parts", "ep"), "mod"))
    return jax.shard_map(local, mesh=mesh, in_specs=in_specs, out_specs=out_specs, check_vma=False)
```

```python
import functools

import jax
import jax.numpy as jnp
from jax import lax
from jax.experimental import pallas as pl
from jax.experimental.pallas import tpu as pltpu
from jax.sharding import PartitionSpec as P

E_MOD = 4
CAP = 16
EXT = 128
BF16 = jnp.bfloat16
F32 = jnp.float32
MIB = 1024 * 1024
SCOPED = 12 * MIB


def cost(flops, nbytes):
    return pl.CostEstimate(flops=flops, bytes_accessed=nbytes, transcendentals=0)


def whole(shape):
    return pl.BlockSpec(shape, lambda *_: (0,) * len(shape))


def nt_dot(lhs, rhs):
    return lax.dot_general(lhs, rhs, (((1,), (1,)), ((), ())), preferred_element_type=F32)


def position(groups):
    return lax.axis_index("ep") // groups, lax.axis_index("mod")


def slot_of_labels(groups, modality_ref, picks_ref):
    tok_rows = modality_ref.shape[1]
    label = lax.broadcasted_iota(jnp.int32, (2 * E_MOD, tok_rows), 0)
    own_expert, core = position(groups)
    expert = jnp.bitwise_xor(label % E_MOD, own_expert)
    modal = jnp.bitwise_xor(label // E_MOD, core)
    mine = modality_ref[...] == modal
    first = mine & (picks_ref[0:1, :] == expert)
    second = mine & (picks_ref[1:2, :] == expert)
    member = first | second
    row = lax.broadcasted_iota(jnp.int32, (tok_rows, tok_rows), 0)
    col = lax.broadcasted_iota(jnp.int32, (tok_rows, tok_rows), 1)
    earlier = (row < col).astype(F32)
    count = jnp.dot(member.astype(F32), earlier, preferred_element_type=F32).astype(jnp.int32)
    return count, first, second, member


def gather_kernel(groups, parts, modality_hbm, picks_hbm, rows_hbm, grads_hbm, *refs):
    outs, (modality, picks, rows, chosen, sems) = refs[:-5], refs[-5:]
    chunk = rows.shape[2] // parts
    small = [
        pltpu.make_async_copy(src, dst, sems.at[i])
        for i, (src, dst) in enumerate([(modality_hbm, modality), (picks_hbm, picks)])
    ]
    large = [
        [
            pltpu.make_async_copy(
                src.at[:, pl.ds(i * chunk, chunk)],
                rows.at[a, :, pl.ds(i * chunk, chunk)],
                sems.at[2 + 2 * i + a],
            )
            for a, src in enumerate([rows_hbm, grads_hbm])
        ]
        for i in range(parts)
    ]
    for copy in small + sum(large, []):
        copy.start()
    for copy in small:
        copy.wait()
    count, _, _, member = slot_of_labels(groups, modality, picks)
    slot = jnp.where(member, count, -1)
    want = lax.broadcasted_iota(jnp.int32, (CAP, slot.shape[1]), 0)
    for s in range(E_MOD):
        hit = (slot[s : s + 1, :] == want).astype(F32)
        chosen[s * CAP : (s + 1) * CAP, :] = hit.astype(BF16)
    for i in range(parts):
        cols = slice(i * chunk, (i + 1) * chunk)
        for a in range(2):
            large[i][a].wait()
            picked = jnp.dot(chosen[...], rows[a, :, cols], preferred_element_type=F32).astype(BF16)
            for s in range(E_MOD):
                block = picked[s * CAP : (s + 1) * CAP, :]
                if s < 2:
                    outs[s][a * CAP : (a + 1) * CAP, cols] = block
                else:
                    outs[2 * s - 2 + a][:, cols] = block


def gather_slots(groups, modality, picks, rows, grads):
    tok_rows, width = rows.shape
    parts = 4
    heights = [2 * CAP] * 2 + [CAP] * (2 * E_MOD - 4)
    return pl.pallas_call(
        functools.partial(gather_kernel, groups, parts),
        in_specs=[pl.BlockSpec(memory_space=pl.ANY)] * 4,
        out_specs=[pl.BlockSpec(memory_space=pltpu.VMEM)] * len(heights),
        out_shape=[jax.ShapeDtypeStruct((h, width), BF16) for h in heights],
        scratch_shapes=[
            pltpu.VMEM(modality.shape, jnp.int32),
            pltpu.VMEM(picks.shape, jnp.int32),
            pltpu.VMEM((2, tok_rows, width), BF16),
            pltpu.VMEM((E_MOD * CAP, tok_rows), BF16),
            pltpu.SemaphoreType.DMA((2 + 2 * parts,)),
        ],
        compiler_params=pltpu.CompilerParams(vmem_limit_bytes=SCOPED),
        cost_estimate=cost(4 * E_MOD * CAP * tok_rows * width, 6 * tok_rows * width),
        name="gather_slots",
    )(in_hbm(modality), in_hbm(picks), in_hbm(rows), in_hbm(grads))


def load_kernel(parts, src, *refs):
    dst, sems = refs[-2:]
    rows = src.shape[1] // parts
    copies = [
        pltpu.make_async_copy(
            src.at[:, pl.ds(i * rows, rows), :], dst.at[:, pl.ds(i * rows, rows), :], sems.at[i]
        )
        for i in range(parts)
    ]
    for copy in copies:
        copy.start()
    for copy in copies:
        copy.wait()


def load(weight, after):
    parts = 8
    return pl.pallas_call(
        functools.partial(load_kernel, parts),
        in_specs=[pl.BlockSpec(memory_space=pl.ANY)] * (1 + len(after)),
        out_specs=pl.BlockSpec(memory_space=pltpu.VMEM),
        out_shape=pltpu.VMEM(weight.shape, weight.dtype),
        scratch_shapes=[pltpu.SemaphoreType.DMA((parts,))],
        compiler_params=pltpu.CompilerParams(vmem_limit_bytes=SCOPED),
        cost_estimate=cost(0, 1024),
        name="load",
    )(in_hbm(weight), *after)


def load_turned_kernel(parts, src, *refs):
    dst, stage, sems = refs[-3:]
    rows, width = stage.shape[1:]
    copies = [
        pltpu.make_async_copy(src.at[0, pl.ds(i * rows, rows), :], stage.at[i], sems.at[i])
        for i in range(parts)
    ]
    for copy in copies:
        copy.start()
    chunk = 512
    for i in range(parts):
        copies[i].wait()
        for start in range(0, width, chunk):
            block = stage[i, :, start : start + chunk]
            dst[start : start + chunk, i * rows : (i + 1) * rows] = block.T


def load_turned(weight, after):
    _, height, width = weight.shape
    rows = 128
    parts = height // rows
    return pl.pallas_call(
        functools.partial(load_turned_kernel, parts),
        in_specs=[pl.BlockSpec(memory_space=pl.ANY)] * (1 + len(after)),
        out_specs=pl.BlockSpec(memory_space=pltpu.VMEM),
        out_shape=pltpu.VMEM((width, height), weight.dtype),
        scratch_shapes=[
            pltpu.VMEM((parts, rows, width), weight.dtype),
            pltpu.SemaphoreType.DMA((parts,)),
        ],
        compiler_params=pltpu.CompilerParams(vmem_limit_bytes=SCOPED),
        cost_estimate=cost(0, 1024),
        name="load_turned",
    )(in_hbm(weight), *after)


def pass_kernel(*refs):
    pass


def pass_after(blocks, *need):
    place = pl.BlockSpec(memory_space=pl.ANY)
    return pl.pallas_call(
        pass_kernel,
        in_specs=[place] * (len(blocks) + len(need)),
        out_specs=[place] * len(blocks),
        out_shape=[jax.ShapeDtypeStruct(block.shape, block.dtype) for block in blocks],
        input_output_aliases={i: i for i in range(len(blocks))},
        compiler_params=pltpu.CompilerParams(vmem_limit_bytes=SCOPED),
        cost_estimate=cost(0, 1024),
        name="pass_after",
    )(*blocks, *need)


def join_kernel(count, *refs):
    blocks, out = refs[:count], refs[-1]
    start = 0
    for block in blocks:
        out[start : start + block.shape[0], :] = block[...]
        start += block.shape[0]


def join(blocks, *need):
    count = len(blocks)
    total = sum(block.shape[0] for block in blocks)
    vmem = pl.BlockSpec(memory_space=pltpu.VMEM)
    return pl.pallas_call(
        functools.partial(join_kernel, count),
        in_specs=[vmem] * count + [pl.BlockSpec(memory_space=pl.ANY)] * len(need),
        out_specs=vmem,
        out_shape=jax.ShapeDtypeStruct((total, blocks[0].shape[1]), BF16),
        compiler_params=pltpu.CompilerParams(vmem_limit_bytes=SCOPED),
        cost_estimate=cost(2 * 10**9, 1024),
        name="join",
    )(*blocks, *need)


def in_hbm(x):
    return pltpu.with_memory_space_constraint(x, pltpu.HBM)


def in_vmem(x):
    return pltpu.with_memory_space_constraint(x, pltpu.VMEM)


def fill(rows, refs, places):
    for i, (index, start) in enumerate(places):
        rows[i * CAP : (i + 1) * CAP, :] = refs[index][start : start + CAP, :]


def pre_kernel(count, places, *refs):
    blocks, (gate_ref, up_ref, _, act_out, slope_out, both_out, rows) = refs[:count], refs[count:]
    fill(rows, blocks, places)
    hidden = gate_ref.shape[2]
    chunk = min(256, hidden)
    for start in range(0, hidden, chunk):
        cols = slice(start, start + chunk)
        gate_pre = jnp.dot(rows[...], gate_ref[0, :, cols], preferred_element_type=F32)
        up_pre = jnp.dot(rows[...], up_ref[0, :, cols], preferred_element_type=F32)
        sig = jax.nn.sigmoid(gate_pre)
        act = gate_pre * sig
        act_out[:, cols] = act
        slope_out[:, cols] = up_pre * (sig * (1.0 + gate_pre * (1.0 - sig)))
        both_out[:, cols] = act * up_pre


def pre_activations(blocks, places, gate_piece, up_piece, need):
    count = len(blocks)
    _, width, hidden = gate_piece.shape
    total = len(places) * CAP
    vmem = pl.BlockSpec(memory_space=pltpu.VMEM)
    return pl.pallas_call(
        functools.partial(pre_kernel, count, places),
        in_specs=[vmem] * (count + 2) + [pl.BlockSpec(memory_space=pl.ANY)],
        out_specs=[vmem] * 3,
        out_shape=[jax.ShapeDtypeStruct((total, hidden), F32)] * 3,
        scratch_shapes=[pltpu.VMEM((total, width), BF16)],
        compiler_params=pltpu.CompilerParams(vmem_limit_bytes=SCOPED),
        cost_estimate=cost(5 * 10**9, 1024),
        name="pre_activations",
    )(*blocks, in_vmem(gate_piece), in_vmem(up_piece), in_vmem(need))


def back_columns(groups, flip, dgate_ref, dup_ref, part, gate_ref, up_ref, outs):
    half = jnp.bitwise_xor(position(groups)[1], flip)
    wide = outs[0].shape[1] - EXT
    own_rows = outs[0].shape[0]
    chunk = 512
    for step in range(wide // chunk):
        rows = pl.ds(pl.multiple_of(half * wide + step * chunk, chunk), chunk)
        grad = nt_dot(dgate_ref[...], gate_ref[0, rows, :]) + nt_dot(dup_ref[...], up_ref[0, rows, :])
        grad = grad.astype(BF16)
        for t in range(groups):
            outs[t][:, step * chunk : (step + 1) * chunk] = grad[t * own_rows : (t + 1) * own_rows, :]
    for t in range(groups):
        outs[t][:, wide:] = part[t * own_rows : (t + 1) * own_rows, :]


def hidden_kernel(count, places, groups, *refs):
    blocks = refs[:count]
    act_ref, slope_ref, both_ref, down_ref, gate_ref, up_ref = refs[count : count + 6]
    outs = refs[count + 6 : count + 6 + groups]
    dgate, dup, part_out, rows = refs[count + 6 + groups :]
    fill(rows, blocks, places)
    hidden = gate_ref.shape[2]
    chunk = min(256, hidden)
    part = jnp.zeros((rows.shape[0], 1), F32)
    for start in range(0, hidden, chunk):
        cols = slice(start, start + chunk)
        grad = jnp.dot(rows[...], down_ref[:, cols], preferred_element_type=F32)
        part = part + jnp.sum(grad * both_ref[:, cols], axis=1, keepdims=True)
        dgate[:, cols] = (grad * slope_ref[:, cols]).astype(BF16)
        dup[:, cols] = (grad * act_ref[:, cols]).astype(BF16)
    part_out[...] = two_terms(part)
    back_columns(groups, 1, dgate, dup, part_out[...], gate_ref, up_ref, outs)


def hidden_grads(blocks, places, groups, factors, down_piece, gate_piece, up_piece):
    count = len(blocks)
    _, width, hidden = gate_piece.shape
    total = len(places) * CAP
    shape = (total // groups, width // 2 + EXT)
    vmem = pl.BlockSpec(memory_space=pltpu.VMEM)
    out = pl.pallas_call(
        functools.partial(hidden_kernel, count, places, groups),
        in_specs=[vmem] * (count + 6),
        out_specs=[vmem] * (groups + 3),
        out_shape=[jax.ShapeDtypeStruct(shape, BF16)] * groups
        + [jax.ShapeDtypeStruct((total, hidden), BF16)] * 2
        + [jax.ShapeDtypeStruct((total, EXT), BF16)],
        scratch_shapes=[pltpu.VMEM((total, width), BF16)],
        compiler_params=pltpu.CompilerParams(vmem_limit_bytes=SCOPED),
        cost_estimate=cost(4 * total * width * hidden, 4 * width * hidden),
        name="hidden_grads",
    )(*blocks, *factors, in_vmem(down_piece), in_vmem(gate_piece), in_vmem(up_piece))
    return out[:groups], out[groups:]


def back_kernel(groups, dgate_ref, dup_ref, part_ref, gate_ref, up_ref, *outs):
    back_columns(groups, 0, dgate_ref, dup_ref, part_ref[...], gate_ref, up_ref, outs)


def back_half(groups, dgate, dup, part, gate_piece, up_piece):
    _, width, hidden = gate_piece.shape
    total = dgate.shape[0]
    shape = (total // groups, width // 2 + EXT)
    vmem = pl.BlockSpec(memory_space=pltpu.VMEM)
    return pl.pallas_call(
        functools.partial(back_kernel, groups),
        in_specs=[vmem] * 5,
        out_specs=[vmem] * groups,
        out_shape=[jax.ShapeDtypeStruct(shape, BF16)] * groups,
        compiler_params=pltpu.CompilerParams(vmem_limit_bytes=SCOPED),
        cost_estimate=cost(2 * total * width * hidden, 2 * width * hidden),
        name="back_half",
    )(dgate, dup, part, in_vmem(gate_piece), in_vmem(up_piece))


def two_terms(value):
    high = value.astype(BF16).astype(F32)
    low = value - high
    lane = lax.broadcasted_iota(jnp.int32, (value.shape[0], EXT), 1)
    return jnp.where(lane == 0, high, jnp.where(lane == 1, low, 0.0)).astype(BF16)


def sum_kernel(groups, *refs):
    ins, outs = refs[:groups], refs[groups:]
    wide = ins[0].shape[1] - EXT
    for s in range(E_MOD):
        rows = slice(s * CAP, (s + 1) * CAP)
        total = ins[0][rows, :].astype(F32)
        for t in range(1, groups):
            total = total + ins[t][rows, :].astype(F32)
        outs[s][:, :wide] = total[:, :wide].astype(BF16)
        outs[s][:, wide:] = two_terms(jnp.sum(total[:, wide:], axis=1, keepdims=True))


def sum_pieces(partials):
    groups = len(partials)
    own_rows, wide = partials[0].shape
    return pl.pallas_call(
        functools.partial(sum_kernel, groups),
        out_shape=[jax.ShapeDtypeStruct((CAP, wide), BF16)] * E_MOD,
        cost_estimate=cost(own_rows * wide, 4 * groups * own_rows * wide),
        compiler_params=pltpu.CompilerParams(vmem_limit_bytes=SCOPED),
        name="sum_pieces",
    )(*partials)


def combine_kernel(groups, modality_ref, picks_ref, weights_ref, *refs):
    blocks, (grad_out, gate_out, table) = refs[: 2 * E_MOD], refs[2 * E_MOD :]
    wide = grad_out.shape[1]
    for i in range(2 * E_MOD):
        table[i * CAP : (i + 1) * CAP, :] = blocks[i][...]
    count, first, second, member = slot_of_labels(groups, modality_ref, picks_ref)
    slot = jnp.where(member, count, -1)
    scale = jnp.where(first, weights_ref[0:1, :], jnp.where(second, weights_ref[1:2, :], 0.0))
    own = jnp.where(position(groups)[1] == 0, first.astype(F32), second.astype(F32))
    tok_rows = slot.shape[1]
    want = lax.broadcasted_iota(jnp.int32, (CAP, tok_rows), 0)
    mix = []
    gate = jnp.zeros((1, tok_rows), F32)
    for i in range(2 * E_MOD):
        hit = slot[i : i + 1, :] == want
        mix.append(jnp.where(hit, scale[i : i + 1, :], 0.0))
        part = jnp.sum(table[i * CAP : (i + 1) * CAP, wide:].astype(F32), axis=1, keepdims=True)
        gate = gate + jnp.sum(
            jnp.where(hit, own[i : i + 1, :] * part, 0.0), axis=0, keepdims=True
        )
    gate_out[...] = gate
    mix = jnp.concatenate(mix, axis=0).T
    high = mix.astype(BF16)
    low = (mix - high.astype(F32)).astype(BF16)
    values = table[:, :wide]
    total = jnp.dot(high, values, preferred_element_type=F32)
    total = total + jnp.dot(low, values, preferred_element_type=F32)
    grad_out[...] = total.astype(BF16)


def combine(groups, modality, picks, weights, blocks):
    tok_rows = modality.shape[1]
    wide = blocks[0].shape[1] - EXT
    count = len(blocks)
    vmem = pl.BlockSpec(memory_space=pltpu.VMEM)
    return pl.pallas_call(
        functools.partial(combine_kernel, groups),
        in_specs=[vmem] * (3 + count),
        out_specs=[vmem] * 2,
        out_shape=[
            jax.ShapeDtypeStruct((tok_rows, wide), BF16),
            jax.ShapeDtypeStruct((1, tok_rows), F32),
        ],
        scratch_shapes=[pltpu.VMEM((count * CAP, wide + EXT), BF16)],
        cost_estimate=cost(4 * count * CAP * tok_rows * wide, 4 * tok_rows * wide),
        compiler_params=pltpu.CompilerParams(vmem_limit_bytes=SCOPED),
        name="combine",
    )(modality, picks, weights, *blocks)


def local(tokens, cotangent, modality, picks, gate_weights, gate_proj, up_proj, down_proj):
    device_count = lax.axis_size("ep")
    groups = device_count // E_MOD
    modality = modality.reshape(1, -1)
    picks = picks.T
    weights = gate_weights.T

    def to_expert(x, s, t=0):
        return lax.ppermute(
            x,
            "ep",
            [
                (e * groups + j, (e ^ s) * groups + (j + t) % groups)
                for e in range(E_MOD)
                for j in range(groups)
            ],
        )

    def to_piece(x, t):
        return to_expert(x, 0, t)

    def to_source(x, s, flip):
        return lax.ppermute(
            x,
            ("ep", "mod"),
            [
                ((e * groups + j) * 2 + m, ((e ^ s) * groups + j) * 2 + (m ^ flip))
                for e in range(E_MOD)
                for j in range(groups)
                for m in range(2)
            ],
        )

    sent = gather_slots(groups, modality, picks, tokens, cotangent)
    far = [[to_expert(sent[2 * s - 2], s) for s in range(2, E_MOD)]]
    near = [sent[0], to_expert(sent[1], 1)]
    own_pieces = [to_piece(sent[0], t) for t in range(1, groups)]
    gate_piece = load(gate_proj, sent[:1])
    later = [sent[2 * s - 1] for s in range(2, E_MOD)]
    later = pass_after(later, in_vmem(gate_piece), *own_pieces)
    far.append([to_expert(x, s) for x, s in zip(later, range(2, E_MOD))])
    near_pieces = [[x, to_piece(near[1], t)] for t, x in enumerate(own_pieces, 1)]
    far[0] = join(far[0], in_vmem(gate_piece), near[1])
    up_piece = load(up_proj, [far[0]])
    far[0] = [far[0]] + [to_piece(far[0], t) for t in range(1, groups)]
    far[1] = join(far[1], in_vmem(gate_piece), in_vmem(up_piece))
    down_piece = load_turned(down_proj, [far[1], in_vmem(gate_piece), in_vmem(up_piece)])
    far[1] = [far[1]] + [to_piece(far[1], t) for t in range(1, groups)]
    near = near + sum(near_pieces, [])
    blocks = [near + far[a] for a in range(2)]
    places = [
        tuple(
            place
            for t in range(groups)
            for place in [(2 * t, a * CAP), (2 * t + 1, a * CAP)]
            + [(2 * groups + t, i * CAP) for i in range(E_MOD - 2)]
        )
        for a in range(2)
    ]
    factors = pre_activations(blocks[0], places[0], gate_piece, up_piece, down_piece)
    first, (dgate, dup, part) = hidden_grads(
        blocks[1], places[1], groups, factors, down_piece, gate_piece, up_piece
    )
    second = back_half(groups, dgate, dup, part, gate_piece, up_piece)
    first = [first[0]] + [to_piece(first[t], groups - t) for t in range(1, groups)]
    waiting = pass_after(second[1:], *first[1:])
    second = [second[0]] + [to_piece(x, groups - t) for t, x in enumerate(waiting, 1)]
    arrived = []
    for flip, partials in ((1, first), (0, second)):
        sums = sum_pieces(partials)
        arrived.append(
            [sums[s] if s + flip == 0 else to_source(sums[s], s, flip) for s in range(E_MOD)]
        )
    token_grad, gate_grad = combine(groups, modality, picks, weights, arrived[1] + arrived[0])
    return token_grad, gate_grad.reshape(-1, 1)


def solution(mesh):
    in_specs = (
        P(("parts", "ep"), None),
        P(("parts", "ep"), None),
        P(("parts", "ep")),
        P(("parts", "ep"), None),
        P(("parts", "ep"), None),
        P("mod", None, "ep"),
        P("mod", None, "ep"),
        P("mod", "ep", None),
    )
    out_specs = (P(("parts", "ep"), "mod"), P(("parts", "ep"), "mod"))
    return jax.shard_map(local, mesh=mesh, in_specs=in_specs, out_specs=out_specs, check_vma=False)
```

```python
import functools

import jax
import jax.numpy as jnp
from jax import lax
from jax.experimental import pallas as pl
from jax.experimental.pallas import tpu as pltpu
from jax.sharding import PartitionSpec as P

E_MOD = 4
CAP = 16
EXT = 128
BF16 = jnp.bfloat16
F32 = jnp.float32
MIB = 1024 * 1024
SCOPED = 10 * MIB


def cost(flops, nbytes):
    return pl.CostEstimate(flops=flops, bytes_accessed=nbytes, transcendentals=0)


def whole(shape):
    return pl.BlockSpec(shape, lambda *_: (0,) * len(shape))


def nt_dot(lhs, rhs):
    return lax.dot_general(lhs, rhs, (((1,), (1,)), ((), ())), preferred_element_type=F32)


def position(groups):
    return lax.axis_index("ep") // groups, lax.axis_index("mod")


def slot_of_labels(groups, modality_ref, picks_ref):
    tok_rows = modality_ref.shape[1]
    label = lax.broadcasted_iota(jnp.int32, (2 * E_MOD, tok_rows), 0)
    own_expert, core = position(groups)
    expert = jnp.bitwise_xor(label % E_MOD, own_expert)
    modal = jnp.bitwise_xor(label // E_MOD, core)
    mine = modality_ref[...] == modal
    first = mine & (picks_ref[0:1, :] == expert)
    second = mine & (picks_ref[1:2, :] == expert)
    member = first | second
    row = lax.broadcasted_iota(jnp.int32, (tok_rows, tok_rows), 0)
    col = lax.broadcasted_iota(jnp.int32, (tok_rows, tok_rows), 1)
    earlier = (row < col).astype(F32)
    count = jnp.dot(member.astype(F32), earlier, preferred_element_type=F32).astype(jnp.int32)
    return count, first, second, member


def gather_kernel(groups, parts, modality_hbm, picks_hbm, rows_hbm, grads_hbm, *refs):
    outs, (modality, picks, rows, chosen, sems) = refs[:-5], refs[-5:]
    chunk = rows.shape[2] // parts
    small = [
        pltpu.make_async_copy(src, dst, sems.at[i])
        for i, (src, dst) in enumerate([(modality_hbm, modality), (picks_hbm, picks)])
    ]
    large = [
        [
            pltpu.make_async_copy(
                src.at[:, pl.ds(i * chunk, chunk)],
                rows.at[a, :, pl.ds(i * chunk, chunk)],
                sems.at[2 + 2 * i + a],
            )
            for a, src in enumerate([rows_hbm, grads_hbm])
        ]
        for i in range(parts)
    ]
    for copy in small + sum(large, []):
        copy.start()
    for copy in small:
        copy.wait()
    count, _, _, member = slot_of_labels(groups, modality, picks)
    slot = jnp.where(member, count, -1)
    want = lax.broadcasted_iota(jnp.int32, (CAP, slot.shape[1]), 0)
    for s in range(E_MOD):
        hit = (slot[s : s + 1, :] == want).astype(F32)
        chosen[s * CAP : (s + 1) * CAP, :] = hit.astype(BF16)
    for i in range(parts):
        cols = slice(i * chunk, (i + 1) * chunk)
        for a in range(2):
            large[i][a].wait()
            picked = jnp.dot(chosen[...], rows[a, :, cols], preferred_element_type=F32).astype(BF16)
            for s in range(E_MOD):
                block = picked[s * CAP : (s + 1) * CAP, :]
                if s < 2:
                    outs[s][a * CAP : (a + 1) * CAP, cols] = block
                else:
                    outs[2 * s - 2 + a][:, cols] = block


def gather_slots(groups, modality, picks, rows, grads):
    tok_rows, width = rows.shape
    parts = 4
    heights = [2 * CAP] * 2 + [CAP] * (2 * E_MOD - 4)
    return pl.pallas_call(
        functools.partial(gather_kernel, groups, parts),
        in_specs=[pl.BlockSpec(memory_space=pl.ANY)] * 4,
        out_specs=[pl.BlockSpec(memory_space=pltpu.VMEM)] * len(heights),
        out_shape=[jax.ShapeDtypeStruct((h, width), BF16) for h in heights],
        scratch_shapes=[
            pltpu.VMEM(modality.shape, jnp.int32),
            pltpu.VMEM(picks.shape, jnp.int32),
            pltpu.VMEM((2, tok_rows, width), BF16),
            pltpu.VMEM((E_MOD * CAP, tok_rows), BF16),
            pltpu.SemaphoreType.DMA((2 + 2 * parts,)),
        ],
        compiler_params=pltpu.CompilerParams(vmem_limit_bytes=SCOPED),
        cost_estimate=cost(4 * E_MOD * CAP * tok_rows * width, 6 * tok_rows * width),
        name="gather_slots",
    )(in_hbm(modality), in_hbm(picks), in_hbm(rows), in_hbm(grads))


def load_kernel(parts, src, *refs):
    dst, sems = refs[-2:]
    rows = src.shape[1] // parts
    copies = [
        pltpu.make_async_copy(
            src.at[:, pl.ds(i * rows, rows), :], dst.at[:, pl.ds(i * rows, rows), :], sems.at[i]
        )
        for i in range(parts)
    ]
    for copy in copies:
        copy.start()
    for copy in copies:
        copy.wait()


def load(weight, after):
    parts = 8
    return pl.pallas_call(
        functools.partial(load_kernel, parts),
        in_specs=[pl.BlockSpec(memory_space=pl.ANY)] * (1 + len(after)),
        out_specs=pl.BlockSpec(memory_space=pltpu.VMEM),
        out_shape=pltpu.VMEM(weight.shape, weight.dtype),
        scratch_shapes=[pltpu.SemaphoreType.DMA((parts,))],
        compiler_params=pltpu.CompilerParams(vmem_limit_bytes=SCOPED),
        cost_estimate=cost(2 * 10**9, 1024),
        name="load",
    )(in_hbm(weight), *after)


def load_turned_kernel(parts, src, *refs):
    dst, stage, sems = refs[-3:]
    rows, width = stage.shape[1:]
    copies = [
        pltpu.make_async_copy(src.at[0, pl.ds(i * rows, rows), :], stage.at[i], sems.at[i])
        for i in range(parts)
    ]
    for copy in copies:
        copy.start()
    chunk = 512
    for i in range(parts):
        copies[i].wait()
        for start in range(0, width, chunk):
            block = stage[i, :, start : start + chunk]
            dst[start : start + chunk, i * rows : (i + 1) * rows] = block.T


def load_turned(weight, after):
    _, height, width = weight.shape
    rows = 128
    parts = height // rows
    return pl.pallas_call(
        functools.partial(load_turned_kernel, parts),
        in_specs=[pl.BlockSpec(memory_space=pl.ANY)] * (1 + len(after)),
        out_specs=pl.BlockSpec(memory_space=pltpu.VMEM),
        out_shape=pltpu.VMEM((width, height), weight.dtype),
        scratch_shapes=[
            pltpu.VMEM((parts, rows, width), weight.dtype),
            pltpu.SemaphoreType.DMA((parts,)),
        ],
        compiler_params=pltpu.CompilerParams(vmem_limit_bytes=SCOPED),
        cost_estimate=cost(10 * 10**9, 1024),
        name="load_turned",
    )(in_hbm(weight), *after)


def pass_kernel(*refs):
    pass


def pass_after(blocks, *need):
    place = pl.BlockSpec(memory_space=pl.ANY)
    return pl.pallas_call(
        pass_kernel,
        in_specs=[place] * (len(blocks) + len(need)),
        out_specs=[place] * len(blocks),
        out_shape=[jax.ShapeDtypeStruct(block.shape, block.dtype) for block in blocks],
        input_output_aliases={i: i for i in range(len(blocks))},
        compiler_params=pltpu.CompilerParams(vmem_limit_bytes=SCOPED),
        cost_estimate=cost(2 * 10**9, 1024),
        name="pass_after",
    )(*blocks, *need)


def join_kernel(count, *refs):
    blocks, out = refs[:count], refs[-1]
    start = 0
    for block in blocks:
        out[start : start + block.shape[0], :] = block[...]
        start += block.shape[0]


def join(blocks, *need):
    count = len(blocks)
    total = sum(block.shape[0] for block in blocks)
    vmem = pl.BlockSpec(memory_space=pltpu.VMEM)
    return pl.pallas_call(
        functools.partial(join_kernel, count),
        in_specs=[vmem] * count + [pl.BlockSpec(memory_space=pl.ANY)] * len(need),
        out_specs=vmem,
        out_shape=jax.ShapeDtypeStruct((total, blocks[0].shape[1]), BF16),
        compiler_params=pltpu.CompilerParams(vmem_limit_bytes=SCOPED),
        cost_estimate=cost(2 * 10**9, 1024),
        name="join",
    )(*blocks, *need)


def in_hbm(x):
    return pltpu.with_memory_space_constraint(x, pltpu.HBM)


def in_vmem(x):
    return pltpu.with_memory_space_constraint(x, pltpu.VMEM)


def fill(rows, refs, places):
    for i, (index, start) in enumerate(places):
        rows[i * CAP : (i + 1) * CAP, :] = refs[index][start : start + CAP, :]


def pre_kernel(count, places, *refs):
    blocks, (gate_ref, up_ref, _, act_out, slope_out, both_out, rows) = refs[:count], refs[count:]
    fill(rows, blocks, places)
    hidden = gate_ref.shape[2]
    chunk = min(256, hidden)
    for start in range(0, hidden, chunk):
        cols = slice(start, start + chunk)
        gate_pre = jnp.dot(rows[...], gate_ref[0, :, cols], preferred_element_type=F32)
        up_pre = jnp.dot(rows[...], up_ref[0, :, cols], preferred_element_type=F32)
        sig = jax.nn.sigmoid(gate_pre)
        act = gate_pre * sig
        act_out[:, cols] = act
        slope_out[:, cols] = up_pre * (sig * (1.0 + gate_pre * (1.0 - sig)))
        both_out[:, cols] = act * up_pre


def pre_activations(blocks, places, gate_piece, up_piece, need):
    count = len(blocks)
    _, width, hidden = gate_piece.shape
    total = len(places) * CAP
    vmem = pl.BlockSpec(memory_space=pltpu.VMEM)
    return pl.pallas_call(
        functools.partial(pre_kernel, count, places),
        in_specs=[vmem] * (count + 2) + [pl.BlockSpec(memory_space=pl.ANY)],
        out_specs=[vmem] * 3,
        out_shape=[jax.ShapeDtypeStruct((total, hidden), F32)] * 3,
        scratch_shapes=[pltpu.VMEM((total, width), BF16)],
        compiler_params=pltpu.CompilerParams(vmem_limit_bytes=SCOPED),
        cost_estimate=cost(5 * 10**9, 1024),
        name="pre_activations",
    )(*blocks, in_vmem(gate_piece), in_vmem(up_piece), in_vmem(need))


def back_columns(groups, flip, dgate_ref, dup_ref, part, gate_ref, up_ref, outs):
    half = jnp.bitwise_xor(position(groups)[1], flip)
    wide = outs[0].shape[1] - EXT
    own_rows = outs[0].shape[0]
    chunk = 512
    for step in range(wide // chunk):
        rows = pl.ds(pl.multiple_of(half * wide + step * chunk, chunk), chunk)
        grad = nt_dot(dgate_ref[...], gate_ref[0, rows, :]) + nt_dot(dup_ref[...], up_ref[0, rows, :])
        grad = grad.astype(BF16)
        for t in range(groups):
            outs[t][:, step * chunk : (step + 1) * chunk] = grad[t * own_rows : (t + 1) * own_rows, :]
    for t in range(groups):
        outs[t][:, wide:] = part[t * own_rows : (t + 1) * own_rows, :]


def hidden_kernel(count, places, groups, *refs):
    blocks = refs[:count]
    act_ref, slope_ref, both_ref, down_ref, gate_ref, up_ref = refs[count : count + 6]
    outs = refs[count + 6 : count + 6 + groups]
    dgate, dup, part_out, rows = refs[count + 6 + groups :]
    fill(rows, blocks, places)
    hidden = gate_ref.shape[2]
    chunk = min(256, hidden)
    part = jnp.zeros((rows.shape[0], 1), F32)
    for start in range(0, hidden, chunk):
        cols = slice(start, start + chunk)
        grad = jnp.dot(rows[...], down_ref[:, cols], preferred_element_type=F32)
        part = part + jnp.sum(grad * both_ref[:, cols], axis=1, keepdims=True)
        dgate[:, cols] = (grad * slope_ref[:, cols]).astype(BF16)
        dup[:, cols] = (grad * act_ref[:, cols]).astype(BF16)
    part_out[...] = two_terms(part)
    back_columns(groups, 1, dgate, dup, part_out[...], gate_ref, up_ref, outs)


def hidden_grads(blocks, places, groups, factors, down_piece, gate_piece, up_piece):
    count = len(blocks)
    _, width, hidden = gate_piece.shape
    total = len(places) * CAP
    shape = (total // groups, width // 2 + EXT)
    vmem = pl.BlockSpec(memory_space=pltpu.VMEM)
    out = pl.pallas_call(
        functools.partial(hidden_kernel, count, places, groups),
        in_specs=[vmem] * (count + 6),
        out_specs=[vmem] * (groups + 3),
        out_shape=[jax.ShapeDtypeStruct(shape, BF16)] * groups
        + [jax.ShapeDtypeStruct((total, hidden), BF16)] * 2
        + [jax.ShapeDtypeStruct((total, EXT), BF16)],
        scratch_shapes=[pltpu.VMEM((total, width), BF16)],
        compiler_params=pltpu.CompilerParams(vmem_limit_bytes=SCOPED),
        cost_estimate=cost(4 * total * width * hidden, 4 * width * hidden),
        name="hidden_grads",
    )(*blocks, *factors, in_vmem(down_piece), in_vmem(gate_piece), in_vmem(up_piece))
    return out[:groups], out[groups:]


def back_kernel(groups, dgate_ref, dup_ref, part_ref, gate_ref, up_ref, *outs):
    back_columns(groups, 0, dgate_ref, dup_ref, part_ref[...], gate_ref, up_ref, outs)


def back_half(groups, dgate, dup, part, gate_piece, up_piece):
    _, width, hidden = gate_piece.shape
    total = dgate.shape[0]
    shape = (total // groups, width // 2 + EXT)
    vmem = pl.BlockSpec(memory_space=pltpu.VMEM)
    return pl.pallas_call(
        functools.partial(back_kernel, groups),
        in_specs=[vmem] * 5,
        out_specs=[vmem] * groups,
        out_shape=[jax.ShapeDtypeStruct(shape, BF16)] * groups,
        compiler_params=pltpu.CompilerParams(vmem_limit_bytes=SCOPED),
        cost_estimate=cost(2 * total * width * hidden, 2 * width * hidden),
        name="back_half",
    )(dgate, dup, part, in_vmem(gate_piece), in_vmem(up_piece))


def two_terms(value):
    high = value.astype(BF16).astype(F32)
    low = value - high
    lane = lax.broadcasted_iota(jnp.int32, (value.shape[0], EXT), 1)
    return jnp.where(lane == 0, high, jnp.where(lane == 1, low, 0.0)).astype(BF16)


def sum_kernel(groups, *refs):
    ins, outs = refs[:groups], refs[groups:]
    wide = ins[0].shape[1] - EXT
    for s in range(E_MOD):
        rows = slice(s * CAP, (s + 1) * CAP)
        total = ins[0][rows, :].astype(F32)
        for t in range(1, groups):
            total = total + ins[t][rows, :].astype(F32)
        outs[s][:, :wide] = total[:, :wide].astype(BF16)
        outs[s][:, wide:] = two_terms(jnp.sum(total[:, wide:], axis=1, keepdims=True))


def sum_pieces(partials):
    groups = len(partials)
    own_rows, wide = partials[0].shape
    return pl.pallas_call(
        functools.partial(sum_kernel, groups),
        out_shape=[jax.ShapeDtypeStruct((CAP, wide), BF16)] * E_MOD,
        cost_estimate=cost(own_rows * wide, 4 * groups * own_rows * wide),
        compiler_params=pltpu.CompilerParams(vmem_limit_bytes=SCOPED),
        name="sum_pieces",
    )(*partials)


def combine_kernel(groups, order, modality_ref, picks_ref, weights_ref, *refs):
    blocks, (grad_out, gate_out, table) = refs[: 2 * E_MOD], refs[2 * E_MOD :]
    wide = grad_out.shape[1]
    for i, block in zip(order, blocks):
        table[i * CAP : (i + 1) * CAP, :] = block[...]
    count, first, second, member = slot_of_labels(groups, modality_ref, picks_ref)
    slot = jnp.where(member, count, -1)
    scale = jnp.where(first, weights_ref[0:1, :], jnp.where(second, weights_ref[1:2, :], 0.0))
    own = jnp.where(position(groups)[1] == 0, first.astype(F32), second.astype(F32))
    tok_rows = slot.shape[1]
    want = lax.broadcasted_iota(jnp.int32, (CAP, tok_rows), 0)
    mix = []
    gate = jnp.zeros((1, tok_rows), F32)
    for i in range(2 * E_MOD):
        hit = slot[i : i + 1, :] == want
        mix.append(jnp.where(hit, scale[i : i + 1, :], 0.0))
        part = jnp.sum(table[i * CAP : (i + 1) * CAP, wide:].astype(F32), axis=1, keepdims=True)
        gate = gate + jnp.sum(
            jnp.where(hit, own[i : i + 1, :] * part, 0.0), axis=0, keepdims=True
        )
    gate_out[...] = gate
    mix = jnp.concatenate(mix, axis=0).T
    high = mix.astype(BF16)
    low = (mix - high.astype(F32)).astype(BF16)
    values = table[:, :wide]
    total = jnp.dot(high, values, preferred_element_type=F32)
    total = total + jnp.dot(low, values, preferred_element_type=F32)
    grad_out[...] = total.astype(BF16)


def combine(groups, order, modality, picks, weights, blocks):
    tok_rows = modality.shape[1]
    wide = blocks[0].shape[1] - EXT
    count = len(blocks)
    vmem = pl.BlockSpec(memory_space=pltpu.VMEM)
    return pl.pallas_call(
        functools.partial(combine_kernel, groups, order),
        in_specs=[vmem] * (3 + count),
        out_specs=[vmem] * 2,
        out_shape=[
            jax.ShapeDtypeStruct((tok_rows, wide), BF16),
            jax.ShapeDtypeStruct((1, tok_rows), F32),
        ],
        scratch_shapes=[pltpu.VMEM((count * CAP, wide + EXT), BF16)],
        cost_estimate=cost(4 * count * CAP * tok_rows * wide, 4 * tok_rows * wide),
        compiler_params=pltpu.CompilerParams(vmem_limit_bytes=SCOPED),
        name="combine",
    )(modality, picks, weights, *blocks)


def local(tokens, cotangent, modality, picks, gate_weights, gate_proj, up_proj, down_proj):
    device_count = lax.axis_size("ep")
    groups = device_count // E_MOD
    modality = modality.reshape(1, -1)
    picks = picks.T
    weights = gate_weights.T

    def to_expert(x, s, t=0):
        return lax.ppermute(
            x,
            "ep",
            [
                (e * groups + j, (e ^ s) * groups + (j + t) % groups)
                for e in range(E_MOD)
                for j in range(groups)
            ],
        )

    def to_piece(x, t):
        return to_expert(x, 0, t)

    def to_source(x, s, flip):
        return lax.ppermute(
            x,
            ("ep", "mod"),
            [
                ((e * groups + j) * 2 + m, ((e ^ s) * groups + j) * 2 + (m ^ flip))
                for e in range(E_MOD)
                for j in range(groups)
                for m in range(2)
            ],
        )

    sent = gather_slots(groups, modality, picks, tokens, cotangent)
    far = [[to_expert(sent[2 * s - 2], s) for s in range(2, E_MOD)]]
    near = [sent[0], to_expert(sent[1], 1)]
    own_pieces = [to_piece(sent[0], t) for t in range(1, groups)]
    gate_piece = load(gate_proj, sent[:1])
    later = [sent[2 * s - 1] for s in range(2, E_MOD)]
    later = pass_after(later, in_vmem(gate_piece))
    far.append([to_expert(x, s) for x, s in zip(later, range(2, E_MOD))])
    near_pieces = [[x, to_piece(near[1], t)] for t, x in enumerate(own_pieces, 1)]
    up_piece = load(up_proj, [near[1], *own_pieces, in_vmem(gate_piece)])
    far[0] = join(far[0], in_vmem(gate_piece), in_vmem(up_piece))
    far[0] = [far[0]] + [to_piece(far[0], t) for t in range(1, groups)]
    down_piece = load_turned(down_proj, [far[0][0], *sum(near_pieces, []), in_vmem(gate_piece), in_vmem(up_piece)])
    far[1] = join(far[1], in_vmem(gate_piece), in_vmem(up_piece), in_vmem(down_piece))
    far[1] = [far[1]] + [to_piece(far[1], t) for t in range(1, groups)]
    near = near + sum(near_pieces, [])
    blocks = [near + far[a] for a in range(2)]
    places = [
        tuple(
            place
            for t in range(groups)
            for place in [(2 * t, a * CAP), (2 * t + 1, a * CAP)]
            + [(2 * groups + t, i * CAP) for i in range(E_MOD - 2)]
        )
        for a in range(2)
    ]
    factors = pre_activations(blocks[0], places[0], gate_piece, up_piece, down_piece)
    first, (dgate, dup, part) = hidden_grads(
        blocks[1], places[1], groups, factors, down_piece, gate_piece, up_piece
    )
    second = back_half(groups, dgate, dup, part, gate_piece, up_piece)
    first = [first[0]] + [to_piece(first[t], groups - t) for t in range(1, groups)]
    waiting = pass_after(second[1:], *first[1:])
    second = [second[0]] + [to_piece(x, groups - t) for t, x in enumerate(waiting, 1)]
    crossed, kept = sum_pieces(first), sum_pieces(second)
    arrived = {0: kept[0]}
    for s in range(1, E_MOD):
        arrived[s] = to_source(kept[s], s, 0)
    for s in range(E_MOD):
        arrived[E_MOD + s] = to_source(crossed[s], s, 1)
    order = tuple(reversed(arrived))
    token_grad, gate_grad = combine(
        groups, order, modality, picks, weights, [arrived[i] for i in order]
    )
    return token_grad, gate_grad.reshape(-1, 1)


def solution(mesh):
    in_specs = (
        P(("parts", "ep"), None),
        P(("parts", "ep"), None),
        P(("parts", "ep")),
        P(("parts", "ep"), None),
        P(("parts", "ep"), None),
        P("mod", None, "ep"),
        P("mod", None, "ep"),
        P("mod", "ep", None),
    )
    out_specs = (P(("parts", "ep"), "mod"), P(("parts", "ep"), "mod"))
    return jax.shard_map(local, mesh=mesh, in_specs=in_specs, out_specs=out_specs, check_vma=False)
```

```python
import functools

import jax
import jax.numpy as jnp
from jax import lax
from jax.experimental import pallas as pl
from jax.experimental.pallas import tpu as pltpu
from jax.sharding import PartitionSpec as P

E_MOD = 4
CAP = 16
EXT = 128
BF16 = jnp.bfloat16
F32 = jnp.float32
MIB = 1024 * 1024
SCOPED = 10 * MIB


def cost(flops, nbytes):
    return pl.CostEstimate(flops=flops, bytes_accessed=nbytes, transcendentals=0)


def whole(shape):
    return pl.BlockSpec(shape, lambda *_: (0,) * len(shape))


def nt_dot(lhs, rhs):
    return lax.dot_general(lhs, rhs, (((1,), (1,)), ((), ())), preferred_element_type=F32)


def position(groups):
    return lax.axis_index("ep") // groups, lax.axis_index("mod")


def slot_of_labels(groups, modality_ref, picks_ref):
    tok_rows = modality_ref.shape[1]
    label = lax.broadcasted_iota(jnp.int32, (2 * E_MOD, tok_rows), 0)
    own_expert, core = position(groups)
    expert = jnp.bitwise_xor(label % E_MOD, own_expert)
    modal = jnp.bitwise_xor(label // E_MOD, core)
    mine = modality_ref[...] == modal
    first = mine & (picks_ref[0:1, :] == expert)
    second = mine & (picks_ref[1:2, :] == expert)
    member = first | second
    row = lax.broadcasted_iota(jnp.int32, (tok_rows, tok_rows), 0)
    col = lax.broadcasted_iota(jnp.int32, (tok_rows, tok_rows), 1)
    earlier = (row < col).astype(F32)
    count = jnp.dot(member.astype(F32), earlier, preferred_element_type=F32).astype(jnp.int32)
    return count, first, second, member


def gather_kernel(groups, parts, modality_hbm, picks_hbm, rows_hbm, grads_hbm, *refs):
    outs, (modality, picks, rows, chosen, sems) = refs[:-5], refs[-5:]
    chunk = rows.shape[2] // parts
    small = [
        pltpu.make_async_copy(src, dst, sems.at[i])
        for i, (src, dst) in enumerate([(modality_hbm, modality), (picks_hbm, picks)])
    ]
    large = [
        [
            pltpu.make_async_copy(
                src.at[:, pl.ds(i * chunk, chunk)],
                rows.at[a, :, pl.ds(i * chunk, chunk)],
                sems.at[2 + 2 * i + a],
            )
            for a, src in enumerate([rows_hbm, grads_hbm])
        ]
        for i in range(parts)
    ]
    for copy in small + sum(large, []):
        copy.start()
    for copy in small:
        copy.wait()
    count, _, _, member = slot_of_labels(groups, modality, picks)
    slot = jnp.where(member, count, -1)
    want = lax.broadcasted_iota(jnp.int32, (CAP, slot.shape[1]), 0)
    for s in range(E_MOD):
        hit = (slot[s : s + 1, :] == want).astype(F32)
        chosen[s * CAP : (s + 1) * CAP, :] = hit.astype(BF16)
    for i in range(parts):
        cols = slice(i * chunk, (i + 1) * chunk)
        for a in range(2):
            large[i][a].wait()
            picked = jnp.dot(chosen[...], rows[a, :, cols], preferred_element_type=F32).astype(BF16)
            for s in range(E_MOD):
                block = picked[s * CAP : (s + 1) * CAP, :]
                if s < 2:
                    outs[s][a * CAP : (a + 1) * CAP, cols] = block
                else:
                    outs[2 * s - 2 + a][:, cols] = block


def gather_slots(groups, modality, picks, rows, grads):
    tok_rows, width = rows.shape
    parts = 4
    heights = [2 * CAP] * 2 + [CAP] * (2 * E_MOD - 4)
    return pl.pallas_call(
        functools.partial(gather_kernel, groups, parts),
        in_specs=[pl.BlockSpec(memory_space=pl.ANY)] * 4,
        out_specs=[pl.BlockSpec(memory_space=pltpu.VMEM)] * len(heights),
        out_shape=[jax.ShapeDtypeStruct((h, width), BF16) for h in heights],
        scratch_shapes=[
            pltpu.VMEM(modality.shape, jnp.int32),
            pltpu.VMEM(picks.shape, jnp.int32),
            pltpu.VMEM((2, tok_rows, width), BF16),
            pltpu.VMEM((E_MOD * CAP, tok_rows), BF16),
            pltpu.SemaphoreType.DMA((2 + 2 * parts,)),
        ],
        compiler_params=pltpu.CompilerParams(vmem_limit_bytes=SCOPED),
        cost_estimate=cost(4 * E_MOD * CAP * tok_rows * width, 6 * tok_rows * width),
        name="gather_slots",
    )(in_hbm(modality), in_hbm(picks), in_hbm(rows), in_hbm(grads))


def load_kernel(parts, src, *refs):
    dst, sems = refs[-2:]
    rows = src.shape[1] // parts
    copies = [
        pltpu.make_async_copy(
            src.at[:, pl.ds(i * rows, rows), :], dst.at[:, pl.ds(i * rows, rows), :], sems.at[i]
        )
        for i in range(parts)
    ]
    for copy in copies:
        copy.start()
    for copy in copies:
        copy.wait()


def load(weight, after):
    parts = 8
    return pl.pallas_call(
        functools.partial(load_kernel, parts),
        in_specs=[pl.BlockSpec(memory_space=pl.ANY)] * (1 + len(after)),
        out_specs=pl.BlockSpec(memory_space=pltpu.VMEM),
        out_shape=pltpu.VMEM(weight.shape, weight.dtype),
        scratch_shapes=[pltpu.SemaphoreType.DMA((parts,))],
        compiler_params=pltpu.CompilerParams(vmem_limit_bytes=SCOPED),
        cost_estimate=cost(0, 1024),
        name="load",
    )(in_hbm(weight), *after)


def load_turned_kernel(parts, src, *refs):
    dst, stage, sems = refs[-3:]
    rows, width = stage.shape[1:]
    copies = [
        pltpu.make_async_copy(src.at[0, pl.ds(i * rows, rows), :], stage.at[i], sems.at[i])
        for i in range(parts)
    ]
    for copy in copies:
        copy.start()
    chunk = 512
    for i in range(parts):
        copies[i].wait()
        for start in range(0, width, chunk):
            block = stage[i, :, start : start + chunk]
            dst[start : start + chunk, i * rows : (i + 1) * rows] = block.T


def load_turned(weight, after):
    _, height, width = weight.shape
    rows = 128
    parts = height // rows
    return pl.pallas_call(
        functools.partial(load_turned_kernel, parts),
        in_specs=[pl.BlockSpec(memory_space=pl.ANY)] * (1 + len(after)),
        out_specs=pl.BlockSpec(memory_space=pltpu.VMEM),
        out_shape=pltpu.VMEM((width, height), weight.dtype),
        scratch_shapes=[
            pltpu.VMEM((parts, rows, width), weight.dtype),
            pltpu.SemaphoreType.DMA((parts,)),
        ],
        compiler_params=pltpu.CompilerParams(vmem_limit_bytes=SCOPED),
        cost_estimate=cost(0, 1024),
        name="load_turned",
    )(in_hbm(weight), *after)


def pass_kernel(*refs):
    pass


def pass_after(blocks, *need):
    place = pl.BlockSpec(memory_space=pl.ANY)
    return pl.pallas_call(
        pass_kernel,
        in_specs=[place] * (len(blocks) + len(need)),
        out_specs=[place] * len(blocks),
        out_shape=[jax.ShapeDtypeStruct(block.shape, block.dtype) for block in blocks],
        input_output_aliases={i: i for i in range(len(blocks))},
        compiler_params=pltpu.CompilerParams(vmem_limit_bytes=SCOPED),
        cost_estimate=cost(0, 1024),
        name="pass_after",
    )(*blocks, *need)


def join_kernel(count, *refs):
    blocks, out = refs[:count], refs[-1]
    start = 0
    for block in blocks:
        out[start : start + block.shape[0], :] = block[...]
        start += block.shape[0]


def join(blocks, *need):
    count = len(blocks)
    total = sum(block.shape[0] for block in blocks)
    vmem = pl.BlockSpec(memory_space=pltpu.VMEM)
    return pl.pallas_call(
        functools.partial(join_kernel, count),
        in_specs=[vmem] * count + [pl.BlockSpec(memory_space=pl.ANY)] * len(need),
        out_specs=vmem,
        out_shape=jax.ShapeDtypeStruct((total, blocks[0].shape[1]), BF16),
        compiler_params=pltpu.CompilerParams(vmem_limit_bytes=SCOPED),
        cost_estimate=cost(3 * 10**9, 1024),
        name="join",
    )(*blocks, *need)


def in_hbm(x):
    return pltpu.with_memory_space_constraint(x, pltpu.HBM)


def in_vmem(x):
    return pltpu.with_memory_space_constraint(x, pltpu.VMEM)


def fill(rows, refs, places):
    for i, (index, start) in enumerate(places):
        rows[i * CAP : (i + 1) * CAP, :] = refs[index][start : start + CAP, :]


def pre_kernel(count, places, *refs):
    blocks, (gate_ref, up_ref, _, act_out, slope_out, both_out, rows) = refs[:count], refs[count:]
    fill(rows, blocks, places)
    hidden = gate_ref.shape[2]
    chunk = min(256, hidden)
    for start in range(0, hidden, chunk):
        cols = slice(start, start + chunk)
        gate_pre = jnp.dot(rows[...], gate_ref[0, :, cols], preferred_element_type=F32)
        up_pre = jnp.dot(rows[...], up_ref[0, :, cols], preferred_element_type=F32)
        sig = jax.nn.sigmoid(gate_pre)
        act = gate_pre * sig
        act_out[:, cols] = act
        slope_out[:, cols] = up_pre * (sig * (1.0 + gate_pre * (1.0 - sig)))
        both_out[:, cols] = act * up_pre


def pre_activations(blocks, places, gate_piece, up_piece, need):
    count = len(blocks)
    _, width, hidden = gate_piece.shape
    total = len(places) * CAP
    vmem = pl.BlockSpec(memory_space=pltpu.VMEM)
    return pl.pallas_call(
        functools.partial(pre_kernel, count, places),
        in_specs=[vmem] * (count + 2) + [pl.BlockSpec(memory_space=pl.ANY)],
        out_specs=[vmem] * 3,
        out_shape=[jax.ShapeDtypeStruct((total, hidden), F32)] * 3,
        scratch_shapes=[pltpu.VMEM((total, width), BF16)],
        compiler_params=pltpu.CompilerParams(vmem_limit_bytes=SCOPED),
        cost_estimate=cost(5 * 10**9, 1024),
        name="pre_activations",
    )(*blocks, in_vmem(gate_piece), in_vmem(up_piece), in_vmem(need))


def back_columns(groups, flip, dgate_ref, dup_ref, part, gate_ref, up_ref, outs):
    half = jnp.bitwise_xor(position(groups)[1], flip)
    wide = outs[0].shape[1] - EXT
    own_rows = outs[0].shape[0]
    chunk = 512
    for step in range(wide // chunk):
        rows = pl.ds(pl.multiple_of(half * wide + step * chunk, chunk), chunk)
        grad = nt_dot(dgate_ref[...], gate_ref[0, rows, :]) + nt_dot(dup_ref[...], up_ref[0, rows, :])
        grad = grad.astype(BF16)
        for t in range(groups):
            outs[t][:, step * chunk : (step + 1) * chunk] = grad[t * own_rows : (t + 1) * own_rows, :]
    for t in range(groups):
        outs[t][:, wide:] = part[t * own_rows : (t + 1) * own_rows, :]


def hidden_kernel(count, places, groups, *refs):
    blocks = refs[:count]
    act_ref, slope_ref, both_ref, down_ref, gate_ref, up_ref = refs[count : count + 6]
    outs = refs[count + 6 : count + 6 + groups]
    dgate, dup, part_out, rows = refs[count + 6 + groups :]
    fill(rows, blocks, places)
    hidden = gate_ref.shape[2]
    chunk = min(256, hidden)
    part = jnp.zeros((rows.shape[0], 1), F32)
    for start in range(0, hidden, chunk):
        cols = slice(start, start + chunk)
        grad = jnp.dot(rows[...], down_ref[:, cols], preferred_element_type=F32)
        part = part + jnp.sum(grad * both_ref[:, cols], axis=1, keepdims=True)
        dgate[:, cols] = (grad * slope_ref[:, cols]).astype(BF16)
        dup[:, cols] = (grad * act_ref[:, cols]).astype(BF16)
    part_out[...] = two_terms(part)
    back_columns(groups, 1, dgate, dup, part_out[...], gate_ref, up_ref, outs)


def hidden_grads(blocks, places, groups, factors, down_piece, gate_piece, up_piece):
    count = len(blocks)
    _, width, hidden = gate_piece.shape
    total = len(places) * CAP
    shape = (total // groups, width // 2 + EXT)
    vmem = pl.BlockSpec(memory_space=pltpu.VMEM)
    out = pl.pallas_call(
        functools.partial(hidden_kernel, count, places, groups),
        in_specs=[vmem] * (count + 6),
        out_specs=[vmem] * (groups + 3),
        out_shape=[jax.ShapeDtypeStruct(shape, BF16)] * groups
        + [jax.ShapeDtypeStruct((total, hidden), BF16)] * 2
        + [jax.ShapeDtypeStruct((total, EXT), BF16)],
        scratch_shapes=[pltpu.VMEM((total, width), BF16)],
        compiler_params=pltpu.CompilerParams(vmem_limit_bytes=SCOPED),
        cost_estimate=cost(4 * total * width * hidden, 4 * width * hidden),
        name="hidden_grads",
    )(*blocks, *factors, in_vmem(down_piece), in_vmem(gate_piece), in_vmem(up_piece))
    return out[:groups], out[groups:]


def back_kernel(groups, dgate_ref, dup_ref, part_ref, gate_ref, up_ref, *outs):
    back_columns(groups, 0, dgate_ref, dup_ref, part_ref[...], gate_ref, up_ref, outs)


def back_half(groups, dgate, dup, part, gate_piece, up_piece):
    _, width, hidden = gate_piece.shape
    total = dgate.shape[0]
    shape = (total // groups, width // 2 + EXT)
    vmem = pl.BlockSpec(memory_space=pltpu.VMEM)
    return pl.pallas_call(
        functools.partial(back_kernel, groups),
        in_specs=[vmem] * 5,
        out_specs=[vmem] * groups,
        out_shape=[jax.ShapeDtypeStruct(shape, BF16)] * groups,
        compiler_params=pltpu.CompilerParams(vmem_limit_bytes=SCOPED),
        cost_estimate=cost(2 * total * width * hidden, 2 * width * hidden),
        name="back_half",
    )(dgate, dup, part, in_vmem(gate_piece), in_vmem(up_piece))


def two_terms(value):
    high = value.astype(BF16).astype(F32)
    low = value - high
    lane = lax.broadcasted_iota(jnp.int32, (value.shape[0], EXT), 1)
    return jnp.where(lane == 0, high, jnp.where(lane == 1, low, 0.0)).astype(BF16)


def sum_kernel(groups, *refs):
    ins, outs = refs[:groups], refs[groups:]
    wide = ins[0].shape[1] - EXT
    for s in range(E_MOD):
        rows = slice(s * CAP, (s + 1) * CAP)
        total = ins[0][rows, :].astype(F32)
        for t in range(1, groups):
            total = total + ins[t][rows, :].astype(F32)
        outs[s][:, :wide] = total[:, :wide].astype(BF16)
        outs[s][:, wide:] = two_terms(jnp.sum(total[:, wide:], axis=1, keepdims=True))


def sum_pieces(partials):
    groups = len(partials)
    own_rows, wide = partials[0].shape
    return pl.pallas_call(
        functools.partial(sum_kernel, groups),
        out_shape=[jax.ShapeDtypeStruct((CAP, wide), BF16)] * E_MOD,
        cost_estimate=cost(own_rows * wide, 4 * groups * own_rows * wide),
        compiler_params=pltpu.CompilerParams(vmem_limit_bytes=SCOPED),
        name="sum_pieces",
    )(*partials)


def mix_kernel(groups, modality_ref, picks_ref, weights_ref, mix_out, gate_out):
    count, first, second, member = slot_of_labels(groups, modality_ref, picks_ref)
    slot = jnp.where(member, count, -1)
    scale = jnp.where(first, weights_ref[0:1, :], jnp.where(second, weights_ref[1:2, :], 0.0))
    own = jnp.where(position(groups)[1] == 0, first.astype(F32), second.astype(F32))
    want = lax.broadcasted_iota(jnp.int32, (CAP, slot.shape[1]), 0)
    mix = []
    for i in range(2 * E_MOD):
        hit = slot[i : i + 1, :] == want
        mix.append(jnp.where(hit, scale[i : i + 1, :], 0.0))
        gate_out[i * CAP : (i + 1) * CAP, :] = jnp.where(hit, own[i : i + 1, :], 0.0)
    mix = jnp.concatenate(mix, axis=0).T
    high = mix.astype(BF16)
    mix_out[0] = high
    mix_out[1] = (mix - high.astype(F32)).astype(BF16)


def mixing(groups, modality, picks, weights):
    tok_rows = modality.shape[1]
    slots = 2 * E_MOD * CAP
    vmem = pl.BlockSpec(memory_space=pltpu.VMEM)
    return pl.pallas_call(
        functools.partial(mix_kernel, groups),
        in_specs=[vmem] * 3,
        out_specs=[vmem] * 2,
        out_shape=[
            jax.ShapeDtypeStruct((2, tok_rows, slots), BF16),
            jax.ShapeDtypeStruct((slots, tok_rows), F32),
        ],
        compiler_params=pltpu.CompilerParams(vmem_limit_bytes=SCOPED),
        cost_estimate=cost(MIB, 1024),
        name="mixing",
    )(modality, picks, weights)


def combine_kernel(order, mix_ref, hit_ref, *refs):
    blocks, (grad_out, gate_out, table) = refs[: len(order)], refs[len(order) :]
    wide = grad_out.shape[1]
    for i, block in zip(order, blocks):
        table[i * CAP : (i + 1) * CAP, :] = block[...]
    part = jnp.sum(table[:, wide:].astype(F32), axis=1, keepdims=True)
    gate_out[...] = jnp.sum(hit_ref[...] * part, axis=0, keepdims=True)
    total = jnp.dot(mix_ref[0], table[:, :wide], preferred_element_type=F32)
    total = total + jnp.dot(mix_ref[1], table[:, :wide], preferred_element_type=F32)
    grad_out[...] = total.astype(BF16)


def combine(order, mix, hits, blocks):
    tok_rows = hits.shape[1]
    wide = blocks[0].shape[1] - EXT
    count = len(blocks)
    vmem = pl.BlockSpec(memory_space=pltpu.VMEM)
    return pl.pallas_call(
        functools.partial(combine_kernel, order),
        in_specs=[vmem] * (2 + count),
        out_specs=[vmem] * 2,
        out_shape=[
            jax.ShapeDtypeStruct((tok_rows, wide), BF16),
            jax.ShapeDtypeStruct((1, tok_rows), F32),
        ],
        scratch_shapes=[pltpu.VMEM((count * CAP, wide + EXT), BF16)],
        compiler_params=pltpu.CompilerParams(vmem_limit_bytes=SCOPED),
        cost_estimate=cost(4 * count * CAP * tok_rows * wide, 4 * tok_rows * wide),
        name="combine",
    )(mix, hits, *blocks)


def local(tokens, cotangent, modality, picks, gate_weights, gate_proj, up_proj, down_proj):
    device_count = lax.axis_size("ep")
    groups = device_count // E_MOD
    modality = modality.reshape(1, -1)
    picks = picks.T
    weights = gate_weights.T

    def to_expert(x, s, t=0):
        return lax.ppermute(
            x,
            "ep",
            [
                (e * groups + j, (e ^ s) * groups + (j + t) % groups)
                for e in range(E_MOD)
                for j in range(groups)
            ],
        )

    def to_piece(x, t):
        return to_expert(x, 0, t)

    def to_source(x, s, flip):
        return lax.ppermute(
            x,
            ("ep", "mod"),
            [
                ((e * groups + j) * 2 + m, ((e ^ s) * groups + j) * 2 + (m ^ flip))
                for e in range(E_MOD)
                for j in range(groups)
                for m in range(2)
            ],
        )

    mix, hits = mixing(groups, modality, picks, weights)
    sent = gather_slots(groups, modality, picks, tokens, cotangent)
    far = [[to_expert(sent[2 * s - 2], s) for s in range(2, E_MOD)]]
    near = [sent[0], to_expert(sent[1], 1)]
    own_pieces = [to_piece(sent[0], t) for t in range(1, groups)]
    gate_piece = load(gate_proj, sent[:1])
    later = [sent[2 * s - 1] for s in range(2, E_MOD)]
    later = pass_after(later, in_vmem(gate_piece), *own_pieces)
    far.append([to_expert(x, s) for x, s in zip(later, range(2, E_MOD))])
    near_pieces = [[x, to_piece(near[1], t)] for t, x in enumerate(own_pieces, 1)]
    up_piece = load(up_proj, [near[1], in_vmem(gate_piece)])
    far[0] = join(far[0], in_vmem(gate_piece), in_vmem(up_piece))
    far[0] = [far[0]] + [to_piece(far[0], t) for t in range(1, groups)]
    down_piece = load_turned(down_proj, [far[0][0], *sum(near_pieces, []), in_vmem(gate_piece), in_vmem(up_piece)])
    far[1] = join(far[1], in_vmem(gate_piece), in_vmem(up_piece), in_vmem(down_piece))
    far[1] = [far[1]] + [to_piece(far[1], t) for t in range(1, groups)]
    near = near + sum(near_pieces, [])
    blocks = [near + far[a] for a in range(2)]
    places = [
        tuple(
            place
            for t in range(groups)
            for place in [(2 * t, a * CAP), (2 * t + 1, a * CAP)]
            + [(2 * groups + t, i * CAP) for i in range(E_MOD - 2)]
        )
        for a in range(2)
    ]
    factors = pre_activations(blocks[0], places[0], gate_piece, up_piece, down_piece)
    first, (dgate, dup, part) = hidden_grads(
        blocks[1], places[1], groups, factors, down_piece, gate_piece, up_piece
    )
    second = back_half(groups, dgate, dup, part, gate_piece, up_piece)
    first = [first[0]] + [to_piece(first[t], groups - t) for t in range(1, groups)]
    waiting = pass_after(second[1:], *first[1:])
    second = [second[0]] + [to_piece(x, groups - t) for t, x in enumerate(waiting, 1)]
    crossed, kept = sum_pieces(first), sum_pieces(second)
    arrived = {0: kept[0]}
    for s in range(1, E_MOD):
        arrived[s] = to_source(kept[s], s, 0)
    for s in range(E_MOD):
        arrived[E_MOD + s] = to_source(crossed[s], s, 1)
    order = tuple(reversed(arrived))
    token_grad, gate_grad = combine(order, mix, hits, [arrived[i] for i in order])
    return token_grad, gate_grad.reshape(-1, 1)


def solution(mesh):
    in_specs = (
        P(("parts", "ep"), None),
        P(("parts", "ep"), None),
        P(("parts", "ep")),
        P(("parts", "ep"), None),
        P(("parts", "ep"), None),
        P("mod", None, "ep"),
        P("mod", None, "ep"),
        P("mod", "ep", None),
    )
    out_specs = (P(("parts", "ep"), "mod"), P(("parts", "ep"), "mod"))
    return jax.shard_map(local, mesh=mesh, in_specs=in_specs, out_specs=out_specs, check_vma=False)
```

```python
import functools

import jax
import jax.numpy as jnp
from jax import lax
from jax.experimental import pallas as pl
from jax.experimental.pallas import tpu as pltpu
from jax.sharding import PartitionSpec as P

E_MOD = 4
CAP = 16
EXT = 128
BF16 = jnp.bfloat16
F32 = jnp.float32
MIB = 1024 * 1024
SCOPED = 10 * MIB


def cost(flops, nbytes):
    return pl.CostEstimate(flops=flops, bytes_accessed=nbytes, transcendentals=0)


def whole(shape):
    return pl.BlockSpec(shape, lambda *_: (0,) * len(shape))


def nt_dot(lhs, rhs):
    return lax.dot_general(lhs, rhs, (((1,), (1,)), ((), ())), preferred_element_type=F32)


def position(groups):
    return lax.axis_index("ep") // groups, lax.axis_index("mod")


def slot_of_labels(groups, modality_ref, picks_ref):
    tok_rows = modality_ref.shape[1]
    label = lax.broadcasted_iota(jnp.int32, (2 * E_MOD, tok_rows), 0)
    own_expert, core = position(groups)
    expert = jnp.bitwise_xor(label % E_MOD, own_expert)
    modal = jnp.bitwise_xor(label // E_MOD, core)
    mine = modality_ref[...] == modal
    first = mine & (picks_ref[0:1, :] == expert)
    second = mine & (picks_ref[1:2, :] == expert)
    member = first | second
    row = lax.broadcasted_iota(jnp.int32, (tok_rows, tok_rows), 0)
    col = lax.broadcasted_iota(jnp.int32, (tok_rows, tok_rows), 1)
    earlier = (row < col).astype(F32)
    count = jnp.dot(member.astype(F32), earlier, preferred_element_type=F32).astype(jnp.int32)
    return count, first, second, member


def gather_kernel(groups, parts, modality_hbm, picks_hbm, rows_hbm, grads_hbm, *refs):
    outs, (modality, picks, rows, chosen, sems) = refs[:-5], refs[-5:]
    chunk = rows.shape[2] // parts
    small = [
        pltpu.make_async_copy(src, dst, sems.at[i])
        for i, (src, dst) in enumerate([(modality_hbm, modality), (picks_hbm, picks)])
    ]
    large = [
        [
            pltpu.make_async_copy(
                src.at[:, pl.ds(i * chunk, chunk)],
                rows.at[a, :, pl.ds(i * chunk, chunk)],
                sems.at[2 + 2 * i + a],
            )
            for a, src in enumerate([rows_hbm, grads_hbm])
        ]
        for i in range(parts)
    ]
    for copy in small + sum(large, []):
        copy.start()
    for copy in small:
        copy.wait()
    count, _, _, member = slot_of_labels(groups, modality, picks)
    slot = jnp.where(member, count, -1)
    want = lax.broadcasted_iota(jnp.int32, (CAP, slot.shape[1]), 0)
    for s in range(E_MOD):
        hit = (slot[s : s + 1, :] == want).astype(F32)
        chosen[s * CAP : (s + 1) * CAP, :] = hit.astype(BF16)
    for i in range(parts):
        cols = slice(i * chunk, (i + 1) * chunk)
        for a in range(2):
            large[i][a].wait()
            picked = jnp.dot(chosen[...], rows[a, :, cols], preferred_element_type=F32).astype(BF16)
            for s in range(E_MOD):
                block = picked[s * CAP : (s + 1) * CAP, :]
                if s < 2:
                    outs[s][a * CAP : (a + 1) * CAP, cols] = block
                else:
                    outs[2 * s - 2 + a][:, cols] = block


def gather_slots(groups, modality, picks, rows, grads):
    tok_rows, width = rows.shape
    parts = 4
    heights = [2 * CAP] * 2 + [CAP] * (2 * E_MOD - 4)
    return pl.pallas_call(
        functools.partial(gather_kernel, groups, parts),
        in_specs=[pl.BlockSpec(memory_space=pl.ANY)] * 4,
        out_specs=[pl.BlockSpec(memory_space=pltpu.VMEM)] * len(heights),
        out_shape=[jax.ShapeDtypeStruct((h, width), BF16) for h in heights],
        scratch_shapes=[
            pltpu.VMEM(modality.shape, jnp.int32),
            pltpu.VMEM(picks.shape, jnp.int32),
            pltpu.VMEM((2, tok_rows, width), BF16),
            pltpu.VMEM((E_MOD * CAP, tok_rows), BF16),
            pltpu.SemaphoreType.DMA((2 + 2 * parts,)),
        ],
        compiler_params=pltpu.CompilerParams(vmem_limit_bytes=SCOPED),
        cost_estimate=cost(4 * E_MOD * CAP * tok_rows * width, 6 * tok_rows * width),
        name="gather_slots",
    )(in_hbm(modality), in_hbm(picks), in_hbm(rows), in_hbm(grads))


def load_kernel(parts, src, *refs):
    dst, sems = refs[-2:]
    rows = src.shape[1] // parts
    copies = [
        pltpu.make_async_copy(
            src.at[:, pl.ds(i * rows, rows), :], dst.at[:, pl.ds(i * rows, rows), :], sems.at[i]
        )
        for i in range(parts)
    ]
    for copy in copies:
        copy.start()
    for copy in copies:
        copy.wait()


def load(weight, after):
    parts = 8
    return pl.pallas_call(
        functools.partial(load_kernel, parts),
        in_specs=[pl.BlockSpec(memory_space=pl.ANY)] * (1 + len(after)),
        out_specs=pl.BlockSpec(memory_space=pltpu.VMEM),
        out_shape=pltpu.VMEM(weight.shape, weight.dtype),
        scratch_shapes=[pltpu.SemaphoreType.DMA((parts,))],
        compiler_params=pltpu.CompilerParams(vmem_limit_bytes=SCOPED),
        cost_estimate=cost(0, 1024),
        name="load",
    )(in_hbm(weight), *after)


def load_turned_kernel(parts, src, *refs):
    dst, stage, sems = refs[-3:]
    rows, width = stage.shape[1:]
    copies = [
        pltpu.make_async_copy(src.at[0, pl.ds(i * rows, rows), :], stage.at[i], sems.at[i])
        for i in range(parts)
    ]
    for copy in copies:
        copy.start()
    chunk = 512
    for i in range(parts):
        copies[i].wait()
        for start in range(0, width, chunk):
            block = stage[i, :, start : start + chunk]
            dst[start : start + chunk, i * rows : (i + 1) * rows] = block.T


def load_turned(weight, after):
    _, height, width = weight.shape
    rows = 128
    parts = height // rows
    return pl.pallas_call(
        functools.partial(load_turned_kernel, parts),
        in_specs=[pl.BlockSpec(memory_space=pl.ANY)] * (1 + len(after)),
        out_specs=pl.BlockSpec(memory_space=pltpu.VMEM),
        out_shape=pltpu.VMEM((width, height), weight.dtype),
        scratch_shapes=[
            pltpu.VMEM((parts, rows, width), weight.dtype),
            pltpu.SemaphoreType.DMA((parts,)),
        ],
        compiler_params=pltpu.CompilerParams(vmem_limit_bytes=SCOPED),
        cost_estimate=cost(0, 1024),
        name="load_turned",
    )(in_hbm(weight), *after)


def pass_kernel(*refs):
    pass


def pass_after(blocks, *need):
    place = pl.BlockSpec(memory_space=pl.ANY)
    return pl.pallas_call(
        pass_kernel,
        in_specs=[place] * (len(blocks) + len(need)),
        out_specs=[place] * len(blocks),
        out_shape=[jax.ShapeDtypeStruct(block.shape, block.dtype) for block in blocks],
        input_output_aliases={i: i for i in range(len(blocks))},
        compiler_params=pltpu.CompilerParams(vmem_limit_bytes=SCOPED),
        cost_estimate=cost(0, 1024),
        name="pass_after",
    )(*blocks, *need)


def join_kernel(count, *refs):
    blocks, out = refs[:count], refs[-1]
    start = 0
    for block in blocks:
        out[start : start + block.shape[0], :] = block[...]
        start += block.shape[0]


def join(blocks, *need):
    count = len(blocks)
    total = sum(block.shape[0] for block in blocks)
    vmem = pl.BlockSpec(memory_space=pltpu.VMEM)
    return pl.pallas_call(
        functools.partial(join_kernel, count),
        in_specs=[vmem] * count + [pl.BlockSpec(memory_space=pl.ANY)] * len(need),
        out_specs=vmem,
        out_shape=jax.ShapeDtypeStruct((total, blocks[0].shape[1]), BF16),
        compiler_params=pltpu.CompilerParams(vmem_limit_bytes=SCOPED),
        cost_estimate=cost(3 * 10**9, 1024),
        name="join",
    )(*blocks, *need)


def in_hbm(x):
    return pltpu.with_memory_space_constraint(x, pltpu.HBM)


def in_vmem(x):
    return pltpu.with_memory_space_constraint(x, pltpu.VMEM)


def fill(rows, refs, places):
    for i, (index, start) in enumerate(places):
        rows[i * CAP : (i + 1) * CAP, :] = refs[index][start : start + CAP, :]


def pre_kernel(count, places, *refs):
    blocks, (gate_ref, up_ref, _, act_out, slope_out, both_out, rows) = refs[:count], refs[count:]
    fill(rows, blocks, places)
    hidden = gate_ref.shape[2]
    chunk = min(256, hidden)
    for start in range(0, hidden, chunk):
        cols = slice(start, start + chunk)
        gate_pre = jnp.dot(rows[...], gate_ref[0, :, cols], preferred_element_type=F32)
        up_pre = jnp.dot(rows[...], up_ref[0, :, cols], preferred_element_type=F32)
        sig = jax.nn.sigmoid(gate_pre)
        act = gate_pre * sig
        act_out[:, cols] = act
        slope_out[:, cols] = up_pre * (sig * (1.0 + gate_pre * (1.0 - sig)))
        both_out[:, cols] = act * up_pre


def pre_activations(blocks, places, gate_piece, up_piece, need):
    count = len(blocks)
    _, width, hidden = gate_piece.shape
    total = len(places) * CAP
    vmem = pl.BlockSpec(memory_space=pltpu.VMEM)
    return pl.pallas_call(
        functools.partial(pre_kernel, count, places),
        in_specs=[vmem] * (count + 2) + [pl.BlockSpec(memory_space=pl.ANY)],
        out_specs=[vmem] * 3,
        out_shape=[jax.ShapeDtypeStruct((total, hidden), F32)] * 3,
        scratch_shapes=[pltpu.VMEM((total, width), BF16)],
        compiler_params=pltpu.CompilerParams(vmem_limit_bytes=SCOPED),
        cost_estimate=cost(5 * 10**9, 1024),
        name="pre_activations",
    )(*blocks, in_vmem(gate_piece), in_vmem(up_piece), in_vmem(need))


def back_columns(groups, flip, dgate_ref, dup_ref, part, gate_ref, up_ref, outs):
    half = jnp.bitwise_xor(position(groups)[1], flip)
    wide = outs[0].shape[1] - EXT
    chunk = 512
    places = [slice(i * 2 * CAP, (i + 1) * 2 * CAP) for i in range(len(outs))]
    for step in range(wide // chunk):
        rows = pl.ds(pl.multiple_of(half * wide + step * chunk, chunk), chunk)
        grad = nt_dot(dgate_ref[...], gate_ref[0, rows, :]) + nt_dot(dup_ref[...], up_ref[0, rows, :])
        grad = grad.astype(BF16)
        for out, place in zip(outs, places):
            out[:, step * chunk : (step + 1) * chunk] = grad[place, :]
    for out, place in zip(outs, places):
        out[:, wide:] = part[place, :]


def hidden_kernel(count, places, first_row, groups, *refs):
    blocks = refs[:count]
    act_ref, slope_ref, both_ref, down_ref, gate_ref, up_ref = refs[count : count + 6]
    outs = refs[-4 - groups : -4]
    dgate, dup, part_out, rows = refs[-4:]
    fill(rows, blocks, places)
    hidden = gate_ref.shape[2]
    chunk = min(256, hidden)
    used = slice(first_row, first_row + rows.shape[0])
    part = jnp.zeros((rows.shape[0], 1), F32)
    for start in range(0, hidden, chunk):
        cols = slice(start, start + chunk)
        grad = jnp.dot(rows[...], down_ref[:, cols], preferred_element_type=F32)
        part = part + jnp.sum(grad * both_ref[used, cols], axis=1, keepdims=True)
        dgate[:, cols] = (grad * slope_ref[used, cols]).astype(BF16)
        dup[:, cols] = (grad * act_ref[used, cols]).astype(BF16)
    part_out[...] = two_terms(part)
    back_columns(groups, 1, dgate, dup, part_out[...], gate_ref, up_ref, outs)


def hidden_grads(blocks, places, first_row, groups, factors, pieces, after):
    count = len(blocks)
    gate_piece, up_piece, down_piece = pieces
    _, width, hidden = gate_piece.shape
    total = len(places) * CAP
    shape = (2 * CAP, width // 2 + EXT)
    vmem = pl.BlockSpec(memory_space=pltpu.VMEM)
    out = pl.pallas_call(
        functools.partial(hidden_kernel, count, places, first_row, groups),
        in_specs=[vmem] * (count + 6) + [pl.BlockSpec(memory_space=pl.ANY)] * len(after),
        out_specs=[vmem] * (groups + 3),
        out_shape=[jax.ShapeDtypeStruct(shape, BF16)] * groups
        + [jax.ShapeDtypeStruct((total, hidden), BF16)] * 2
        + [jax.ShapeDtypeStruct((total, EXT), BF16)],
        scratch_shapes=[pltpu.VMEM((total, width), BF16)],
        compiler_params=pltpu.CompilerParams(vmem_limit_bytes=SCOPED),
        cost_estimate=cost(4 * total * width * hidden, 4 * width * hidden),
        name="hidden_grads",
    )(*blocks, *factors, in_vmem(down_piece), in_vmem(gate_piece), in_vmem(up_piece), *after)
    return list(out[:groups]), list(out[groups:])


def back_kernel(groups, *refs):
    parts, (gate_ref, up_ref) = (refs[:3], refs[3:6]), refs[6:8]
    outs, (dgate, dup) = refs[-2 - 2 * groups : -2], refs[-2:]
    half = dgate.shape[0] // 2
    for i, (dgate_ref, dup_ref, _) in enumerate(parts):
        dgate[i * half : (i + 1) * half, :] = dgate_ref[...]
        dup[i * half : (i + 1) * half, :] = dup_ref[...]
    part = jnp.concatenate([refs[2][...], refs[5][...]], axis=0)
    back_columns(groups, 0, dgate, dup, part, gate_ref, up_ref, outs)


def back_half(groups, near, far, pieces, after):
    gate_piece, up_piece, _ = pieces
    _, width, hidden = gate_piece.shape
    total = 2 * near[0].shape[0]
    shape = (2 * CAP, width // 2 + EXT)
    vmem = pl.BlockSpec(memory_space=pltpu.VMEM)
    out = pl.pallas_call(
        functools.partial(back_kernel, groups),
        in_specs=[vmem] * 8 + [pl.BlockSpec(memory_space=pl.ANY)] * len(after),
        out_specs=[vmem] * (2 * groups),
        out_shape=[jax.ShapeDtypeStruct(shape, BF16)] * (2 * groups),
        scratch_shapes=[pltpu.VMEM((total, hidden), BF16)] * 2,
        compiler_params=pltpu.CompilerParams(vmem_limit_bytes=SCOPED),
        cost_estimate=cost(2 * total * width * hidden, 2 * width * hidden),
        name="back_half",
    )(*near, *far, in_vmem(gate_piece), in_vmem(up_piece), *after)
    return list(out[:groups]), list(out[groups:])


def two_terms(value):
    high = value.astype(BF16).astype(F32)
    low = value - high
    lane = lax.broadcasted_iota(jnp.int32, (value.shape[0], EXT), 1)
    return jnp.where(lane == 0, high, jnp.where(lane == 1, low, 0.0)).astype(BF16)


def sum_kernel(groups, *refs):
    ins, outs = refs[:groups], refs[groups:]
    wide = ins[0].shape[1] - EXT
    for s in range(2):
        rows = slice(s * CAP, (s + 1) * CAP)
        total = ins[0][rows, :].astype(F32)
        for t in range(1, groups):
            total = total + ins[t][rows, :].astype(F32)
        outs[s][:, :wide] = total[:, :wide].astype(BF16)
        outs[s][:, wide:] = two_terms(jnp.sum(total[:, wide:], axis=1, keepdims=True))


def sum_pieces(partials):
    groups = len(partials)
    own_rows, wide = partials[0].shape
    return pl.pallas_call(
        functools.partial(sum_kernel, groups),
        out_shape=[jax.ShapeDtypeStruct((CAP, wide), BF16)] * 2,
        cost_estimate=cost(own_rows * wide, 4 * groups * own_rows * wide),
        compiler_params=pltpu.CompilerParams(vmem_limit_bytes=SCOPED),
        name="sum_pieces",
    )(*partials)


def mix_kernel(groups, modality_ref, picks_ref, weights_ref, mix_out, gate_out):
    count, first, second, member = slot_of_labels(groups, modality_ref, picks_ref)
    slot = jnp.where(member, count, -1)
    scale = jnp.where(first, weights_ref[0:1, :], jnp.where(second, weights_ref[1:2, :], 0.0))
    own = jnp.where(position(groups)[1] == 0, first.astype(F32), second.astype(F32))
    want = lax.broadcasted_iota(jnp.int32, (CAP, slot.shape[1]), 0)
    mix = []
    for i in range(2 * E_MOD):
        hit = slot[i : i + 1, :] == want
        mix.append(jnp.where(hit, scale[i : i + 1, :], 0.0))
        gate_out[i * CAP : (i + 1) * CAP, :] = jnp.where(hit, own[i : i + 1, :], 0.0)
    mix = jnp.concatenate(mix, axis=0).T
    high = mix.astype(BF16)
    mix_out[0] = high
    mix_out[1] = (mix - high.astype(F32)).astype(BF16)


def mixing(groups, modality, picks, weights):
    tok_rows = modality.shape[1]
    slots = 2 * E_MOD * CAP
    vmem = pl.BlockSpec(memory_space=pltpu.VMEM)
    return pl.pallas_call(
        functools.partial(mix_kernel, groups),
        in_specs=[vmem] * 3,
        out_specs=[vmem] * 2,
        out_shape=[
            jax.ShapeDtypeStruct((2, tok_rows, slots), BF16),
            jax.ShapeDtypeStruct((slots, tok_rows), F32),
        ],
        compiler_params=pltpu.CompilerParams(vmem_limit_bytes=SCOPED),
        cost_estimate=cost(MIB, 1024),
        name="mixing",
    )(modality, picks, weights)


def combine_kernel(order, mix_ref, hit_ref, *refs):
    blocks, (grad_out, gate_out, table) = refs[: len(order)], refs[len(order) :]
    wide = grad_out.shape[1]
    for i, block in zip(order, blocks):
        table[i * CAP : (i + 1) * CAP, :] = block[...]
    part = jnp.sum(table[:, wide:].astype(F32), axis=1, keepdims=True)
    gate_out[...] = jnp.sum(hit_ref[...] * part, axis=0, keepdims=True)
    total = jnp.dot(mix_ref[0], table[:, :wide], preferred_element_type=F32)
    total = total + jnp.dot(mix_ref[1], table[:, :wide], preferred_element_type=F32)
    grad_out[...] = total.astype(BF16)


def combine(order, mix, hits, blocks):
    tok_rows = hits.shape[1]
    wide = blocks[0].shape[1] - EXT
    count = len(blocks)
    vmem = pl.BlockSpec(memory_space=pltpu.VMEM)
    return pl.pallas_call(
        functools.partial(combine_kernel, order),
        in_specs=[vmem] * (2 + count),
        out_specs=[vmem] * 2,
        out_shape=[
            jax.ShapeDtypeStruct((tok_rows, wide), BF16),
            jax.ShapeDtypeStruct((1, tok_rows), F32),
        ],
        scratch_shapes=[pltpu.VMEM((count * CAP, wide + EXT), BF16)],
        compiler_params=pltpu.CompilerParams(vmem_limit_bytes=SCOPED),
        cost_estimate=cost(4 * count * CAP * tok_rows * wide, 4 * tok_rows * wide),
        name="combine",
    )(mix, hits, *blocks)


def local(tokens, cotangent, modality, picks, gate_weights, gate_proj, up_proj, down_proj):
    device_count = lax.axis_size("ep")
    groups = device_count // E_MOD
    modality = modality.reshape(1, -1)
    picks = picks.T
    weights = gate_weights.T

    def to_expert(x, s, t=0):
        return lax.ppermute(
            x,
            "ep",
            [
                (e * groups + j, (e ^ s) * groups + (j + t) % groups)
                for e in range(E_MOD)
                for j in range(groups)
            ],
        )

    def to_piece(x, t):
        return to_expert(x, 0, t)

    def to_source(x, s, flip):
        return lax.ppermute(
            x,
            ("ep", "mod"),
            [
                ((e * groups + j) * 2 + m, ((e ^ s) * groups + j) * 2 + (m ^ flip))
                for e in range(E_MOD)
                for j in range(groups)
                for m in range(2)
            ],
        )

    mix, hits = mixing(groups, modality, picks, weights)
    sent = gather_slots(groups, modality, picks, tokens, cotangent)
    far = [[to_expert(sent[2 * s - 2], s) for s in range(2, E_MOD)]]
    near = [sent[0], to_expert(sent[1], 1)]
    own_pieces = [to_piece(sent[0], t) for t in range(1, groups)]
    gate_piece = load(gate_proj, sent[:1])
    later = [sent[2 * s - 1] for s in range(2, E_MOD)]
    later = pass_after(later, in_vmem(gate_piece), *own_pieces)
    far.append([to_expert(x, s) for x, s in zip(later, range(2, E_MOD))])
    near_pieces = [[x, to_piece(near[1], t)] for t, x in enumerate(own_pieces, 1)]
    up_piece = load(up_proj, [near[1], in_vmem(gate_piece)])
    far[0] = join(far[0], in_vmem(gate_piece), in_vmem(up_piece))
    far[0] = [far[0]] + [to_piece(far[0], t) for t in range(1, groups)]
    down_piece = load_turned(down_proj, [far[0][0], *sum(near_pieces, []), in_vmem(gate_piece), in_vmem(up_piece)])
    far[1] = join(far[1], in_vmem(gate_piece), in_vmem(up_piece), in_vmem(down_piece))
    far[1] = [far[1]] + [to_piece(far[1], t) for t in range(1, groups)]
    near = near + sum(near_pieces, [])
    pieces = (gate_piece, up_piece, down_piece)
    near_places, far_places = [
        [(i, start) for i in range(count) for start in starts]
        for count, starts in ((2 * groups, [0]), (groups, [0, CAP]))
    ]
    pre_places = near_places + [(2 * groups + i, start) for i, start in far_places]
    factors = pre_activations(near + far[0], pre_places, gate_piece, up_piece, down_piece)

    def exchange(parts):
        return [parts[0]] + [to_piece(parts[t], groups - t) for t in range(1, groups)]

    near_places = [(i, CAP) for i, _ in near_places]
    near_rows = len(near_places) * CAP
    near_first, near_back = hidden_grads(near, near_places, 0, groups, factors, pieces, [])
    near_first = exchange(near_first)
    far_first, far_back = hidden_grads(
        far[1], far_places, near_rows, groups, factors, pieces, near_back[2:]
    )
    far_first = exchange(far_first)
    near_second, far_second = back_half(groups, near_back, far_back, pieces, near_first[1:])
    near_second = exchange(near_second)
    far_second[1:] = pass_after(far_second[1:], *far_first[1:])
    far_second = exchange(far_second)
    crossed = sum_pieces(far_first)
    kept = sum_pieces(far_second)
    crossed = [*pass_after(sum_pieces(near_first), kept[0]), *crossed]
    kept = [*sum_pieces(near_second), *kept]
    arrived = {0: kept[0]}
    for s in range(1, E_MOD):
        arrived[s] = to_source(kept[s], s, 0)
    for s in range(E_MOD):
        arrived[E_MOD + s] = to_source(crossed[s], s, 1)
    order = (5, 4, 7, 6, 1, 3, 2, 0)
    token_grad, gate_grad = combine(order, mix, hits, [arrived[i] for i in order])
    return token_grad, gate_grad.reshape(-1, 1)


def solution(mesh):
    in_specs = (
        P(("parts", "ep"), None),
        P(("parts", "ep"), None),
        P(("parts", "ep")),
        P(("parts", "ep"), None),
        P(("parts", "ep"), None),
        P("mod", None, "ep"),
        P("mod", None, "ep"),
        P("mod", "ep", None),
    )
    out_specs = (P(("parts", "ep"), "mod"), P(("parts", "ep"), "mod"))
    return jax.shard_map(local, mesh=mesh, in_specs=in_specs, out_specs=out_specs, check_vma=False)
```

```python
import functools

import jax
import jax.numpy as jnp
from jax import lax
from jax.experimental import pallas as pl
from jax.experimental.pallas import tpu as pltpu
from jax.sharding import PartitionSpec as P

E_MOD = 4
CAP = 16
EXT = 128
BF16 = jnp.bfloat16
F32 = jnp.float32
MIB = 1024 * 1024
SCOPED = 10 * MIB


def cost(flops, nbytes):
    return pl.CostEstimate(flops=flops, bytes_accessed=nbytes, transcendentals=0)


def whole(shape):
    return pl.BlockSpec(shape, lambda *_: (0,) * len(shape))


def position(groups):
    return lax.axis_index("ep") // groups, lax.axis_index("mod")


def slot_of_labels(groups, modality_ref, picks_ref):
    tok_rows = modality_ref.shape[1]
    label = lax.broadcasted_iota(jnp.int32, (2 * E_MOD, tok_rows), 0)
    own_expert, core = position(groups)
    expert = jnp.bitwise_xor(label % E_MOD, own_expert)
    modal = jnp.bitwise_xor(label // E_MOD, core)
    mine = modality_ref[...] == modal
    first = mine & (picks_ref[0:1, :] == expert)
    second = mine & (picks_ref[1:2, :] == expert)
    member = first | second
    row = lax.broadcasted_iota(jnp.int32, (tok_rows, tok_rows), 0)
    col = lax.broadcasted_iota(jnp.int32, (tok_rows, tok_rows), 1)
    earlier = (row < col).astype(F32)
    count = jnp.dot(member.astype(F32), earlier, preferred_element_type=F32).astype(jnp.int32)
    return count, first, second, member


def gather_kernel(groups, parts, modality_hbm, picks_hbm, rows_hbm, grads_hbm, *refs):
    outs, (modality, picks, rows, chosen, sems) = refs[:-5], refs[-5:]
    chunk = rows.shape[2] // parts
    small = [
        pltpu.make_async_copy(src, dst, sems.at[i])
        for i, (src, dst) in enumerate([(modality_hbm, modality), (picks_hbm, picks)])
    ]
    large = [
        [
            pltpu.make_async_copy(
                src.at[:, pl.ds(i * chunk, chunk)],
                rows.at[a, :, pl.ds(i * chunk, chunk)],
                sems.at[2 + 2 * i + a],
            )
            for a, src in enumerate([rows_hbm, grads_hbm])
        ]
        for i in range(parts)
    ]
    for copy in small + sum(large, []):
        copy.start()
    for copy in small:
        copy.wait()
    count, _, _, member = slot_of_labels(groups, modality, picks)
    slot = jnp.where(member, count, -1)
    want = lax.broadcasted_iota(jnp.int32, (CAP, slot.shape[1]), 0)
    for s in range(E_MOD):
        hit = (slot[s : s + 1, :] == want).astype(F32)
        chosen[s * CAP : (s + 1) * CAP, :] = hit.astype(BF16)
    for i in range(parts):
        cols = slice(i * chunk, (i + 1) * chunk)
        for a in range(2):
            large[i][a].wait()
            picked = jnp.dot(chosen[...], rows[a, :, cols], preferred_element_type=F32).astype(BF16)
            for s in range(E_MOD):
                block = picked[s * CAP : (s + 1) * CAP, :]
                if s < 2:
                    outs[s][a * CAP : (a + 1) * CAP, cols] = block
                else:
                    outs[2 * s - 2 + a][:, cols] = block


def gather_slots(groups, modality, picks, rows, grads):
    tok_rows, width = rows.shape
    parts = 4
    heights = [2 * CAP] * 2 + [CAP] * (2 * E_MOD - 4)
    return pl.pallas_call(
        functools.partial(gather_kernel, groups, parts),
        in_specs=[pl.BlockSpec(memory_space=pl.ANY)] * 4,
        out_specs=[pl.BlockSpec(memory_space=pltpu.VMEM)] * len(heights),
        out_shape=[jax.ShapeDtypeStruct((h, width), BF16) for h in heights],
        scratch_shapes=[
            pltpu.VMEM(modality.shape, jnp.int32),
            pltpu.VMEM(picks.shape, jnp.int32),
            pltpu.VMEM((2, tok_rows, width), BF16),
            pltpu.VMEM((E_MOD * CAP, tok_rows), BF16),
            pltpu.SemaphoreType.DMA((2 + 2 * parts,)),
        ],
        compiler_params=pltpu.CompilerParams(vmem_limit_bytes=SCOPED),
        cost_estimate=cost(4 * E_MOD * CAP * tok_rows * width, 6 * tok_rows * width),
        name="gather_slots",
    )(in_hbm(modality), in_hbm(picks), in_hbm(rows), in_hbm(grads))


def load_kernel(parts, src, *refs):
    dst, sems = refs[-2:]
    rows = src.shape[1] // parts
    copies = [
        pltpu.make_async_copy(
            src.at[:, pl.ds(i * rows, rows), :], dst.at[:, pl.ds(i * rows, rows), :], sems.at[i]
        )
        for i in range(parts)
    ]
    for copy in copies:
        copy.start()
    for copy in copies:
        copy.wait()


def load(weight, after):
    parts = 8
    return pl.pallas_call(
        functools.partial(load_kernel, parts),
        in_specs=[pl.BlockSpec(memory_space=pl.ANY)] * (1 + len(after)),
        out_specs=pl.BlockSpec(memory_space=pltpu.VMEM),
        out_shape=pltpu.VMEM(weight.shape, weight.dtype),
        scratch_shapes=[pltpu.SemaphoreType.DMA((parts,))],
        compiler_params=pltpu.CompilerParams(vmem_limit_bytes=SCOPED),
        cost_estimate=cost(0, 1024),
        name="load",
    )(in_hbm(weight), *after)


def load_turned_kernel(parts, src, *refs):
    dst, stage, sems = refs[-3:]
    rows, width = stage.shape[1:]
    copies = [
        pltpu.make_async_copy(src.at[0, pl.ds(i * rows, rows), :], stage.at[i], sems.at[i])
        for i in range(parts)
    ]
    for copy in copies:
        copy.start()
    chunk = 512
    for i in range(parts):
        copies[i].wait()
        for start in range(0, width, chunk):
            block = stage[i, :, start : start + chunk]
            dst[start : start + chunk, i * rows : (i + 1) * rows] = block.T


def load_turned(weight, after):
    _, height, width = weight.shape
    rows = 128
    parts = height // rows
    return pl.pallas_call(
        functools.partial(load_turned_kernel, parts),
        in_specs=[pl.BlockSpec(memory_space=pl.ANY)] * (1 + len(after)),
        out_specs=pl.BlockSpec(memory_space=pltpu.VMEM),
        out_shape=pltpu.VMEM((width, height), weight.dtype),
        scratch_shapes=[
            pltpu.VMEM((parts, rows, width), weight.dtype),
            pltpu.SemaphoreType.DMA((parts,)),
        ],
        compiler_params=pltpu.CompilerParams(vmem_limit_bytes=SCOPED),
        cost_estimate=cost(0, 1024),
        name="load_turned",
    )(in_hbm(weight), *after)


def pass_kernel(*refs):
    pass


def pass_after(blocks, *need):
    place = pl.BlockSpec(memory_space=pl.ANY)
    return pl.pallas_call(
        pass_kernel,
        in_specs=[place] * (len(blocks) + len(need)),
        out_specs=[place] * len(blocks),
        out_shape=[jax.ShapeDtypeStruct(block.shape, block.dtype) for block in blocks],
        input_output_aliases={i: i for i in range(len(blocks))},
        compiler_params=pltpu.CompilerParams(vmem_limit_bytes=SCOPED),
        cost_estimate=cost(0, 1024),
        name="pass_after",
    )(*blocks, *need)


def join_kernel(count, *refs):
    blocks, out = refs[:count], refs[-1]
    start = 0
    for block in blocks:
        out[start : start + block.shape[0], :] = block[...]
        start += block.shape[0]


def join(blocks, *need):
    count = len(blocks)
    total = sum(block.shape[0] for block in blocks)
    vmem = pl.BlockSpec(memory_space=pltpu.VMEM)
    return pl.pallas_call(
        functools.partial(join_kernel, count),
        in_specs=[vmem] * count + [pl.BlockSpec(memory_space=pl.ANY)] * len(need),
        out_specs=vmem,
        out_shape=jax.ShapeDtypeStruct((total, blocks[0].shape[1]), BF16),
        compiler_params=pltpu.CompilerParams(vmem_limit_bytes=SCOPED),
        cost_estimate=cost(3 * 10**9, 1024),
        name="join",
    )(*blocks, *need)


def in_hbm(x):
    return pltpu.with_memory_space_constraint(x, pltpu.HBM)


def in_vmem(x):
    return pltpu.with_memory_space_constraint(x, pltpu.VMEM)


def fill(rows, refs, places):
    for i, (index, start) in enumerate(places):
        rows[i * CAP : (i + 1) * CAP, :] = refs[index][start : start + CAP, :]


def pre_kernel(count, places, *refs):
    blocks, (gate_ref, up_ref, _, act_out, slope_out, both_out, rows) = refs[:count], refs[count:]
    fill(rows, blocks, places)
    hidden = gate_ref.shape[2]
    chunk = min(256, hidden)
    for start in range(0, hidden, chunk):
        cols = slice(start, start + chunk)
        gate_pre = jnp.dot(rows[...], gate_ref[0, :, cols], preferred_element_type=F32)
        up_pre = jnp.dot(rows[...], up_ref[0, :, cols], preferred_element_type=F32)
        sig = jax.nn.sigmoid(gate_pre)
        act = gate_pre * sig
        act_out[:, cols] = act
        slope_out[:, cols] = up_pre * (sig * (1.0 + gate_pre * (1.0 - sig)))
        both_out[:, cols] = act * up_pre


def pre_activations(blocks, places, gate_piece, up_piece, need):
    count = len(blocks)
    _, width, hidden = gate_piece.shape
    total = len(places) * CAP
    vmem = pl.BlockSpec(memory_space=pltpu.VMEM)
    return pl.pallas_call(
        functools.partial(pre_kernel, count, places),
        in_specs=[vmem] * (count + 2) + [pl.BlockSpec(memory_space=pl.ANY)],
        out_specs=[vmem] * 3,
        out_shape=[jax.ShapeDtypeStruct((total, hidden), F32)] * 3,
        scratch_shapes=[pltpu.VMEM((total, width), BF16)],
        compiler_params=pltpu.CompilerParams(vmem_limit_bytes=SCOPED),
        cost_estimate=cost(5 * 10**9, 1024),
        name="pre_activations",
    )(*blocks, in_vmem(gate_piece), in_vmem(up_piece), in_vmem(need))


def back_columns(groups, flip, dgate_ref, dup_ref, part, gate_ref, up_ref, outs):
    half = jnp.bitwise_xor(position(groups)[1], flip)
    wide = outs[0].shape[1] - EXT
    own_rows = outs[0].shape[0]
    dgate, dup = dgate_ref[...].T, dup_ref[...].T
    chunk = 512
    for step in range(wide // chunk):
        rows = pl.ds(pl.multiple_of(half * wide + step * chunk, chunk), chunk)
        grad = jnp.dot(gate_ref[0, rows, :], dgate, preferred_element_type=F32)
        grad = grad + jnp.dot(up_ref[0, rows, :], dup, preferred_element_type=F32)
        grad = grad.T.astype(BF16)
        for t in range(groups):
            outs[t][:, step * chunk : (step + 1) * chunk] = grad[t * own_rows : (t + 1) * own_rows, :]
    for t in range(groups):
        outs[t][:, wide:] = part[t * own_rows : (t + 1) * own_rows, :]


def hidden_kernel(count, places, groups, *refs):
    blocks = refs[:count]
    act_ref, slope_ref, both_ref, down_ref, gate_ref, up_ref = refs[count : count + 6]
    outs = refs[count + 6 : count + 6 + groups]
    dgate, dup, part_out, rows = refs[count + 6 + groups :]
    fill(rows, blocks, places)
    hidden = gate_ref.shape[2]
    chunk = min(256, hidden)
    part = jnp.zeros((rows.shape[0], 1), F32)
    for start in range(0, hidden, chunk):
        cols = slice(start, start + chunk)
        grad = jnp.dot(rows[...], down_ref[:, cols], preferred_element_type=F32)
        part = part + jnp.sum(grad * both_ref[:, cols], axis=1, keepdims=True)
        dgate[:, cols] = (grad * slope_ref[:, cols]).astype(BF16)
        dup[:, cols] = (grad * act_ref[:, cols]).astype(BF16)
    part_out[...] = two_terms(part)
    back_columns(groups, 1, dgate, dup, part_out[...], gate_ref, up_ref, outs)


def hidden_grads(blocks, places, groups, factors, down_piece, gate_piece, up_piece):
    count = len(blocks)
    _, width, hidden = gate_piece.shape
    total = len(places) * CAP
    shape = (total // groups, width // 2 + EXT)
    vmem = pl.BlockSpec(memory_space=pltpu.VMEM)
    out = pl.pallas_call(
        functools.partial(hidden_kernel, count, places, groups),
        in_specs=[vmem] * (count + 6),
        out_specs=[vmem] * (groups + 3),
        out_shape=[jax.ShapeDtypeStruct(shape, BF16)] * groups
        + [jax.ShapeDtypeStruct((total, hidden), BF16)] * 2
        + [jax.ShapeDtypeStruct((total, EXT), BF16)],
        scratch_shapes=[pltpu.VMEM((total, width), BF16)],
        compiler_params=pltpu.CompilerParams(vmem_limit_bytes=SCOPED),
        cost_estimate=cost(4 * total * width * hidden, 4 * width * hidden),
        name="hidden_grads",
    )(*blocks, *factors, in_vmem(down_piece), in_vmem(gate_piece), in_vmem(up_piece))
    return out[:groups], out[groups:]


def back_kernel(groups, dgate_ref, dup_ref, part_ref, gate_ref, up_ref, *outs):
    back_columns(groups, 0, dgate_ref, dup_ref, part_ref[...], gate_ref, up_ref, outs)


def back_half(groups, dgate, dup, part, gate_piece, up_piece):
    _, width, hidden = gate_piece.shape
    total = dgate.shape[0]
    shape = (total // groups, width // 2 + EXT)
    vmem = pl.BlockSpec(memory_space=pltpu.VMEM)
    return pl.pallas_call(
        functools.partial(back_kernel, groups),
        in_specs=[vmem] * 5,
        out_specs=[vmem] * groups,
        out_shape=[jax.ShapeDtypeStruct(shape, BF16)] * groups,
        compiler_params=pltpu.CompilerParams(vmem_limit_bytes=SCOPED),
        cost_estimate=cost(2 * total * width * hidden, 2 * width * hidden),
        name="back_half",
    )(dgate, dup, part, in_vmem(gate_piece), in_vmem(up_piece))


def two_terms(value):
    high = value.astype(BF16).astype(F32)
    low = value - high
    lane = lax.broadcasted_iota(jnp.int32, (value.shape[0], EXT), 1)
    return jnp.where(lane == 0, high, jnp.where(lane == 1, low, 0.0)).astype(BF16)


def sum_kernel(groups, *refs):
    ins, outs = refs[:groups], refs[groups:]
    wide = ins[0].shape[1] - EXT
    for s in range(E_MOD):
        rows = slice(s * CAP, (s + 1) * CAP)
        total = ins[0][rows, :].astype(F32)
        for t in range(1, groups):
            total = total + ins[t][rows, :].astype(F32)
        outs[s][:, :wide] = total[:, :wide].astype(BF16)
        outs[s][:, wide:] = two_terms(jnp.sum(total[:, wide:], axis=1, keepdims=True))


def sum_pieces(partials):
    groups = len(partials)
    own_rows, wide = partials[0].shape
    return pl.pallas_call(
        functools.partial(sum_kernel, groups),
        out_shape=[jax.ShapeDtypeStruct((CAP, wide), BF16)] * E_MOD,
        cost_estimate=cost(own_rows * wide, 4 * groups * own_rows * wide),
        compiler_params=pltpu.CompilerParams(vmem_limit_bytes=SCOPED),
        name="sum_pieces",
    )(*partials)


def mix_kernel(groups, modality_ref, picks_ref, weights_ref, mix_out, gate_out):
    count, first, second, member = slot_of_labels(groups, modality_ref, picks_ref)
    slot = jnp.where(member, count, -1)
    scale = jnp.where(first, weights_ref[0:1, :], jnp.where(second, weights_ref[1:2, :], 0.0))
    own = jnp.where(position(groups)[1] == 0, first.astype(F32), second.astype(F32))
    want = lax.broadcasted_iota(jnp.int32, (CAP, slot.shape[1]), 0)
    mix = []
    for i in range(2 * E_MOD):
        hit = slot[i : i + 1, :] == want
        mix.append(jnp.where(hit, scale[i : i + 1, :], 0.0))
        gate_out[i * CAP : (i + 1) * CAP, :] = jnp.where(hit, own[i : i + 1, :], 0.0)
    mix = jnp.concatenate(mix, axis=0).T
    high = mix.astype(BF16)
    mix_out[0] = high
    mix_out[1] = (mix - high.astype(F32)).astype(BF16)


def mixing(groups, modality, picks, weights):
    tok_rows = modality.shape[1]
    slots = 2 * E_MOD * CAP
    vmem = pl.BlockSpec(memory_space=pltpu.VMEM)
    return pl.pallas_call(
        functools.partial(mix_kernel, groups),
        in_specs=[vmem] * 3,
        out_specs=[vmem] * 2,
        out_shape=[
            jax.ShapeDtypeStruct((2, tok_rows, slots), BF16),
            jax.ShapeDtypeStruct((slots, tok_rows), F32),
        ],
        compiler_params=pltpu.CompilerParams(vmem_limit_bytes=SCOPED),
        cost_estimate=cost(MIB, 1024),
        name="mixing",
    )(modality, picks, weights)


def combine_kernel(order, mix_ref, hit_ref, *refs):
    blocks, (grad_out, gate_out, table) = refs[: len(order)], refs[len(order) :]
    wide = grad_out.shape[1]
    for i, block in zip(order, blocks):
        table[i * CAP : (i + 1) * CAP, :] = block[...]
    part = jnp.sum(table[:, wide:].astype(F32), axis=1, keepdims=True)
    gate_out[...] = jnp.sum(hit_ref[...] * part, axis=0, keepdims=True)
    total = jnp.dot(mix_ref[0], table[:, :wide], preferred_element_type=F32)
    total = total + jnp.dot(mix_ref[1], table[:, :wide], preferred_element_type=F32)
    grad_out[...] = total.astype(BF16)


def combine(order, mix, hits, blocks):
    tok_rows = hits.shape[1]
    wide = blocks[0].shape[1] - EXT
    count = len(blocks)
    vmem = pl.BlockSpec(memory_space=pltpu.VMEM)
    return pl.pallas_call(
        functools.partial(combine_kernel, order),
        in_specs=[vmem] * (2 + count),
        out_specs=[vmem] * 2,
        out_shape=[
            jax.ShapeDtypeStruct((tok_rows, wide), BF16),
            jax.ShapeDtypeStruct((1, tok_rows), F32),
        ],
        scratch_shapes=[pltpu.VMEM((count * CAP, wide + EXT), BF16)],
        compiler_params=pltpu.CompilerParams(vmem_limit_bytes=SCOPED),
        cost_estimate=cost(4 * count * CAP * tok_rows * wide, 4 * tok_rows * wide),
        name="combine",
    )(mix, hits, *blocks)


def local(tokens, cotangent, modality, picks, gate_weights, gate_proj, up_proj, down_proj):
    device_count = lax.axis_size("ep")
    groups = device_count // E_MOD
    modality = modality.reshape(1, -1)
    picks = picks.T
    weights = gate_weights.T

    def to_expert(x, s, t=0):
        return lax.ppermute(
            x,
            "ep",
            [
                (e * groups + j, (e ^ s) * groups + (j + t) % groups)
                for e in range(E_MOD)
                for j in range(groups)
            ],
        )

    def to_piece(x, t):
        return to_expert(x, 0, t)

    def to_source(x, s, flip):
        return lax.ppermute(
            x,
            ("ep", "mod"),
            [
                ((e * groups + j) * 2 + m, ((e ^ s) * groups + j) * 2 + (m ^ flip))
                for e in range(E_MOD)
                for j in range(groups)
                for m in range(2)
            ],
        )

    mix, hits = mixing(groups, modality, picks, weights)
    sent = gather_slots(groups, modality, picks, tokens, cotangent)
    far = [[to_expert(sent[2 * s - 2], s) for s in range(2, E_MOD)]]
    near = [sent[0], to_expert(sent[1], 1)]
    own_pieces = [to_piece(sent[0], t) for t in range(1, groups)]
    gate_piece = load(gate_proj, sent[:1])
    later = [sent[2 * s - 1] for s in range(2, E_MOD)]
    later = pass_after(later, in_vmem(gate_piece), *own_pieces)
    far.append([to_expert(x, s) for x, s in zip(later, range(2, E_MOD))])
    near_pieces = [[x, to_piece(near[1], t)] for t, x in enumerate(own_pieces, 1)]
    up_piece = load(up_proj, [near[1], in_vmem(gate_piece)])
    far[0] = join(far[0], in_vmem(gate_piece), in_vmem(up_piece))
    far[0] = [far[0]] + [to_piece(far[0], t) for t in range(1, groups)]
    down_piece = load_turned(down_proj, [far[0][0], *sum(near_pieces, []), in_vmem(gate_piece), in_vmem(up_piece)])
    far[1] = join(far[1], in_vmem(gate_piece), in_vmem(up_piece), in_vmem(down_piece))
    far[1] = [far[1]] + [to_piece(far[1], t) for t in range(1, groups)]
    near = near + sum(near_pieces, [])
    blocks = [near + far[a] for a in range(2)]
    places = [
        tuple(
            place
            for t in range(groups)
            for place in [(2 * t, a * CAP), (2 * t + 1, a * CAP)]
            + [(2 * groups + t, i * CAP) for i in range(E_MOD - 2)]
        )
        for a in range(2)
    ]
    factors = pre_activations(blocks[0], places[0], gate_piece, up_piece, down_piece)
    first, (dgate, dup, part) = hidden_grads(
        blocks[1], places[1], groups, factors, down_piece, gate_piece, up_piece
    )
    second = back_half(groups, dgate, dup, part, gate_piece, up_piece)
    first = [first[0]] + [to_piece(first[t], groups - t) for t in range(1, groups)]
    waiting = pass_after(second[1:], *first[1:])
    second = [second[0]] + [to_piece(x, groups - t) for t, x in enumerate(waiting, 1)]
    crossed, kept = sum_pieces(first), sum_pieces(second)
    arrived = {0: kept[0]}
    for s in range(1, E_MOD):
        arrived[s] = to_source(kept[s], s, 0)
    for s in range(E_MOD):
        arrived[E_MOD + s] = to_source(crossed[s], s, 1)
    order = tuple(reversed(arrived))
    token_grad, gate_grad = combine(order, mix, hits, [arrived[i] for i in order])
    return token_grad, gate_grad.reshape(-1, 1)


def solution(mesh):
    in_specs = (
        P(("parts", "ep"), None),
        P(("parts", "ep"), None),
        P(("parts", "ep")),
        P(("parts", "ep"), None),
        P(("parts", "ep"), None),
        P("mod", None, "ep"),
        P("mod", None, "ep"),
        P("mod", "ep", None),
    )
    out_specs = (P(("parts", "ep"), "mod"), P(("parts", "ep"), "mod"))
    return jax.shard_map(local, mesh=mesh, in_specs=in_specs, out_specs=out_specs, check_vma=False)
```

```python
import functools

import jax
import jax.numpy as jnp
from jax import lax
from jax.experimental import pallas as pl
from jax.experimental.pallas import tpu as pltpu
from jax.sharding import PartitionSpec as P

E_MOD = 4
CAP = 16
EXT = 128
BF16 = jnp.bfloat16
F32 = jnp.float32
MIB = 1024 * 1024
SCOPED = 10 * MIB


def cost(flops, nbytes):
    return pl.CostEstimate(flops=flops, bytes_accessed=nbytes, transcendentals=0)


def whole(shape):
    return pl.BlockSpec(shape, lambda *_: (0,) * len(shape))


def position(groups):
    return lax.axis_index("ep") // groups, lax.axis_index("mod")


def slot_of_labels(groups, modality_ref, picks_ref):
    tok_rows = modality_ref.shape[1]
    label = lax.broadcasted_iota(jnp.int32, (2 * E_MOD, tok_rows), 0)
    own_expert, core = position(groups)
    expert = jnp.bitwise_xor(label % E_MOD, own_expert)
    modal = jnp.bitwise_xor(label // E_MOD, core)
    mine = modality_ref[...] == modal
    first = mine & (picks_ref[0:1, :] == expert)
    second = mine & (picks_ref[1:2, :] == expert)
    member = first | second
    row = lax.broadcasted_iota(jnp.int32, (tok_rows, tok_rows), 0)
    col = lax.broadcasted_iota(jnp.int32, (tok_rows, tok_rows), 1)
    earlier = (row < col).astype(F32)
    count = jnp.dot(member.astype(F32), earlier, preferred_element_type=F32).astype(jnp.int32)
    return count, first, second, member


def gather_kernel(groups, parts, modality_hbm, picks_hbm, rows_hbm, grads_hbm, *refs):
    outs, (modality, picks, rows, chosen, sems) = refs[:-5], refs[-5:]
    chunk = rows.shape[2] // parts
    small = [
        pltpu.make_async_copy(src, dst, sems.at[i])
        for i, (src, dst) in enumerate([(modality_hbm, modality), (picks_hbm, picks)])
    ]
    large = [
        [
            pltpu.make_async_copy(
                src.at[:, pl.ds(i * chunk, chunk)],
                rows.at[a, :, pl.ds(i * chunk, chunk)],
                sems.at[2 + 2 * i + a],
            )
            for a, src in enumerate([rows_hbm, grads_hbm])
        ]
        for i in range(parts)
    ]
    for copy in small + sum(large, []):
        copy.start()
    for copy in small:
        copy.wait()
    count, _, _, member = slot_of_labels(groups, modality, picks)
    slot = jnp.where(member, count, -1)
    want = lax.broadcasted_iota(jnp.int32, (CAP, slot.shape[1]), 0)
    for s in range(E_MOD):
        hit = (slot[s : s + 1, :] == want).astype(F32)
        chosen[s * CAP : (s + 1) * CAP, :] = hit.astype(BF16)
    for i in range(parts):
        cols = slice(i * chunk, (i + 1) * chunk)
        for a in range(2):
            large[i][a].wait()
            picked = jnp.dot(chosen[...], rows[a, :, cols], preferred_element_type=F32).astype(BF16)
            for s in range(E_MOD):
                block = picked[s * CAP : (s + 1) * CAP, :]
                if s < 2:
                    outs[s][a * CAP : (a + 1) * CAP, cols] = block
                else:
                    outs[2 * s - 2 + a][:, cols] = block


def gather_slots(groups, modality, picks, rows, grads):
    tok_rows, width = rows.shape
    parts = 4
    heights = [2 * CAP] * 2 + [CAP] * (2 * E_MOD - 4)
    return pl.pallas_call(
        functools.partial(gather_kernel, groups, parts),
        in_specs=[pl.BlockSpec(memory_space=pl.ANY)] * 4,
        out_specs=[pl.BlockSpec(memory_space=pltpu.VMEM)] * len(heights),
        out_shape=[jax.ShapeDtypeStruct((h, width), BF16) for h in heights],
        scratch_shapes=[
            pltpu.VMEM(modality.shape, jnp.int32),
            pltpu.VMEM(picks.shape, jnp.int32),
            pltpu.VMEM((2, tok_rows, width), BF16),
            pltpu.VMEM((E_MOD * CAP, tok_rows), BF16),
            pltpu.SemaphoreType.DMA((2 + 2 * parts,)),
        ],
        compiler_params=pltpu.CompilerParams(vmem_limit_bytes=SCOPED),
        cost_estimate=cost(4 * E_MOD * CAP * tok_rows * width, 6 * tok_rows * width),
        name="gather_slots",
    )(in_hbm(modality), in_hbm(picks), in_hbm(rows), in_hbm(grads))


def load_kernel(parts, src, *refs):
    dst, sems = refs[-2:]
    rows = src.shape[1] // parts
    copies = [
        pltpu.make_async_copy(
            src.at[:, pl.ds(i * rows, rows), :], dst.at[:, pl.ds(i * rows, rows), :], sems.at[i]
        )
        for i in range(parts)
    ]
    for copy in copies:
        copy.start()
    for copy in copies:
        copy.wait()


def load(weight, after):
    parts = 8
    return pl.pallas_call(
        functools.partial(load_kernel, parts),
        in_specs=[pl.BlockSpec(memory_space=pl.ANY)] * (1 + len(after)),
        out_specs=pl.BlockSpec(memory_space=pltpu.VMEM),
        out_shape=pltpu.VMEM(weight.shape, weight.dtype),
        scratch_shapes=[pltpu.SemaphoreType.DMA((parts,))],
        compiler_params=pltpu.CompilerParams(vmem_limit_bytes=SCOPED),
        cost_estimate=cost(0, 1024),
        name="load",
    )(in_hbm(weight), *after)


def load_turned_kernel(parts, src, *refs):
    dst, stage, sems = refs[-3:]
    rows, width = stage.shape[1:]
    copies = [
        pltpu.make_async_copy(src.at[0, pl.ds(i * rows, rows), :], stage.at[i], sems.at[i])
        for i in range(parts)
    ]
    for copy in copies:
        copy.start()
    chunk = 512
    for i in range(parts):
        copies[i].wait()
        for start in range(0, width, chunk):
            block = stage[i, :, start : start + chunk]
            dst[start : start + chunk, i * rows : (i + 1) * rows] = block.T


def load_turned(weight, after):
    _, height, width = weight.shape
    rows = 128
    parts = height // rows
    return pl.pallas_call(
        functools.partial(load_turned_kernel, parts),
        in_specs=[pl.BlockSpec(memory_space=pl.ANY)] * (1 + len(after)),
        out_specs=pl.BlockSpec(memory_space=pltpu.VMEM),
        out_shape=pltpu.VMEM((width, height), weight.dtype),
        scratch_shapes=[
            pltpu.VMEM((parts, rows, width), weight.dtype),
            pltpu.SemaphoreType.DMA((parts,)),
        ],
        compiler_params=pltpu.CompilerParams(vmem_limit_bytes=SCOPED),
        cost_estimate=cost(0, 1024),
        name="load_turned",
    )(in_hbm(weight), *after)


def pass_kernel(*refs):
    pass


def pass_after(blocks, *need):
    place = pl.BlockSpec(memory_space=pl.ANY)
    return pl.pallas_call(
        pass_kernel,
        in_specs=[place] * (len(blocks) + len(need)),
        out_specs=[place] * len(blocks),
        out_shape=[jax.ShapeDtypeStruct(block.shape, block.dtype) for block in blocks],
        input_output_aliases={i: i for i in range(len(blocks))},
        compiler_params=pltpu.CompilerParams(vmem_limit_bytes=SCOPED),
        cost_estimate=cost(0, 1024),
        name="pass_after",
    )(*blocks, *need)


def join_kernel(count, *refs):
    blocks, out = refs[:count], refs[-1]
    start = 0
    for block in blocks:
        out[start : start + block.shape[0], :] = block[...]
        start += block.shape[0]


def join(blocks, *need):
    count = len(blocks)
    total = sum(block.shape[0] for block in blocks)
    vmem = pl.BlockSpec(memory_space=pltpu.VMEM)
    return pl.pallas_call(
        functools.partial(join_kernel, count),
        in_specs=[vmem] * count + [pl.BlockSpec(memory_space=pl.ANY)] * len(need),
        out_specs=vmem,
        out_shape=jax.ShapeDtypeStruct((total, blocks[0].shape[1]), BF16),
        compiler_params=pltpu.CompilerParams(vmem_limit_bytes=SCOPED),
        cost_estimate=cost(3 * 10**9, 1024),
        name="join",
    )(*blocks, *need)


def in_hbm(x):
    return pltpu.with_memory_space_constraint(x, pltpu.HBM)


def in_vmem(x):
    return pltpu.with_memory_space_constraint(x, pltpu.VMEM)


def fill(rows, refs, places):
    for i, (index, start) in enumerate(places):
        rows[i * CAP : (i + 1) * CAP, :] = refs[index][start : start + CAP, :]


def pre_kernel(count, places, *refs):
    blocks, (gate_ref, up_ref, _, act_out, slope_out, both_out, rows) = refs[:count], refs[count:]
    fill(rows, blocks, places)
    hidden = gate_ref.shape[2]
    chunk = min(256, hidden)
    for start in range(0, hidden, chunk):
        cols = slice(start, start + chunk)
        gate_pre = jnp.dot(rows[...], gate_ref[0, :, cols], preferred_element_type=F32)
        up_pre = jnp.dot(rows[...], up_ref[0, :, cols], preferred_element_type=F32)
        sig = jax.nn.sigmoid(gate_pre)
        act = gate_pre * sig
        act_out[:, cols] = act
        slope_out[:, cols] = up_pre * (sig * (1.0 + gate_pre * (1.0 - sig)))
        both_out[:, cols] = act * up_pre


def pre_activations(blocks, places, gate_piece, up_piece, need):
    count = len(blocks)
    _, width, hidden = gate_piece.shape
    total = len(places) * CAP
    vmem = pl.BlockSpec(memory_space=pltpu.VMEM)
    return pl.pallas_call(
        functools.partial(pre_kernel, count, places),
        in_specs=[vmem] * (count + 2) + [pl.BlockSpec(memory_space=pl.ANY)],
        out_specs=[vmem] * 3,
        out_shape=[jax.ShapeDtypeStruct((total, hidden), F32)] * 3,
        scratch_shapes=[pltpu.VMEM((total, width), BF16)],
        compiler_params=pltpu.CompilerParams(vmem_limit_bytes=SCOPED),
        cost_estimate=cost(5 * 10**9, 1024),
        name="pre_activations",
    )(*blocks, in_vmem(gate_piece), in_vmem(up_piece), in_vmem(need))


def back_columns(groups, flip, dgate_ref, dup_ref, part, gate_ref, up_ref, outs):
    half = jnp.bitwise_xor(position(groups)[1], flip)
    wide = outs[0].shape[1] - EXT
    own_rows = outs[0].shape[0]
    dgate, dup = dgate_ref[...].T, dup_ref[...].T
    chunk = 512
    for step in range(wide // chunk):
        rows = pl.ds(pl.multiple_of(half * wide + step * chunk, chunk), chunk)
        grad = jnp.dot(gate_ref[0, rows, :], dgate, preferred_element_type=F32)
        grad = grad + jnp.dot(up_ref[0, rows, :], dup, preferred_element_type=F32)
        grad = grad.T.astype(BF16)
        for t in range(groups):
            outs[t][:, step * chunk : (step + 1) * chunk] = grad[t * own_rows : (t + 1) * own_rows, :]
    for t in range(groups):
        outs[t][:, wide:] = part[t * own_rows : (t + 1) * own_rows, :]


def hidden_kernel(count, places, groups, *refs):
    blocks = refs[:count]
    act_ref, slope_ref, both_ref, down_ref, gate_ref, up_ref = refs[count : count + 6]
    outs = refs[count + 6 : count + 6 + groups]
    dgate, dup, part_out, rows = refs[count + 6 + groups :]
    fill(rows, blocks, places)
    hidden = gate_ref.shape[2]
    chunk = min(256, hidden)
    part = jnp.zeros((rows.shape[0], 1), F32)
    for start in range(0, hidden, chunk):
        cols = slice(start, start + chunk)
        grad = jnp.dot(rows[...], down_ref[:, cols], preferred_element_type=F32)
        part = part + jnp.sum(grad * both_ref[:, cols], axis=1, keepdims=True)
        dgate[:, cols] = (grad * slope_ref[:, cols]).astype(BF16)
        dup[:, cols] = (grad * act_ref[:, cols]).astype(BF16)
    part_out[...] = two_terms(part)
    back_columns(groups, 0, dgate, dup, part_out[...], gate_ref, up_ref, outs)


def hidden_grads(blocks, places, groups, factors, down_piece, gate_piece, up_piece):
    count = len(blocks)
    _, width, hidden = gate_piece.shape
    total = len(places) * CAP
    shape = (total // groups, width // 2 + EXT)
    vmem = pl.BlockSpec(memory_space=pltpu.VMEM)
    out = pl.pallas_call(
        functools.partial(hidden_kernel, count, places, groups),
        in_specs=[vmem] * (count + 6),
        out_specs=[vmem] * (groups + 3),
        out_shape=[jax.ShapeDtypeStruct(shape, BF16)] * groups
        + [jax.ShapeDtypeStruct((total, hidden), BF16)] * 2
        + [jax.ShapeDtypeStruct((total, EXT), BF16)],
        scratch_shapes=[pltpu.VMEM((total, width), BF16)],
        compiler_params=pltpu.CompilerParams(vmem_limit_bytes=SCOPED),
        cost_estimate=cost(4 * total * width * hidden, 4 * width * hidden),
        name="hidden_grads",
    )(*blocks, *factors, in_vmem(down_piece), in_vmem(gate_piece), in_vmem(up_piece))
    return out[:groups], out[groups:]


def back_kernel(groups, dgate_ref, dup_ref, part_ref, gate_ref, up_ref, *outs):
    back_columns(groups, 1, dgate_ref, dup_ref, part_ref[...], gate_ref, up_ref, outs)


def back_half(groups, dgate, dup, part, gate_piece, up_piece):
    _, width, hidden = gate_piece.shape
    total = dgate.shape[0]
    shape = (total // groups, width // 2 + EXT)
    vmem = pl.BlockSpec(memory_space=pltpu.VMEM)
    return pl.pallas_call(
        functools.partial(back_kernel, groups),
        in_specs=[vmem] * 5,
        out_specs=[vmem] * groups,
        out_shape=[jax.ShapeDtypeStruct(shape, BF16)] * groups,
        compiler_params=pltpu.CompilerParams(vmem_limit_bytes=SCOPED),
        cost_estimate=cost(2 * total * width * hidden, 2 * width * hidden),
        name="back_half",
    )(dgate, dup, part, in_vmem(gate_piece), in_vmem(up_piece))


def two_terms(value):
    high = value.astype(BF16).astype(F32)
    low = value - high
    lane = lax.broadcasted_iota(jnp.int32, (value.shape[0], EXT), 1)
    return jnp.where(lane == 0, high, jnp.where(lane == 1, low, 0.0)).astype(BF16)


def sum_kernel(groups, *refs):
    ins, outs = refs[:groups], refs[groups:]
    wide = ins[0].shape[1] - EXT
    for s in range(E_MOD):
        rows = slice(s * CAP, (s + 1) * CAP)
        total = ins[0][rows, :].astype(F32)
        for t in range(1, groups):
            total = total + ins[t][rows, :].astype(F32)
        outs[s][:, :wide] = total[:, :wide].astype(BF16)
        outs[s][:, wide:] = two_terms(jnp.sum(total[:, wide:], axis=1, keepdims=True))


def sum_pieces(partials):
    groups = len(partials)
    own_rows, wide = partials[0].shape
    return pl.pallas_call(
        functools.partial(sum_kernel, groups),
        out_shape=[jax.ShapeDtypeStruct((CAP, wide), BF16)] * E_MOD,
        cost_estimate=cost(own_rows * wide, 4 * groups * own_rows * wide),
        compiler_params=pltpu.CompilerParams(vmem_limit_bytes=SCOPED),
        name="sum_pieces",
    )(*partials)


def mix_kernel(groups, modality_ref, picks_ref, weights_ref, mix_out, gate_out):
    count, first, second, member = slot_of_labels(groups, modality_ref, picks_ref)
    slot = jnp.where(member, count, -1)
    scale = jnp.where(first, weights_ref[0:1, :], jnp.where(second, weights_ref[1:2, :], 0.0))
    own = jnp.where(position(groups)[1] == 0, first.astype(F32), second.astype(F32))
    want = lax.broadcasted_iota(jnp.int32, (CAP, slot.shape[1]), 0)
    mix = []
    for i in range(2 * E_MOD):
        hit = slot[i : i + 1, :] == want
        mix.append(jnp.where(hit, scale[i : i + 1, :], 0.0))
        gate_out[i * CAP : (i + 1) * CAP, :] = jnp.where(hit, own[i : i + 1, :], 0.0)
    mix = jnp.concatenate(mix, axis=0).T
    high = mix.astype(BF16)
    mix_out[0] = high
    mix_out[1] = (mix - high.astype(F32)).astype(BF16)


def mixing(groups, modality, picks, weights):
    tok_rows = modality.shape[1]
    slots = 2 * E_MOD * CAP
    vmem = pl.BlockSpec(memory_space=pltpu.VMEM)
    return pl.pallas_call(
        functools.partial(mix_kernel, groups),
        in_specs=[vmem] * 3,
        out_specs=[vmem] * 2,
        out_shape=[
            jax.ShapeDtypeStruct((2, tok_rows, slots), BF16),
            jax.ShapeDtypeStruct((slots, tok_rows), F32),
        ],
        compiler_params=pltpu.CompilerParams(vmem_limit_bytes=SCOPED),
        cost_estimate=cost(MIB, 1024),
        name="mixing",
    )(modality, picks, weights)


def combine_kernel(order, mix_ref, hit_ref, *refs):
    blocks, (grad_out, gate_out, table) = refs[: len(order)], refs[len(order) :]
    wide = grad_out.shape[1]
    for i, block in zip(order, blocks):
        table[i * CAP : (i + 1) * CAP, :] = block[...]
    part = jnp.sum(table[:, wide:].astype(F32), axis=1, keepdims=True)
    gate_out[...] = jnp.sum(hit_ref[...] * part, axis=0, keepdims=True)
    total = jnp.dot(mix_ref[0], table[:, :wide], preferred_element_type=F32)
    total = total + jnp.dot(mix_ref[1], table[:, :wide], preferred_element_type=F32)
    grad_out[...] = total.astype(BF16)


def combine(order, mix, hits, blocks):
    tok_rows = hits.shape[1]
    wide = blocks[0].shape[1] - EXT
    count = len(blocks)
    vmem = pl.BlockSpec(memory_space=pltpu.VMEM)
    return pl.pallas_call(
        functools.partial(combine_kernel, order),
        in_specs=[vmem] * (2 + count),
        out_specs=[vmem] * 2,
        out_shape=[
            jax.ShapeDtypeStruct((tok_rows, wide), BF16),
            jax.ShapeDtypeStruct((1, tok_rows), F32),
        ],
        scratch_shapes=[pltpu.VMEM((count * CAP, wide + EXT), BF16)],
        compiler_params=pltpu.CompilerParams(vmem_limit_bytes=SCOPED),
        cost_estimate=cost(4 * count * CAP * tok_rows * wide, 4 * tok_rows * wide),
        name="combine",
    )(mix, hits, *blocks)


def local(tokens, cotangent, modality, picks, gate_weights, gate_proj, up_proj, down_proj):
    device_count = lax.axis_size("ep")
    groups = device_count // E_MOD
    modality = modality.reshape(1, -1)
    picks = picks.T
    weights = gate_weights.T

    def to_expert(x, s, t=0):
        return lax.ppermute(
            x,
            "ep",
            [
                (e * groups + j, (e ^ s) * groups + (j + t) % groups)
                for e in range(E_MOD)
                for j in range(groups)
            ],
        )

    def to_piece(x, t):
        return to_expert(x, 0, t)

    def to_source(x, s, flip):
        return lax.ppermute(
            x,
            ("ep", "mod"),
            [
                ((e * groups + j) * 2 + m, ((e ^ s) * groups + j) * 2 + (m ^ flip))
                for e in range(E_MOD)
                for j in range(groups)
                for m in range(2)
            ],
        )

    mix, hits = mixing(groups, modality, picks, weights)
    sent = gather_slots(groups, modality, picks, tokens, cotangent)
    far = [[to_expert(sent[2 * s - 2], s) for s in range(2, E_MOD)]]
    near = [sent[0], to_expert(sent[1], 1)]
    own_pieces = [to_piece(sent[0], t) for t in range(1, groups)]
    gate_piece = load(gate_proj, sent[:1])
    later = [sent[2 * s - 1] for s in range(2, E_MOD)]
    later = pass_after(later, in_vmem(gate_piece), *own_pieces)
    far.append([to_expert(x, s) for x, s in zip(later, range(2, E_MOD))])
    near_pieces = [[x, to_piece(near[1], t)] for t, x in enumerate(own_pieces, 1)]
    up_piece = load(up_proj, [near[1], in_vmem(gate_piece)])
    far[0] = join(far[0], in_vmem(gate_piece), in_vmem(up_piece))
    far[0] = [far[0]] + [to_piece(far[0], t) for t in range(1, groups)]
    down_piece = load_turned(down_proj, [far[0][0], *sum(near_pieces, []), in_vmem(gate_piece), in_vmem(up_piece)])
    far[1] = join(far[1], in_vmem(gate_piece), in_vmem(up_piece), in_vmem(down_piece))
    far[1] = [far[1]] + [to_piece(far[1], t) for t in range(1, groups)]
    near = near + sum(near_pieces, [])
    blocks = [near + far[a] for a in range(2)]
    places = [
        tuple(
            place
            for t in range(groups)
            for place in [(2 * t, a * CAP), (2 * t + 1, a * CAP)]
            + [(2 * groups + t, i * CAP) for i in range(E_MOD - 2)]
        )
        for a in range(2)
    ]
    factors = pre_activations(blocks[0], places[0], gate_piece, up_piece, down_piece)
    first, (dgate, dup, part) = hidden_grads(
        blocks[1], places[1], groups, factors, down_piece, gate_piece, up_piece
    )
    second = back_half(groups, dgate, dup, part, gate_piece, up_piece)
    first = [first[0]] + [to_piece(first[t], groups - t) for t in range(1, groups)]
    waiting = pass_after(second[1:], *first[1:])
    second = [second[0]] + [to_piece(x, groups - t) for t, x in enumerate(waiting, 1)]
    kept, crossed = sum_pieces(first), sum_pieces(second)
    arrived = {0: kept[0]}
    for s in range(1, E_MOD):
        arrived[s] = to_source(kept[s], s, 0)
    for s in range(E_MOD):
        arrived[E_MOD + s] = to_source(crossed[s], s, 1)
    order = tuple(reversed(arrived))
    token_grad, gate_grad = combine(order, mix, hits, [arrived[i] for i in order])
    return token_grad, gate_grad.reshape(-1, 1)


def solution(mesh):
    in_specs = (
        P(("parts", "ep"), None),
        P(("parts", "ep"), None),
        P(("parts", "ep")),
        P(("parts", "ep"), None),
        P(("parts", "ep"), None),
        P("mod", None, "ep"),
        P("mod", None, "ep"),
        P("mod", "ep", None),
    )
    out_specs = (P(("parts", "ep"), "mod"), P(("parts", "ep"), "mod"))
    return jax.shard_map(local, mesh=mesh, in_specs=in_specs, out_specs=out_specs, check_vma=False)
```

```python
import functools

import jax
import jax.numpy as jnp
from jax import lax
from jax.experimental import pallas as pl
from jax.experimental.pallas import tpu as pltpu
from jax.sharding import PartitionSpec as P

E_MOD = 4
CAP = 16
EXT = 128
BF16 = jnp.bfloat16
F32 = jnp.float32
MIB = 1024 * 1024
SCOPED = 10 * MIB


def cost(flops, nbytes):
    return pl.CostEstimate(flops=flops, bytes_accessed=nbytes, transcendentals=0)


def whole(shape):
    return pl.BlockSpec(shape, lambda *_: (0,) * len(shape))


def position(groups):
    return lax.axis_index("ep") // groups, lax.axis_index("mod")


def slot_of_labels(groups, modality_ref, picks_ref):
    tok_rows = modality_ref.shape[1]
    label = lax.broadcasted_iota(jnp.int32, (2 * E_MOD, tok_rows), 0)
    own_expert, core = position(groups)
    expert = jnp.bitwise_xor(label % E_MOD, own_expert)
    modal = jnp.bitwise_xor(label // E_MOD, core)
    mine = modality_ref[...] == modal
    first = mine & (picks_ref[0:1, :] == expert)
    second = mine & (picks_ref[1:2, :] == expert)
    member = first | second
    row = lax.broadcasted_iota(jnp.int32, (tok_rows, tok_rows), 0)
    col = lax.broadcasted_iota(jnp.int32, (tok_rows, tok_rows), 1)
    earlier = (row < col).astype(F32)
    count = jnp.dot(member.astype(F32), earlier, preferred_element_type=F32).astype(jnp.int32)
    return count, first, second, member


def gather_kernel(groups, parts, modality_hbm, picks_hbm, rows_hbm, grads_hbm, *refs):
    outs, (modality, picks, rows, chosen, sems) = refs[:-5], refs[-5:]
    chunk = rows.shape[2] // parts
    small = [
        pltpu.make_async_copy(src, dst, sems.at[i])
        for i, (src, dst) in enumerate([(modality_hbm, modality), (picks_hbm, picks)])
    ]
    large = [
        [
            pltpu.make_async_copy(
                src.at[:, pl.ds(i * chunk, chunk)],
                rows.at[a, :, pl.ds(i * chunk, chunk)],
                sems.at[2 + 2 * i + a],
            )
            for a, src in enumerate([rows_hbm, grads_hbm])
        ]
        for i in range(parts)
    ]
    for copy in small + sum(large, []):
        copy.start()
    for copy in small:
        copy.wait()
    count, _, _, member = slot_of_labels(groups, modality, picks)
    slot = jnp.where(member, count, -1)
    want = lax.broadcasted_iota(jnp.int32, (CAP, slot.shape[1]), 0)
    for s in range(E_MOD):
        hit = (slot[s : s + 1, :] == want).astype(F32)
        chosen[s * CAP : (s + 1) * CAP, :] = hit.astype(BF16)
    for i in range(parts):
        cols = slice(i * chunk, (i + 1) * chunk)
        for a in range(2):
            large[i][a].wait()
            picked = jnp.dot(chosen[...], rows[a, :, cols], preferred_element_type=F32).astype(BF16)
            for s in range(E_MOD):
                block = picked[s * CAP : (s + 1) * CAP, :]
                if s < 2:
                    outs[s][a * CAP : (a + 1) * CAP, cols] = block
                else:
                    outs[2 * s - 2 + a][:, cols] = block


def gather_slots(groups, modality, picks, rows, grads):
    tok_rows, width = rows.shape
    parts = 4
    heights = [2 * CAP] * 2 + [CAP] * (2 * E_MOD - 4)
    return pl.pallas_call(
        functools.partial(gather_kernel, groups, parts),
        in_specs=[pl.BlockSpec(memory_space=pl.ANY)] * 4,
        out_specs=[pl.BlockSpec(memory_space=pltpu.VMEM)] * len(heights),
        out_shape=[jax.ShapeDtypeStruct((h, width), BF16) for h in heights],
        scratch_shapes=[
            pltpu.VMEM(modality.shape, jnp.int32),
            pltpu.VMEM(picks.shape, jnp.int32),
            pltpu.VMEM((2, tok_rows, width), BF16),
            pltpu.VMEM((E_MOD * CAP, tok_rows), BF16),
            pltpu.SemaphoreType.DMA((2 + 2 * parts,)),
        ],
        compiler_params=pltpu.CompilerParams(vmem_limit_bytes=SCOPED),
        cost_estimate=cost(4 * E_MOD * CAP * tok_rows * width, 6 * tok_rows * width),
        name="gather_slots",
    )(in_hbm(modality), in_hbm(picks), in_hbm(rows), in_hbm(grads))


def load_kernel(parts, src, *refs):
    dst, sems = refs[-2:]
    rows = src.shape[1] // parts
    copies = [
        pltpu.make_async_copy(
            src.at[:, pl.ds(i * rows, rows), :], dst.at[:, pl.ds(i * rows, rows), :], sems.at[i]
        )
        for i in range(parts)
    ]
    for copy in copies:
        copy.start()
    for copy in copies:
        copy.wait()


def load(weight, after):
    parts = 8
    return pl.pallas_call(
        functools.partial(load_kernel, parts),
        in_specs=[pl.BlockSpec(memory_space=pl.ANY)] * (1 + len(after)),
        out_specs=pl.BlockSpec(memory_space=pltpu.VMEM),
        out_shape=pltpu.VMEM(weight.shape, weight.dtype),
        scratch_shapes=[pltpu.SemaphoreType.DMA((parts,))],
        compiler_params=pltpu.CompilerParams(vmem_limit_bytes=SCOPED),
        cost_estimate=cost(0, 1024),
        name="load",
    )(in_hbm(weight), *after)


def load_turned_kernel(parts, src, *refs):
    dst, stage, sems = refs[-3:]
    rows, width = stage.shape[1:]
    copies = [
        pltpu.make_async_copy(src.at[0, pl.ds(i * rows, rows), :], stage.at[i], sems.at[i])
        for i in range(parts)
    ]
    for copy in copies:
        copy.start()
    chunk = 512
    for i in range(parts):
        copies[i].wait()
        for start in range(0, width, chunk):
            block = stage[i, :, start : start + chunk]
            dst[start : start + chunk, i * rows : (i + 1) * rows] = block.T


def load_turned(weight, after):
    _, height, width = weight.shape
    rows = 128
    parts = height // rows
    return pl.pallas_call(
        functools.partial(load_turned_kernel, parts),
        in_specs=[pl.BlockSpec(memory_space=pl.ANY)] * (1 + len(after)),
        out_specs=pl.BlockSpec(memory_space=pltpu.VMEM),
        out_shape=pltpu.VMEM((width, height), weight.dtype),
        scratch_shapes=[
            pltpu.VMEM((parts, rows, width), weight.dtype),
            pltpu.SemaphoreType.DMA((parts,)),
        ],
        compiler_params=pltpu.CompilerParams(vmem_limit_bytes=SCOPED),
        cost_estimate=cost(0, 1024),
        name="load_turned",
    )(in_hbm(weight), *after)


def pass_kernel(*refs):
    pass


def pass_after(blocks, *need):
    place = pl.BlockSpec(memory_space=pl.ANY)
    return pl.pallas_call(
        pass_kernel,
        in_specs=[place] * (len(blocks) + len(need)),
        out_specs=[place] * len(blocks),
        out_shape=[jax.ShapeDtypeStruct(block.shape, block.dtype) for block in blocks],
        input_output_aliases={i: i for i in range(len(blocks))},
        compiler_params=pltpu.CompilerParams(vmem_limit_bytes=SCOPED),
        cost_estimate=cost(0, 1024),
        name="pass_after",
    )(*blocks, *need)


def join_kernel(count, *refs):
    blocks, out = refs[:count], refs[-1]
    start = 0
    for block in blocks:
        out[start : start + block.shape[0], :] = block[...]
        start += block.shape[0]


def join(blocks, *need):
    count = len(blocks)
    total = sum(block.shape[0] for block in blocks)
    vmem = pl.BlockSpec(memory_space=pltpu.VMEM)
    return pl.pallas_call(
        functools.partial(join_kernel, count),
        in_specs=[vmem] * count + [pl.BlockSpec(memory_space=pl.ANY)] * len(need),
        out_specs=vmem,
        out_shape=jax.ShapeDtypeStruct((total, blocks[0].shape[1]), BF16),
        compiler_params=pltpu.CompilerParams(vmem_limit_bytes=SCOPED),
        cost_estimate=cost(3 * 10**9, 1024),
        name="join",
    )(*blocks, *need)


def in_hbm(x):
    return pltpu.with_memory_space_constraint(x, pltpu.HBM)


def in_vmem(x):
    return pltpu.with_memory_space_constraint(x, pltpu.VMEM)


def fill(rows, refs, places):
    for i, (index, start) in enumerate(places):
        rows[i * CAP : (i + 1) * CAP, :] = refs[index][start : start + CAP, :]


def pre_kernel(count, places, *refs):
    blocks, (gate_ref, up_ref, _, act_out, slope_out, both_out, rows) = refs[:count], refs[count:]
    fill(rows, blocks, places)
    hidden = gate_ref.shape[2]
    chunk = min(256, hidden)
    for start in range(0, hidden, chunk):
        cols = slice(start, start + chunk)
        gate_pre = jnp.dot(rows[...], gate_ref[0, :, cols], preferred_element_type=F32)
        up_pre = jnp.dot(rows[...], up_ref[0, :, cols], preferred_element_type=F32)
        sig = jax.nn.sigmoid(gate_pre)
        act = gate_pre * sig
        act_out[:, cols] = act
        slope_out[:, cols] = up_pre * (sig * (1.0 + gate_pre * (1.0 - sig)))
        both_out[:, cols] = act * up_pre


def pre_activations(blocks, places, gate_piece, up_piece, need):
    count = len(blocks)
    _, width, hidden = gate_piece.shape
    total = len(places) * CAP
    vmem = pl.BlockSpec(memory_space=pltpu.VMEM)
    return pl.pallas_call(
        functools.partial(pre_kernel, count, places),
        in_specs=[vmem] * (count + 2) + [pl.BlockSpec(memory_space=pl.ANY)],
        out_specs=[vmem] * 3,
        out_shape=[jax.ShapeDtypeStruct((total, hidden), F32)] * 3,
        scratch_shapes=[pltpu.VMEM((total, width), BF16)],
        compiler_params=pltpu.CompilerParams(vmem_limit_bytes=SCOPED),
        cost_estimate=cost(5 * 10**9, 1024),
        name="pre_activations",
    )(*blocks, in_vmem(gate_piece), in_vmem(up_piece), in_vmem(need))


def back_columns(groups, flip, dgate_ref, dup_ref, part, gate_ref, up_ref, outs):
    half = jnp.bitwise_xor(position(groups)[1], flip)
    wide = outs[0].shape[1] - EXT
    own_rows = outs[0].shape[0]
    dgate, dup = dgate_ref[...].T, dup_ref[...].T
    chunk = 512
    for step in range(wide // chunk):
        rows = pl.ds(pl.multiple_of(half * wide + step * chunk, chunk), chunk)
        grad = jnp.dot(gate_ref[0, rows, :], dgate, preferred_element_type=F32)
        grad = grad + jnp.dot(up_ref[0, rows, :], dup, preferred_element_type=F32)
        grad = grad.T.astype(BF16)
        for t in range(groups):
            outs[t][:, step * chunk : (step + 1) * chunk] = grad[t * own_rows : (t + 1) * own_rows, :]
    for t in range(groups):
        outs[t][:, wide:] = part[t * own_rows : (t + 1) * own_rows, :]


def hidden_kernel(count, places, groups, *refs):
    blocks = refs[:count]
    act_ref, slope_ref, both_ref, down_ref, gate_ref, up_ref = refs[count : count + 6]
    outs = refs[count + 6 : count + 6 + groups]
    dgate, dup, part_out, rows = refs[count + 6 + groups :]
    fill(rows, blocks, places)
    hidden = gate_ref.shape[2]
    chunk = min(256, hidden)
    part = jnp.zeros((rows.shape[0], 1), F32)
    for start in range(0, hidden, chunk):
        cols = slice(start, start + chunk)
        grad = jnp.dot(rows[...], down_ref[:, cols], preferred_element_type=F32)
        part = part + jnp.sum(grad * both_ref[:, cols], axis=1, keepdims=True)
        dgate[:, cols] = (grad * slope_ref[:, cols]).astype(BF16)
        dup[:, cols] = (grad * act_ref[:, cols]).astype(BF16)
    part_out[...] = two_terms(part)
    back_columns(groups, 1, dgate, dup, part_out[...], gate_ref, up_ref, outs)


def hidden_grads(blocks, places, groups, factors, down_piece, gate_piece, up_piece):
    count = len(blocks)
    _, width, hidden = gate_piece.shape
    total = len(places) * CAP
    shape = (total // groups, width // 2 + EXT)
    vmem = pl.BlockSpec(memory_space=pltpu.VMEM)
    out = pl.pallas_call(
        functools.partial(hidden_kernel, count, places, groups),
        in_specs=[vmem] * (count + 6),
        out_specs=[vmem] * (groups + 3),
        out_shape=[jax.ShapeDtypeStruct(shape, BF16)] * groups
        + [jax.ShapeDtypeStruct((total, hidden), BF16)] * 2
        + [jax.ShapeDtypeStruct((total, EXT), BF16)],
        scratch_shapes=[pltpu.VMEM((total, width), BF16)],
        compiler_params=pltpu.CompilerParams(vmem_limit_bytes=SCOPED),
        cost_estimate=cost(4 * total * width * hidden, 4 * width * hidden),
        name="hidden_grads",
    )(*blocks, *factors, in_vmem(down_piece), in_vmem(gate_piece), in_vmem(up_piece))
    return out[:groups], out[groups:]


def back_kernel(groups, dgate_ref, dup_ref, part_ref, gate_ref, up_ref, *outs):
    back_columns(groups, 0, dgate_ref, dup_ref, part_ref[...], gate_ref, up_ref, outs)


def back_half(groups, dgate, dup, part, gate_piece, up_piece):
    _, width, hidden = gate_piece.shape
    total = dgate.shape[0]
    shape = (total // groups, width // 2 + EXT)
    vmem = pl.BlockSpec(memory_space=pltpu.VMEM)
    return pl.pallas_call(
        functools.partial(back_kernel, groups),
        in_specs=[vmem] * 5,
        out_specs=[vmem] * groups,
        out_shape=[jax.ShapeDtypeStruct(shape, BF16)] * groups,
        compiler_params=pltpu.CompilerParams(vmem_limit_bytes=SCOPED),
        cost_estimate=cost(2 * total * width * hidden, 2 * width * hidden),
        name="back_half",
    )(dgate, dup, part, in_vmem(gate_piece), in_vmem(up_piece))


def two_terms(value):
    high = value.astype(BF16).astype(F32)
    low = value - high
    lane = lax.broadcasted_iota(jnp.int32, (value.shape[0], EXT), 1)
    return jnp.where(lane == 0, high, jnp.where(lane == 1, low, 0.0)).astype(BF16)


def sum_kernel(groups, *refs):
    ins, outs = refs[:groups], refs[-E_MOD:]
    wide = ins[0].shape[1] - EXT
    for s in range(E_MOD):
        rows = slice(s * CAP, (s + 1) * CAP)
        total = ins[0][rows, :].astype(F32)
        for t in range(1, groups):
            total = total + ins[t][rows, :].astype(F32)
        outs[s][:, :wide] = total[:, :wide].astype(BF16)
        outs[s][:, wide:] = two_terms(jnp.sum(total[:, wide:], axis=1, keepdims=True))


def sum_pieces(partials, *after):
    groups = len(partials)
    own_rows, wide = partials[0].shape
    return pl.pallas_call(
        functools.partial(sum_kernel, groups),
        in_specs=[pl.BlockSpec(memory_space=pltpu.VMEM)] * groups
        + [pl.BlockSpec(memory_space=pl.ANY)] * len(after),
        out_specs=[pl.BlockSpec(memory_space=pltpu.VMEM)] * E_MOD,
        out_shape=[jax.ShapeDtypeStruct((CAP, wide), BF16)] * E_MOD,
        cost_estimate=cost(own_rows * wide, 4 * groups * own_rows * wide),
        compiler_params=pltpu.CompilerParams(vmem_limit_bytes=SCOPED),
        name="sum_pieces",
    )(*partials, *after)


def mix_kernel(groups, modality_ref, picks_ref, weights_ref, mix_out, gate_out):
    count, first, second, member = slot_of_labels(groups, modality_ref, picks_ref)
    slot = jnp.where(member, count, -1)
    scale = jnp.where(first, weights_ref[0:1, :], jnp.where(second, weights_ref[1:2, :], 0.0))
    own = jnp.where(position(groups)[1] == 0, first.astype(F32), second.astype(F32))
    want = lax.broadcasted_iota(jnp.int32, (CAP, slot.shape[1]), 0)
    mix = []
    for i in range(2 * E_MOD):
        hit = slot[i : i + 1, :] == want
        mix.append(jnp.where(hit, scale[i : i + 1, :], 0.0))
        gate_out[i * CAP : (i + 1) * CAP, :] = jnp.where(hit, own[i : i + 1, :], 0.0)
    mix = jnp.concatenate(mix, axis=0).T
    high = mix.astype(BF16)
    mix_out[0] = high
    mix_out[1] = (mix - high.astype(F32)).astype(BF16)


def mixing(groups, modality, picks, weights):
    tok_rows = modality.shape[1]
    slots = 2 * E_MOD * CAP
    vmem = pl.BlockSpec(memory_space=pltpu.VMEM)
    return pl.pallas_call(
        functools.partial(mix_kernel, groups),
        in_specs=[vmem] * 3,
        out_specs=[vmem] * 2,
        out_shape=[
            jax.ShapeDtypeStruct((2, tok_rows, slots), BF16),
            jax.ShapeDtypeStruct((slots, tok_rows), F32),
        ],
        compiler_params=pltpu.CompilerParams(vmem_limit_bytes=SCOPED),
        cost_estimate=cost(MIB, 1024),
        name="mixing",
    )(modality, picks, weights)


def combine_kernel(order, mix_ref, hit_ref, *refs):
    blocks, (grad_out, gate_out, table) = refs[: len(order)], refs[len(order) :]
    wide = grad_out.shape[1]
    for i, block in zip(order, blocks):
        table[i * CAP : (i + 1) * CAP, :] = block[...]
    part = jnp.sum(table[:, wide:].astype(F32), axis=1, keepdims=True)
    gate_out[...] = jnp.sum(hit_ref[...] * part, axis=0, keepdims=True)
    total = jnp.dot(mix_ref[0], table[:, :wide], preferred_element_type=F32)
    total = total + jnp.dot(mix_ref[1], table[:, :wide], preferred_element_type=F32)
    grad_out[...] = total.astype(BF16)


def combine(order, mix, hits, blocks):
    tok_rows = hits.shape[1]
    wide = blocks[0].shape[1] - EXT
    count = len(blocks)
    vmem = pl.BlockSpec(memory_space=pltpu.VMEM)
    return pl.pallas_call(
        functools.partial(combine_kernel, order),
        in_specs=[vmem] * (2 + count),
        out_specs=[vmem] * 2,
        out_shape=[
            jax.ShapeDtypeStruct((tok_rows, wide), BF16),
            jax.ShapeDtypeStruct((1, tok_rows), F32),
        ],
        scratch_shapes=[pltpu.VMEM((count * CAP, wide + EXT), BF16)],
        compiler_params=pltpu.CompilerParams(vmem_limit_bytes=SCOPED),
        cost_estimate=cost(4 * count * CAP * tok_rows * wide, 4 * tok_rows * wide),
        name="combine",
    )(mix, hits, *blocks)


def local(tokens, cotangent, modality, picks, gate_weights, gate_proj, up_proj, down_proj):
    device_count = lax.axis_size("ep")
    groups = device_count // E_MOD
    modality = modality.reshape(1, -1)
    picks = picks.T
    weights = gate_weights.T

    def to_expert(x, s, t=0):
        return lax.ppermute(
            x,
            "ep",
            [
                (e * groups + j, (e ^ s) * groups + (j + t) % groups)
                for e in range(E_MOD)
                for j in range(groups)
            ],
        )

    def to_piece(x, t):
        return to_expert(x, 0, t)

    def to_source(x, s, flip):
        return lax.ppermute(
            x,
            ("ep", "mod"),
            [
                ((e * groups + j) * 2 + m, ((e ^ s) * groups + j) * 2 + (m ^ flip))
                for e in range(E_MOD)
                for j in range(groups)
                for m in range(2)
            ],
        )

    mix, hits = mixing(groups, modality, picks, weights)
    sent = gather_slots(groups, modality, picks, tokens, cotangent)
    far = [[to_expert(sent[2 * s - 2], s) for s in range(2, E_MOD)]]
    near = [sent[0], to_expert(sent[1], 1)]
    own_pieces = [to_piece(sent[0], t) for t in range(1, groups)]
    gate_piece = load(gate_proj, sent[:1])
    later = [sent[2 * s - 1] for s in range(2, E_MOD)]
    later = pass_after(later, in_vmem(gate_piece), *own_pieces)
    far.append([to_expert(x, s) for x, s in zip(later, range(2, E_MOD))])
    near_pieces = [[x, to_piece(near[1], t)] for t, x in enumerate(own_pieces, 1)]
    up_piece = load(up_proj, [near[1], in_vmem(gate_piece)])
    far[0] = join(far[0], in_vmem(gate_piece), in_vmem(up_piece))
    far[0] = [far[0]] + [to_piece(far[0], t) for t in range(1, groups)]
    down_piece = load_turned(down_proj, [far[0][0], *sum(near_pieces, []), in_vmem(gate_piece), in_vmem(up_piece)])
    far[1] = join(far[1], in_vmem(gate_piece), in_vmem(up_piece), in_vmem(down_piece))
    far[1] = [far[1]] + [to_piece(far[1], t) for t in range(1, groups)]
    near = near + sum(near_pieces, [])
    blocks = [near + far[a] for a in range(2)]
    places = [
        tuple(
            place
            for t in range(groups)
            for place in [(2 * t, a * CAP), (2 * t + 1, a * CAP)]
            + [(2 * groups + t, i * CAP) for i in range(E_MOD - 2)]
        )
        for a in range(2)
    ]
    factors = pre_activations(blocks[0], places[0], gate_piece, up_piece, down_piece)
    first, (dgate, dup, part) = hidden_grads(
        blocks[1], places[1], groups, factors, down_piece, gate_piece, up_piece
    )
    second = back_half(groups, dgate, dup, part, gate_piece, up_piece)
    first = [first[0]] + [to_piece(first[t], groups - t) for t in range(1, groups)]
    crossed = sum_pieces(first, second[0])
    arrived = {E_MOD + s: to_source(crossed[s], s, 1) for s in range(E_MOD)}
    waiting = pass_after(second[1:], arrived[E_MOD])
    second = [second[0]] + [to_piece(x, groups - t) for t, x in enumerate(waiting, 1)]
    kept = sum_pieces(second)
    arrived[0] = kept[0]
    for s in range(1, E_MOD):
        arrived[s] = to_source(kept[s], s, 0)
    order = tuple(reversed(sorted(arrived)))
    token_grad, gate_grad = combine(order, mix, hits, [arrived[i] for i in order])
    return token_grad, gate_grad.reshape(-1, 1)


def solution(mesh):
    in_specs = (
        P(("parts", "ep"), None),
        P(("parts", "ep"), None),
        P(("parts", "ep")),
        P(("parts", "ep"), None),
        P(("parts", "ep"), None),
        P("mod", None, "ep"),
        P("mod", None, "ep"),
        P("mod", "ep", None),
    )
    out_specs = (P(("parts", "ep"), "mod"), P(("parts", "ep"), "mod"))
    return jax.shard_map(local, mesh=mesh, in_specs=in_specs, out_specs=out_specs, check_vma=False)
```

```python
import functools

import jax
import jax.numpy as jnp
from jax import lax
from jax.experimental import pallas as pl
from jax.experimental.pallas import tpu as pltpu
from jax.sharding import PartitionSpec as P

E_MOD = 4
CAP = 16
EXT = 128
BF16 = jnp.bfloat16
F32 = jnp.float32
MIB = 1024 * 1024
SCOPED = 10 * MIB


def cost(flops, nbytes):
    return pl.CostEstimate(flops=flops, bytes_accessed=nbytes, transcendentals=0)


def whole(shape):
    return pl.BlockSpec(shape, lambda *_: (0,) * len(shape))


def position(groups):
    return lax.axis_index("ep") // groups, lax.axis_index("mod")


def slot_of_labels(groups, modality_ref, picks_ref):
    tok_rows = modality_ref.shape[1]
    label = lax.broadcasted_iota(jnp.int32, (2 * E_MOD, tok_rows), 0)
    own_expert, core = position(groups)
    expert = jnp.bitwise_xor(label % E_MOD, own_expert)
    modal = jnp.bitwise_xor(label // E_MOD, core)
    mine = modality_ref[...] == modal
    first = mine & (picks_ref[0:1, :] == expert)
    second = mine & (picks_ref[1:2, :] == expert)
    member = first | second
    row = lax.broadcasted_iota(jnp.int32, (tok_rows, tok_rows), 0)
    col = lax.broadcasted_iota(jnp.int32, (tok_rows, tok_rows), 1)
    earlier = (row < col).astype(F32)
    count = jnp.dot(member.astype(F32), earlier, preferred_element_type=F32).astype(jnp.int32)
    return count, first, second, member


def gather_kernel(groups, parts, modality_hbm, picks_hbm, rows_hbm, grads_hbm, *refs):
    outs, (modality, picks, rows, chosen, sems) = refs[:-5], refs[-5:]
    chunk = rows.shape[2] // parts
    small = [
        pltpu.make_async_copy(src, dst, sems.at[i])
        for i, (src, dst) in enumerate([(modality_hbm, modality), (picks_hbm, picks)])
    ]
    large = [
        [
            pltpu.make_async_copy(
                src.at[:, pl.ds(i * chunk, chunk)],
                rows.at[a, :, pl.ds(i * chunk, chunk)],
                sems.at[2 + 2 * i + a],
            )
            for a, src in enumerate([rows_hbm, grads_hbm])
        ]
        for i in range(parts)
    ]
    for copy in small + sum(large, []):
        copy.start()
    for copy in small:
        copy.wait()
    count, _, _, member = slot_of_labels(groups, modality, picks)
    slot = jnp.where(member, count, -1)
    want = lax.broadcasted_iota(jnp.int32, (CAP, slot.shape[1]), 0)
    for s in range(E_MOD):
        hit = (slot[s : s + 1, :] == want).astype(F32)
        chosen[s * CAP : (s + 1) * CAP, :] = hit.astype(BF16)
    for i in range(parts):
        cols = slice(i * chunk, (i + 1) * chunk)
        for a in range(2):
            large[i][a].wait()
            picked = jnp.dot(chosen[...], rows[a, :, cols], preferred_element_type=F32).astype(BF16)
            for s in range(E_MOD):
                block = picked[s * CAP : (s + 1) * CAP, :]
                if s < 2:
                    outs[s][a * CAP : (a + 1) * CAP, cols] = block
                else:
                    outs[2 * s - 2 + a][:, cols] = block


def gather_slots(groups, modality, picks, rows, grads):
    tok_rows, width = rows.shape
    parts = 4
    heights = [2 * CAP] * 2 + [CAP] * (2 * E_MOD - 4)
    return pl.pallas_call(
        functools.partial(gather_kernel, groups, parts),
        in_specs=[pl.BlockSpec(memory_space=pl.ANY)] * 4,
        out_specs=[pl.BlockSpec(memory_space=pltpu.VMEM)] * len(heights),
        out_shape=[jax.ShapeDtypeStruct((h, width), BF16) for h in heights],
        scratch_shapes=[
            pltpu.VMEM(modality.shape, jnp.int32),
            pltpu.VMEM(picks.shape, jnp.int32),
            pltpu.VMEM((2, tok_rows, width), BF16),
            pltpu.VMEM((E_MOD * CAP, tok_rows), BF16),
            pltpu.SemaphoreType.DMA((2 + 2 * parts,)),
        ],
        compiler_params=pltpu.CompilerParams(vmem_limit_bytes=SCOPED),
        cost_estimate=cost(4 * E_MOD * CAP * tok_rows * width, 6 * tok_rows * width),
        name="gather_slots",
    )(in_hbm(modality), in_hbm(picks), in_hbm(rows), in_hbm(grads))


def load_kernel(parts, src, *refs):
    dst, sems = refs[-2:]
    rows = src.shape[1] // parts
    copies = [
        pltpu.make_async_copy(
            src.at[:, pl.ds(i * rows, rows), :], dst.at[:, pl.ds(i * rows, rows), :], sems.at[i]
        )
        for i in range(parts)
    ]
    for copy in copies:
        copy.start()
    for copy in copies:
        copy.wait()


def load(weight, after):
    parts = 8
    return pl.pallas_call(
        functools.partial(load_kernel, parts),
        in_specs=[pl.BlockSpec(memory_space=pl.ANY)] * (1 + len(after)),
        out_specs=pl.BlockSpec(memory_space=pltpu.VMEM),
        out_shape=pltpu.VMEM(weight.shape, weight.dtype),
        scratch_shapes=[pltpu.SemaphoreType.DMA((parts,))],
        compiler_params=pltpu.CompilerParams(vmem_limit_bytes=SCOPED),
        cost_estimate=cost(0, 1024),
        name="load",
    )(in_hbm(weight), *after)


def load_turned_kernel(parts, src, *refs):
    dst, stage, sems = refs[-3:]
    rows, width = stage.shape[1:]
    copies = [
        pltpu.make_async_copy(src.at[0, pl.ds(i * rows, rows), :], stage.at[i], sems.at[i])
        for i in range(parts)
    ]
    for copy in copies:
        copy.start()
    chunk = 512
    for i in range(parts):
        copies[i].wait()
        for start in range(0, width, chunk):
            block = stage[i, :, start : start + chunk]
            dst[start : start + chunk, i * rows : (i + 1) * rows] = block.T


def load_turned(weight, after):
    _, height, width = weight.shape
    rows = 128
    parts = height // rows
    return pl.pallas_call(
        functools.partial(load_turned_kernel, parts),
        in_specs=[pl.BlockSpec(memory_space=pl.ANY)] * (1 + len(after)),
        out_specs=pl.BlockSpec(memory_space=pltpu.VMEM),
        out_shape=pltpu.VMEM((width, height), weight.dtype),
        scratch_shapes=[
            pltpu.VMEM((parts, rows, width), weight.dtype),
            pltpu.SemaphoreType.DMA((parts,)),
        ],
        compiler_params=pltpu.CompilerParams(vmem_limit_bytes=SCOPED),
        cost_estimate=cost(0, 1024),
        name="load_turned",
    )(in_hbm(weight), *after)


def pass_kernel(*refs):
    pass


def pass_after(blocks, *need):
    place = pl.BlockSpec(memory_space=pl.ANY)
    return pl.pallas_call(
        pass_kernel,
        in_specs=[place] * (len(blocks) + len(need)),
        out_specs=[place] * len(blocks),
        out_shape=[jax.ShapeDtypeStruct(block.shape, block.dtype) for block in blocks],
        input_output_aliases={i: i for i in range(len(blocks))},
        compiler_params=pltpu.CompilerParams(vmem_limit_bytes=SCOPED),
        cost_estimate=cost(0, 1024),
        name="pass_after",
    )(*blocks, *need)


def join_kernel(count, *refs):
    blocks, out = refs[:count], refs[-1]
    start = 0
    for block in blocks:
        out[start : start + block.shape[0], :] = block[...]
        start += block.shape[0]


def join(blocks, *need):
    count = len(blocks)
    total = sum(block.shape[0] for block in blocks)
    vmem = pl.BlockSpec(memory_space=pltpu.VMEM)
    return pl.pallas_call(
        functools.partial(join_kernel, count),
        in_specs=[vmem] * count + [pl.BlockSpec(memory_space=pl.ANY)] * len(need),
        out_specs=vmem,
        out_shape=jax.ShapeDtypeStruct((total, blocks[0].shape[1]), BF16),
        compiler_params=pltpu.CompilerParams(vmem_limit_bytes=SCOPED),
        cost_estimate=cost(3 * 10**9, 1024),
        name="join",
    )(*blocks, *need)


def in_hbm(x):
    return pltpu.with_memory_space_constraint(x, pltpu.HBM)


def in_vmem(x):
    return pltpu.with_memory_space_constraint(x, pltpu.VMEM)


def fill(rows, refs, places):
    for i, (index, start) in enumerate(places):
        rows[i * CAP : (i + 1) * CAP, :] = refs[index][start : start + CAP, :]


def pre_kernel(count, places, *refs):
    blocks, (gate_ref, up_ref, _, act_out, slope_out, both_out, rows) = refs[:count], refs[count:]
    fill(rows, blocks, places)
    hidden = gate_ref.shape[2]
    chunk = min(256, hidden)
    for start in range(0, hidden, chunk):
        cols = slice(start, start + chunk)
        gate_pre = jnp.dot(rows[...], gate_ref[0, :, cols], preferred_element_type=F32)
        up_pre = jnp.dot(rows[...], up_ref[0, :, cols], preferred_element_type=F32)
        sig = jax.nn.sigmoid(gate_pre)
        act = gate_pre * sig
        act_out[:, cols] = act
        slope_out[:, cols] = up_pre * (sig * (1.0 + gate_pre * (1.0 - sig)))
        both_out[:, cols] = act * up_pre


def pre_activations(blocks, places, gate_piece, up_piece, need):
    count = len(blocks)
    _, width, hidden = gate_piece.shape
    total = len(places) * CAP
    vmem = pl.BlockSpec(memory_space=pltpu.VMEM)
    return pl.pallas_call(
        functools.partial(pre_kernel, count, places),
        in_specs=[vmem] * (count + 2) + [pl.BlockSpec(memory_space=pl.ANY)],
        out_specs=[vmem] * 3,
        out_shape=[jax.ShapeDtypeStruct((total, hidden), F32)] * 3,
        scratch_shapes=[pltpu.VMEM((total, width), BF16)],
        compiler_params=pltpu.CompilerParams(vmem_limit_bytes=SCOPED),
        cost_estimate=cost(5 * 10**9, 1024),
        name="pre_activations",
    )(*blocks, in_vmem(gate_piece), in_vmem(up_piece), in_vmem(need))


def back_columns(groups, flip, dgate_ref, dup_ref, part, gate_ref, up_ref, outs):
    half = jnp.bitwise_xor(position(groups)[1], flip)
    wide = outs[0].shape[1] - EXT
    places, start = [], 0
    for out in outs:
        places.append(slice(start, start + out.shape[0]))
        start += out.shape[0]
    dgate, dup = dgate_ref[...].T, dup_ref[...].T
    chunk = 512
    for step in range(wide // chunk):
        rows = pl.ds(pl.multiple_of(half * wide + step * chunk, chunk), chunk)
        grad = jnp.dot(gate_ref[0, rows, :], dgate, preferred_element_type=F32)
        grad = grad + jnp.dot(up_ref[0, rows, :], dup, preferred_element_type=F32)
        grad = grad.T.astype(BF16)
        for out, place in zip(outs, places):
            out[:, step * chunk : (step + 1) * chunk] = grad[place, :]
    for out, place in zip(outs, places):
        out[:, wide:] = part[place, :]


def hidden_kernel(count, places, groups, *refs):
    blocks = refs[:count]
    act_ref, slope_ref, both_ref, down_ref, gate_ref, up_ref = refs[count : count + 6]
    outs = refs[count + 6 : -4]
    dgate, dup, part_out, rows = refs[-4:]
    fill(rows, blocks, places)
    hidden = gate_ref.shape[2]
    chunk = min(256, hidden)
    part = jnp.zeros((rows.shape[0], 1), F32)
    for start in range(0, hidden, chunk):
        cols = slice(start, start + chunk)
        grad = jnp.dot(rows[...], down_ref[:, cols], preferred_element_type=F32)
        part = part + jnp.sum(grad * both_ref[:, cols], axis=1, keepdims=True)
        dgate[:, cols] = (grad * slope_ref[:, cols]).astype(BF16)
        dup[:, cols] = (grad * act_ref[:, cols]).astype(BF16)
    part_out[...] = two_terms(part)
    back_columns(groups, 1, dgate, dup, part_out[...], gate_ref, up_ref, outs)


def hidden_grads(blocks, places, groups, factors, down_piece, gate_piece, up_piece):
    count = len(blocks)
    _, width, hidden = gate_piece.shape
    total = len(places) * CAP
    shape = (total // groups // 2, width // 2 + EXT)
    vmem = pl.BlockSpec(memory_space=pltpu.VMEM)
    out = pl.pallas_call(
        functools.partial(hidden_kernel, count, places, groups),
        in_specs=[vmem] * (count + 6),
        out_specs=[vmem] * (2 * groups + 3),
        out_shape=[jax.ShapeDtypeStruct(shape, BF16)] * (2 * groups)
        + [jax.ShapeDtypeStruct((total, hidden), BF16)] * 2
        + [jax.ShapeDtypeStruct((total, EXT), BF16)],
        scratch_shapes=[pltpu.VMEM((total, width), BF16)],
        compiler_params=pltpu.CompilerParams(vmem_limit_bytes=SCOPED),
        cost_estimate=cost(4 * total * width * hidden, 4 * width * hidden),
        name="hidden_grads",
    )(*blocks, *factors, in_vmem(down_piece), in_vmem(gate_piece), in_vmem(up_piece))
    return list(out[:-3]), out[-3:]


def back_kernel(groups, dgate_ref, dup_ref, part_ref, gate_ref, up_ref, *outs):
    back_columns(groups, 0, dgate_ref, dup_ref, part_ref[...], gate_ref, up_ref, outs)


def back_half(groups, dgate, dup, part, gate_piece, up_piece):
    _, width, hidden = gate_piece.shape
    total = dgate.shape[0]
    shape = (total // groups // 2, width // 2 + EXT)
    vmem = pl.BlockSpec(memory_space=pltpu.VMEM)
    return pl.pallas_call(
        functools.partial(back_kernel, groups),
        in_specs=[vmem] * 5,
        out_specs=[vmem] * (2 * groups),
        out_shape=[jax.ShapeDtypeStruct(shape, BF16)] * (2 * groups),
        compiler_params=pltpu.CompilerParams(vmem_limit_bytes=SCOPED),
        cost_estimate=cost(2 * total * width * hidden, 2 * width * hidden),
        name="back_half",
    )(dgate, dup, part, in_vmem(gate_piece), in_vmem(up_piece))


def two_terms(value):
    high = value.astype(BF16).astype(F32)
    low = value - high
    lane = lax.broadcasted_iota(jnp.int32, (value.shape[0], EXT), 1)
    return jnp.where(lane == 0, high, jnp.where(lane == 1, low, 0.0)).astype(BF16)


def sum_kernel(groups, *refs):
    ins, outs = refs[: 2 * groups], refs[2 * groups :]
    wide = ins[0].shape[1] - EXT
    for s in range(E_MOD):
        half, place = divmod(s, 2)
        rows = slice(place * CAP, (place + 1) * CAP)
        total = ins[half][rows, :].astype(F32)
        for t in range(1, groups):
            total = total + ins[2 * t + half][rows, :].astype(F32)
        outs[s][:, :wide] = total[:, :wide].astype(BF16)
        outs[s][:, wide:] = two_terms(jnp.sum(total[:, wide:], axis=1, keepdims=True))


def sum_pieces(partials):
    groups = len(partials) // 2
    own_rows, wide = partials[0].shape
    return pl.pallas_call(
        functools.partial(sum_kernel, groups),
        out_shape=[jax.ShapeDtypeStruct((CAP, wide), BF16)] * E_MOD,
        cost_estimate=cost(own_rows * wide, 4 * groups * own_rows * wide),
        compiler_params=pltpu.CompilerParams(vmem_limit_bytes=SCOPED),
        name="sum_pieces",
    )(*partials)


def mix_kernel(groups, modality_ref, picks_ref, weights_ref, mix_out, gate_out):
    count, first, second, member = slot_of_labels(groups, modality_ref, picks_ref)
    slot = jnp.where(member, count, -1)
    scale = jnp.where(first, weights_ref[0:1, :], jnp.where(second, weights_ref[1:2, :], 0.0))
    own = jnp.where(position(groups)[1] == 0, first.astype(F32), second.astype(F32))
    want = lax.broadcasted_iota(jnp.int32, (CAP, slot.shape[1]), 0)
    mix = []
    for i in range(2 * E_MOD):
        hit = slot[i : i + 1, :] == want
        mix.append(jnp.where(hit, scale[i : i + 1, :], 0.0))
        gate_out[i * CAP : (i + 1) * CAP, :] = jnp.where(hit, own[i : i + 1, :], 0.0)
    mix = jnp.concatenate(mix, axis=0).T
    high = mix.astype(BF16)
    mix_out[0] = high
    mix_out[1] = (mix - high.astype(F32)).astype(BF16)


def mixing(groups, modality, picks, weights):
    tok_rows = modality.shape[1]
    slots = 2 * E_MOD * CAP
    vmem = pl.BlockSpec(memory_space=pltpu.VMEM)
    return pl.pallas_call(
        functools.partial(mix_kernel, groups),
        in_specs=[vmem] * 3,
        out_specs=[vmem] * 2,
        out_shape=[
            jax.ShapeDtypeStruct((2, tok_rows, slots), BF16),
            jax.ShapeDtypeStruct((slots, tok_rows), F32),
        ],
        compiler_params=pltpu.CompilerParams(vmem_limit_bytes=SCOPED),
        cost_estimate=cost(MIB, 1024),
        name="mixing",
    )(modality, picks, weights)


def combine_kernel(order, mix_ref, hit_ref, *refs):
    blocks, (grad_out, gate_out, table) = refs[: len(order)], refs[len(order) :]
    wide = grad_out.shape[1]
    for i, block in zip(order, blocks):
        table[i * CAP : (i + 1) * CAP, :] = block[...]
    part = jnp.sum(table[:, wide:].astype(F32), axis=1, keepdims=True)
    gate_out[...] = jnp.sum(hit_ref[...] * part, axis=0, keepdims=True)
    total = jnp.dot(mix_ref[0], table[:, :wide], preferred_element_type=F32)
    total = total + jnp.dot(mix_ref[1], table[:, :wide], preferred_element_type=F32)
    grad_out[...] = total.astype(BF16)


def combine(order, mix, hits, blocks):
    tok_rows = hits.shape[1]
    wide = blocks[0].shape[1] - EXT
    count = len(blocks)
    vmem = pl.BlockSpec(memory_space=pltpu.VMEM)
    return pl.pallas_call(
        functools.partial(combine_kernel, order),
        in_specs=[vmem] * (2 + count),
        out_specs=[vmem] * 2,
        out_shape=[
            jax.ShapeDtypeStruct((tok_rows, wide), BF16),
            jax.ShapeDtypeStruct((1, tok_rows), F32),
        ],
        scratch_shapes=[pltpu.VMEM((count * CAP, wide + EXT), BF16)],
        compiler_params=pltpu.CompilerParams(vmem_limit_bytes=SCOPED),
        cost_estimate=cost(4 * count * CAP * tok_rows * wide, 4 * tok_rows * wide),
        name="combine",
    )(mix, hits, *blocks)


def local(tokens, cotangent, modality, picks, gate_weights, gate_proj, up_proj, down_proj):
    device_count = lax.axis_size("ep")
    groups = device_count // E_MOD
    modality = modality.reshape(1, -1)
    picks = picks.T
    weights = gate_weights.T

    def to_expert(x, s, t=0):
        return lax.ppermute(
            x,
            "ep",
            [
                (e * groups + j, (e ^ s) * groups + (j + t) % groups)
                for e in range(E_MOD)
                for j in range(groups)
            ],
        )

    def to_piece(x, t):
        return to_expert(x, 0, t)

    def to_source(x, s, flip):
        return lax.ppermute(
            x,
            ("ep", "mod"),
            [
                ((e * groups + j) * 2 + m, ((e ^ s) * groups + j) * 2 + (m ^ flip))
                for e in range(E_MOD)
                for j in range(groups)
                for m in range(2)
            ],
        )

    mix, hits = mixing(groups, modality, picks, weights)
    sent = gather_slots(groups, modality, picks, tokens, cotangent)
    far = [[to_expert(sent[2 * s - 2], s) for s in range(2, E_MOD)]]
    near = [sent[0], to_expert(sent[1], 1)]
    own_pieces = [to_piece(sent[0], t) for t in range(1, groups)]
    gate_piece = load(gate_proj, sent[:1])
    later = [sent[2 * s - 1] for s in range(2, E_MOD)]
    later = pass_after(later, in_vmem(gate_piece), *own_pieces)
    far.append([to_expert(x, s) for x, s in zip(later, range(2, E_MOD))])
    near_pieces = [[x, to_piece(near[1], t)] for t, x in enumerate(own_pieces, 1)]
    up_piece = load(up_proj, [near[1], in_vmem(gate_piece)])
    far[0] = join(far[0], in_vmem(gate_piece), in_vmem(up_piece))
    far[0] = [far[0]] + [to_piece(far[0], t) for t in range(1, groups)]
    down_piece = load_turned(down_proj, [far[0][0], *sum(near_pieces, []), in_vmem(gate_piece), in_vmem(up_piece)])
    far[1] = join(far[1], in_vmem(gate_piece), in_vmem(up_piece), in_vmem(down_piece))
    far[1] = [far[1]] + [to_piece(far[1], t) for t in range(1, groups)]
    near = near + sum(near_pieces, [])
    blocks = [near + far[a] for a in range(2)]
    places = [
        tuple(
            place
            for t in range(groups)
            for place in [(2 * t, a * CAP), (2 * t + 1, a * CAP)]
            + [(2 * groups + t, i * CAP) for i in range(E_MOD - 2)]
        )
        for a in range(2)
    ]
    factors = pre_activations(blocks[0], places[0], gate_piece, up_piece, down_piece)
    first, (dgate, dup, part) = hidden_grads(
        blocks[1], places[1], groups, factors, down_piece, gate_piece, up_piece
    )
    second = list(back_half(groups, dgate, dup, part, gate_piece, up_piece))
    first = first[:2] + [to_piece(first[i], groups - i // 2) for i in range(2, 2 * groups)]
    waiting = pass_after(second[2:], *first[2:])
    second = second[:2] + [to_piece(x, groups - i // 2) for i, x in enumerate(waiting, 2)]
    crossed, kept = sum_pieces(first), sum_pieces(second)
    arrived = {0: kept[0]}
    for s in range(1, E_MOD):
        arrived[s] = to_source(kept[s], s, 0)
    for s in range(E_MOD):
        arrived[E_MOD + s] = to_source(crossed[s], s, 1)
    order = tuple(reversed(arrived))
    token_grad, gate_grad = combine(order, mix, hits, [arrived[i] for i in order])
    return token_grad, gate_grad.reshape(-1, 1)


def solution(mesh):
    in_specs = (
        P(("parts", "ep"), None),
        P(("parts", "ep"), None),
        P(("parts", "ep")),
        P(("parts", "ep"), None),
        P(("parts", "ep"), None),
        P("mod", None, "ep"),
        P("mod", None, "ep"),
        P("mod", "ep", None),
    )
    out_specs = (P(("parts", "ep"), "mod"), P(("parts", "ep"), "mod"))
    return jax.shard_map(local, mesh=mesh, in_specs=in_specs, out_specs=out_specs, check_vma=False)
```

```python
import functools

import jax
import jax.numpy as jnp
from jax import lax
from jax.experimental import pallas as pl
from jax.experimental.pallas import tpu as pltpu
from jax.sharding import PartitionSpec as P

E_MOD = 4
CAP = 16
EXT = 128
BF16 = jnp.bfloat16
F32 = jnp.float32
MIB = 1024 * 1024
SCOPED = 10 * MIB


def cost(flops, nbytes):
    return pl.CostEstimate(flops=flops, bytes_accessed=nbytes, transcendentals=0)


def whole(shape):
    return pl.BlockSpec(shape, lambda *_: (0,) * len(shape))


def position(groups):
    return lax.axis_index("ep") // groups, lax.axis_index("mod")


def slot_of_labels(groups, modality_ref, picks_ref):
    tok_rows = modality_ref.shape[1]
    label = lax.broadcasted_iota(jnp.int32, (2 * E_MOD, tok_rows), 0)
    own_expert, core = position(groups)
    expert = jnp.bitwise_xor(label % E_MOD, own_expert)
    modal = jnp.bitwise_xor(label // E_MOD, core)
    mine = modality_ref[...] == modal
    first = mine & (picks_ref[0:1, :] == expert)
    second = mine & (picks_ref[1:2, :] == expert)
    member = first | second
    row = lax.broadcasted_iota(jnp.int32, (tok_rows, tok_rows), 0)
    col = lax.broadcasted_iota(jnp.int32, (tok_rows, tok_rows), 1)
    earlier = (row < col).astype(F32)
    count = jnp.dot(member.astype(F32), earlier, preferred_element_type=F32).astype(jnp.int32)
    return count, first, second, member


def gather_kernel(groups, parts, modality_hbm, picks_hbm, rows_hbm, grads_hbm, *refs):
    outs, (modality, picks, rows, chosen, sems) = refs[:-5], refs[-5:]
    chunk = rows.shape[2] // parts
    small = [
        pltpu.make_async_copy(src, dst, sems.at[i])
        for i, (src, dst) in enumerate([(modality_hbm, modality), (picks_hbm, picks)])
    ]
    large = [
        [
            pltpu.make_async_copy(
                src.at[:, pl.ds(i * chunk, chunk)],
                rows.at[a, :, pl.ds(i * chunk, chunk)],
                sems.at[2 + 2 * i + a],
            )
            for a, src in enumerate([rows_hbm, grads_hbm])
        ]
        for i in range(parts)
    ]
    for copy in small + sum(large, []):
        copy.start()
    for copy in small:
        copy.wait()
    count, _, _, member = slot_of_labels(groups, modality, picks)
    slot = jnp.where(member, count, -1)
    want = lax.broadcasted_iota(jnp.int32, (CAP, slot.shape[1]), 0)
    for s in range(E_MOD):
        hit = (slot[s : s + 1, :] == want).astype(F32)
        chosen[s * CAP : (s + 1) * CAP, :] = hit.astype(BF16)
    for i in range(parts):
        cols = slice(i * chunk, (i + 1) * chunk)
        for a in range(2):
            large[i][a].wait()
            picked = jnp.dot(chosen[...], rows[a, :, cols], preferred_element_type=F32).astype(BF16)
            for s in range(E_MOD):
                block = picked[s * CAP : (s + 1) * CAP, :]
                if s < 2:
                    outs[s][a * CAP : (a + 1) * CAP, cols] = block
                else:
                    outs[2 * s - 2 + a][:, cols] = block


def gather_slots(groups, modality, picks, rows, grads):
    tok_rows, width = rows.shape
    parts = 4
    heights = [2 * CAP] * 2 + [CAP] * (2 * E_MOD - 4)
    return pl.pallas_call(
        functools.partial(gather_kernel, groups, parts),
        in_specs=[pl.BlockSpec(memory_space=pl.ANY)] * 4,
        out_specs=[pl.BlockSpec(memory_space=pltpu.VMEM)] * len(heights),
        out_shape=[jax.ShapeDtypeStruct((h, width), BF16) for h in heights],
        scratch_shapes=[
            pltpu.VMEM(modality.shape, jnp.int32),
            pltpu.VMEM(picks.shape, jnp.int32),
            pltpu.VMEM((2, tok_rows, width), BF16),
            pltpu.VMEM((E_MOD * CAP, tok_rows), BF16),
            pltpu.SemaphoreType.DMA((2 + 2 * parts,)),
        ],
        compiler_params=pltpu.CompilerParams(vmem_limit_bytes=SCOPED),
        cost_estimate=cost(4 * E_MOD * CAP * tok_rows * width, 6 * tok_rows * width),
        name="gather_slots",
    )(in_hbm(modality), in_hbm(picks), in_hbm(rows), in_hbm(grads))


def load_kernel(parts, src, *refs):
    dst, sems = refs[-2:]
    rows = src.shape[1] // parts
    copies = [
        pltpu.make_async_copy(
            src.at[:, pl.ds(i * rows, rows), :], dst.at[:, pl.ds(i * rows, rows), :], sems.at[i]
        )
        for i in range(parts)
    ]
    for copy in copies:
        copy.start()
    for copy in copies:
        copy.wait()


def load(weight, after):
    parts = 8
    return pl.pallas_call(
        functools.partial(load_kernel, parts),
        in_specs=[pl.BlockSpec(memory_space=pl.ANY)] * (1 + len(after)),
        out_specs=pl.BlockSpec(memory_space=pltpu.VMEM),
        out_shape=pltpu.VMEM(weight.shape, weight.dtype),
        scratch_shapes=[pltpu.SemaphoreType.DMA((parts,))],
        compiler_params=pltpu.CompilerParams(vmem_limit_bytes=SCOPED),
        cost_estimate=cost(3 * 10**9, 1024),
        name="load",
    )(in_hbm(weight), *after)


def load_turned_kernel(parts, src, *refs):
    dst, stage, sems = refs[-3:]
    rows, width = stage.shape[1:]
    copies = [
        pltpu.make_async_copy(src.at[0, pl.ds(i * rows, rows), :], stage.at[i], sems.at[i])
        for i in range(parts)
    ]
    for copy in copies:
        copy.start()
    chunk = 512
    for i in range(parts):
        copies[i].wait()
        for start in range(0, width, chunk):
            block = stage[i, :, start : start + chunk]
            dst[start : start + chunk, i * rows : (i + 1) * rows] = block.T


def load_turned(weight, after):
    _, height, width = weight.shape
    rows = 128
    parts = height // rows
    return pl.pallas_call(
        functools.partial(load_turned_kernel, parts),
        in_specs=[pl.BlockSpec(memory_space=pl.ANY)] * (1 + len(after)),
        out_specs=pl.BlockSpec(memory_space=pltpu.VMEM),
        out_shape=pltpu.VMEM((width, height), weight.dtype),
        scratch_shapes=[
            pltpu.VMEM((parts, rows, width), weight.dtype),
            pltpu.SemaphoreType.DMA((parts,)),
        ],
        compiler_params=pltpu.CompilerParams(vmem_limit_bytes=SCOPED),
        cost_estimate=cost(1 * 10**9, 1024),
        name="load_turned",
    )(in_hbm(weight), *after)


def pass_kernel(*refs):
    pass


def pass_after(blocks, *need):
    place = pl.BlockSpec(memory_space=pl.ANY)
    return pl.pallas_call(
        pass_kernel,
        in_specs=[place] * (len(blocks) + len(need)),
        out_specs=[place] * len(blocks),
        out_shape=[jax.ShapeDtypeStruct(block.shape, block.dtype) for block in blocks],
        input_output_aliases={i: i for i in range(len(blocks))},
        compiler_params=pltpu.CompilerParams(vmem_limit_bytes=SCOPED),
        cost_estimate=cost(3 * 10**9, 1024),
        name="pass_after",
    )(*blocks, *need)


def join_kernel(count, *refs):
    blocks, out = refs[:count], refs[-1]
    start = 0
    for block in blocks:
        out[start : start + block.shape[0], :] = block[...]
        start += block.shape[0]


def join(blocks, *need):
    count = len(blocks)
    total = sum(block.shape[0] for block in blocks)
    vmem = pl.BlockSpec(memory_space=pltpu.VMEM)
    return pl.pallas_call(
        functools.partial(join_kernel, count),
        in_specs=[vmem] * count + [pl.BlockSpec(memory_space=pl.ANY)] * len(need),
        out_specs=vmem,
        out_shape=jax.ShapeDtypeStruct((total, blocks[0].shape[1]), BF16),
        compiler_params=pltpu.CompilerParams(vmem_limit_bytes=SCOPED),
        cost_estimate=cost(2 * 10**9, 1024),
        name="join",
    )(*blocks, *need)


def in_hbm(x):
    return pltpu.with_memory_space_constraint(x, pltpu.HBM)


def in_vmem(x):
    return pltpu.with_memory_space_constraint(x, pltpu.VMEM)


def fill(rows, refs, places):
    for i, (index, start) in enumerate(places):
        rows[i * CAP : (i + 1) * CAP, :] = refs[index][start : start + CAP, :]


def pre_kernel(count, places, *refs):
    blocks, (gate_ref, up_ref, _, act_out, slope_out, both_out, rows) = refs[:count], refs[count:]
    fill(rows, blocks, places)
    hidden = gate_ref.shape[2]
    chunk = min(256, hidden)
    for start in range(0, hidden, chunk):
        cols = slice(start, start + chunk)
        gate_pre = jnp.dot(rows[...], gate_ref[0, :, cols], preferred_element_type=F32)
        up_pre = jnp.dot(rows[...], up_ref[0, :, cols], preferred_element_type=F32)
        sig = jax.nn.sigmoid(gate_pre)
        act = gate_pre * sig
        act_out[:, cols] = act
        slope_out[:, cols] = up_pre * (sig * (1.0 + gate_pre * (1.0 - sig)))
        both_out[:, cols] = act * up_pre


def pre_activations(blocks, places, gate_piece, up_piece, need):
    count = len(blocks)
    _, width, hidden = gate_piece.shape
    total = len(places) * CAP
    vmem = pl.BlockSpec(memory_space=pltpu.VMEM)
    return pl.pallas_call(
        functools.partial(pre_kernel, count, places),
        in_specs=[vmem] * (count + 2) + [pl.BlockSpec(memory_space=pl.ANY)],
        out_specs=[vmem] * 3,
        out_shape=[jax.ShapeDtypeStruct((total, hidden), F32)] * 3,
        scratch_shapes=[pltpu.VMEM((total, width), BF16)],
        compiler_params=pltpu.CompilerParams(vmem_limit_bytes=SCOPED),
        cost_estimate=cost(5 * 10**9, 1024),
        name="pre_activations",
    )(*blocks, in_vmem(gate_piece), in_vmem(up_piece), in_vmem(need))


def back_columns(groups, flip, dgate_ref, dup_ref, part, gate_ref, up_ref, outs):
    half = jnp.bitwise_xor(position(groups)[1], flip)
    wide = outs[0].shape[1] - EXT
    own_rows = outs[0].shape[0]
    dgate, dup = dgate_ref[...].T, dup_ref[...].T
    chunk = 512
    for step in range(wide // chunk):
        rows = pl.ds(pl.multiple_of(half * wide + step * chunk, chunk), chunk)
        grad = jnp.dot(gate_ref[0, rows, :], dgate, preferred_element_type=F32)
        grad = grad + jnp.dot(up_ref[0, rows, :], dup, preferred_element_type=F32)
        grad = grad.T.astype(BF16)
        for t in range(groups):
            outs[t][:, step * chunk : (step + 1) * chunk] = grad[t * own_rows : (t + 1) * own_rows, :]
    for t in range(groups):
        outs[t][:, wide:] = part[t * own_rows : (t + 1) * own_rows, :]


def hidden_kernel(count, places, groups, *refs):
    blocks = refs[:count]
    act_ref, slope_ref, both_ref, down_ref, gate_ref, up_ref = refs[count : count + 6]
    outs = refs[count + 6 : count + 6 + groups]
    dgate, dup, part_out, rows = refs[count + 6 + groups :]
    fill(rows, blocks, places)
    hidden = gate_ref.shape[2]
    chunk = min(256, hidden)
    part = jnp.zeros((rows.shape[0], 1), F32)
    for start in range(0, hidden, chunk):
        cols = slice(start, start + chunk)
        grad = jnp.dot(rows[...], down_ref[:, cols], preferred_element_type=F32)
        part = part + jnp.sum(grad * both_ref[:, cols], axis=1, keepdims=True)
        dgate[:, cols] = (grad * slope_ref[:, cols]).astype(BF16)
        dup[:, cols] = (grad * act_ref[:, cols]).astype(BF16)
    part_out[...] = two_terms(part)
    back_columns(groups, 1, dgate, dup, part_out[...], gate_ref, up_ref, outs)


def hidden_grads(blocks, places, groups, factors, down_piece, gate_piece, up_piece):
    count = len(blocks)
    _, width, hidden = gate_piece.shape
    total = len(places) * CAP
    shape = (total // groups, width // 2 + EXT)
    vmem = pl.BlockSpec(memory_space=pltpu.VMEM)
    out = pl.pallas_call(
        functools.partial(hidden_kernel, count, places, groups),
        in_specs=[vmem] * (count + 6),
        out_specs=[vmem] * (groups + 3),
        out_shape=[jax.ShapeDtypeStruct(shape, BF16)] * groups
        + [jax.ShapeDtypeStruct((total, hidden), BF16)] * 2
        + [jax.ShapeDtypeStruct((total, EXT), BF16)],
        scratch_shapes=[pltpu.VMEM((total, width), BF16)],
        compiler_params=pltpu.CompilerParams(vmem_limit_bytes=SCOPED),
        cost_estimate=cost(4 * total * width * hidden, 4 * width * hidden),
        name="hidden_grads",
    )(*blocks, *factors, in_vmem(down_piece), in_vmem(gate_piece), in_vmem(up_piece))
    return out[:groups], out[groups:]


def back_kernel(groups, dgate_ref, dup_ref, part_ref, gate_ref, up_ref, *outs):
    back_columns(groups, 0, dgate_ref, dup_ref, part_ref[...], gate_ref, up_ref, outs)


def back_half(groups, dgate, dup, part, gate_piece, up_piece):
    _, width, hidden = gate_piece.shape
    total = dgate.shape[0]
    shape = (total // groups, width // 2 + EXT)
    vmem = pl.BlockSpec(memory_space=pltpu.VMEM)
    return pl.pallas_call(
        functools.partial(back_kernel, groups),
        in_specs=[vmem] * 5,
        out_specs=[vmem] * groups,
        out_shape=[jax.ShapeDtypeStruct(shape, BF16)] * groups,
        compiler_params=pltpu.CompilerParams(vmem_limit_bytes=SCOPED),
        cost_estimate=cost(2 * total * width * hidden, 2 * width * hidden),
        name="back_half",
    )(dgate, dup, part, in_vmem(gate_piece), in_vmem(up_piece))


def two_terms(value):
    high = value.astype(BF16).astype(F32)
    low = value - high
    lane = lax.broadcasted_iota(jnp.int32, (value.shape[0], EXT), 1)
    return jnp.where(lane == 0, high, jnp.where(lane == 1, low, 0.0)).astype(BF16)


def sum_kernel(groups, *refs):
    ins, outs = refs[:groups], refs[groups:]
    wide = ins[0].shape[1] - EXT
    for s in range(E_MOD):
        rows = slice(s * CAP, (s + 1) * CAP)
        total = ins[0][rows, :].astype(F32)
        for t in range(1, groups):
            total = total + ins[t][rows, :].astype(F32)
        outs[s][:, :wide] = total[:, :wide].astype(BF16)
        outs[s][:, wide:] = two_terms(jnp.sum(total[:, wide:], axis=1, keepdims=True))


def sum_pieces(partials):
    groups = len(partials)
    own_rows, wide = partials[0].shape
    return pl.pallas_call(
        functools.partial(sum_kernel, groups),
        out_shape=[jax.ShapeDtypeStruct((CAP, wide), BF16)] * E_MOD,
        cost_estimate=cost(own_rows * wide, 4 * groups * own_rows * wide),
        compiler_params=pltpu.CompilerParams(vmem_limit_bytes=SCOPED),
        name="sum_pieces",
    )(*partials)


def mix_kernel(groups, modality_ref, picks_ref, weights_ref, mix_out, gate_out):
    count, first, second, member = slot_of_labels(groups, modality_ref, picks_ref)
    slot = jnp.where(member, count, -1)
    scale = jnp.where(first, weights_ref[0:1, :], jnp.where(second, weights_ref[1:2, :], 0.0))
    own = jnp.where(position(groups)[1] == 0, first.astype(F32), second.astype(F32))
    want = lax.broadcasted_iota(jnp.int32, (CAP, slot.shape[1]), 0)
    mix = []
    for i in range(2 * E_MOD):
        hit = slot[i : i + 1, :] == want
        mix.append(jnp.where(hit, scale[i : i + 1, :], 0.0))
        gate_out[i * CAP : (i + 1) * CAP, :] = jnp.where(hit, own[i : i + 1, :], 0.0)
    mix = jnp.concatenate(mix, axis=0).T
    high = mix.astype(BF16)
    mix_out[0] = high
    mix_out[1] = (mix - high.astype(F32)).astype(BF16)


def mixing(groups, modality, picks, weights):
    tok_rows = modality.shape[1]
    slots = 2 * E_MOD * CAP
    vmem = pl.BlockSpec(memory_space=pltpu.VMEM)
    return pl.pallas_call(
        functools.partial(mix_kernel, groups),
        in_specs=[vmem] * 3,
        out_specs=[vmem] * 2,
        out_shape=[
            jax.ShapeDtypeStruct((2, tok_rows, slots), BF16),
            jax.ShapeDtypeStruct((slots, tok_rows), F32),
        ],
        compiler_params=pltpu.CompilerParams(vmem_limit_bytes=SCOPED),
        cost_estimate=cost(MIB, 1024),
        name="mixing",
    )(modality, picks, weights)


def combine_kernel(order, mix_ref, hit_ref, *refs):
    blocks, (grad_out, gate_out, table) = refs[: len(order)], refs[len(order) :]
    wide = grad_out.shape[1]
    for i, block in zip(order, blocks):
        table[i * CAP : (i + 1) * CAP, :] = block[...]
    part = jnp.sum(table[:, wide:].astype(F32), axis=1, keepdims=True)
    gate_out[...] = jnp.sum(hit_ref[...] * part, axis=0, keepdims=True)
    total = jnp.dot(mix_ref[0], table[:, :wide], preferred_element_type=F32)
    total = total + jnp.dot(mix_ref[1], table[:, :wide], preferred_element_type=F32)
    grad_out[...] = total.astype(BF16)


def combine(order, mix, hits, blocks):
    tok_rows = hits.shape[1]
    wide = blocks[0].shape[1] - EXT
    count = len(blocks)
    vmem = pl.BlockSpec(memory_space=pltpu.VMEM)
    return pl.pallas_call(
        functools.partial(combine_kernel, order),
        in_specs=[vmem] * (2 + count),
        out_specs=[vmem] * 2,
        out_shape=[
            jax.ShapeDtypeStruct((tok_rows, wide), BF16),
            jax.ShapeDtypeStruct((1, tok_rows), F32),
        ],
        scratch_shapes=[pltpu.VMEM((count * CAP, wide + EXT), BF16)],
        compiler_params=pltpu.CompilerParams(vmem_limit_bytes=SCOPED),
        cost_estimate=cost(4 * count * CAP * tok_rows * wide, 4 * tok_rows * wide),
        name="combine",
    )(mix, hits, *blocks)


def local(tokens, cotangent, modality, picks, gate_weights, gate_proj, up_proj, down_proj):
    device_count = lax.axis_size("ep")
    groups = device_count // E_MOD
    modality = modality.reshape(1, -1)
    picks = picks.T
    weights = gate_weights.T

    def to_expert(x, s, t=0):
        return lax.ppermute(
            x,
            "ep",
            [
                (e * groups + j, (e ^ s) * groups + (j + t) % groups)
                for e in range(E_MOD)
                for j in range(groups)
            ],
        )

    def to_piece(x, t):
        return to_expert(x, 0, t)

    def to_source(x, s, flip):
        return lax.ppermute(
            x,
            ("ep", "mod"),
            [
                ((e * groups + j) * 2 + m, ((e ^ s) * groups + j) * 2 + (m ^ flip))
                for e in range(E_MOD)
                for j in range(groups)
                for m in range(2)
            ],
        )

    mix, hits = mixing(groups, modality, picks, weights)
    sent = gather_slots(groups, modality, picks, tokens, cotangent)
    far = [[to_expert(sent[2 * s - 2], s) for s in range(2, E_MOD)]]
    near = [sent[0], to_expert(sent[1], 1)]
    own_pieces = [to_piece(sent[0], t) for t in range(1, groups)]
    gate_piece = load(gate_proj, sent[:1])
    later = [sent[2 * s - 1] for s in range(2, E_MOD)]
    later = pass_after(later, in_vmem(gate_piece), *own_pieces)
    far.append([to_expert(x, s) for x, s in zip(later, range(2, E_MOD))])
    near_pieces = [[x, to_piece(near[1], t)] for t, x in enumerate(own_pieces, 1)]
    up_piece = load(up_proj, [near[1], in_vmem(gate_piece)])
    far[0] = join(far[0], in_vmem(gate_piece), in_vmem(up_piece))
    far[0] = [far[0]] + [to_piece(far[0], t) for t in range(1, groups)]
    down_piece = load_turned(down_proj, [far[0][0], *sum(near_pieces, []), in_vmem(gate_piece), in_vmem(up_piece)])
    far[1] = join(far[1], in_vmem(gate_piece), in_vmem(up_piece), in_vmem(down_piece))
    far[1] = [far[1]] + [to_piece(far[1], t) for t in range(1, groups)]
    near = near + sum(near_pieces, [])
    blocks = [near + far[a] for a in range(2)]
    places = [
        tuple(
            place
            for t in range(groups)
            for place in [(2 * t, a * CAP), (2 * t + 1, a * CAP)]
            + [(2 * groups + t, i * CAP) for i in range(E_MOD - 2)]
        )
        for a in range(2)
    ]
    factors = pre_activations(blocks[0], places[0], gate_piece, up_piece, down_piece)
    first, (dgate, dup, part) = hidden_grads(
        blocks[1], places[1], groups, factors, down_piece, gate_piece, up_piece
    )
    second = back_half(groups, dgate, dup, part, gate_piece, up_piece)
    first = [first[0]] + [to_piece(first[t], groups - t) for t in range(1, groups)]
    waiting = pass_after(second[1:], *first[1:])
    second = [second[0]] + [to_piece(x, groups - t) for t, x in enumerate(waiting, 1)]
    crossed, kept = sum_pieces(first), sum_pieces(second)
    arrived = {0: kept[0]}
    for s in range(1, E_MOD):
        arrived[s] = to_source(kept[s], s, 0)
    for s in range(E_MOD):
        arrived[E_MOD + s] = to_source(crossed[s], s, 1)
    order = tuple(reversed(arrived))
    token_grad, gate_grad = combine(order, mix, hits, [arrived[i] for i in order])
    return token_grad, gate_grad.reshape(-1, 1)


def solution(mesh):
    in_specs = (
        P(("parts", "ep"), None),
        P(("parts", "ep"), None),
        P(("parts", "ep")),
        P(("parts", "ep"), None),
        P(("parts", "ep"), None),
        P("mod", None, "ep"),
        P("mod", None, "ep"),
        P("mod", "ep", None),
    )
    out_specs = (P(("parts", "ep"), "mod"), P(("parts", "ep"), "mod"))
    return jax.shard_map(local, mesh=mesh, in_specs=in_specs, out_specs=out_specs, check_vma=False)
```

```python
import functools

import jax
import jax.numpy as jnp
from jax import lax
from jax.experimental import pallas as pl
from jax.experimental.pallas import tpu as pltpu
from jax.sharding import PartitionSpec as P

E_MOD = 4
CAP = 16
EXT = 128
BF16 = jnp.bfloat16
F32 = jnp.float32
MIB = 1024 * 1024
SCOPED = 10 * MIB


def cost(flops, nbytes):
    return pl.CostEstimate(flops=flops, bytes_accessed=nbytes, transcendentals=0)


def whole(shape):
    return pl.BlockSpec(shape, lambda *_: (0,) * len(shape))


def position(groups):
    return lax.axis_index("ep") // groups, lax.axis_index("mod")


def slot_of_labels(groups, modality_ref, picks_ref):
    tok_rows = modality_ref.shape[1]
    label = lax.broadcasted_iota(jnp.int32, (2 * E_MOD, tok_rows), 0)
    own_expert, core = position(groups)
    expert = jnp.bitwise_xor(label % E_MOD, own_expert)
    modal = jnp.bitwise_xor(label // E_MOD, core)
    mine = modality_ref[...] == modal
    first = mine & (picks_ref[0:1, :] == expert)
    second = mine & (picks_ref[1:2, :] == expert)
    member = first | second
    row = lax.broadcasted_iota(jnp.int32, (tok_rows, tok_rows), 0)
    col = lax.broadcasted_iota(jnp.int32, (tok_rows, tok_rows), 1)
    earlier = (row < col).astype(F32)
    count = jnp.dot(member.astype(F32), earlier, preferred_element_type=F32).astype(jnp.int32)
    return count, first, second, member


def gather_kernel(groups, parts, modality_hbm, picks_hbm, rows_hbm, grads_hbm, *refs):
    outs, (modality, picks, rows, chosen, sems) = refs[:-5], refs[-5:]
    chunk = rows.shape[2] // parts
    small = [
        pltpu.make_async_copy(src, dst, sems.at[i])
        for i, (src, dst) in enumerate([(modality_hbm, modality), (picks_hbm, picks)])
    ]
    large = [
        [
            pltpu.make_async_copy(
                src.at[:, pl.ds(i * chunk, chunk)],
                rows.at[a, :, pl.ds(i * chunk, chunk)],
                sems.at[2 + 2 * i + a],
            )
            for a, src in enumerate([rows_hbm, grads_hbm])
        ]
        for i in range(parts)
    ]
    for copy in small + sum(large, []):
        copy.start()
    for copy in small:
        copy.wait()
    count, _, _, member = slot_of_labels(groups, modality, picks)
    slot = jnp.where(member, count, -1)
    want = lax.broadcasted_iota(jnp.int32, (CAP, slot.shape[1]), 0)
    for s in range(E_MOD):
        hit = (slot[s : s + 1, :] == want).astype(F32)
        chosen[s * CAP : (s + 1) * CAP, :] = hit.astype(BF16)
    for i in range(parts):
        cols = slice(i * chunk, (i + 1) * chunk)
        for a in range(2):
            large[i][a].wait()
            picked = jnp.dot(chosen[...], rows[a, :, cols], preferred_element_type=F32).astype(BF16)
            for s in range(E_MOD):
                block = picked[s * CAP : (s + 1) * CAP, :]
                if s < 2:
                    outs[s][a * CAP : (a + 1) * CAP, cols] = block
                else:
                    outs[2 * s - 2 + a][:, cols] = block


def gather_slots(groups, modality, picks, rows, grads):
    tok_rows, width = rows.shape
    parts = 4
    heights = [2 * CAP] * 2 + [CAP] * (2 * E_MOD - 4)
    return pl.pallas_call(
        functools.partial(gather_kernel, groups, parts),
        in_specs=[pl.BlockSpec(memory_space=pl.ANY)] * 4,
        out_specs=[pl.BlockSpec(memory_space=pltpu.VMEM)] * len(heights),
        out_shape=[jax.ShapeDtypeStruct((h, width), BF16) for h in heights],
        scratch_shapes=[
            pltpu.VMEM(modality.shape, jnp.int32),
            pltpu.VMEM(picks.shape, jnp.int32),
            pltpu.VMEM((2, tok_rows, width), BF16),
            pltpu.VMEM((E_MOD * CAP, tok_rows), BF16),
            pltpu.SemaphoreType.DMA((2 + 2 * parts,)),
        ],
        compiler_params=pltpu.CompilerParams(vmem_limit_bytes=SCOPED),
        cost_estimate=cost(4 * E_MOD * CAP * tok_rows * width, 6 * tok_rows * width),
        name="gather_slots",
    )(in_hbm(modality), in_hbm(picks), in_hbm(rows), in_hbm(grads))


def load_kernel(parts, src, *refs):
    dst, sems = refs[-2:]
    rows = src.shape[1] // parts
    copies = [
        pltpu.make_async_copy(
            src.at[:, pl.ds(i * rows, rows), :], dst.at[:, pl.ds(i * rows, rows), :], sems.at[i]
        )
        for i in range(parts)
    ]
    for copy in copies:
        copy.start()
    for copy in copies:
        copy.wait()


def load(weight, after):
    parts = 8
    return pl.pallas_call(
        functools.partial(load_kernel, parts),
        in_specs=[pl.BlockSpec(memory_space=pl.ANY)] * (1 + len(after)),
        out_specs=pl.BlockSpec(memory_space=pltpu.VMEM),
        out_shape=pltpu.VMEM(weight.shape, weight.dtype),
        scratch_shapes=[pltpu.SemaphoreType.DMA((parts,))],
        compiler_params=pltpu.CompilerParams(vmem_limit_bytes=SCOPED),
        cost_estimate=cost(0, 1024),
        name="load",
    )(in_hbm(weight), *after)


def load_turned_kernel(parts, src, *refs):
    dst, stage, sems = refs[-3:]
    rows, width = stage.shape[1:]
    copies = [
        pltpu.make_async_copy(src.at[0, pl.ds(i * rows, rows), :], stage.at[i], sems.at[i])
        for i in range(parts)
    ]
    for copy in copies:
        copy.start()
    chunk = 512
    for i in range(parts):
        copies[i].wait()
        for start in range(0, width, chunk):
            block = stage[i, :, start : start + chunk]
            dst[start : start + chunk, i * rows : (i + 1) * rows] = block.T


def load_turned(weight, after):
    _, height, width = weight.shape
    rows = 128
    parts = height // rows
    return pl.pallas_call(
        functools.partial(load_turned_kernel, parts),
        in_specs=[pl.BlockSpec(memory_space=pl.ANY)] * (1 + len(after)),
        out_specs=pl.BlockSpec(memory_space=pltpu.VMEM),
        out_shape=pltpu.VMEM((width, height), weight.dtype),
        scratch_shapes=[
            pltpu.VMEM((parts, rows, width), weight.dtype),
            pltpu.SemaphoreType.DMA((parts,)),
        ],
        compiler_params=pltpu.CompilerParams(vmem_limit_bytes=SCOPED),
        cost_estimate=cost(0, 1024),
        name="load_turned",
    )(in_hbm(weight), *after)


def pass_kernel(*refs):
    pass


def pass_after(blocks, *need):
    place = pl.BlockSpec(memory_space=pl.ANY)
    return pl.pallas_call(
        pass_kernel,
        in_specs=[place] * (len(blocks) + len(need)),
        out_specs=[place] * len(blocks),
        out_shape=[jax.ShapeDtypeStruct(block.shape, block.dtype) for block in blocks],
        input_output_aliases={i: i for i in range(len(blocks))},
        compiler_params=pltpu.CompilerParams(vmem_limit_bytes=SCOPED),
        cost_estimate=cost(0, 1024),
        name="pass_after",
    )(*blocks, *need)


def join_kernel(count, *refs):
    blocks, out = refs[:count], refs[-1]
    start = 0
    for block in blocks:
        out[start : start + block.shape[0], :] = block[...]
        start += block.shape[0]


def join(blocks, *need):
    count = len(blocks)
    total = sum(block.shape[0] for block in blocks)
    vmem = pl.BlockSpec(memory_space=pltpu.VMEM)
    return pl.pallas_call(
        functools.partial(join_kernel, count),
        in_specs=[vmem] * count + [pl.BlockSpec(memory_space=pl.ANY)] * len(need),
        out_specs=vmem,
        out_shape=jax.ShapeDtypeStruct((total, blocks[0].shape[1]), BF16),
        compiler_params=pltpu.CompilerParams(vmem_limit_bytes=SCOPED),
        cost_estimate=cost(3 * 10**9, 1024),
        name="join",
    )(*blocks, *need)


def in_hbm(x):
    return pltpu.with_memory_space_constraint(x, pltpu.HBM)


def in_vmem(x):
    return pltpu.with_memory_space_constraint(x, pltpu.VMEM)


def fill(rows, refs, places):
    for i, (index, start) in enumerate(places):
        rows[i * CAP : (i + 1) * CAP, :] = refs[index][start : start + CAP, :]


def pre_kernel(count, places, *refs):
    blocks, (gate_ref, up_ref, _, act_out, slope_out, both_out, rows) = refs[:count], refs[count:]
    fill(rows, blocks, places)
    hidden = gate_ref.shape[2]
    chunk = min(256, hidden)
    for start in range(0, hidden, chunk):
        cols = slice(start, start + chunk)
        gate_pre = jnp.dot(rows[...], gate_ref[0, :, cols], preferred_element_type=F32)
        up_pre = jnp.dot(rows[...], up_ref[0, :, cols], preferred_element_type=F32)
        sig = jax.nn.sigmoid(gate_pre)
        act = gate_pre * sig
        act_out[:, cols] = act
        slope_out[:, cols] = up_pre * (sig * (1.0 + gate_pre * (1.0 - sig)))
        both_out[:, cols] = act * up_pre


def pre_activations(blocks, places, gate_piece, up_piece, need):
    count = len(blocks)
    _, width, hidden = gate_piece.shape
    total = len(places) * CAP
    vmem = pl.BlockSpec(memory_space=pltpu.VMEM)
    return pl.pallas_call(
        functools.partial(pre_kernel, count, places),
        in_specs=[vmem] * (count + 2) + [pl.BlockSpec(memory_space=pl.ANY)],
        out_specs=[vmem] * 3,
        out_shape=[jax.ShapeDtypeStruct((total, hidden), F32)] * 3,
        scratch_shapes=[pltpu.VMEM((total, width), BF16)],
        compiler_params=pltpu.CompilerParams(vmem_limit_bytes=SCOPED),
        cost_estimate=cost(5 * 10**9, 1024),
        name="pre_activations",
    )(*blocks, in_vmem(gate_piece), in_vmem(up_piece), in_vmem(need))


def back_columns(groups, flip, dgate_ref, dup_ref, part, gate_ref, up_ref, outs):
    half = jnp.bitwise_xor(position(groups)[1], flip)
    wide = outs[0].shape[1] - EXT
    own_rows = outs[0].shape[0]
    dgate, dup = dgate_ref[...].T, dup_ref[...].T
    chunk = 1024
    for step in range(wide // chunk):
        rows = pl.ds(pl.multiple_of(half * wide + step * chunk, chunk), chunk)
        grad = jnp.dot(gate_ref[0, rows, :], dgate, preferred_element_type=F32)
        grad = grad + jnp.dot(up_ref[0, rows, :], dup, preferred_element_type=F32)
        grad = grad.T.astype(BF16)
        for t in range(groups):
            outs[t][:, step * chunk : (step + 1) * chunk] = grad[t * own_rows : (t + 1) * own_rows, :]
    for t in range(groups):
        outs[t][:, wide:] = part[t * own_rows : (t + 1) * own_rows, :]


def hidden_kernel(count, places, groups, *refs):
    blocks = refs[:count]
    act_ref, slope_ref, both_ref, down_ref, gate_ref, up_ref = refs[count : count + 6]
    outs = refs[count + 6 : count + 6 + groups]
    dgate, dup, part_out, rows = refs[count + 6 + groups :]
    fill(rows, blocks, places)
    hidden = gate_ref.shape[2]
    chunk = min(256, hidden)
    part = jnp.zeros((rows.shape[0], 1), F32)
    for start in range(0, hidden, chunk):
        cols = slice(start, start + chunk)
        grad = jnp.dot(rows[...], down_ref[:, cols], preferred_element_type=F32)
        part = part + jnp.sum(grad * both_ref[:, cols], axis=1, keepdims=True)
        dgate[:, cols] = (grad * slope_ref[:, cols]).astype(BF16)
        dup[:, cols] = (grad * act_ref[:, cols]).astype(BF16)
    part_out[...] = two_terms(part)
    back_columns(groups, 1, dgate, dup, part_out[...], gate_ref, up_ref, outs)


def hidden_grads(blocks, places, groups, factors, down_piece, gate_piece, up_piece):
    count = len(blocks)
    _, width, hidden = gate_piece.shape
    total = len(places) * CAP
    shape = (total // groups, width // 2 + EXT)
    vmem = pl.BlockSpec(memory_space=pltpu.VMEM)
    out = pl.pallas_call(
        functools.partial(hidden_kernel, count, places, groups),
        in_specs=[vmem] * (count + 6),
        out_specs=[vmem] * (groups + 3),
        out_shape=[jax.ShapeDtypeStruct(shape, BF16)] * groups
        + [jax.ShapeDtypeStruct((total, hidden), BF16)] * 2
        + [jax.ShapeDtypeStruct((total, EXT), BF16)],
        scratch_shapes=[pltpu.VMEM((total, width), BF16)],
        compiler_params=pltpu.CompilerParams(vmem_limit_bytes=SCOPED),
        cost_estimate=cost(4 * total * width * hidden, 4 * width * hidden),
        name="hidden_grads",
    )(*blocks, *factors, in_vmem(down_piece), in_vmem(gate_piece), in_vmem(up_piece))
    return out[:groups], out[groups:]


def back_kernel(groups, dgate_ref, dup_ref, part_ref, gate_ref, up_ref, *outs):
    back_columns(groups, 0, dgate_ref, dup_ref, part_ref[...], gate_ref, up_ref, outs)


def back_half(groups, dgate, dup, part, gate_piece, up_piece):
    _, width, hidden = gate_piece.shape
    total = dgate.shape[0]
    shape = (total // groups, width // 2 + EXT)
    vmem = pl.BlockSpec(memory_space=pltpu.VMEM)
    return pl.pallas_call(
        functools.partial(back_kernel, groups),
        in_specs=[vmem] * 5,
        out_specs=[vmem] * groups,
        out_shape=[jax.ShapeDtypeStruct(shape, BF16)] * groups,
        compiler_params=pltpu.CompilerParams(vmem_limit_bytes=SCOPED),
        cost_estimate=cost(2 * total * width * hidden, 2 * width * hidden),
        name="back_half",
    )(dgate, dup, part, in_vmem(gate_piece), in_vmem(up_piece))


def two_terms(value):
    high = value.astype(BF16).astype(F32)
    low = value - high
    lane = lax.broadcasted_iota(jnp.int32, (value.shape[0], EXT), 1)
    return jnp.where(lane == 0, high, jnp.where(lane == 1, low, 0.0)).astype(BF16)


def sum_kernel(groups, *refs):
    ins, outs = refs[:groups], refs[groups:]
    wide = ins[0].shape[1] - EXT
    for s in range(E_MOD):
        rows = slice(s * CAP, (s + 1) * CAP)
        total = ins[0][rows, :].astype(F32)
        for t in range(1, groups):
            total = total + ins[t][rows, :].astype(F32)
        outs[s][:, :wide] = total[:, :wide].astype(BF16)
        outs[s][:, wide:] = two_terms(jnp.sum(total[:, wide:], axis=1, keepdims=True))


def sum_pieces(partials):
    groups = len(partials)
    own_rows, wide = partials[0].shape
    return pl.pallas_call(
        functools.partial(sum_kernel, groups),
        out_shape=[jax.ShapeDtypeStruct((CAP, wide), BF16)] * E_MOD,
        cost_estimate=cost(own_rows * wide, 4 * groups * own_rows * wide),
        compiler_params=pltpu.CompilerParams(vmem_limit_bytes=SCOPED),
        name="sum_pieces",
    )(*partials)


def mix_kernel(groups, modality_ref, picks_ref, weights_ref, mix_out, gate_out):
    count, first, second, member = slot_of_labels(groups, modality_ref, picks_ref)
    slot = jnp.where(member, count, -1)
    scale = jnp.where(first, weights_ref[0:1, :], jnp.where(second, weights_ref[1:2, :], 0.0))
    own = jnp.where(position(groups)[1] == 0, first.astype(F32), second.astype(F32))
    want = lax.broadcasted_iota(jnp.int32, (CAP, slot.shape[1]), 0)
    mix = []
    for i in range(2 * E_MOD):
        hit = slot[i : i + 1, :] == want
        mix.append(jnp.where(hit, scale[i : i + 1, :], 0.0))
        gate_out[i * CAP : (i + 1) * CAP, :] = jnp.where(hit, own[i : i + 1, :], 0.0)
    mix = jnp.concatenate(mix, axis=0).T
    high = mix.astype(BF16)
    mix_out[0] = high
    mix_out[1] = (mix - high.astype(F32)).astype(BF16)


def mixing(groups, modality, picks, weights):
    tok_rows = modality.shape[1]
    slots = 2 * E_MOD * CAP
    vmem = pl.BlockSpec(memory_space=pltpu.VMEM)
    return pl.pallas_call(
        functools.partial(mix_kernel, groups),
        in_specs=[vmem] * 3,
        out_specs=[vmem] * 2,
        out_shape=[
            jax.ShapeDtypeStruct((2, tok_rows, slots), BF16),
            jax.ShapeDtypeStruct((slots, tok_rows), F32),
        ],
        compiler_params=pltpu.CompilerParams(vmem_limit_bytes=SCOPED),
        cost_estimate=cost(MIB, 1024),
        name="mixing",
    )(modality, picks, weights)


def combine_kernel(order, mix_ref, hit_ref, *refs):
    blocks, (grad_out, gate_out, table) = refs[: len(order)], refs[len(order) :]
    wide = grad_out.shape[1]
    for i, block in zip(order, blocks):
        table[i * CAP : (i + 1) * CAP, :] = block[...]
    part = jnp.sum(table[:, wide:].astype(F32), axis=1, keepdims=True)
    gate_out[...] = jnp.sum(hit_ref[...] * part, axis=0, keepdims=True)
    total = jnp.dot(mix_ref[0], table[:, :wide], preferred_element_type=F32)
    total = total + jnp.dot(mix_ref[1], table[:, :wide], preferred_element_type=F32)
    grad_out[...] = total.astype(BF16)


def combine(order, mix, hits, blocks):
    tok_rows = hits.shape[1]
    wide = blocks[0].shape[1] - EXT
    count = len(blocks)
    vmem = pl.BlockSpec(memory_space=pltpu.VMEM)
    return pl.pallas_call(
        functools.partial(combine_kernel, order),
        in_specs=[vmem] * (2 + count),
        out_specs=[vmem] * 2,
        out_shape=[
            jax.ShapeDtypeStruct((tok_rows, wide), BF16),
            jax.ShapeDtypeStruct((1, tok_rows), F32),
        ],
        scratch_shapes=[pltpu.VMEM((count * CAP, wide + EXT), BF16)],
        compiler_params=pltpu.CompilerParams(vmem_limit_bytes=SCOPED),
        cost_estimate=cost(4 * count * CAP * tok_rows * wide, 4 * tok_rows * wide),
        name="combine",
    )(mix, hits, *blocks)


def local(tokens, cotangent, modality, picks, gate_weights, gate_proj, up_proj, down_proj):
    device_count = lax.axis_size("ep")
    groups = device_count // E_MOD
    modality = modality.reshape(1, -1)
    picks = picks.T
    weights = gate_weights.T

    def to_expert(x, s, t=0):
        return lax.ppermute(
            x,
            "ep",
            [
                (e * groups + j, (e ^ s) * groups + (j + t) % groups)
                for e in range(E_MOD)
                for j in range(groups)
            ],
        )

    def to_piece(x, t):
        return to_expert(x, 0, t)

    def to_source(x, s, flip):
        return lax.ppermute(
            x,
            ("ep", "mod"),
            [
                ((e * groups + j) * 2 + m, ((e ^ s) * groups + j) * 2 + (m ^ flip))
                for e in range(E_MOD)
                for j in range(groups)
                for m in range(2)
            ],
        )

    mix, hits = mixing(groups, modality, picks, weights)
    sent = gather_slots(groups, modality, picks, tokens, cotangent)
    far = [[to_expert(sent[2 * s - 2], s) for s in range(2, E_MOD)]]
    near = [sent[0], to_expert(sent[1], 1)]
    own_pieces = [to_piece(sent[0], t) for t in range(1, groups)]
    gate_piece = load(gate_proj, sent[:1])
    later = [sent[2 * s - 1] for s in range(2, E_MOD)]
    later = pass_after(later, in_vmem(gate_piece), *own_pieces)
    far.append([to_expert(x, s) for x, s in zip(later, range(2, E_MOD))])
    near_pieces = [[x, to_piece(near[1], t)] for t, x in enumerate(own_pieces, 1)]
    up_piece = load(up_proj, [near[1], in_vmem(gate_piece)])
    far[0] = join(far[0], in_vmem(gate_piece), in_vmem(up_piece))
    far[0] = [far[0]] + [to_piece(far[0], t) for t in range(1, groups)]
    down_piece = load_turned(down_proj, [far[0][0], *sum(near_pieces, []), in_vmem(gate_piece), in_vmem(up_piece)])
    far[1] = join(far[1], in_vmem(gate_piece), in_vmem(up_piece), in_vmem(down_piece))
    far[1] = [far[1]] + [to_piece(far[1], t) for t in range(1, groups)]
    near = near + sum(near_pieces, [])
    blocks = [near + far[a] for a in range(2)]
    places = [
        tuple(
            place
            for t in range(groups)
            for place in [(2 * t, a * CAP), (2 * t + 1, a * CAP)]
            + [(2 * groups + t, i * CAP) for i in range(E_MOD - 2)]
        )
        for a in range(2)
    ]
    factors = pre_activations(blocks[0], places[0], gate_piece, up_piece, down_piece)
    first, (dgate, dup, part) = hidden_grads(
        blocks[1], places[1], groups, factors, down_piece, gate_piece, up_piece
    )
    second = back_half(groups, dgate, dup, part, gate_piece, up_piece)
    first = [first[0]] + [to_piece(first[t], groups - t) for t in range(1, groups)]
    waiting = pass_after(second[1:], *first[1:])
    second = [second[0]] + [to_piece(x, groups - t) for t, x in enumerate(waiting, 1)]
    crossed, kept = sum_pieces(first), sum_pieces(second)
    arrived = {0: kept[0]}
    for s in range(1, E_MOD):
        arrived[s] = to_source(kept[s], s, 0)
    for s in range(E_MOD):
        arrived[E_MOD + s] = to_source(crossed[s], s, 1)
    order = tuple(reversed(arrived))
    token_grad, gate_grad = combine(order, mix, hits, [arrived[i] for i in order])
    return token_grad, gate_grad.reshape(-1, 1)


def solution(mesh):
    in_specs = (
        P(("parts", "ep"), None),
        P(("parts", "ep"), None),
        P(("parts", "ep")),
        P(("parts", "ep"), None),
        P(("parts", "ep"), None),
        P("mod", None, "ep"),
        P("mod", None, "ep"),
        P("mod", "ep", None),
    )
    out_specs = (P(("parts", "ep"), "mod"), P(("parts", "ep"), "mod"))
    return jax.shard_map(local, mesh=mesh, in_specs=in_specs, out_specs=out_specs, check_vma=False)
```

```python
import functools

import jax
import jax.numpy as jnp
from jax import lax
from jax.experimental import pallas as pl
from jax.experimental.pallas import tpu as pltpu
from jax.sharding import PartitionSpec as P

E_MOD = 4
CAP = 16
EXT = 128
BF16 = jnp.bfloat16
F32 = jnp.float32
MIB = 1024 * 1024
SCOPED = 10 * MIB


def cost(flops, nbytes):
    return pl.CostEstimate(flops=flops, bytes_accessed=nbytes, transcendentals=0)


def whole(shape):
    return pl.BlockSpec(shape, lambda *_: (0,) * len(shape))


def position(groups):
    return lax.axis_index("ep") // groups, lax.axis_index("mod")


def slot_of_labels(groups, modality_ref, picks_ref):
    tok_rows = modality_ref.shape[1]
    label = lax.broadcasted_iota(jnp.int32, (2 * E_MOD, tok_rows), 0)
    own_expert, core = position(groups)
    expert = jnp.bitwise_xor(label % E_MOD, own_expert)
    modal = jnp.bitwise_xor(label // E_MOD, core)
    mine = modality_ref[...] == modal
    first = mine & (picks_ref[0:1, :] == expert)
    second = mine & (picks_ref[1:2, :] == expert)
    member = first | second
    row = lax.broadcasted_iota(jnp.int32, (tok_rows, tok_rows), 0)
    col = lax.broadcasted_iota(jnp.int32, (tok_rows, tok_rows), 1)
    earlier = (row < col).astype(F32)
    count = jnp.dot(member.astype(F32), earlier, preferred_element_type=F32).astype(jnp.int32)
    return count, first, second, member


def gather_kernel(groups, parts, modality_hbm, picks_hbm, rows_hbm, grads_hbm, *refs):
    outs, (modality, picks, rows, chosen, sems) = refs[:-5], refs[-5:]
    chunk = rows.shape[2] // parts
    small = [
        pltpu.make_async_copy(src, dst, sems.at[i])
        for i, (src, dst) in enumerate([(modality_hbm, modality), (picks_hbm, picks)])
    ]
    large = [
        [
            pltpu.make_async_copy(
                src.at[:, pl.ds(i * chunk, chunk)],
                rows.at[a, :, pl.ds(i * chunk, chunk)],
                sems.at[2 + 2 * i + a],
            )
            for a, src in enumerate([rows_hbm, grads_hbm])
        ]
        for i in range(parts)
    ]
    for copy in small + sum(large, []):
        copy.start()
    for copy in small:
        copy.wait()
    count, _, _, member = slot_of_labels(groups, modality, picks)
    slot = jnp.where(member, count, -1)
    want = lax.broadcasted_iota(jnp.int32, (CAP, slot.shape[1]), 0)
    for s in range(E_MOD):
        hit = (slot[s : s + 1, :] == want).astype(F32)
        chosen[s * CAP : (s + 1) * CAP, :] = hit.astype(BF16)
    for i in range(parts):
        cols = slice(i * chunk, (i + 1) * chunk)
        for a in range(2):
            large[i][a].wait()
            picked = jnp.dot(chosen[...], rows[a, :, cols], preferred_element_type=F32).astype(BF16)
            for s in range(E_MOD):
                block = picked[s * CAP : (s + 1) * CAP, :]
                if s < 2:
                    outs[s][a * CAP : (a + 1) * CAP, cols] = block
                else:
                    outs[2 * s - 2 + a][:, cols] = block


def gather_slots(groups, modality, picks, rows, grads):
    tok_rows, width = rows.shape
    parts = 4
    heights = [2 * CAP] * 2 + [CAP] * (2 * E_MOD - 4)
    return pl.pallas_call(
        functools.partial(gather_kernel, groups, parts),
        in_specs=[pl.BlockSpec(memory_space=pl.ANY)] * 4,
        out_specs=[pl.BlockSpec(memory_space=pltpu.VMEM)] * len(heights),
        out_shape=[jax.ShapeDtypeStruct((h, width), BF16) for h in heights],
        scratch_shapes=[
            pltpu.VMEM(modality.shape, jnp.int32),
            pltpu.VMEM(picks.shape, jnp.int32),
            pltpu.VMEM((2, tok_rows, width), BF16),
            pltpu.VMEM((E_MOD * CAP, tok_rows), BF16),
            pltpu.SemaphoreType.DMA((2 + 2 * parts,)),
        ],
        compiler_params=pltpu.CompilerParams(vmem_limit_bytes=SCOPED),
        cost_estimate=cost(4 * E_MOD * CAP * tok_rows * width, 6 * tok_rows * width),
        name="gather_slots",
    )(in_hbm(modality), in_hbm(picks), in_hbm(rows), in_hbm(grads))


def load_kernel(parts, src, *refs):
    dst, sems = refs[-2:]
    rows = src.shape[1] // parts
    copies = [
        pltpu.make_async_copy(
            src.at[:, pl.ds(i * rows, rows), :], dst.at[:, pl.ds(i * rows, rows), :], sems.at[i]
        )
        for i in range(parts)
    ]
    for copy in copies:
        copy.start()
    for copy in copies:
        copy.wait()


def load(weight, after):
    parts = 8
    return pl.pallas_call(
        functools.partial(load_kernel, parts),
        in_specs=[pl.BlockSpec(memory_space=pl.ANY)] * (1 + len(after)),
        out_specs=pl.BlockSpec(memory_space=pltpu.VMEM),
        out_shape=pltpu.VMEM(weight.shape, weight.dtype),
        scratch_shapes=[pltpu.SemaphoreType.DMA((parts,))],
        compiler_params=pltpu.CompilerParams(vmem_limit_bytes=SCOPED),
        cost_estimate=cost(0, 1024),
        name="load",
    )(in_hbm(weight), *after)


def load_turned_kernel(parts, src, *refs):
    dst, stage, sems = refs[-3:]
    rows, width = stage.shape[1:]
    copies = [
        pltpu.make_async_copy(src.at[0, pl.ds(i * rows, rows), :], stage.at[i], sems.at[i])
        for i in range(parts)
    ]
    for copy in copies:
        copy.start()
    chunk = 512
    for i in range(parts):
        copies[i].wait()
        for start in range(0, width, chunk):
            block = stage[i, :, start : start + chunk]
            dst[start : start + chunk, i * rows : (i + 1) * rows] = block.T


def load_turned(weight, after):
    _, height, width = weight.shape
    rows = 128
    parts = height // rows
    return pl.pallas_call(
        functools.partial(load_turned_kernel, parts),
        in_specs=[pl.BlockSpec(memory_space=pl.ANY)] * (1 + len(after)),
        out_specs=pl.BlockSpec(memory_space=pltpu.VMEM),
        out_shape=pltpu.VMEM((width, height), weight.dtype),
        scratch_shapes=[
            pltpu.VMEM((parts, rows, width), weight.dtype),
            pltpu.SemaphoreType.DMA((parts,)),
        ],
        compiler_params=pltpu.CompilerParams(vmem_limit_bytes=SCOPED),
        cost_estimate=cost(0, 1024),
        name="load_turned",
    )(in_hbm(weight), *after)


def pass_kernel(*refs):
    pass


def pass_after(blocks, *need):
    place = pl.BlockSpec(memory_space=pl.ANY)
    return pl.pallas_call(
        pass_kernel,
        in_specs=[place] * (len(blocks) + len(need)),
        out_specs=[place] * len(blocks),
        out_shape=[jax.ShapeDtypeStruct(block.shape, block.dtype) for block in blocks],
        input_output_aliases={i: i for i in range(len(blocks))},
        compiler_params=pltpu.CompilerParams(vmem_limit_bytes=SCOPED),
        cost_estimate=cost(0, 1024),
        name="pass_after",
    )(*blocks, *need)


def join_kernel(count, *refs):
    blocks, out = refs[:count], refs[-1]
    start = 0
    for block in blocks:
        out[start : start + block.shape[0], :] = block[...]
        start += block.shape[0]


def join(blocks, *need):
    count = len(blocks)
    total = sum(block.shape[0] for block in blocks)
    vmem = pl.BlockSpec(memory_space=pltpu.VMEM)
    return pl.pallas_call(
        functools.partial(join_kernel, count),
        in_specs=[vmem] * count + [pl.BlockSpec(memory_space=pl.ANY)] * len(need),
        out_specs=vmem,
        out_shape=jax.ShapeDtypeStruct((total, blocks[0].shape[1]), BF16),
        compiler_params=pltpu.CompilerParams(vmem_limit_bytes=SCOPED),
        cost_estimate=cost(3 * 10**9, 1024),
        name="join",
    )(*blocks, *need)


def in_hbm(x):
    return pltpu.with_memory_space_constraint(x, pltpu.HBM)


def in_vmem(x):
    return pltpu.with_memory_space_constraint(x, pltpu.VMEM)


def fill(rows, refs, places):
    for i, (index, start) in enumerate(places):
        rows[i * CAP : (i + 1) * CAP, :] = refs[index][start : start + CAP, :]


def pre_kernel(count, places, *refs):
    blocks, (gate_ref, up_ref, _, act_out, slope_out, both_out, rows) = refs[:count], refs[count:]
    fill(rows, blocks, places)
    hidden = gate_ref.shape[2]
    chunk = min(512, hidden)
    for start in range(0, hidden, chunk):
        cols = slice(start, start + chunk)
        gate_pre = jnp.dot(rows[...], gate_ref[0, :, cols], preferred_element_type=F32)
        up_pre = jnp.dot(rows[...], up_ref[0, :, cols], preferred_element_type=F32)
        sig = jax.nn.sigmoid(gate_pre)
        act = gate_pre * sig
        act_out[:, cols] = act
        slope_out[:, cols] = up_pre * (sig * (1.0 + gate_pre * (1.0 - sig)))
        both_out[:, cols] = act * up_pre


def pre_activations(blocks, places, gate_piece, up_piece, need):
    count = len(blocks)
    _, width, hidden = gate_piece.shape
    total = len(places) * CAP
    vmem = pl.BlockSpec(memory_space=pltpu.VMEM)
    return pl.pallas_call(
        functools.partial(pre_kernel, count, places),
        in_specs=[vmem] * (count + 2) + [pl.BlockSpec(memory_space=pl.ANY)],
        out_specs=[vmem] * 3,
        out_shape=[jax.ShapeDtypeStruct((total, hidden), F32)] * 3,
        scratch_shapes=[pltpu.VMEM((total, width), BF16)],
        compiler_params=pltpu.CompilerParams(vmem_limit_bytes=SCOPED),
        cost_estimate=cost(5 * 10**9, 1024),
        name="pre_activations",
    )(*blocks, in_vmem(gate_piece), in_vmem(up_piece), in_vmem(need))


def back_columns(groups, flip, dgate_ref, dup_ref, part, gate_ref, up_ref, outs):
    half = jnp.bitwise_xor(position(groups)[1], flip)
    wide = outs[0].shape[1] - EXT
    own_rows = outs[0].shape[0]
    dgate, dup = dgate_ref[...].T, dup_ref[...].T
    chunk = 1024
    for step in range(wide // chunk):
        rows = pl.ds(pl.multiple_of(half * wide + step * chunk, chunk), chunk)
        grad = jnp.dot(gate_ref[0, rows, :], dgate, preferred_element_type=F32)
        grad = grad + jnp.dot(up_ref[0, rows, :], dup, preferred_element_type=F32)
        grad = grad.T.astype(BF16)
        for t in range(groups):
            outs[t][:, step * chunk : (step + 1) * chunk] = grad[t * own_rows : (t + 1) * own_rows, :]
    for t in range(groups):
        outs[t][:, wide:] = part[t * own_rows : (t + 1) * own_rows, :]


def hidden_kernel(count, places, groups, *refs):
    blocks = refs[:count]
    act_ref, slope_ref, both_ref, down_ref, gate_ref, up_ref = refs[count : count + 6]
    outs = refs[count + 6 : count + 6 + groups]
    dgate, dup, part_out, rows = refs[count + 6 + groups :]
    fill(rows, blocks, places)
    hidden = gate_ref.shape[2]
    chunk = min(512, hidden)
    part = jnp.zeros((rows.shape[0], 1), F32)
    for start in range(0, hidden, chunk):
        cols = slice(start, start + chunk)
        grad = jnp.dot(rows[...], down_ref[:, cols], preferred_element_type=F32)
        part = part + jnp.sum(grad * both_ref[:, cols], axis=1, keepdims=True)
        dgate[:, cols] = (grad * slope_ref[:, cols]).astype(BF16)
        dup[:, cols] = (grad * act_ref[:, cols]).astype(BF16)
    part_out[...] = two_terms(part)
    back_columns(groups, 1, dgate, dup, part_out[...], gate_ref, up_ref, outs)


def hidden_grads(blocks, places, groups, factors, down_piece, gate_piece, up_piece):
    count = len(blocks)
    _, width, hidden = gate_piece.shape
    total = len(places) * CAP
    shape = (total // groups, width // 2 + EXT)
    vmem = pl.BlockSpec(memory_space=pltpu.VMEM)
    out = pl.pallas_call(
        functools.partial(hidden_kernel, count, places, groups),
        in_specs=[vmem] * (count + 6),
        out_specs=[vmem] * (groups + 3),
        out_shape=[jax.ShapeDtypeStruct(shape, BF16)] * groups
        + [jax.ShapeDtypeStruct((total, hidden), BF16)] * 2
        + [jax.ShapeDtypeStruct((total, EXT), BF16)],
        scratch_shapes=[pltpu.VMEM((total, width), BF16)],
        compiler_params=pltpu.CompilerParams(vmem_limit_bytes=SCOPED),
        cost_estimate=cost(4 * total * width * hidden, 4 * width * hidden),
        name="hidden_grads",
    )(*blocks, *factors, in_vmem(down_piece), in_vmem(gate_piece), in_vmem(up_piece))
    return out[:groups], out[groups:]


def back_kernel(groups, dgate_ref, dup_ref, part_ref, gate_ref, up_ref, *outs):
    back_columns(groups, 0, dgate_ref, dup_ref, part_ref[...], gate_ref, up_ref, outs)


def back_half(groups, dgate, dup, part, gate_piece, up_piece):
    _, width, hidden = gate_piece.shape
    total = dgate.shape[0]
    shape = (total // groups, width // 2 + EXT)
    vmem = pl.BlockSpec(memory_space=pltpu.VMEM)
    return pl.pallas_call(
        functools.partial(back_kernel, groups),
        in_specs=[vmem] * 5,
        out_specs=[vmem] * groups,
        out_shape=[jax.ShapeDtypeStruct(shape, BF16)] * groups,
        compiler_params=pltpu.CompilerParams(vmem_limit_bytes=SCOPED),
        cost_estimate=cost(2 * total * width * hidden, 2 * width * hidden),
        name="back_half",
    )(dgate, dup, part, in_vmem(gate_piece), in_vmem(up_piece))


def two_terms(value):
    high = value.astype(BF16).astype(F32)
    low = value - high
    lane = lax.broadcasted_iota(jnp.int32, (value.shape[0], EXT), 1)
    return jnp.where(lane == 0, high, jnp.where(lane == 1, low, 0.0)).astype(BF16)


def sum_kernel(groups, *refs):
    ins, outs = refs[:groups], refs[groups:]
    wide = ins[0].shape[1] - EXT
    for s in range(E_MOD):
        rows = slice(s * CAP, (s + 1) * CAP)
        total = ins[0][rows, :].astype(F32)
        for t in range(1, groups):
            total = total + ins[t][rows, :].astype(F32)
        outs[s][:, :wide] = total[:, :wide].astype(BF16)
        outs[s][:, wide:] = two_terms(jnp.sum(total[:, wide:], axis=1, keepdims=True))


def sum_pieces(partials):
    groups = len(partials)
    own_rows, wide = partials[0].shape
    return pl.pallas_call(
        functools.partial(sum_kernel, groups),
        out_shape=[jax.ShapeDtypeStruct((CAP, wide), BF16)] * E_MOD,
        cost_estimate=cost(own_rows * wide, 4 * groups * own_rows * wide),
        compiler_params=pltpu.CompilerParams(vmem_limit_bytes=SCOPED),
        name="sum_pieces",
    )(*partials)


def mix_kernel(groups, modality_ref, picks_ref, weights_ref, mix_out, gate_out):
    count, first, second, member = slot_of_labels(groups, modality_ref, picks_ref)
    slot = jnp.where(member, count, -1)
    scale = jnp.where(first, weights_ref[0:1, :], jnp.where(second, weights_ref[1:2, :], 0.0))
    own = jnp.where(position(groups)[1] == 0, first.astype(F32), second.astype(F32))
    want = lax.broadcasted_iota(jnp.int32, (CAP, slot.shape[1]), 0)
    mix = []
    for i in range(2 * E_MOD):
        hit = slot[i : i + 1, :] == want
        mix.append(jnp.where(hit, scale[i : i + 1, :], 0.0))
        gate_out[i * CAP : (i + 1) * CAP, :] = jnp.where(hit, own[i : i + 1, :], 0.0)
    mix = jnp.concatenate(mix, axis=0).T
    high = mix.astype(BF16)
    mix_out[0] = high
    mix_out[1] = (mix - high.astype(F32)).astype(BF16)


def mixing(groups, modality, picks, weights):
    tok_rows = modality.shape[1]
    slots = 2 * E_MOD * CAP
    vmem = pl.BlockSpec(memory_space=pltpu.VMEM)
    return pl.pallas_call(
        functools.partial(mix_kernel, groups),
        in_specs=[vmem] * 3,
        out_specs=[vmem] * 2,
        out_shape=[
            jax.ShapeDtypeStruct((2, tok_rows, slots), BF16),
            jax.ShapeDtypeStruct((slots, tok_rows), F32),
        ],
        compiler_params=pltpu.CompilerParams(vmem_limit_bytes=SCOPED),
        cost_estimate=cost(MIB, 1024),
        name="mixing",
    )(modality, picks, weights)


def combine_kernel(order, mix_ref, hit_ref, *refs):
    blocks, (grad_out, gate_out, table) = refs[: len(order)], refs[len(order) :]
    wide = grad_out.shape[1]
    for i, block in zip(order, blocks):
        table[i * CAP : (i + 1) * CAP, :] = block[...]
    part = jnp.sum(table[:, wide:].astype(F32), axis=1, keepdims=True)
    gate_out[...] = jnp.sum(hit_ref[...] * part, axis=0, keepdims=True)
    total = jnp.dot(mix_ref[0], table[:, :wide], preferred_element_type=F32)
    total = total + jnp.dot(mix_ref[1], table[:, :wide], preferred_element_type=F32)
    grad_out[...] = total.astype(BF16)


def combine(order, mix, hits, blocks):
    tok_rows = hits.shape[1]
    wide = blocks[0].shape[1] - EXT
    count = len(blocks)
    vmem = pl.BlockSpec(memory_space=pltpu.VMEM)
    return pl.pallas_call(
        functools.partial(combine_kernel, order),
        in_specs=[vmem] * (2 + count),
        out_specs=[vmem] * 2,
        out_shape=[
            jax.ShapeDtypeStruct((tok_rows, wide), BF16),
            jax.ShapeDtypeStruct((1, tok_rows), F32),
        ],
        scratch_shapes=[pltpu.VMEM((count * CAP, wide + EXT), BF16)],
        compiler_params=pltpu.CompilerParams(vmem_limit_bytes=SCOPED),
        cost_estimate=cost(4 * count * CAP * tok_rows * wide, 4 * tok_rows * wide),
        name="combine",
    )(mix, hits, *blocks)


def local(tokens, cotangent, modality, picks, gate_weights, gate_proj, up_proj, down_proj):
    device_count = lax.axis_size("ep")
    groups = device_count // E_MOD
    modality = modality.reshape(1, -1)
    picks = picks.T
    weights = gate_weights.T

    def to_expert(x, s, t=0):
        return lax.ppermute(
            x,
            "ep",
            [
                (e * groups + j, (e ^ s) * groups + (j + t) % groups)
                for e in range(E_MOD)
                for j in range(groups)
            ],
        )

    def to_piece(x, t):
        return to_expert(x, 0, t)

    def to_source(x, s, flip):
        return lax.ppermute(
            x,
            ("ep", "mod"),
            [
                ((e * groups + j) * 2 + m, ((e ^ s) * groups + j) * 2 + (m ^ flip))
                for e in range(E_MOD)
                for j in range(groups)
                for m in range(2)
            ],
        )

    mix, hits = mixing(groups, modality, picks, weights)
    sent = gather_slots(groups, modality, picks, tokens, cotangent)
    far = [[to_expert(sent[2 * s - 2], s) for s in range(2, E_MOD)]]
    near = [sent[0], to_expert(sent[1], 1)]
    own_pieces = [to_piece(sent[0], t) for t in range(1, groups)]
    gate_piece = load(gate_proj, sent[:1])
    later = [sent[2 * s - 1] for s in range(2, E_MOD)]
    later = pass_after(later, in_vmem(gate_piece), *own_pieces)
    far.append([to_expert(x, s) for x, s in zip(later, range(2, E_MOD))])
    near_pieces = [[x, to_piece(near[1], t)] for t, x in enumerate(own_pieces, 1)]
    up_piece = load(up_proj, [near[1], in_vmem(gate_piece)])
    far[0] = join(far[0], in_vmem(gate_piece), in_vmem(up_piece))
    far[0] = [far[0]] + [to_piece(far[0], t) for t in range(1, groups)]
    down_piece = load_turned(down_proj, [far[0][0], *sum(near_pieces, []), in_vmem(gate_piece), in_vmem(up_piece)])
    far[1] = join(far[1], in_vmem(gate_piece), in_vmem(up_piece), in_vmem(down_piece))
    far[1] = [far[1]] + [to_piece(far[1], t) for t in range(1, groups)]
    near = near + sum(near_pieces, [])
    blocks = [near + far[a] for a in range(2)]
    places = [
        tuple(
            place
            for t in range(groups)
            for place in [(2 * t, a * CAP), (2 * t + 1, a * CAP)]
            + [(2 * groups + t, i * CAP) for i in range(E_MOD - 2)]
        )
        for a in range(2)
    ]
    factors = pre_activations(blocks[0], places[0], gate_piece, up_piece, down_piece)
    first, (dgate, dup, part) = hidden_grads(
        blocks[1], places[1], groups, factors, down_piece, gate_piece, up_piece
    )
    second = back_half(groups, dgate, dup, part, gate_piece, up_piece)
    first = [first[0]] + [to_piece(first[t], groups - t) for t in range(1, groups)]
    waiting = pass_after(second[1:], *first[1:])
    second = [second[0]] + [to_piece(x, groups - t) for t, x in enumerate(waiting, 1)]
    crossed, kept = sum_pieces(first), sum_pieces(second)
    arrived = {0: kept[0]}
    for s in range(1, E_MOD):
        arrived[s] = to_source(kept[s], s, 0)
    for s in range(E_MOD):
        arrived[E_MOD + s] = to_source(crossed[s], s, 1)
    order = tuple(reversed(arrived))
    token_grad, gate_grad = combine(order, mix, hits, [arrived[i] for i in order])
    return token_grad, gate_grad.reshape(-1, 1)


def solution(mesh):
    in_specs = (
        P(("parts", "ep"), None),
        P(("parts", "ep"), None),
        P(("parts", "ep")),
        P(("parts", "ep"), None),
        P(("parts", "ep"), None),
        P("mod", None, "ep"),
        P("mod", None, "ep"),
        P("mod", "ep", None),
    )
    out_specs = (P(("parts", "ep"), "mod"), P(("parts", "ep"), "mod"))
    return jax.shard_map(local, mesh=mesh, in_specs=in_specs, out_specs=out_specs, check_vma=False)
```
